32 devices in a mesh: dp: 8 (over z, y), tensor: 4 (over x, core).
Axes of the slice: x: 2, y: 2, z: 4, core: 2. Of those that a mesh axis runs over, the one named last changes fastest.
Arguments:
- tokens: bfloat16 [4096, 768], P('dp'), may hold values from -6 to 6
- cotangent: bfloat16 [4096, 768], P('dp'), may hold values from -6 to 6
- gain_attn: float32 [768], replicated, may hold values from 0.5 to 1.5
- w_qkv: bfloat16 [768, 2304], P(None, 'tensor'), may hold values from -0.21875 to 0.21875
- w_out: bfloat16 [768, 768], P('tensor'), may hold values from -1.75 to 1.75
- gain_ffn: float32 [768], replicated, may hold values from 0.5 to 1.5
- w_router: bfloat16 [768, 16], replicated, may hold values from -0.15625 to 0.15625
- w_shared_gate: bfloat16 [768, 2048], P(None, 'tensor'), may hold values from -0.21875 to 0.21875
- w_shared_up: bfloat16 [768, 2048], P(None, 'tensor'), may hold values from -0.21875 to 0.21875
- w_shared_down: bfloat16 [2048, 768], P('tensor'), may hold values from -0.125 to 0.125
- routed_gate_weight: bfloat16 [768, 32768], P(None, ('dp', 'tensor')), may hold values from -0.21875 to 0.21875
- routed_up_weight: bfloat16 [768, 32768], P(None, ('dp', 'tensor')), may hold values from -0.21875 to 0.21875
- w_expert_down: bfloat16 [32768, 768], P(('dp', 'tensor')), may hold values from -0.125 to 0.125
- seq_lengths: int32 [8, 8], P('dp'), may hold values from 0 to 512, as said below
- token_order: int32 [4096], P('dp'), may hold values from 0 to 4095, as said below
- inverse_order: int32 [4096], P('dp'), may hold values from 0 to 4095, as said below
- routes: int32 [4096, 2], P('dp'), may hold values from 0 to 15, all different within a row; in each aligned block of 512 rows (0 to 511, 512 to 1023, ...) at most 128 rows name the same one
- fill_order: int32 [8, 1024], P('dp'), may hold values from 0 to 1023, each once within a row
Outputs:
- out: bfloat16 [4096, 768], P('dp')
- grad_tokens: bfloat16 [4096, 768], P('dp')
- grad_gain_attn: float32 [768], P('dp')
- grad_w_qkv: float32 [768, 2304], P('dp', 'tensor')
- grad_w_out: float32 [768, 768], P('tensor', 'dp')
- grad_gain_ffn: float32 [768], P('dp')
- grad_w_router: float32 [768, 16], P('dp')
- grad_w_shared_gate: float32 [768, 2048], P('dp', 'tensor')
- grad_w_shared_up: float32 [768, 2048], P('dp', 'tensor')
- grad_w_shared_down: float32 [2048, 768], P('tensor', 'dp')
- grad_w_expert_gate: float32 [768, 32768], P(None, ('dp', 'tensor'))
- routed_up_weight_gradient: float32 [768, 32768], P(None, ('dp', 'tensor'))
- grad_w_expert_down: float32 [32768, 768], P(('dp', 'tensor'))
The draws below stay inside these ranges and needn't reach their ends.
Inputs may be any that keep to these rules, and one draw needn't show every extreme that they name: `token_order`: each block of 512 balanced positions takes the same number of tokens from every block of 512 initial positions, and the tokens that go from one such block to another keep their order. The inverse of token_order: token_order[inverse_order[t]] = t. `seq_lengths`: each row sums to 512; a zero is an unused entry; some row is one sequence of 512 tokens. `routes`: A row names two different experts; in the rows of one block of 512 balanced positions no expert is named more than 128 times, a bound that some block reaches. `fill_order`: each row is a permutation of its block's pair indices.
All inputs are finite; a program needn't handle non-finite values.
Results may differ from the reference program's by a relative error of at most 0.014.
The reference program's roundings to bfloat16 on the way count: a program that leaves them out, or rounds other values in their place, can miss the bound.
Values may be sent and summed in bfloat16 or wider, within the bound.
No kernel may reach another device: no remote copies, remote signals or barrier semaphores. Data moves between devices by JAX's collectives and lax.ppermute only.
A program may use at most 256 MiB of HBM per device.

```python
import math
import jax
import jax.numpy as jnp
import numpy as np
from jax import lax

MODEL_WIDTH = 768
HEADS = 12
HD = 64
EXPERT_HIDDEN = 2048
SFF = 2048
ROUTED_EXPERTS = 16
TOK_DEV = 512
SEQ_SLOTS = 8
TOKENS = 4096
GROUPS = 2
SLOT = 128
CAP = 640


def order_tables(key):
    key = jax.random.fold_in(key, 17)
    devices_dp = TOKENS // TOK_DEV
    block_rows = TOK_DEV // devices_dp
    source_key, target_key = jax.random.split(key)
    labels = jnp.repeat(jnp.arange(devices_dp, dtype=jnp.int32), block_rows)
    shuffle = jax.vmap(lambda sub_key: jax.random.permutation(sub_key, labels))
    target_of = shuffle(jax.random.split(source_key, devices_dp))
    source_of = shuffle(jax.random.split(target_key, devices_dp))
    source_sorted = jnp.argsort(target_of, axis=1, stable=True).astype(jnp.int32)
    target_sorted = jnp.argsort(source_of, axis=1, stable=True).astype(jnp.int32)
    device_ids = jnp.arange(devices_dp, dtype=jnp.int32)[:, None]
    token_ids = (device_ids * TOK_DEV + source_sorted).reshape(-1)
    place_grid = (device_ids * TOK_DEV + target_sorted).reshape(devices_dp, devices_dp, block_rows)
    place_ids = jnp.transpose(place_grid, (1, 0, 2)).reshape(-1)
    inverse = jnp.zeros(TOKENS, jnp.int32).at[token_ids].set(place_ids)
    forward_pass = jnp.zeros(TOKENS, jnp.int32).at[place_ids].set(token_ids)
    return (forward_pass, inverse)


def draw_token_order(key, part):
    return order_tables(key)[0]


def draw_inverse_order(key, part):
    return order_tables(key)[1]


def draw_seq_lengths(key, part):
    key = jax.random.fold_in(key, 5)
    devices_dp = TOKENS // TOK_DEV
    cut_key, pick_key = jax.random.split(key)
    cuts = jnp.sort(jax.random.randint(cut_key, (devices_dp, SEQ_SLOTS - 1), 0, TOK_DEV + 1, dtype=jnp.int32), axis=1)
    edges = jnp.concatenate([jnp.zeros((devices_dp, 1), jnp.int32), cuts, jnp.full((devices_dp, 1), TOK_DEV, jnp.int32)], 1)
    lengths = edges[:, 1:] - edges[:, :-1]
    chosen = jax.random.randint(pick_key, (), 0, devices_dp, dtype=jnp.int32)
    single = jnp.zeros(SEQ_SLOTS, jnp.int32).at[0].set(TOK_DEV)
    picked = (jnp.arange(devices_dp, dtype=jnp.int32) == chosen)[:, None]
    return jnp.where(picked, single[None, :], lengths).astype(jnp.int32)


def with_spikes(values, rng, source, target, shards_of, factor):
    def block_of(dim):
        return (jnp.arange(values.shape[dim]) // (values.shape[dim] // shards_of)).reshape((-1,) + (1,) * (values.ndim - 1 - dim))

    one_side = jax.random.permutation(rng, shards_of)[block_of(target)]
    other_side = (block_of(target) + shards_of // 2) % shards_of
    return jnp.where((block_of(source) == one_side) | (block_of(source) == other_side), factor * values, values)


def block_levels(own_key, dims, shards, low, largest):
    factor_of, own = 1.0, jax.random.fold_in(own_key, 6)
    for axis_at, blocks in shards:
        heights = jnp.exp(jax.random.uniform(jax.random.fold_in(own, axis_at), (blocks,), jnp.float32, low / len(shards), largest / len(shards)))
        factor_of = factor_of * jnp.repeat(heights, dims[axis_at] // blocks).reshape([-1 if axis == axis_at else 1 for axis in range(len(dims))])
    return factor_of


def routed_block(own_key, own, number, rows, number_of, top, bound, slope):
    order = jax.random.permutation(own_key, number_of)
    packed, common = shares(number_of, rows * top, bound, slope, True), shares(number_of, rows * top, bound, slope, False)
    places = jnp.arange(number_of)

    def named(sizes, offset_by):
        used = int((sizes > 0).sum())
        fixed = max(1, used // 4)
        moved = fixed + (places - fixed + offset_by * (used - fixed)) % max(1, number_of - fixed)
        return jnp.zeros((number_of,), jnp.int32).at[order[jnp.where(places < fixed, places, moved)]].set(jnp.asarray(sizes, jnp.int32))

    sizes = jnp.where(number % 4 == 0, named(packed, number // 4), named(common, number - number // 4 - 1))
    mixed = jax.random.permutation(jax.random.fold_in(own, 3), number_of)
    giver, sink = mixed[0:number_of // 2 * 2:2], mixed[1:number_of // 2 * 2:2]
    slack = jnp.minimum(sizes[giver] - 1, bound - sizes[sink]) // 2
    slack = jnp.where((giver == order[0]) | (sink == order[0]) | (sizes[sink] == 0), 0, jnp.maximum(slack, 0))
    moved = jax.random.randint(jax.random.fold_in(own, 4), (number_of // 2,), 0, 1 << 20) % (slack + 1)
    sizes = sizes.at[giver].add(-moved).at[sink].add(moved)
    items = jnp.searchsorted(jnp.cumsum(sizes), jnp.arange(rows * top), side="right").astype(jnp.int32)
    listing = items.reshape(top, rows).T
    listing = listing[jax.random.permutation(jax.random.fold_in(own, 1), rows)]
    offset_by = jax.random.randint(jax.random.fold_in(own, 2), (rows, 1), 0, top)
    return jnp.take_along_axis(listing, (jnp.arange(top)[None, :] + offset_by) % top, axis=1)


def shares(count, total, most, lean, full):
    portions = [(1 << 20) // math.isqrt(standing ** lean) + 1 for standing in range(1, count + 1)]
    largest = most if full else min(most, max(-(-total // count), total * portions[0] // sum(portions)))
    least = 1 if total - largest >= count - 1 else 0
    given, rest = [largest] + [least] * (count - 1), total - largest - least * (count - 1)
    while rest > 0:
        free = [i for i in range(1, count) if given[i] < largest] or [i for i in range(1, count) if given[i] < most]
        pool, left = sum([portions[i] for i in free]), rest
        for i in free:
            addition = min(most - given[i], max(1, left * portions[i] // pool), rest)
            given[i] = given[i] + addition
            rest = rest - addition
    return np.array(given)


def centred(key, shape, scale, most, shards=(), kind=jnp.bfloat16):
    level = block_levels(key, shape, shards, -0.22, 0.18) if shards else 1.0
    values = jax.random.normal(key, shape, jnp.float32) * scale * level
    return jnp.minimum(jnp.maximum(values, -most), most).astype(kind)


def gaussian_with(rng, shape, width, bound, pieces, heavy, kind=jnp.bfloat16):
    values = width * jax.random.normal(rng, shape, jnp.float32)
    if pieces:
        values = values * block_levels(rng, shape, pieces, -0.22, 0.18)
    return jnp.clip(with_spikes(values, jax.random.fold_in(rng, 3), *heavy), -bound, bound).astype(kind)


def setup_inputs(seed: int = 0) -> dict:
    splits = jax.random.split(jax.random.key(seed), 19)
    tokens = centred(splits[0], (TOKENS, MODEL_WIDTH), 1.0, 6.0, ((0, 8),))
    cotangent = gaussian_with(splits[1], (TOKENS, MODEL_WIDTH), 1.0, 6.0, ((0, 8),), (0, 1, 8, 2.0))
    gain_attn = jnp.clip(1.0 + 0.1 * jax.random.normal(splits[2], (MODEL_WIDTH,), jnp.float32), 0.5, 1.5)
    w_qkv = centred(splits[3], (MODEL_WIDTH, HEADS * 3 * HD), MODEL_WIDTH ** -0.5, 0.21875, ((1, 4),))
    w_out = centred(splits[4], (HEADS * HD, MODEL_WIDTH), (HEADS * HD // 64) ** -0.5, 1.75, ((0, 4),))
    gain_ffn = jnp.clip(1.0 + 0.1 * jax.random.normal(splits[5], (MODEL_WIDTH,), jnp.float32), 0.5, 1.5)
    w_router = centred(splits[6], (MODEL_WIDTH, ROUTED_EXPERTS), (2 * MODEL_WIDTH) ** -0.5, 0.15625)
    w_shared_gate = centred(splits[7], (MODEL_WIDTH, SFF), MODEL_WIDTH ** -0.5, 0.21875, ((1, 4),))
    w_shared_up = centred(splits[8], (MODEL_WIDTH, SFF), MODEL_WIDTH ** -0.5, 0.21875, ((1, 4),))
    w_shared_down = centred(splits[9], (SFF, MODEL_WIDTH), SFF ** -0.5, 0.125, ((0, 4),))
    routed_gate_weight = centred(splits[10], (MODEL_WIDTH, ROUTED_EXPERTS * EXPERT_HIDDEN), MODEL_WIDTH ** -0.5, 0.21875, ((1, 32),))
    routed_up_weight = centred(splits[11], (MODEL_WIDTH, ROUTED_EXPERTS * EXPERT_HIDDEN), MODEL_WIDTH ** -0.5, 0.21875, ((1, 32),))
    w_expert_down = centred(splits[12], (ROUTED_EXPERTS * EXPERT_HIDDEN, MODEL_WIDTH), EXPERT_HIDDEN ** -0.5, 0.125, ((0, 32),))
    seq_lengths = draw_seq_lengths(jax.random.fold_in(splits[18], 71), 0)
    token_order = draw_token_order(jax.random.fold_in(splits[18], 71), 0)
    inverse_order = draw_inverse_order(jax.random.fold_in(splits[18], 71), 0)
    routes_keys = jax.random.split(jax.random.fold_in(splits[16], 1), TOKENS // TOK_DEV)
    routes_turns = jax.random.permutation(jax.random.fold_in(splits[16], 3), TOKENS // TOK_DEV)
    routes = jax.vmap(lambda own, number: routed_block(jax.random.fold_in(splits[16], 2), own, number, TOK_DEV, ROUTED_EXPERTS, 2, SLOT, 1))(routes_keys, routes_turns).reshape((TOKENS, 2))
    fill_order = jax.vmap(lambda own: jax.random.permutation(own, 2 * TOK_DEV))(jax.random.split(splits[17], (TOKENS // TOK_DEV))).reshape((TOKENS // TOK_DEV, 2 * TOK_DEV)).astype(jnp.int32)
    return {"tokens": tokens, "cotangent": cotangent, "gain_attn": gain_attn, "w_qkv": w_qkv, "w_out": w_out, "gain_ffn": gain_ffn, "w_router": w_router, "w_shared_gate": w_shared_gate, "w_shared_up": w_shared_up, "w_shared_down": w_shared_down, "routed_gate_weight": routed_gate_weight, "routed_up_weight": routed_up_weight, "w_expert_down": w_expert_down, "seq_lengths": seq_lengths, "token_order": token_order, "inverse_order": inverse_order, "routes": routes, "fill_order": fill_order}


@jax.custom_vjp
def low(v):
    return lax.optimization_barrier(v.astype(jnp.bfloat16)).astype(jnp.float32)

@jax.custom_vjp
def low_back(v):
    return v

def low_keep(v):
    return (low(v), None)

def low_pass(kept, grad):
    return (grad,)

def back_keep(v):
    return (v, None)

def back_low(kept, grad):
    return (low(grad),)
low.defvjp(low_keep, low_pass)
low_back.defvjp(back_keep, back_low)
highest = lax.Precision.HIGHEST
epsilon = 1e-06

def exact_dot(left, right):
    return jnp.dot(left, right, precision=highest, preferred_element_type=jnp.float32)

def rms_norm(values, gain):
    inverse_root = lax.rsqrt(lax.optimization_barrier(jnp.mean(values * values, -1, keepdims=True)) + epsilon)
    return values * inverse_root * gain

def rope_tables(positions, head_size):
    half_size = head_size // 2
    exponent = jnp.arange(half_size, dtype=jnp.float32) * (-2.0 / head_size)
    inverse_freq = jnp.power(10000.0, exponent)
    angles = positions.astype(jnp.float32)[:, None] * inverse_freq[None, :]
    return (jnp.cos(angles), jnp.sin(angles))

def rope_turn(values, cosine, sine):
    half_size = values.shape[-1] // 2
    first_half = values[..., :half_size]
    second_half = values[..., half_size:]
    return jnp.concatenate([first_half * cosine - second_half * sine, second_half * cosine + first_half * sine], -1)

def segment_layout(lengths_row, row_count):
    seq_ends = jnp.cumsum(lengths_row).astype(jnp.int32)
    local_places = jnp.arange(row_count, dtype=jnp.int32)
    passed = local_places[:, None] >= seq_ends[None, :]
    segment = lax.optimization_barrier(jnp.sum(passed.astype(jnp.int32), 1))
    seq_start = lax.optimization_barrier(jnp.max(jnp.where(passed, seq_ends[None, :], 0), 1)).astype(jnp.int32)
    return (segment, local_places - seq_start)

def slot_tables(routes, fill_order):
    devices_dp = TOKENS // TOK_DEV
    slot_rows = 4 * TOK_DEV // ROUTED_EXPERTS
    expert_token_rows = devices_dp * slot_rows
    pair_count = 2 * TOK_DEV
    pair_expert = jnp.take_along_axis(routes.reshape(devices_dp, pair_count), fill_order, 1)
    member = (pair_expert[:, :, None] == jnp.arange(ROUTED_EXPERTS, dtype=jnp.int32)[None, None, :]).astype(jnp.int32)
    pair_rank = lax.optimization_barrier(jnp.sum(jnp.cumsum(member, 1) * member, 2)) - 1
    counts = lax.optimization_barrier(jnp.sum(member, 1))
    earlier = jnp.take_along_axis(jnp.cumsum(counts, 0) - counts, pair_expert, 1)
    kept = (earlier + pair_rank < CAP).astype(jnp.float32)
    device_ids = jnp.arange(devices_dp, dtype=jnp.int32)[:, None]
    position = (pair_expert * expert_token_rows + device_ids * slot_rows + pair_rank).reshape(-1).astype(jnp.int32)
    pair_ids = (device_ids * pair_count + fill_order).reshape(-1).astype(jnp.int32)
    pair_slot = jnp.zeros(2 * TOKENS, jnp.int32).at[pair_ids].set(position).reshape(TOKENS, 2)
    slot_token = jnp.zeros(ROUTED_EXPERTS * expert_token_rows, jnp.int32).at[position].set(pair_ids // 2).reshape(ROUTED_EXPERTS, expert_token_rows)
    slot_keep = jnp.zeros(ROUTED_EXPERTS * expert_token_rows, jnp.float32).at[position].set(kept.reshape(-1)).reshape(ROUTED_EXPERTS, expert_token_rows)
    return (pair_slot, slot_token, slot_keep)

def attend_block(arrays, query_key_value_weight):
    normed_block, segment_block, cosine_block, sine_block = arrays
    row_count = normed_block.shape[0]
    projected = low_back(exact_dot(low(normed_block), query_key_value_weight)).reshape(row_count, HEADS, 3, HD)
    query = low(rope_turn(projected[:, :, 0], cosine_block, sine_block))
    keys = low(rope_turn(projected[:, :, 1], cosine_block, sine_block))
    values = low(projected[:, :, 2])
    places = jnp.arange(row_count, dtype=jnp.int32)
    allowed = (segment_block[:, None] == segment_block[None, :]) & (places[None, :] <= places[:, None])
    scores = low_back(jnp.einsum('qhd,khd->hqk', query, keys, precision=highest) * HD ** (-0.5))
    scores = jnp.where(allowed[None], scores, -1e+30)
    exponent_vals = jnp.exp(scores - lax.optimization_barrier(jnp.max(scores, -1, keepdims=True)))
    weights = exponent_vals / lax.optimization_barrier(jnp.sum(exponent_vals, -1, keepdims=True))
    mixed = jnp.einsum('hqk,khd->qhd', low(weights), values, precision=highest)
    return low(low_back(mixed)).reshape(row_count, HEADS * HD)

def expert_block(arrays, normed_low):
    token_ids, keep_column, gate_weight, up_weight, down_weight = arrays
    token_rows = normed_low[token_ids]
    piece_width = EXPERT_HIDDEN // GROUPS
    combined = jnp.zeros((token_rows.shape[0], token_rows.shape[1]), jnp.float32)
    for group_id in range(GROUPS):
        columns = slice(group_id * piece_width, (group_id + 1) * piece_width)
        entry_rows = low_back(token_rows)
        gate_value = low_back(exact_dot(entry_rows, gate_weight[:, columns]))
        up_value = low_back(exact_dot(entry_rows, up_weight[:, columns]))
        hidden = low(jax.nn.silu(gate_value) * up_value)
        combined = combined + low(low_back(exact_dot(hidden, down_weight[columns, :])))
    return combined * keep_column[:, None]

def reference(tokens, cotangent, gain_attn, w_qkv, w_out, gain_ffn, w_router, w_shared_gate, w_shared_up, w_shared_down, routed_gate_weight, routed_up_weight, w_expert_down, seq_lengths, token_order, inverse_order, routes, fill_order):
    devices_dp = TOKENS // TOK_DEV
    segment, position = jax.vmap(lambda lengths_row: segment_layout(lengths_row, TOK_DEV))(seq_lengths)
    cosine, sine = rope_tables(position.reshape(-1), HD)
    cosine = cosine.reshape(devices_dp, TOK_DEV, 1, HD // 2)
    sine = sine.reshape(devices_dp, TOK_DEV, 1, HD // 2)
    pair_slot, slot_token, slot_keep = slot_tables(routes, fill_order)
    balanced = tokens.astype(jnp.float32)[token_order]
    grad_out = cotangent.astype(jnp.float32)[token_order]

    def forward_pass(balanced_input, attention_gain, query_key_value_weight, output_weight, feedforward_gain, router_matrix, shared_gate_weight, shared_up_weight, shared_down_weight, expert_gate_weight, expert_up_weight, expert_down_weight):
        normed_attn = rms_norm(balanced_input, attention_gain).reshape(devices_dp, TOK_DEV, MODEL_WIDTH)
        mixed = lax.map(jax.checkpoint(lambda arrays: attend_block(arrays, query_key_value_weight)), (normed_attn, segment, cosine, sine))
        after_attn = balanced_input + low_back(exact_dot(mixed.reshape(TOKENS, HEADS * HD), output_weight))
        normed_low = low(rms_norm(after_attn, feedforward_gain))
        logits = low_back(exact_dot(normed_low, router_matrix))
        gates = jax.nn.softmax(jnp.take_along_axis(logits, routes, 1), -1)
        shared_gate = low_back(exact_dot(normed_low, shared_gate_weight))
        shared_up = low_back(exact_dot(normed_low, shared_up_weight))
        shared_out = low_back(exact_dot(low(jax.nn.silu(shared_gate) * shared_up), shared_down_weight))
        gate_stack = jnp.transpose(expert_gate_weight.reshape(MODEL_WIDTH, ROUTED_EXPERTS, EXPERT_HIDDEN), (1, 0, 2))
        stacked_up_weights = jnp.transpose(expert_up_weight.reshape(MODEL_WIDTH, ROUTED_EXPERTS, EXPERT_HIDDEN), (1, 0, 2))
        down_stack = expert_down_weight.reshape(ROUTED_EXPERTS, EXPERT_HIDDEN, MODEL_WIDTH)
        expert_out = lax.map(jax.checkpoint(lambda arrays: expert_block(arrays, normed_low)), (slot_token, slot_keep, gate_stack, stacked_up_weights, down_stack))
        picked = expert_out.reshape(-1, MODEL_WIDTH)[pair_slot]
        return after_attn + shared_out + lax.optimization_barrier(jnp.sum(gates[:, :, None] * picked, 1))
    weights_all = (gain_attn, w_qkv.astype(jnp.float32), w_out.astype(jnp.float32), gain_ffn, w_router.astype(jnp.float32), w_shared_gate.astype(jnp.float32), w_shared_up.astype(jnp.float32), w_shared_down.astype(jnp.float32), routed_gate_weight.astype(jnp.float32), routed_up_weight.astype(jnp.float32), w_expert_down.astype(jnp.float32))
    result, pullback = jax.vjp(forward_pass, balanced, *weights_all)
    grads = pullback(grad_out)
    final = result[inverse_order].astype(jnp.bfloat16)
    grad_tokens = grads[0][inverse_order].astype(jnp.bfloat16)
    return (final, grad_tokens, grads[1], grads[2], grads[3], grads[4], grads[5], grads[6], grads[7], grads[8], grads[9], grads[10], grads[11])
```

```python
import jax
import jax.numpy as jnp
from jax import lax
from jax.sharding import Mesh, PartitionSpec as P

HD = 64
EPSILON = 1e-06
BF = jnp.bfloat16
F32 = jnp.float32
DP = ("dz", "dy")
TP = ("hi", "lo")


def dot(left, right):
    return jnp.dot(left, right, preferred_element_type=F32)


def dot_t(left, right):
    return lax.dot_general(left, right, (((0,), (0,)), ((), ())), preferred_element_type=F32)


def dot_bt(left, right):
    return lax.dot_general(left, right, (((1,), (1,)), ((), ())), preferred_element_type=F32)


def swap(values, axis):
    return lax.ppermute(values, axis, [(0, 1), (1, 0)])


def gather_rel(values, axes):
    for axis in axes:
        values = jnp.concatenate([values, swap(values, axis)], 0)
    return values


def exchange(values):
    return lax.all_to_all(values, DP, split_axis=0, concat_axis=0, tiled=True)


def scatter_dp(grads):
    dz, dy = lax.axis_size("dz"), lax.axis_size("dy")
    my_z, my_y = lax.axis_index("dz"), lax.axis_index("dy")
    chunk = grads.shape[0] // (dz * dy)
    columns = grads.shape[1]
    view = grads.reshape(dz, dy, chunk, columns)
    keep = lax.dynamic_index_in_dim(view, my_y, 1, keepdims=False)
    send = lax.dynamic_index_in_dim(view, 1 - my_y, 1, keepdims=False).astype(BF)
    keep = keep + swap(send, "dy").astype(F32)
    step = 1
    while step < dz:
        view = keep.reshape(-1, 2, chunk, columns)
        bit = (my_z // step) % 2
        send = lax.dynamic_index_in_dim(view, 1 - bit, 1, keepdims=False).astype(BF)
        keep = lax.dynamic_index_in_dim(view, bit, 1, keepdims=False)
        got = lax.ppermute(send, "dz", [(i, i ^ step) for i in range(dz)])
        keep = keep + got.astype(F32)
        step *= 2
    return keep.reshape(chunk, columns)


def rope_tables(positions, head_size):
    half_size = head_size // 2
    exponent = jnp.arange(half_size, dtype=F32) * (-2.0 / head_size)
    inverse_freq = jnp.power(10000.0, exponent)
    angles = positions.astype(F32)[:, None] * inverse_freq[None, :]
    return (jnp.cos(angles), jnp.sin(angles))


def rope_turn(values, cosine, sine):
    half_size = values.shape[-1] // 2
    first_half = values[..., :half_size]
    second_half = values[..., half_size:]
    return jnp.concatenate(
        [first_half * cosine - second_half * sine, second_half * cosine + first_half * sine], -1
    )


def rope_back(grads, cosine, sine):
    half_size = grads.shape[-1] // 2
    first_half = grads[..., :half_size]
    second_half = grads[..., half_size:]
    return jnp.concatenate(
        [first_half * cosine + second_half * sine, second_half * cosine - first_half * sine], -1
    )


def segment_layout(lengths_row, row_count):
    seq_ends = jnp.cumsum(lengths_row)
    local_places = jnp.arange(row_count, dtype=jnp.int32)
    passed = local_places[:, None] >= seq_ends[None, :]
    segment = jnp.sum(passed.astype(jnp.int32), 1)
    seq_start = jnp.max(jnp.where(passed, seq_ends[None, :], 0), 1)
    return (segment, local_places - seq_start)


def inverse_root(values):
    return lax.rsqrt(jnp.mean(values * values, -1, keepdims=True) + EPSILON)


def rms_backward(values, root, gain, grad_normed):
    scaled = grad_normed * gain
    return root * scaled - values * root**3 * jnp.mean(scaled * values, -1, keepdims=True)


def silu_parts(gate_in):
    sigmoid_val = jax.nn.sigmoid(gate_in)
    return (gate_in * sigmoid_val, sigmoid_val * (1.0 + gate_in * (1.0 - sigmoid_val)))


def bucket_rank(buckets, bucket_count):
    count = buckets.shape[0]
    member = (buckets[:, None] == jnp.arange(bucket_count, dtype=jnp.int32)[None, :]).astype(BF)
    places = jnp.arange(count, dtype=jnp.int32)
    earlier = (places[None, :] < places[:, None]).astype(BF)
    return jnp.sum(dot(earlier, member) * member.astype(F32), 1).astype(jnp.int32)


def on_device(
    tokens,
    cotangent,
    gain_attn,
    w_qkv,
    w_out,
    gain_ffn,
    w_router,
    w_shared_gate,
    w_shared_up,
    w_shared_down,
    routed_gate_weight,
    routed_up_weight,
    w_expert_down,
    seq_lengths,
    token_order,
    inverse_order,
    routes,
    fill_order,
):
    devices_dp = lax.axis_size(DP)
    devices_tp = lax.axis_size(TP)
    row_count, width = tokens.shape
    block_rows = row_count // devices_dp
    shard_block = block_rows // devices_tp
    shard_rows = row_count // devices_tp
    half_rows = row_count // 2
    experts_all = w_router.shape[1]
    slot_rows = 4 * row_count // experts_all
    capacity = 5 * row_count * devices_dp // (2 * experts_all)
    heads = w_out.shape[0] // HD
    per_dp = max(1, experts_all // devices_dp)
    copies = max(1, devices_dp // experts_all)
    sub_axes = ("lo",) if per_dp == 2 else TP
    sub = devices_tp // per_dp
    my_hi, my_lo = lax.axis_index("hi"), lax.axis_index("lo")
    my_dp = lax.axis_index(DP)
    my_block = my_lo * 2 + my_hi
    pick = my_hi if per_dp == 2 else 0
    my_part = my_lo if per_dp == 2 else my_block
    part_rows = slot_rows // sub
    my_expert = my_dp // copies * per_dp + pick
    ints = jnp.int32

    def relative(block, rank):
        return (
            ((rank // shard_block) ^ my_block) * shard_rows
            + block * shard_block
            + rank % shard_block
        )

    target = inverse_order // row_count
    anchor_row = relative(target, bucket_rank(target, devices_dp))
    all_rows = jnp.arange(row_count, dtype=ints)
    pick_own = (anchor_row[None, :] == all_rows[:shard_rows, None]).astype(BF)
    sent_tokens = dot(pick_own, tokens).astype(BF).reshape(devices_dp, shard_block, width)
    sent_cotangent = dot(pick_own, cotangent).astype(BF).reshape(devices_dp, shard_block, width)
    own_tokens = exchange(sent_tokens).reshape(shard_rows, width)
    own_cotangent = exchange(sent_cotangent).reshape(shard_rows, width)
    low_tokens = gather_rel(own_tokens, TP)
    grad_low = gather_rel(own_cotangent, TP)

    source = token_order // row_count
    local_row = relative(source, bucket_rank(source, devices_dp))
    place_pick = local_row[None, :] == all_rows[:, None]
    segment_in, place_in = segment_layout(seq_lengths[0], row_count)
    segment = jnp.sum(jnp.where(place_pick, segment_in[None, :], 0), 1)
    place = jnp.sum(jnp.where(place_pick, place_in[None, :], 0), 1)
    fill = fill_order[0]
    fill_place = (fill % 2) * row_count + fill // 2
    fill_pick = (
        fill_place[:, None] == jnp.arange(2 * row_count, dtype=ints)[None, :]
    ).astype(BF)
    expert_ids = jnp.arange(experts_all, dtype=ints)
    pair_expert = jnp.concatenate([routes[:, 0], routes[:, 1]])
    member = dot(fill_pick, (pair_expert[:, None] == expert_ids[None, :]).astype(BF))
    pair_places = jnp.arange(2 * row_count, dtype=ints)
    earlier = (pair_places[None, :] < pair_places[:, None]).astype(BF)
    ranks = (member * (dot(earlier, member.astype(BF)) + 1.0)).astype(BF)
    pair_ranks = dot_t(fill_pick, ranks)
    token_ranks = (pair_ranks[:row_count] + pair_ranks[row_count:]).astype(BF)
    place_low = place_pick.astype(BF)
    row_ranks = dot(place_low, token_ranks).astype(ints)
    expert_sums = dot(
        place_low, jnp.broadcast_to((routes[:, :1] + routes[:, 1:] + 1), (row_count, 128)).astype(BF)
    ).astype(BF)
    target_expert = jnp.arange(devices_dp, dtype=ints) // copies * per_dp + pick
    target_ranks = jnp.sum(
        jnp.where(target_expert[:, None, None] == expert_ids[None, None, :], row_ranks[None], 0), 2
    )
    slots = my_part * part_rows + 1 + jnp.arange(part_rows, dtype=ints)
    slot_pick = (
        (target_ranks[:, None, :] == slots[None, :, None])
        .astype(BF)
        .reshape(devices_dp * part_rows, row_count)
    )

    grad_wide = jnp.concatenate([grad_low, expert_sums], 1)
    sent_grads = dot(slot_pick, grad_wide).astype(BF)
    got_grads = exchange(sent_grads.reshape(devices_dp, part_rows, -1))
    got_grads = gather_rel(got_grads.reshape(devices_dp * part_rows, -1), sub_axes)

    balanced = low_tokens.astype(F32)
    root_attn = inverse_root(balanced)
    normed_attn_low = (balanced * root_attn * gain_attn).astype(BF)
    cosine, sine = rope_tables(place, HD)
    cosine = cosine[:, None, :]
    sine = sine[:, None, :]
    projected = dot(normed_attn_low, w_qkv).reshape(row_count, heads, 3, HD)
    query = rope_turn(projected[:, :, 0], cosine, sine).astype(BF)
    keys = rope_turn(projected[:, :, 1], cosine, sine).astype(BF)
    values = projected[:, :, 2].astype(BF)
    allowed = ((segment[:, None] == segment[None, :]) & (place[None, :] <= place[:, None]))[None]
    scale = HD**-0.5

    def score():
        scores = jnp.einsum("qhd,khd->hqk", query, keys, preferred_element_type=F32) * scale
        return jnp.where(allowed, scores, -1e30)

    scores = score()
    top_score = jnp.max(scores, -1, keepdims=True)
    exponent_vals = jnp.exp(scores - top_score)
    row_total = jnp.sum(exponent_vals, -1, keepdims=True)
    weights = exponent_vals / row_total
    mixed = jnp.einsum("hqk,khd->qhd", weights.astype(BF), values, preferred_element_type=F32)
    mixed_low = mixed.reshape(row_count, heads * HD).astype(BF)
    attn_part = dot(mixed_low, w_out)

    def half_sum(part):
        half = part[:half_rows] + swap(part[half_rows:].astype(BF), "lo").astype(F32)
        half = half.astype(BF)
        got = swap(jnp.concatenate([half[shard_rows:], half[:shard_rows]], 0), "hi")
        return half.astype(F32) + got.astype(F32)

    def own_sum(part):
        half = part[:half_rows] + swap(part[half_rows:].astype(BF), "lo").astype(F32)
        return half[:shard_rows] + swap(half[shard_rows:].astype(BF), "hi").astype(F32)

    after_attn = balanced[:half_rows] + half_sum(attn_part)
    root_ffn = inverse_root(after_attn)
    normed_low = gather_rel((after_attn * root_ffn * gain_ffn).astype(BF), ("lo",))

    sent_rows = dot(slot_pick, normed_low).astype(BF).reshape(devices_dp, part_rows, width)
    got_rows = exchange(sent_rows).reshape(devices_dp * part_rows, width)
    rows = gather_rel(got_rows, sub_axes)

    shared_gate = dot(normed_low, w_shared_gate)
    shared_up = dot(normed_low, w_shared_up)
    shared_act, shared_slope = silu_parts(shared_gate)
    shared_hidden = (shared_act * shared_up).astype(BF)
    shared_part = dot(shared_hidden, w_shared_down)
    shared_hidden_grad = dot_bt(grad_low, w_shared_down)
    grad_sgate = (shared_hidden_grad * shared_up * shared_slope).astype(BF)
    grad_sup = (shared_hidden_grad * shared_act).astype(BF)
    shared_normed_grad = dot_bt(grad_sgate, w_shared_gate) + dot_bt(grad_sup, w_shared_up)
    shared_grads = jnp.concatenate(
        [
            dot_t(normed_low, grad_sgate),
            dot_t(normed_low, grad_sup),
            dot_t(grad_low, shared_hidden),
        ],
        1,
    )

    grad_rows = got_grads[:, :width]
    other = got_grads[:, width : width + 1].astype(ints) - 1 - my_expert
    valid = got_grads[:, width : width + 1] > 0
    part_of = jnp.arange(sub, dtype=ints) ^ my_part
    order_key = (
        jnp.arange(devices_dp, dtype=ints)[None, :, None] * slot_rows
        + part_of[:, None, None] * part_rows
        + jnp.arange(part_rows, dtype=ints)[None, None, :]
    ).reshape(-1)
    before = (order_key[None, :] < order_key[:, None]).astype(BF)
    filled = dot(before, jnp.broadcast_to(valid, (valid.shape[0], 128)).astype(BF))[:, :1]
    kept = valid & (filled < capacity)
    logits = dot(rows, w_router)
    is_mine = (expert_ids == my_expert)[None, :]
    is_other = expert_ids[None, :] == other
    gap = jnp.sum(jnp.where(is_mine, logits, 0.0) - jnp.where(is_other, logits, 0.0), 1, keepdims=True)
    gate = jax.nn.sigmoid(gap)
    gate_other = jax.nn.sigmoid(-gap)
    expert_gate = dot(rows, routed_gate_weight)
    expert_up = dot(rows, routed_up_weight)
    expert_act, expert_slope = silu_parts(expert_gate)
    expert_hidden = (expert_act * expert_up).astype(BF)
    expert_part = dot(expert_hidden, w_expert_down).astype(BF)
    expert_part = jnp.where(kept, expert_part, jnp.zeros((), BF))
    pair_grads = jnp.where(kept, gate * grad_rows.astype(F32), 0.0).astype(BF)
    gate_grad = jnp.sum(expert_part.astype(F32) * grad_rows.astype(F32), 1, keepdims=True)
    chosen_grad = gate * gate_other * gate_grad
    logit_grad = (chosen_grad * (is_mine.astype(F32) - is_other.astype(F32))).astype(BF)
    hidden_grad = dot_bt(pair_grads, w_expert_down)
    grad_egate = (hidden_grad * expert_up * expert_slope).astype(BF)
    grad_eup = (hidden_grad * expert_act).astype(BF)
    row_grads = (dot_bt(grad_egate, routed_gate_weight) + dot_bt(grad_eup, routed_up_weight)).astype(
        BF
    ).astype(F32) + dot_bt(logit_grad, w_router)

    def sub_sum(part):
        for axis in reversed(sub_axes):
            half = part.shape[0] // 2
            part = part[:half].astype(F32) + swap(part[half:].astype(BF), axis).astype(F32)
        return part

    own_slots = devices_dp * part_rows
    back_grads = sub_sum(row_grads).astype(BF).reshape(devices_dp, part_rows, width)
    back_grads = exchange(back_grads).reshape(own_slots, width)
    back_parts = (gate[:own_slots] * sub_sum(expert_part)).astype(BF)
    back_parts = exchange(back_parts.reshape(devices_dp, part_rows, width)).reshape(
        own_slots, width
    )
    grad_w_expert_down = dot_t(expert_hidden, pair_grads)
    grad_w_expert_gate = dot_t(rows, grad_egate)
    grad_w_expert_up = dot_t(rows, grad_eup)
    router_part = dot_t(logit_grad, rows)

    normed_grad = half_sum(shared_normed_grad + dot_t(slot_pick, back_grads))
    grad_out = grad_low[:half_rows].astype(F32)
    after_grad = grad_out + rms_backward(after_attn, root_ffn, gain_ffn, normed_grad)
    after_grad_low = gather_rel(after_grad.astype(BF), ("lo",))
    gain_ffn_part = 0.5 * jnp.sum(normed_grad * after_attn * root_ffn, 0)

    ffn_total = own_sum(shared_part + dot_t(slot_pick, back_parts))
    result = (after_attn[:shard_rows] + ffn_total).astype(BF)

    grad_w_out = dot_t(after_grad_low, mixed_low)
    mixed_grad = dot_bt(after_grad_low, w_out).astype(BF).reshape(row_count, heads, HD)
    weight_grad = jnp.einsum("qhd,khd->hqk", mixed_grad, values, preferred_element_type=F32)
    row_delta = jnp.sum(weights * weight_grad, -1, keepdims=True)
    grad_scores = (weights * (weight_grad - row_delta)).astype(BF)
    query_grad = jnp.einsum("hqk,khd->qhd", grad_scores, keys, preferred_element_type=F32) * scale
    key_grad = jnp.einsum("hqk,qhd->khd", grad_scores, query, preferred_element_type=F32) * scale
    value_grad = jnp.einsum(
        "hqk,qhd->khd", weights.astype(BF), mixed_grad, preferred_element_type=F32
    )
    projected_grad = jnp.stack(
        [rope_back(query_grad, cosine, sine), rope_back(key_grad, cosine, sine), value_grad], 2
    )
    projected_grad = projected_grad.astype(BF).reshape(row_count, heads * 3 * HD)
    attn_grad_part = dot_bt(projected_grad, w_qkv)
    gain_attn_part = jnp.sum(attn_grad_part * balanced * root_attn, 0)
    attn_normed_grad = own_sum(attn_grad_part)
    input_grad = after_grad[:shard_rows] + rms_backward(
        balanced[:shard_rows], root_attn[:shard_rows], gain_attn, attn_normed_grad
    )
    grad_w_qkv = dot_t(normed_attn_low, projected_grad)

    def to_initial(own):
        got = exchange(own.reshape(devices_dp, shard_block, width)).reshape(shard_rows, width)
        got = gather_rel(got, TP)
        back_pick = (anchor_row[:, None] == all_rows[None, :]).astype(BF)
        return dot(back_pick, got).astype(BF)

    final = to_initial(result)
    grad_tokens = to_initial(input_grad.astype(BF))

    small = jnp.concatenate(
        [gain_ffn_part[None], gain_attn_part[None], router_part, jnp.zeros((6, width), F32)], 0
    )
    small = small + swap(small, "hi")
    small = small + swap(small, "lo")
    small = small.reshape(-1, devices_dp, width // devices_dp).transpose(1, 0, 2)
    small = jnp.sum(exchange(small), 0)
    grad_shared = scatter_dp(shared_grads)
    hidden = w_shared_gate.shape[1]
    return (
        final,
        grad_tokens,
        small[1],
        scatter_dp(grad_w_qkv),
        scatter_dp(grad_w_out).T,
        small[0],
        small[2 : 2 + experts_all].T,
        grad_shared[:, :hidden],
        grad_shared[:, hidden : 2 * hidden],
        grad_shared[:, 2 * hidden :].T,
        grad_w_expert_gate,
        grad_w_expert_up,
        grad_w_expert_down,
    )


def solution(mesh):
    devices_dp, devices_tp = mesh.shape["dp"], mesh.shape["tensor"]
    fine = Mesh(
        mesh.devices.reshape(devices_dp // 2, 2, devices_tp // 2, 2), ("dz", "dy", "hi", "lo")
    )
    every = DP + TP
    return jax.shard_map(
        on_device,
        mesh=fine,
        in_specs=(
            P(DP, None),
            P(DP, None),
            P(),
            P(None, TP),
            P(TP, None),
            P(),
            P(),
            P(None, TP),
            P(None, TP),
            P(TP, None),
            P(None, every),
            P(None, every),
            P(every, None),
            P(DP, None),
            P(DP),
            P(DP),
            P(DP, None),
            P(DP, None),
        ),
        out_specs=(
            P(DP, None),
            P(DP, None),
            P(DP),
            P(DP, TP),
            P(TP, DP),
            P(DP),
            P(DP, None),
            P(DP, TP),
            P(DP, TP),
            P(TP, DP),
            P(None, every),
            P(None, every),
            P(every, None),
        ),
        check_vma=False,
    )
```

```python
import functools

import jax
import jax.numpy as jnp
from jax import lax
from jax.experimental import pallas as pl
from jax.experimental.pallas import tpu as pltpu
from jax.sharding import Mesh, PartitionSpec as P

HD = 64
EPSILON = 1e-06
BF = jnp.bfloat16
F32 = jnp.float32
I32 = jnp.int32
DP = ("dz", "dy")
TP = ("hi", "lo")
MIB = 1 << 20
HEAD_PAD = 256


def dot(left, right):
    return jnp.dot(left, right, preferred_element_type=F32)


def dot_t(left, right):
    return lax.dot_general(left, right, (((0,), (0,)), ((), ())), preferred_element_type=F32)


def dot_bt(left, right):
    return lax.dot_general(left, right, (((1,), (1,)), ((), ())), preferred_element_type=F32)


def swap(values, axis):
    return lax.ppermute(values, axis, [(0, 1), (1, 0)])


def exchange(values):
    return lax.all_to_all(values, DP, split_axis=0, concat_axis=0, tiled=True)


def after(values, *others):
    return lax.optimization_barrier((values,) + others)[0]


def out(shape, dtype):
    return jax.ShapeDtypeStruct(shape, dtype)


def kernel(body, outs, *args, scalars=None, gflop=0.1, vmem=32):
    specs = [pl.BlockSpec(memory_space=pltpu.VMEM)] * len(args)
    if scalars is not None:
        specs = [pl.BlockSpec(memory_space=pltpu.SMEM)] + specs
        args = (scalars,) + args
    moved = sum(a.size * a.dtype.itemsize for a in args)
    moved += sum(o.size * o.dtype.itemsize for o in outs)
    return pl.pallas_call(
        body,
        out_shape=tuple(outs),
        in_specs=specs,
        out_specs=tuple([pl.BlockSpec(memory_space=pltpu.VMEM)] * len(outs)),
        compiler_params=pltpu.CompilerParams(vmem_limit_bytes=vmem * MIB),
        cost_estimate=pl.CostEstimate(
            flops=int(gflop * 1e9), bytes_accessed=int(moved), transcendentals=0
        ),
    )(*args)


def iota(shape, dim):
    return lax.broadcasted_iota(I32, shape, dim)


def log2(number):
    return number.bit_length() - 1


def silu_parts(gate_in):
    sigmoid_val = 1.0 / (1.0 + jnp.exp(-gate_in))
    return (gate_in * sigmoid_val, sigmoid_val * (1.0 + gate_in * (1.0 - sigmoid_val)))


def inverse_root(values):
    return lax.rsqrt(jnp.mean(values * values, -1, keepdims=True) + EPSILON)


def rms_backward(values, root, gain, grad_normed):
    scaled = grad_normed * gain
    return root * scaled - values * (root * root * root) * jnp.mean(
        scaled * values, -1, keepdims=True
    )


def lane_rank(buckets, bucket_count):
    count = buckets.shape[1]
    rows = max(8, bucket_count)
    member = (iota((rows, count), 0) == buckets).astype(F32)
    earlier = (iota((count, count), 0) < iota((count, count), 1)).astype(F32).astype(BF)
    return jnp.sum(dot(member.astype(BF), earlier) * member, 0, keepdims=True).astype(I32)


def relative_row(block, rank, my_block, shard_block, shard_rows):
    shift = log2(shard_block)
    return (
        ((rank >> shift) ^ my_block) * shard_rows
        + block * shard_block
        + (rank & (shard_block - 1))
    )


def rope_back(grads, cosine, sine):
    half = grads.shape[1] // 2
    return grads * cosine - jnp.concatenate([grads[:, half:], grads[:, :half]], 1) * sine


def select_body(shard_block, blocks, info, inverse, tokens, cotangent, sent, anchor):
    row_count, width = tokens.shape
    shard_rows = sent.shape[0]
    target = inverse[...] >> log2(row_count)
    row = relative_row(target, lane_rank(target, blocks), info[0], shard_block, shard_rows)
    anchor[...] = row
    pick = (iota((shard_rows, row_count), 0) == row).astype(F32).astype(BF)
    sent[:, :width] = dot(pick, tokens[...]).astype(BF)
    sent[:, width:] = dot(pick, cotangent[...]).astype(BF)


def index_body(
    shard_block,
    copies,
    per_dp,
    part_rows,
    experts_all,
    info,
    lengths,
    order,
    routes,
    fill,
    table,
    slot_pick,
    slot_pick_t,
    bias,
    cosine,
    sine,
    meta,
):
    row_count = order.shape[1]
    devices_dp = slot_pick.shape[0] // part_rows
    shard_rows = shard_block * devices_dp
    source = order[...] >> log2(row_count)
    local = relative_row(
        source, lane_rank(source, devices_dp), info[0], shard_block, shard_rows
    )
    place_pick = (iota((row_count, row_count), 0) == local).astype(F32).astype(BF)
    lanes = iota((1, row_count), 1)
    segment = jnp.zeros((1, row_count), I32)
    start = jnp.zeros((1, row_count), I32)
    end = jnp.int32(0)
    for entry in range(lengths.shape[1]):
        end = end + lengths[0, entry]
        passed = lanes >= end
        segment = segment + passed.astype(I32)
        start = jnp.maximum(start, jnp.where(passed, end, 0))
    place = lanes - start
    expert_sum = routes[0:1, :] + routes[1:2, :] + 1
    facts = jnp.concatenate(
        [segment, place >> 1, place & 1, expert_sum, jnp.zeros((4, row_count), I32)], 0
    )
    facts = facts.astype(F32).astype(BF)
    across = dot_bt(facts, place_pick)
    down = dot_bt(place_pick, facts)
    place_row = 2.0 * across[1:2] + across[2:3]
    place_col = 2.0 * down[:, 1:2] + down[:, 2:3]
    allowed = (down[:, 0:1] == across[0:1]) & (place_row <= place_col)
    bias[...] = jnp.where(allowed, 0.0, -1e30).astype(BF)
    at_place = (
        iota((row_count, row_count), 1).astype(F32) == place_col
    ).astype(F32).astype(BF)
    turned = dot(at_place, table[...])
    pieces = [turned[:, i * 128 : (i + 1) * 128] for i in range(3)]
    turned = pieces[0] + pieces[1] + pieces[2]
    cosine[...] = turned[:, :HD]
    sine[...] = turned[:, HD:]
    meta[...] = jnp.broadcast_to(down[:, 3:4], meta.shape).astype(BF)
    pairs = 2 * row_count
    fill_at = (fill[...] & 1) * row_count + (fill[...] >> 1)
    fill_pick = (iota((pairs, pairs), 0) == fill_at).astype(F32).astype(BF)
    expert_rows = max(16, experts_all)
    pair_expert = jnp.concatenate([routes[0:1, :], routes[1:2, :]], 1)
    named = (iota((expert_rows, pairs), 0) == pair_expert).astype(F32).astype(BF)
    member = dot(named, fill_pick)
    earlier = (iota((pairs, pairs), 0) < iota((pairs, pairs), 1)).astype(F32).astype(BF)
    ranks = (member * (dot(member.astype(BF), earlier) + 1.0)).astype(BF)
    ranks = dot_bt(ranks, fill_pick)
    ranks = (ranks[:, :row_count] + ranks[:, row_count:]).astype(BF)
    ranks = dot_bt(ranks, place_pick).astype(I32)
    first = info[2] * part_rows + 1
    slots = iota((part_rows, row_count), 0) + first
    for target in range(devices_dp):
        base = target // copies * per_dp
        chosen = ranks[base : base + 1]
        if per_dp == 2:
            chosen = jnp.where(info[1] == 0, chosen, ranks[base + 1 : base + 2])
        picked = (slots == chosen).astype(F32)
        slot_pick[target * part_rows : (target + 1) * part_rows, :] = picked.astype(BF)
    slot_pick_t[...] = slot_pick[...].astype(F32).T.astype(BF)


def send_grads_body(slot_pick, meta, b0, b1, b2, b3, sent):
    width = b0.shape[1] // 2
    grads = jnp.concatenate([b[:, width:] for b in (b0, b1, b2, b3)], 0)
    sent[:, :width] = dot(slot_pick[...], grads).astype(BF)
    sent[:, width:] = dot(slot_pick[...], meta[...]).astype(BF)


def attend_body(
    heads, gain, w_in, w_out, cosine, sine, bias, b0, b1, b2, b3, keep, send, qkv, mixed, normed
):
    width = b0.shape[1] // 2
    half = keep.shape[0]
    tokens = jnp.concatenate([b[:, :width] for b in (b0, b1, b2, b3)], 0).astype(F32)
    normed[...] = (tokens * inverse_root(tokens) * gain[...]).astype(BF)
    projected = dot(normed[...], w_in[...])
    inner = heads * HD
    turn_cos = jnp.concatenate([cosine[...]] * heads, 1)
    turn_sin = jnp.concatenate([sine[...]] * heads, 1)

    def group(index):
        return projected[:, index * HEAD_PAD : index * HEAD_PAD + inner]

    qkv[:, :inner] = (group(0) * turn_cos + group(3) * turn_sin).astype(BF)
    qkv[:, HEAD_PAD : HEAD_PAD + inner] = (group(1) * turn_cos + group(4) * turn_sin).astype(BF)
    qkv[:, 2 * HEAD_PAD : 2 * HEAD_PAD + inner] = group(2).astype(BF)
    scale = HD**-0.5
    mixed_heads = []
    for head in range(heads):
        at = head * HD
        query = qkv[:, at : at + HD]
        keys = qkv[:, HEAD_PAD + at : HEAD_PAD + at + HD]
        values = qkv[:, 2 * HEAD_PAD + at : 2 * HEAD_PAD + at + HD]
        scores = dot_bt(query, keys) * scale + bias[...].astype(F32)
        powers = jnp.exp(scores - jnp.max(scores, -1, keepdims=True))
        weights = powers * (1.0 / jnp.sum(powers, -1, keepdims=True))
        mixed_heads.append(dot(weights.astype(BF), values))
    mixed[...] = jnp.concatenate(mixed_heads, 1).astype(BF)
    part = dot(mixed[...], w_out[...])
    keep[...] = part[:half]
    send[...] = part[half:].astype(BF)


def fold_body(keep, got, half):
    half[...] = (keep[...] + got[...].astype(F32)).astype(BF)


def fold_own_body(keep, got, own, send):
    rows = own.shape[0]
    own[...] = keep[:rows, :] + got[:rows, :].astype(F32)
    send[...] = (keep[rows:, :] + got[rows:, :].astype(F32)).astype(BF)


def both(half, got):
    rows = half.shape[0] // 2
    mine, other = half[...].astype(F32), got[...].astype(F32)
    return mine + jnp.concatenate([other[rows:], other[:rows]], 0)


def norm_body(gain, half, got, b0, b1, after_attn, normed):
    width = half.shape[1]
    balanced = jnp.concatenate([b0[:, :width], b1[:, :width]], 0).astype(F32)
    values = balanced + both(half, got)
    after_attn[...] = values
    normed[...] = (values * inverse_root(values) * gain[...]).astype(BF)


def send_rows_body(slot_pick, own, got, sent):
    rows = jnp.concatenate([own[...], got[...]], 0)
    sent[...] = dot(slot_pick[...], rows).astype(BF)


def shared_body(
    own, got, b0, b1, b2, b3, w_gate, w_up, w_down, part, back, grad_gate, grad_up, hidden
):
    width = own.shape[1]
    rows = jnp.concatenate([own[...], got[...]], 0)
    grads = jnp.concatenate([b[:, width:] for b in (b0, b1, b2, b3)], 0)
    gate = dot(rows, w_gate[...])
    up = dot(rows, w_up[...])
    act, slope = silu_parts(gate)
    hidden[...] = (act * up).astype(BF)
    part[...] = dot(hidden[...], w_down[...])
    hidden_grad = dot_bt(grads, w_down[...])
    grad_gate[...] = (hidden_grad * up * slope).astype(BF)
    grad_up[...] = (hidden_grad * act).astype(BF)
    back[...] = dot_bt(grad_gate[...], w_gate[...]) + dot_bt(grad_up[...], w_up[...])


def split_store(bit, first, second, keep, send, index):
    mine = bit == 0
    keep[index] = jnp.where(mine, first, second)
    send[index] = jnp.where(mine, second, first).astype(BF)


def shared_grads_body(
    info, own, got, b0, b1, b2, b3, grad_gate, grad_up, hidden, keep, send
):
    width = own.shape[1]
    rows = jnp.concatenate([own[...], got[...]], 0)
    grads = jnp.concatenate([b[:, width:] for b in (b0, b1, b2, b3)], 0)
    columns = hidden.shape[1]
    high, _, chunk, _ = keep.shape
    for which, (left, right) in enumerate(
        ((rows, grad_gate[...]), (rows, grad_up[...]), (grads, hidden[...]))
    ):
        sums = dot_t(left, right)
        cols = slice(which * columns, (which + 1) * columns)
        for z in range(high):
            for y in range(2):
                at = (z * 4 + y) * chunk
                mine = info[3] == 0
                first, second = sums[at : at + chunk], sums[at + 2 * chunk : at + 3 * chunk]
                keep[z, y, :, cols] = jnp.where(mine, first, second)
                send[z, y, :, cols] = jnp.where(mine, second, first).astype(BF)


def product_grads_body(info, left, right, keep, send):
    sums = dot_t(left[...], right[...])
    high, _, chunk, _ = keep.shape
    for z in range(high):
        for y in range(2):
            at = (z * 4 + y) * chunk
            mine = info[3] == 0
            first, second = sums[at : at + chunk], sums[at + 2 * chunk : at + 3 * chunk]
            keep[z, y] = jnp.where(mine, first, second)
            send[z, y] = jnp.where(mine, second, first).astype(BF)


def tree_body(which, info, kept, got, keep, send):
    bit = info[which]
    total = kept[...] + got[...].astype(F32)
    pairs = total.shape[0]
    for index in range(pairs):
        mine = bit == 0
        first, second = total[index, 0], total[index, 1]
        keep[index] = jnp.where(mine, first, second)
        send[index] = jnp.where(mine, second, first).astype(BF)


def meta_body(devices_dp, part_rows, sub, capacity, info, own, got, marks):
    my_part, my_expert = info[2], info[4]
    lanes = iota((part_rows, 128), 1)
    blocks = [(ref, at, part) for part, (ref, at) in enumerate(
        [(own, i) for i in range(sub // 2)] + [(got, i) for i in range(sub // 2)]
    )]
    earlier = jnp.zeros((1, 128), F32)
    for block in range(devices_dp):
        total = earlier
        for ref, at, part in blocks:
            start = (at * devices_dp + block) * part_rows
            value = ref[start : start + part_rows, :].astype(F32)
            valid = value > 0.0
            slot = iota((part_rows, 128), 0) + (my_part ^ part) * part_rows
            kept = valid & (slot.astype(F32) + earlier < capacity)
            other = value.astype(I32) - 1 - my_expert
            mark = (lanes == my_expert).astype(F32) - (lanes == other).astype(F32)
            row = (part * devices_dp + block) * part_rows
            marks[row : row + part_rows, :] = jnp.where(
                lanes == 127, kept.astype(F32), jnp.where(valid, mark, 0.0)
            )
            total = total + jnp.sum(valid.astype(F32), 0, keepdims=True)
        earlier = total


def expert_body(
    tiles,
    rows_own,
    rows_got,
    grads_own,
    grads_got,
    marks,
    w_router,
    w_gate,
    w_up,
    w_down,
    back_keep,
    back_send,
    part_keep,
    part_send,
    rows_all,
    hidden_out,
    grad_gate_out,
    grad_up_out,
    pair_out,
    gates,
    router,
):
    step = pl.program_id(0)
    mine = step < tiles
    width = rows_own.shape[1]
    rows = jnp.where(mine, rows_own[...], rows_got[...])
    grads = jnp.where(mine, grads_own[...], grads_got[...])[:, :width].astype(F32)
    mark = marks[...]
    kept = mark[:, 127:128] > 0.5
    lanes = iota(mark.shape, 1)
    mark = jnp.where(lanes == 127, 0.0, mark)
    logits = dot(rows, w_router[...])
    gap = jnp.sum(logits * mark, 1, keepdims=True)
    gate = 1.0 / (1.0 + jnp.exp(-gap))
    gate_other = 1.0 / (1.0 + jnp.exp(gap))
    rows_all[...] = rows
    gates[...] = jnp.broadcast_to(gate, gates.shape)
    gate_in = dot(rows, w_gate[...])
    up = dot(rows, w_up[...])
    act, slope = silu_parts(gate_in)
    hidden = (act * up).astype(BF)
    hidden_out[...] = hidden
    part = jnp.where(kept, dot(hidden, w_down[...]), 0.0).astype(BF)
    pair = jnp.where(kept, gate * grads, 0.0).astype(BF)
    pair_out[...] = pair
    gate_grad = jnp.sum(part.astype(F32) * grads, 1, keepdims=True)
    logit_grad = (gate * gate_other * gate_grad * mark).astype(BF)
    hidden_grad = dot_bt(pair, w_down[...])
    grad_gate = (hidden_grad * up * slope).astype(BF)
    grad_up = (hidden_grad * act).astype(BF)
    grad_gate_out[...] = grad_gate
    grad_up_out[...] = grad_up
    back = (dot_bt(grad_gate, w_gate[...]) + dot_bt(grad_up, w_up[...])).astype(BF).astype(F32)
    back = back + dot_bt(logit_grad, w_router[...])

    @pl.when(step == 0)
    def _():
        router[...] = jnp.zeros_like(router)

    router[...] += dot_t(logit_grad, rows)

    @pl.when(mine)
    def _():
        back_keep[...] = back
        part_keep[...] = part

    @pl.when(jnp.logical_not(mine))
    def _():
        back_send[...] = back.astype(BF)
        part_send[...] = part


def part_body(keep, got, gates, total):
    gate = jnp.concatenate([gates[...]] * (keep.shape[1] // 128), 1)
    total[...] = (gate * (keep[...].astype(F32) + got[...].astype(F32))).astype(BF)


def combine_body(slot_pick_t, back, addend, keep, send):
    half = keep.shape[0]
    total = addend[...] + dot(slot_pick_t[...], back[...])
    keep[...] = total[:half]
    send[...] = total[half:].astype(BF)


def norm_back_body(gain, half, got, after_attn, b0, b1, after_grad, low, gain_grad):
    width = half.shape[1]
    normed_grad = both(half, got)
    values = after_attn[...]
    root = inverse_root(values)
    grads = jnp.concatenate([b0[:, width:], b1[:, width:]], 0).astype(F32)
    total = grads + rms_backward(values, root, gain[...], normed_grad)
    after_grad[...] = total
    low[...] = total.astype(BF)
    gain_grad[...] = jnp.broadcast_to(
        0.5 * jnp.sum(normed_grad * values * root, 0, keepdims=True), gain_grad.shape
    )


def attend_back_body(
    heads,
    w_out,
    w_in,
    cosine,
    sine,
    bias,
    qkv,
    own,
    got,
    b0,
    b1,
    b2,
    b3,
    keep,
    send,
    projected_grad,
    gain_grad,
):
    width = own.shape[1]
    half = keep.shape[0]
    inner = heads * HD
    grads = jnp.concatenate([own[...], got[...]], 0)
    mixed_grad = dot_bt(grads, w_out[...]).astype(BF)
    scale = HD**-0.5
    parts = [[], [], []]
    for head in range(heads):
        at = head * HD
        query = qkv[:, at : at + HD]
        keys = qkv[:, HEAD_PAD + at : HEAD_PAD + at + HD]
        values = qkv[:, 2 * HEAD_PAD + at : 2 * HEAD_PAD + at + HD]
        scores = dot_bt(query, keys) * scale + bias[...].astype(F32)
        powers = jnp.exp(scores - jnp.max(scores, -1, keepdims=True))
        weights = powers * (1.0 / jnp.sum(powers, -1, keepdims=True))
        mine = mixed_grad[:, at : at + HD]
        weight_grad = dot_bt(mine, values)
        delta = jnp.sum(weights * weight_grad, -1, keepdims=True)
        score_grad = (weights * (weight_grad - delta)).astype(BF)
        parts[0].append(rope_back(dot(score_grad, keys) * scale, cosine[...], sine[...]))
        parts[1].append(rope_back(dot_t(score_grad, query) * scale, cosine[...], sine[...]))
        parts[2].append(dot_t(weights.astype(BF), mine))
    if inner < HEAD_PAD:
        for part in parts:
            part.append(jnp.zeros((grads.shape[0], HEAD_PAD - inner), F32))
    projected_grad[...] = jnp.concatenate(parts[0] + parts[1] + parts[2], 1).astype(BF)
    part = dot_bt(projected_grad[...], w_in[...])
    tokens = jnp.concatenate([b[:, :width] for b in (b0, b1, b2, b3)], 0).astype(F32)
    gain_grad[...] = jnp.broadcast_to(
        jnp.sum(part * tokens * inverse_root(tokens), 0, keepdims=True), gain_grad.shape
    )
    keep[...] = part[:half]
    send[...] = part[half:].astype(BF)


def last_body(gain, own, got, b0, after_grad, out_own, out_got, after_attn, sent):
    rows, width = own.shape
    tokens = b0[:, :width].astype(F32)
    normed_grad = own[...] + got[...].astype(F32)
    total = after_grad[:rows, :] + rms_backward(
        tokens, inverse_root(tokens), gain[...], normed_grad
    )
    sent[:, :width] = (after_attn[:rows, :] + out_own[...] + out_got[...].astype(F32)).astype(BF)
    sent[:, width:] = total.astype(BF)


def return_body(anchor, b0, b1, b2, b3, final, grads):
    row_count, width = final.shape
    pick = (iota((row_count, row_count), 0) == anchor[...]).astype(F32).T.astype(BF)
    rows = jnp.concatenate([b[...] for b in (b0, b1, b2, b3)], 0)
    total = dot(pick, rows).astype(BF)
    final[...] = total[:, :width]
    grads[...] = total[:, width:]


def on_device(
    tokens,
    cotangent,
    gain_attn,
    w_qkv,
    w_out,
    gain_ffn,
    w_router,
    w_shared_gate,
    w_shared_up,
    w_shared_down,
    routed_gate_weight,
    routed_up_weight,
    w_expert_down,
    seq_lengths,
    token_order,
    inverse_order,
    routes,
    fill_order,
):
    devices_dp = lax.axis_size(DP)
    devices_tp = lax.axis_size(TP)
    dz = lax.axis_size("dz")
    row_count, width = tokens.shape
    block_rows = row_count // devices_dp
    shard_block = block_rows // devices_tp
    shard_rows = row_count // devices_tp
    half_rows = row_count // 2
    experts_all = w_router.shape[1]
    slot_rows = 4 * row_count // experts_all
    capacity = 5 * row_count * devices_dp // (2 * experts_all)
    inner = w_out.shape[0]
    heads = inner // HD
    per_dp = max(1, experts_all // devices_dp)
    copies = max(1, devices_dp // experts_all)
    sub = devices_tp // per_dp
    my_hi, my_lo = lax.axis_index("hi"), lax.axis_index("lo")
    my_z, my_y = lax.axis_index("dz"), lax.axis_index("dy")
    my_dp = my_z * 2 + my_y
    my_block = my_lo * 2 + my_hi
    pick = my_hi if per_dp == 2 else 0 * my_hi
    my_part = my_lo if per_dp == 2 else my_block
    part_rows = slot_rows // sub
    own_slots = devices_dp * part_rows
    all_slots = own_slots * sub
    my_expert = my_dp // copies * per_dp + pick
    chunk = width // devices_dp
    z_bits = [(my_z >> i) & 1 for i in range(log2(dz))]
    info = jnp.stack([my_block, pick, my_part, z_bits[0], my_expert, my_y] + z_bits).astype(I32)
    Z0, Y, Z_FIRST = 3, 5, 6

    def padded(columns):
        return jnp.pad(columns.reshape(width, inner), ((0, 0), (0, HEAD_PAD - inner)))

    by_head = w_qkv.reshape(width, heads, 3, HD)
    straight = [padded(by_head[:, :, i]) for i in range(3)]
    turned = [padded(jnp.roll(by_head[:, :, i], HD // 2, -1)) for i in range(2)]
    w_in_back = jnp.concatenate(straight, 1)
    w_in = jnp.concatenate(straight + turned, 1)
    router = jnp.pad(w_router, ((0, 0), (0, 128 - experts_all)))
    half_size = HD // 2
    exponent = jnp.arange(half_size, dtype=F32) * (-2.0 / HD)
    angles = jnp.arange(row_count, dtype=F32)[:, None] * jnp.power(10000.0, exponent)[None, :]
    cosine, sine = jnp.cos(angles), jnp.sin(angles)
    table = jnp.concatenate([cosine, cosine, -sine, sine], 1)
    pieces = []
    for _ in range(3):
        piece = lax.reduce_precision(table, 8, 7)
        pieces.append(piece.astype(BF))
        table = table - piece
    table = jnp.concatenate(pieces, 1)
    gain_attn = gain_attn[None]
    gain_ffn_row = gain_ffn[None]

    sent, anchor = kernel(
        functools.partial(select_body, shard_block, devices_dp),
        [out((shard_rows, 2 * width), BF), out((1, row_count), I32)],
        inverse_order[None],
        tokens,
        cotangent,
        scalars=info,
    )

    def blocks_of(own):
        by_hi = swap(own, "hi")
        by_lo = swap(own, "lo")
        return (own, by_hi, by_lo, swap(by_hi, "lo"))

    own = exchange(sent.reshape(devices_dp, shard_block, 2 * width))
    slot_pick, slot_pick_t, bias, cosine, sine, meta = pl.pallas_call(
        functools.partial(index_body, shard_block, copies, per_dp, part_rows, experts_all),
        out_shape=(
            out((own_slots, row_count), BF),
            out((row_count, own_slots), BF),
            out((row_count, row_count), BF),
            out((row_count, HD), F32),
            out((row_count, HD), F32),
            out((row_count, 128), BF),
        ),
        in_specs=[pl.BlockSpec(memory_space=pltpu.SMEM)] * 2
        + [pl.BlockSpec(memory_space=pltpu.VMEM)] * 4,
        out_specs=tuple([pl.BlockSpec(memory_space=pltpu.VMEM)] * 6),
        compiler_params=pltpu.CompilerParams(vmem_limit_bytes=40 * MIB),
        cost_estimate=pl.CostEstimate(
            flops=4_000_000_000, bytes_accessed=4_000_000, transcendentals=0
        ),
    )(info, seq_lengths, token_order[None], routes.T, fill_order, table)
    blocks = blocks_of(own.reshape(shard_rows, 2 * width))

    (sent_grads,) = kernel(
        send_grads_body, [out((own_slots, width + 128), BF)], slot_pick, meta, *blocks
    )
    got_grads = exchange(sent_grads.reshape(devices_dp, part_rows, width + 128))

    def sub_gather(values):
        values = values.reshape(own_slots, -1)
        if sub == 4:
            values = jnp.concatenate([values, swap(values, "hi")], 0)
        return values, swap(values, "lo")

    grads_own, grads_got = sub_gather(got_grads)
    (marks,) = kernel(
        functools.partial(meta_body, devices_dp, part_rows, sub, capacity),
        [out((all_slots, 128), F32)],
        grads_own[:, width:],
        grads_got[:, width:],
        scalars=info,
    )

    keep, send, qkv, mixed, normed_attn = kernel(
        functools.partial(attend_body, heads),
        [
            out((half_rows, width), F32),
            out((half_rows, width), BF),
            out((row_count, 3 * HEAD_PAD), BF),
            out((row_count, inner), BF),
            out((row_count, width), BF),
        ],
        gain_attn,
        w_in,
        w_out,
        cosine,
        sine,
        bias,
        *blocks,
        gflop=3.0,
    )

    def half_sum(keep, send):
        (half,) = kernel(fold_body, [out((half_rows, width), BF)], keep, swap(send, "lo"))
        return half, swap(half, "hi")

    def own_sum(keep, send):
        own, send = kernel(
            fold_own_body,
            [out((shard_rows, width), F32), out((shard_rows, width), BF)],
            keep,
            swap(send, "lo"),
        )
        return own, swap(send, "hi")

    after_attn, normed_own = kernel(
        norm_body,
        [out((half_rows, width), F32), out((half_rows, width), BF)],
        gain_ffn_row,
        *half_sum(keep, send),
        blocks[0],
        blocks[1],
    )
    normed_got = swap(normed_own, "lo")

    (sent_rows,) = kernel(
        send_rows_body, [out((own_slots, width), BF)], slot_pick, normed_own, normed_got, gflop=0.5
    )
    sent_rows = after(sent_rows, got_grads)
    rows_own, rows_got = sub_gather(exchange(sent_rows.reshape(devices_dp, part_rows, width)))

    units = w_shared_gate.shape[1]
    shared_part, shared_back, grad_sgate, grad_sup, shared_hidden = kernel(
        shared_body,
        [
            out((row_count, width), F32),
            out((row_count, width), F32),
            out((row_count, units), BF),
            out((row_count, units), BF),
            out((row_count, units), BF),
        ],
        normed_own,
        normed_got,
        *blocks,
        w_shared_gate,
        w_shared_up,
        w_shared_down,
        gflop=3.0,
    )
    tree_first = (dz // 2, 2, chunk)
    shared_keep, shared_send = kernel(
        shared_grads_body,
        [out(tree_first + (3 * units,), F32), out(tree_first + (3 * units,), BF)],
        normed_own,
        normed_got,
        *blocks,
        grad_sgate,
        grad_sup,
        shared_hidden,
        scalars=info,
        gflop=3.0,
    )

    def z_swap(values, bit):
        return lax.ppermute(values, "dz", [(i, i ^ (1 << bit)) for i in range(dz)])

    def tree_step(kept, got, which):
        columns = kept.shape[-1]
        kept = kept.reshape(-1, 2, chunk, columns)
        shape = (kept.shape[0], chunk, columns)
        return kernel(
            functools.partial(tree_body, which),
            [out(shape, F32), out(shape, BF)],
            kept,
            got.reshape(kept.shape),
            scalars=info,
        )

    def tree_end(kept, got):
        columns = kept.shape[-1]
        return (kept + got.astype(F32)).reshape(chunk, columns)

    def tree_rest(keep, got, bit):
        for bit in range(bit, log2(dz)):
            keep, send = tree_step(keep, got, Z_FIRST + bit)
            got = z_swap(send, bit)
        return tree_end(keep, got)

    shared_got = z_swap(shared_send, 0)
    rows_own = after(rows_own, shared_send)

    hidden_units = routed_gate_weight.shape[1]
    tile = min(256, own_slots)
    tiles = all_slots // 2 // tile
    steps = 2 * tiles

    def mine_at(i):
        return (jnp.minimum(i, tiles - 1), 0)

    def other_at(i):
        return (jnp.maximum(i - tiles, 0), 0)

    def every_at(i):
        return (i, 0)

    def fixed_at(i):
        return (0, 0)

    half_slots = all_slots // 2
    (
        back_keep,
        back_send,
        part_keep,
        part_send,
        rows_all,
        expert_hidden,
        grad_egate,
        grad_eup,
        pair_grads,
        gates,
        router_part,
    ) = pl.pallas_call(
        functools.partial(expert_body, tiles),
        grid=(steps,),
        in_specs=[
            pl.BlockSpec((tile, width), mine_at),
            pl.BlockSpec((tile, width), other_at),
            pl.BlockSpec((tile, width + 128), mine_at),
            pl.BlockSpec((tile, width + 128), other_at),
            pl.BlockSpec((tile, 128), every_at),
            pl.BlockSpec((width, 128), fixed_at),
            pl.BlockSpec((width, hidden_units), fixed_at),
            pl.BlockSpec((width, hidden_units), fixed_at),
            pl.BlockSpec((hidden_units, width), fixed_at),
        ],
        out_specs=(
            pl.BlockSpec((tile, width), mine_at),
            pl.BlockSpec((tile, width), other_at),
            pl.BlockSpec((tile, width), mine_at),
            pl.BlockSpec((tile, width), other_at),
            pl.BlockSpec((tile, width), every_at),
            pl.BlockSpec((tile, hidden_units), every_at),
            pl.BlockSpec((tile, hidden_units), every_at),
            pl.BlockSpec((tile, hidden_units), every_at),
            pl.BlockSpec((tile, width), every_at),
            pl.BlockSpec((tile, 128), every_at),
            pl.BlockSpec((128, width), fixed_at),
        ),
        out_shape=(
            out((half_slots, width), F32),
            out((half_slots, width), BF),
            out((half_slots, width), BF),
            out((half_slots, width), BF),
            out((all_slots, width), BF),
            out((all_slots, hidden_units), BF),
            out((all_slots, hidden_units), BF),
            out((all_slots, hidden_units), BF),
            out((all_slots, width), BF),
            out((all_slots, 128), F32),
            out((128, width), F32),
        ),
        compiler_params=pltpu.CompilerParams(
            vmem_limit_bytes=44 * MIB, dimension_semantics=("arbitrary",)
        ),
        cost_estimate=pl.CostEstimate(
            flops=12 * all_slots * width * hidden_units,
            bytes_accessed=20_000_000,
            transcendentals=0,
        ),
    )(
        rows_own,
        rows_got,
        grads_own,
        grads_got,
        marks,
        router,
        routed_gate_weight,
        routed_up_weight,
        w_expert_down,
    )

    def sub_scatter(keep, send):
        total = keep.astype(F32) + swap(send, "lo").astype(F32)
        if sub == 4:
            total = total[:own_slots] + swap(total[own_slots:].astype(BF), "hi").astype(F32)
        return total

    back_sum = sub_scatter(back_keep, back_send).astype(BF)
    got_back = exchange(back_sum.reshape(devices_dp, part_rows, width)).reshape(own_slots, width)
    grad_w_expert_down = dot_t(expert_hidden, pair_grads)
    grad_w_expert_gate = dot_t(rows_all, grad_egate)
    grad_w_expert_up = dot_t(rows_all, grad_eup)
    shared_keep, shared_send = tree_step(after(shared_keep, back_keep), shared_got, Y)
    shared_got = swap(shared_send, "dy")
    got_back = after(
        got_back, grad_w_expert_down, grad_w_expert_gate, grad_w_expert_up, shared_send
    )
    if sub == 4:
        part_sum = (gates[:own_slots, :1] * sub_scatter(part_keep, part_send)).astype(BF)
    else:
        (part_sum,) = kernel(
            part_body,
            [out((own_slots, width), BF)],
            part_keep,
            swap(part_send, "lo"),
            gates[:own_slots],
        )

    keep, send = kernel(
        combine_body,
        [out((half_rows, width), F32), out((half_rows, width), BF)],
        slot_pick_t,
        got_back,
        shared_back,
        gflop=0.5,
    )
    part_sum = after(part_sum, keep)
    got_parts = exchange(part_sum.reshape(devices_dp, part_rows, width)).reshape(own_slots, width)
    after_grad, after_grad_own, gain_ffn_part = kernel(
        norm_back_body,
        [out((half_rows, width), F32), out((half_rows, width), BF), out((8, width), F32)],
        gain_ffn_row,
        *half_sum(keep, send),
        after_attn,
        blocks[0],
        blocks[1],
    )
    after_grad_got = swap(after_grad_own, "lo")

    keep, send, projected_grad, gain_attn_part = kernel(
        functools.partial(attend_back_body, heads),
        [
            out((half_rows, width), F32),
            out((half_rows, width), BF),
            out((row_count, 3 * HEAD_PAD), BF),
            out((8, width), F32),
        ],
        w_out,
        w_in_back,
        cosine,
        sine,
        bias,
        qkv,
        after_grad_own,
        after_grad_got,
        *blocks,
        gflop=4.0,
    )
    qkv_keep, qkv_send = kernel(
        product_grads_body,
        [out(tree_first + (3 * HEAD_PAD,), F32), out(tree_first + (3 * HEAD_PAD,), BF)],
        normed_attn,
        projected_grad,
        scalars=info,
        gflop=0.6,
    )
    out_keep, out_send = kernel(
        product_grads_body,
        [out(tree_first + (inner,), F32), out(tree_first + (inner,), BF)],
        jnp.concatenate([after_grad_own, after_grad_got], 0),
        mixed,
        scalars=info,
        gflop=0.2,
    )

    out_part_keep, out_part_send = kernel(
        combine_body,
        [out((half_rows, width), F32), out((half_rows, width), BF)],
        slot_pick_t,
        after(got_parts, after_grad_own),
        shared_part,
        gflop=0.5,
    )
    (sent_last,) = kernel(
        last_body,
        [out((shard_rows, 2 * width), BF)],
        gain_attn,
        *own_sum(keep, send),
        blocks[0],
        after_grad,
        *own_sum(out_part_keep, out_part_send),
        after_attn,
    )
    got_last = exchange(sent_last.reshape(devices_dp, shard_block, 2 * width))
    final, grad_tokens = kernel(
        return_body,
        [out((row_count, width), BF), out((row_count, width), BF)],
        anchor,
        *blocks_of(got_last.reshape(shard_rows, 2 * width)),
        gflop=1.0,
    )

    small = jnp.concatenate(
        [gain_ffn_part[:1], gain_attn_part[:1], router_part[:experts_all], jnp.zeros((6, width), F32)],
        0,
    )
    small = small + swap(small, "hi")
    small = small + swap(small, "lo")
    small = small.reshape(-1, devices_dp, chunk).transpose(1, 0, 2)
    small = jnp.sum(exchange(small), 0)
    grad_shared = tree_rest(after(shared_keep, after_grad_own), shared_got, 1)

    def tree(keep, send):
        got = z_swap(send, 0)
        keep, send = tree_step(keep, got, Y)
        return tree_rest(keep, swap(send, "dy"), 1)

    grad_qkv = tree(qkv_keep, qkv_send)
    grad_qkv = jnp.stack(
        [
            grad_qkv[:, i * HEAD_PAD : i * HEAD_PAD + inner].reshape(chunk, heads, HD)
            for i in range(3)
        ],
        2,
    ).reshape(chunk, 3 * inner)
    return (
        final,
        grad_tokens,
        small[1],
        grad_qkv,
        tree(out_keep, out_send).T,
        small[0],
        small[2 : 2 + experts_all].T,
        grad_shared[:, :units],
        grad_shared[:, units : 2 * units],
        grad_shared[:, 2 * units :].T,
        grad_w_expert_gate,
        grad_w_expert_up,
        grad_w_expert_down,
    )


def solution(mesh):
    devices_dp, devices_tp = mesh.shape["dp"], mesh.shape["tensor"]
    fine = Mesh(
        mesh.devices.reshape(devices_dp // 2, 2, devices_tp // 2, 2), ("dz", "dy", "hi", "lo")
    )
    every = DP + TP
    return jax.shard_map(
        on_device,
        mesh=fine,
        in_specs=(
            P(DP, None),
            P(DP, None),
            P(),
            P(None, TP),
            P(TP, None),
            P(),
            P(),
            P(None, TP),
            P(None, TP),
            P(TP, None),
            P(None, every),
            P(None, every),
            P(every, None),
            P(DP, None),
            P(DP),
            P(DP),
            P(DP, None),
            P(DP, None),
        ),
        out_specs=(
            P(DP, None),
            P(DP, None),
            P(DP),
            P(DP, TP),
            P(TP, DP),
            P(DP),
            P(DP, None),
            P(DP, TP),
            P(DP, TP),
            P(TP, DP),
            P(None, every),
            P(None, every),
            P(every, None),
        ),
        check_vma=False,
    )
```

```python
import functools

import jax
import jax.numpy as jnp
import numpy as np
from jax import lax
from jax.experimental import pallas as pl
from jax.experimental.pallas import tpu as pltpu
from jax.sharding import Mesh, PartitionSpec as P

HD = 64
EPSILON = 1e-06
BF = jnp.bfloat16
F32 = jnp.float32
I32 = jnp.int32
DP = ("dz", "dy")
TP = ("hi", "lo")
MIB = 1 << 20
COST = pl.CostEstimate(flops=1000, bytes_accessed=1000, transcendentals=0)


def dot(left, right):
    return jnp.dot(left, right, preferred_element_type=F32)


def dot_t(left, right):
    return lax.dot_general(left, right, (((0,), (0,)), ((), ())), preferred_element_type=F32)


def dot_bt(left, right):
    return lax.dot_general(left, right, (((1,), (1,)), ((), ())), preferred_element_type=F32)


def swap(values, axis):
    return lax.ppermute(values, axis, [(0, 1), (1, 0)])


def exchange(values):
    return lax.all_to_all(values, DP, split_axis=0, concat_axis=0, tiled=True)


def out(shape, dtype):
    return jax.ShapeDtypeStruct(shape, dtype)


class Far:
    def __init__(self, value):
        self.value = value


class Arriving:
    def __init__(self, buffer, copy):
        self.buffer, self.copy, self.waiting = buffer, copy, True
        self.shape, self.dtype = buffer.shape, buffer.dtype

    def ready(self):
        if self.waiting:
            self.copy.wait()
            self.waiting = False

    def __getitem__(self, index):
        self.ready()
        return self.buffer[index]


class Leaving:
    def __init__(self, buffer, copy):
        self.buffer, self.copy, self.started = buffer, copy, False
        self.shape, self.dtype = buffer.shape, buffer.dtype

    def flush(self):
        if not self.started:
            self.copy.start()
            self.started = True

    def __getitem__(self, index):
        return self.buffer[index]

    def __setitem__(self, index, value):
        self.buffer[index] = value


def in_hbm(values):
    return pltpu.with_memory_space_constraint(values, pltpu.HBM)


def kernel(body, outs, *args, scalars=(), deps=(), vmem=16):
    vmem_spec = pl.BlockSpec(memory_space=pltpu.VMEM)
    hbm_spec = pl.BlockSpec(memory_space=pltpu.HBM)
    any_spec = pl.BlockSpec(memory_space=pl.ANY)
    far_in = [isinstance(a, Far) for a in args]
    far_out = [isinstance(o, Far) for o in outs]
    args = [in_hbm(a.value) if f else a for a, f in zip(args, far_in)]
    outs = [pltpu.HBM(o.value.shape, o.value.dtype) if f else o for o, f in zip(outs, far_out)]
    deps = [in_hbm(d.value) if isinstance(d, Far) else d for d in deps]
    moved = [x for x, f in zip(args + outs, far_in + far_out) if f]
    scratch = [pltpu.VMEM(x.shape, x.dtype) for x in moved]
    if moved:
        scratch.append(pltpu.SemaphoreType.DMA((len(moved),)))
    n_scalars, n_args, n_deps, n_outs = len(scalars), len(args), len(deps), len(outs)

    def wrapped(*refs):
        ins = list(refs[: n_scalars + n_args])
        results = list(refs[n_scalars + n_args + n_deps :][:n_outs])
        buffers = refs[n_scalars + n_args + n_deps + n_outs :]
        at = 0
        for i, far in enumerate(far_in):
            if far:
                ref = ins[n_scalars + i]
                copy = pltpu.make_async_copy(ref, buffers[at], buffers[-1].at[at])
                copy.start()
                ins[n_scalars + i] = Arriving(buffers[at], copy)
                at += 1
        for i, far in enumerate(far_out):
            if far:
                copy = pltpu.make_async_copy(buffers[at], results[i], buffers[-1].at[at])
                results[i] = Leaving(buffers[at], copy)
                at += 1
        body(*ins, *results)
        for ref in ins:
            if isinstance(ref, Arriving):
                ref.ready()
        for ref in results:
            if isinstance(ref, Leaving):
                ref.flush()
        for ref in results:
            if isinstance(ref, Leaving):
                ref.copy.wait()

    return pl.pallas_call(
        wrapped,
        out_shape=tuple(outs),
        in_specs=[pl.BlockSpec(memory_space=pltpu.SMEM)] * n_scalars
        + [hbm_spec if far else vmem_spec for far in far_in]
        + [any_spec] * n_deps,
        out_specs=tuple(hbm_spec if far else vmem_spec for far in far_out),
        scratch_shapes=scratch,
        compiler_params=pltpu.CompilerParams(vmem_limit_bytes=vmem * MIB),
        cost_estimate=COST,
        name=body.func.__name__ if isinstance(body, functools.partial) else body.__name__,
    )(*scalars, *args, *deps)


def tie(values, *deps):
    any_spec = pl.BlockSpec(memory_space=pl.ANY)
    hbm_spec = pl.BlockSpec(memory_space=pltpu.HBM)
    return pl.pallas_call(
        lambda *refs: None,
        out_shape=out(values.shape, values.dtype),
        in_specs=[hbm_spec] + [any_spec] * len(deps),
        out_specs=hbm_spec,
        input_output_aliases={0: 0},
        cost_estimate=COST,
        name="tie",
    )(in_hbm(values), *[in_hbm(d.value) if isinstance(d, Far) else d for d in deps])


def rope_table(places):
    exponent = np.arange(HD // 2, dtype=np.float32) * np.float32(-2.0 / HD)
    angles = np.arange(places, dtype=np.float32)[:, None] * np.power(np.float32(10000.0), exponent)
    cosine = np.cos(angles.astype(np.float64)).astype(np.float32)
    sine = np.sin(angles.astype(np.float64)).astype(np.float32)
    rest = np.concatenate([cosine, cosine, -sine, sine], 1)
    terms = []
    for _ in range(3):
        terms.append(rest.astype(BF))
        rest = rest - terms[-1].astype(np.float32)
    return jnp.asarray(np.concatenate(terms, 1))


def iota(shape, dim):
    return lax.broadcasted_iota(I32, shape, dim)


def log2(number):
    return number.bit_length() - 1


def silu_parts(gate_in):
    sigmoid_val = 1.0 / (1.0 + jnp.exp(-gate_in))
    return (gate_in * sigmoid_val, sigmoid_val * (1.0 + gate_in * (1.0 - sigmoid_val)))


def inverse_root(values):
    return lax.rsqrt(jnp.mean(values * values, -1, keepdims=True) + EPSILON)


def rms_backward(values, root, gain, grad_normed):
    scaled = grad_normed * gain
    return root * scaled - values * (root * root * root) * jnp.mean(
        scaled * values, -1, keepdims=True
    )


def lane_rank(buckets, bucket_count):
    count = buckets.shape[1]
    rows = max(8, bucket_count)
    member = (iota((rows, count), 0) == buckets).astype(F32)
    earlier = (iota((count, count), 0) < iota((count, count), 1)).astype(F32).astype(BF)
    return jnp.sum(dot(member.astype(BF), earlier) * member, 0, keepdims=True).astype(I32)


def relative_row(block, rank, my_block, shard_block, shard_rows):
    shift = log2(shard_block)
    return (
        ((rank >> shift) ^ my_block) * shard_rows
        + block * shard_block
        + (rank & (shard_block - 1))
    )


def rope_back(grads, cosine, sine):
    return grads * cosine - half_turned(grads) * sine


def select_body(shard_block, blocks, info, inverse, tokens, cotangent, sent, anchor):
    row_count, width = tokens.shape
    shard_rows = sent.shape[0]
    target = inverse[...] >> log2(row_count)
    row = relative_row(target, lane_rank(target, blocks), info[0], shard_block, shard_rows)
    anchor[...] = row
    pick = (iota((shard_rows, row_count), 0) == row).astype(F32).astype(BF)
    sent[:, :width] = dot(pick, tokens[...]).astype(BF)
    sent[:, width:] = dot(pick, cotangent[...]).astype(BF)


def index_body(
    shard_block,
    copies,
    per_dp,
    part_rows,
    experts_all,
    info,
    lengths,
    order,
    routes,
    fill,
    table,
    slot_pick,
    slot_pick_t,
    bias,
    cosine,
    sine,
    meta,
):
    row_count = order.shape[1]
    devices_dp = slot_pick.shape[0] // part_rows
    shard_rows = shard_block * devices_dp
    source = order[...] >> log2(row_count)
    local = relative_row(
        source, lane_rank(source, devices_dp), info[0], shard_block, shard_rows
    )
    place_pick = (iota((row_count, row_count), 0) == local).astype(F32).astype(BF)
    lanes = iota((1, row_count), 1)
    segment = jnp.zeros((1, row_count), I32)
    start = jnp.zeros((1, row_count), I32)
    end = jnp.int32(0)
    for entry in range(lengths.shape[1]):
        end = end + lengths[0, entry]
        passed = lanes >= end
        segment = segment + passed.astype(I32)
        start = jnp.maximum(start, jnp.where(passed, end, 0))
    place = lanes - start
    expert_sum = routes[0:1, :] + routes[1:2, :] + 1
    facts = jnp.concatenate(
        [segment, place >> 1, place & 1, expert_sum, jnp.zeros((4, row_count), I32)], 0
    )
    facts = facts.astype(F32).astype(BF)
    across = dot_bt(facts, place_pick)
    down = dot_bt(place_pick, facts)
    place_row = 2.0 * across[1:2] + across[2:3]
    place_col = 2.0 * down[:, 1:2] + down[:, 2:3]
    allowed = (down[:, 0:1] == across[0:1]) & (place_row <= place_col)
    bias[...] = jnp.where(allowed, 0.0, -1e30).astype(BF)
    at_place = (
        iota((row_count, row_count), 1).astype(F32) == place_col
    ).astype(F32).astype(BF)
    turned = dot(at_place, table[...])
    pieces = [turned[:, i * 128 : (i + 1) * 128] for i in range(3)]
    turned = pieces[0] + pieces[1] + pieces[2]
    cosine[...] = turned[:, :HD]
    sine[...] = turned[:, HD:]
    meta[...] = jnp.broadcast_to(down[:, 3:4], meta.shape).astype(BF)
    pairs = 2 * row_count
    fill_at = (fill[...] & 1) * row_count + (fill[...] >> 1)
    fill_pick = (iota((pairs, pairs), 0) == fill_at).astype(F32).astype(BF)
    expert_rows = max(16, experts_all)
    pair_expert = jnp.concatenate([routes[0:1, :], routes[1:2, :]], 1)
    named = (iota((expert_rows, pairs), 0) == pair_expert).astype(F32).astype(BF)
    member = dot(named, fill_pick)
    earlier = (iota((pairs, pairs), 0) < iota((pairs, pairs), 1)).astype(F32).astype(BF)
    ranks = (member * (dot(member.astype(BF), earlier) + 1.0)).astype(BF)
    ranks = dot_bt(ranks, fill_pick)
    ranks = (ranks[:, :row_count] + ranks[:, row_count:]).astype(BF)
    ranks = dot_bt(ranks, place_pick).astype(I32)
    first = info[2] * part_rows + 1
    slots = iota((part_rows, row_count), 0) + first
    for target in range(devices_dp):
        base = target // copies * per_dp
        chosen = ranks[base : base + 1]
        if per_dp == 2:
            chosen = jnp.where(info[1] == 0, chosen, ranks[base + 1 : base + 2])
        picked = (slots == chosen).astype(F32)
        slot_pick[target * part_rows : (target + 1) * part_rows, :] = picked.astype(BF)
    slot_pick_t[...] = slot_pick[...].astype(F32).T.astype(BF)


def send_grads_body(slot_pick, meta, b0, b1, b2, b3, sent):
    width = b0.shape[1] // 2
    grads = jnp.concatenate([b[:, width:] for b in (b0, b1, b2, b3)], 0)
    sent[:, :width] = dot(slot_pick[...], grads).astype(BF)
    sent[:, width:] = dot(slot_pick[...], meta[...]).astype(BF)


def head_parts(projected, heads):
    return [
        [projected[:, (3 * h + i) * HD : (3 * h + i + 1) * HD] for i in range(3)]
        for h in range(heads)
    ]


def half_turned(values):
    half = values.shape[1] // 2
    return jnp.concatenate([values[:, half:], values[:, :half]], 1)


def attend_body(
    heads, gain, w_in_t, w_out, cosine, sine, bias, b0, b1, b2, b3, keep, send, qkv, mixed, normed
):
    width = b0.shape[1] // 2
    half = keep.shape[0]
    tokens = jnp.concatenate([b[:, :width] for b in (b0, b1, b2, b3)], 0).astype(F32)
    normed[...] = (tokens * inverse_root(tokens) * gain[...]).astype(BF)
    normed.flush()
    projected = dot_bt(normed[...], w_in_t[...])
    cosine, sine = cosine[...], sine[...]
    parts = []
    for query, keys, values in head_parts(projected, heads):
        parts.append((query * cosine + half_turned(query) * sine).astype(BF))
        parts.append((keys * cosine + half_turned(keys) * sine).astype(BF))
        parts.append(values.astype(BF))
    qkv[...] = jnp.concatenate(parts, 1)
    qkv.flush()
    scale = HD**-0.5
    mixed_heads = []
    for query, keys, values in head_parts(qkv, heads):
        scores = dot_bt(query, keys) * scale + bias[...].astype(F32)
        powers = jnp.exp(scores - jnp.max(scores, -1, keepdims=True))
        weights = powers * (1.0 / jnp.sum(powers, -1, keepdims=True))
        mixed_heads.append(dot(weights.astype(BF), values))
    mixed[...] = jnp.concatenate(mixed_heads, 1).astype(BF)
    mixed.flush()
    part = dot(mixed[...], w_out[...])
    keep[...] = part[:half]
    send[...] = part[half:].astype(BF)


def fold_body(keep, got, half):
    half[...] = (keep[...] + got[...].astype(F32)).astype(BF)


def fold_own_body(keep, got, own, send):
    rows = own.shape[0]
    own[...] = keep[:rows, :] + got[:rows, :].astype(F32)
    send[...] = (keep[rows:, :] + got[rows:, :].astype(F32)).astype(BF)


def both(half, got):
    rows = half.shape[0] // 2
    mine, other = half[...].astype(F32), got[...].astype(F32)
    return mine + jnp.concatenate([other[rows:], other[:rows]], 0)


def norm_body(gain, half, got, b0, b1, after_attn, normed, far_normed):
    width = half.shape[1]
    balanced = jnp.concatenate([b0[:, :width], b1[:, :width]], 0).astype(F32)
    values = balanced + both(half, got)
    after_attn[...] = values
    after_attn.flush()
    normed[...] = (values * inverse_root(values) * gain[...]).astype(BF)
    far_normed[...] = normed[...]


def send_rows_body(slot_pick, own, got, sent):
    rows = jnp.concatenate([own[...], got[...]], 0)
    sent[...] = dot(slot_pick[...], rows).astype(BF)


def shared_body(
    own, got, b0, b1, b2, b3, w_gate, w_up, w_down, part, back, grad_gate, grad_up, hidden
):
    width = own.shape[1]
    rows = jnp.concatenate([own[...], got[...]], 0)
    grads = jnp.concatenate([b[:, width:] for b in (b0, b1, b2, b3)], 0)
    gate = dot(rows, w_gate[...])
    up = dot(rows, w_up[...])
    act, slope = silu_parts(gate)
    hidden[...] = (act * up).astype(BF)
    part[...] = dot(hidden[...], w_down[...])
    hidden_grad = dot_bt(grads, w_down[...])
    grad_gate[...] = (hidden_grad * up * slope).astype(BF)
    grad_up[...] = (hidden_grad * act).astype(BF)
    back[...] = dot_bt(grad_gate[...], w_gate[...]) + dot_bt(grad_up[...], w_up[...])


def shared_grads_body(
    info, own, got, b0, b1, b2, b3, grad_gate, grad_up, hidden, keep, send
):
    width = own.shape[1]
    rows = jnp.concatenate([own[...], got[...]], 0)
    grads = jnp.concatenate([b[:, width:] for b in (b0, b1, b2, b3)], 0)
    columns = hidden.shape[1]
    high, _, chunk, _ = keep.shape
    for which, (left, right) in enumerate(
        ((rows, grad_gate[...]), (rows, grad_up[...]), (grads, hidden[...]))
    ):
        sums = dot_t(left, right)
        cols = slice(which * columns, (which + 1) * columns)
        for z in range(high):
            for y in range(2):
                at = (z * 4 + y) * chunk
                mine = info[3] == 0
                first, second = sums[at : at + chunk], sums[at + 2 * chunk : at + 3 * chunk]
                keep[z, y, :, cols] = jnp.where(mine, first, second)
                send[z, y, :, cols] = jnp.where(mine, second, first).astype(BF)


def last_grads_body(
    experts, info, normed, projected_grad, own, got, mixed, gain_ffn, gain_attn, router, keep, send
):
    width = normed.shape[1]
    small = jnp.concatenate(
        [
            router[:experts, :],
            gain_ffn[:1, :],
            gain_attn[:1, :],
            jnp.zeros((128 - experts - 2, width), F32),
        ],
        0,
    )
    grads = jnp.concatenate([own[...], got[...]], 0)
    sums = jnp.concatenate(
        [dot_t(normed[...], projected_grad[...]), dot_t(grads, mixed[...]), small.T], 1
    )
    mine = info[5] == 0
    high, chunk, _ = keep.shape
    for z in range(high):
        at = 2 * z * chunk
        first, second = sums[at : at + chunk], sums[at + chunk : at + 2 * chunk]
        keep[z] = jnp.where(mine, first, second)
        send[z] = jnp.where(mine, second, first).astype(BF)


def tree_body(which, info, kept, got, keep, send):
    bit = info[which]
    total = kept[...] + got[...].astype(F32)
    pairs = total.shape[0]
    for index in range(pairs):
        mine = bit == 0
        first, second = total[index, 0], total[index, 1]
        keep[index] = jnp.where(mine, first, second)
        send[index] = jnp.where(mine, second, first).astype(BF)


def last_end_body(small_rows, kept, got, grad_qkv, grad_out, small):
    total = kept[0] + got[0].astype(F32)
    columns, inner = grad_qkv.shape[1], grad_out.shape[0]
    grad_qkv[...] = total[:, :columns]
    grad_out[...] = total[:, columns : columns + inner].T
    small[...] = total[:, columns + inner :].T[:small_rows]


def shared_end_body(kept, got, grad_gate, grad_up, grad_down):
    total = kept[0] + got[0].astype(F32)
    units = grad_gate.shape[1]
    grad_gate[...] = total[:, :units]
    grad_up[...] = total[:, units : 2 * units]
    grad_down[...] = total[:, 2 * units :]


def add_body(keep, got, total):
    total[...] = (keep[...].astype(F32) + got[...].astype(F32)).astype(BF)


def to_bottom_body(slot_pick_t, back, addend, attn_keep, attn_send, keep, send):
    half, width = attn_keep.shape
    total = addend[...] + dot(slot_pick_t[...], back[...])
    keep[:, :width] = total[:half]
    send[:, :width] = total[half:].astype(BF)
    keep[:, width:] = attn_keep[...]
    send[:, width:] = attn_send[...]


def meta_body(devices_dp, part_rows, sub, capacity, width, info, own, got, marks):
    my_part, my_expert = info[2], info[4]
    lanes = iota((part_rows, 128), 1)
    blocks = [(ref, at, part) for part, (ref, at) in enumerate(
        [(own, i) for i in range(sub // 2)] + [(got, i) for i in range(sub // 2)]
    )]
    earlier = jnp.zeros((1, 128), F32)
    for block in range(devices_dp):
        total = earlier
        for ref, at, part in blocks:
            start = (at * devices_dp + block) * part_rows
            value = ref[start : start + part_rows, width:].astype(F32)
            valid = value > 0.0
            slot = iota((part_rows, 128), 0) + (my_part ^ part) * part_rows
            kept = valid & (slot.astype(F32) + earlier < capacity)
            other = value.astype(I32) - 1 - my_expert
            mark = (lanes == my_expert).astype(F32) - (lanes == other).astype(F32)
            row = (part * devices_dp + block) * part_rows
            marks[row : row + part_rows, :] = jnp.where(
                lanes == 127, kept.astype(F32), jnp.where(valid, mark, 0.0)
            )
            total = total + jnp.sum(valid.astype(F32), 0, keepdims=True)
        earlier = total


def expert_body(
    tiles,
    rows_own,
    rows_got,
    grads_own,
    grads_got,
    marks,
    w_router,
    w_gate,
    w_up,
    w_down,
    back_keep,
    back_send,
    part_keep,
    part_send,
    rows_all,
    hidden_out,
    grad_gate_out,
    grad_up_out,
    pair_out,
    gates,
    router,
):
    step = pl.program_id(0)
    mine = step < tiles
    width = rows_own.shape[1]
    rows = jnp.where(mine, rows_own[...], rows_got[...])
    grads = jnp.where(mine, grads_own[...], grads_got[...])[:, :width].astype(F32)
    mark = marks[...]
    kept = mark[:, 127:128] > 0.5
    lanes = iota(mark.shape, 1)
    mark = jnp.where(lanes == 127, 0.0, mark)
    logits = dot_bt(rows, w_router[...])
    gap = jnp.sum(logits * mark, 1, keepdims=True)
    gate = 1.0 / (1.0 + jnp.exp(-gap))
    gate_other = 1.0 / (1.0 + jnp.exp(gap))
    rows_all[...] = rows
    gate_in = dot(rows, w_gate[...])
    up = dot(rows, w_up[...])
    act, slope = silu_parts(gate_in)
    hidden = (act * up).astype(BF)
    hidden_out[...] = hidden
    part = jnp.where(kept, dot(hidden, w_down[...]), 0.0).astype(BF)
    pair = jnp.where(kept, gate * grads, 0.0).astype(BF)
    pair_out[...] = pair
    gate_grad = jnp.sum(part.astype(F32) * grads, 1, keepdims=True)
    logit_grad = (gate * gate_other * gate_grad * mark).astype(BF)
    hidden_grad = dot_bt(pair, w_down[...])
    grad_gate = (hidden_grad * up * slope).astype(BF)
    grad_up = (hidden_grad * act).astype(BF)
    grad_gate_out[...] = grad_gate
    grad_up_out[...] = grad_up
    back = (dot_bt(grad_gate, w_gate[...]) + dot_bt(grad_up, w_up[...])).astype(BF).astype(F32)
    back = back + dot(logit_grad, w_router[...])

    @pl.when(step == 0)
    def _():
        router[...] = jnp.zeros_like(router)

    router[...] += dot_t(logit_grad, rows)

    @pl.when(mine)
    def _():
        back_keep[...] = back.astype(BF)
        part_keep[...] = part
        gates[...] = jnp.broadcast_to(gate, gates.shape)

    @pl.when(jnp.logical_not(mine))
    def _():
        back_send[...] = back.astype(BF)
        part_send[...] = part


def part_body(keep, got, gates, total):
    gate = jnp.concatenate([gates[...]] * (keep.shape[1] // 128), 1)
    total[...] = (gate * (keep[...].astype(F32) + got[...].astype(F32))).astype(BF)


def combine_body(slot_pick_t, back, addend, keep, send):
    half = keep.shape[0]
    total = addend[...] + dot(slot_pick_t[...], back[...])
    keep[...] = total[:half]
    send[...] = total[half:].astype(BF)


def norm_back_body(
    gain, half, got, after_attn, b0, b1, after_grad, low, far_low, gain_grad
):
    width = half.shape[1]
    normed_grad = both(half, got)
    values = after_attn[...]
    root = inverse_root(values)
    grads = jnp.concatenate([b0[:, width:], b1[:, width:]], 0).astype(F32)
    total = grads + rms_backward(values, root, gain[...], normed_grad)
    after_grad[...] = total
    after_grad.flush()
    low[...] = total.astype(BF)
    far_low[...] = low[...]
    far_low.flush()
    gain_grad[...] = jnp.broadcast_to(
        0.5 * jnp.sum(normed_grad * values * root, 0, keepdims=True), gain_grad.shape
    )


def attend_back_body(
    heads,
    w_out,
    w_in_t,
    cosine,
    sine,
    bias,
    qkv,
    own,
    got,
    b0,
    b1,
    b2,
    b3,
    keep,
    send,
    projected_grad,
    gain_grad,
):
    width = own.shape[1]
    half = keep.shape[0]
    grads = jnp.concatenate([own[...], got[...]], 0)
    mixed_grad = dot_bt(grads, w_out[...]).astype(BF)
    scale = HD**-0.5
    cosine, sine = cosine[...], sine[...]
    parts = []
    for head, (query, keys, values) in enumerate(head_parts(qkv, heads)):
        at = head * HD
        scores = dot_bt(query, keys) * scale + bias[...].astype(F32)
        powers = jnp.exp(scores - jnp.max(scores, -1, keepdims=True))
        weights = powers * (1.0 / jnp.sum(powers, -1, keepdims=True))
        mine = mixed_grad[:, at : at + HD]
        weight_grad = dot_bt(mine, values)
        delta = jnp.sum(weights * weight_grad, -1, keepdims=True)
        score_grad = (weights * (weight_grad - delta)).astype(BF)
        parts.append(rope_back(dot(score_grad, keys) * scale, cosine, sine))
        parts.append(rope_back(dot_t(score_grad, query) * scale, cosine, sine))
        parts.append(dot_t(weights.astype(BF), mine))
    projected_grad[...] = jnp.concatenate(parts, 1).astype(BF)
    projected_grad.flush()
    part = dot(projected_grad[...], w_in_t[...])
    tokens = jnp.concatenate([b[:, :width] for b in (b0, b1, b2, b3)], 0).astype(F32)
    gain_grad[...] = jnp.broadcast_to(
        jnp.sum(part * tokens * inverse_root(tokens), 0, keepdims=True), gain_grad.shape
    )
    keep[...] = part[:half]
    send[...] = part[half:].astype(BF)


def last_body(gain, own, got, b0, after_grad, after_attn, sent):
    rows = own.shape[0]
    width = own.shape[1] // 2
    tokens = b0[:, :width].astype(F32)
    sums = own[...] + got[...].astype(F32)
    total = after_grad[:rows, :] + rms_backward(
        tokens, inverse_root(tokens), gain[...], sums[:, width:]
    )
    sent[:, :width] = (after_attn[:rows, :] + sums[:, :width]).astype(BF)
    sent[:, width:] = total.astype(BF)


def return_body(anchor, b0, b1, b2, b3, final, grads):
    row_count, width = final.shape
    pick = (iota((row_count, row_count), 0) == anchor[...]).astype(F32).T.astype(BF)
    rows = jnp.concatenate([b[...] for b in (b0, b1, b2, b3)], 0)
    total = dot(pick, rows).astype(BF)
    final[...] = total[:, :width]
    grads[...] = total[:, width:]


def on_device(
    tokens,
    cotangent,
    gain_attn,
    w_qkv,
    w_out,
    gain_ffn,
    w_router,
    w_shared_gate,
    w_shared_up,
    w_shared_down,
    routed_gate_weight,
    routed_up_weight,
    w_expert_down,
    seq_lengths,
    token_order,
    inverse_order,
    routes,
    fill_order,
):
    devices_dp = lax.axis_size(DP)
    devices_tp = lax.axis_size(TP)
    dz = lax.axis_size("dz")
    row_count, width = tokens.shape
    block_rows = row_count // devices_dp
    shard_block = block_rows // devices_tp
    shard_rows = row_count // devices_tp
    half_rows = row_count // 2
    experts_all = w_router.shape[1]
    slot_rows = 4 * row_count // experts_all
    capacity = 5 * row_count * devices_dp // (2 * experts_all)
    inner = w_out.shape[0]
    heads = inner // HD
    per_dp = max(1, experts_all // devices_dp)
    copies = max(1, devices_dp // experts_all)
    sub = devices_tp // per_dp
    my_hi, my_lo = lax.axis_index("hi"), lax.axis_index("lo")
    my_z, my_y = lax.axis_index("dz"), lax.axis_index("dy")
    my_dp = my_z * 2 + my_y
    my_block = my_lo * 2 + my_hi
    pick = my_hi if per_dp == 2 else 0 * my_hi
    my_part = my_lo if per_dp == 2 else my_block
    part_rows = slot_rows // sub
    own_slots = devices_dp * part_rows
    all_slots = own_slots * sub
    my_expert = my_dp // copies * per_dp + pick
    chunk = width // devices_dp
    z_bits = [(my_z >> i) & 1 for i in range(log2(dz))]
    info = jnp.stack([my_block, pick, my_part, z_bits[0], my_expert, my_y] + z_bits).astype(I32)
    Z0, Y, Z_FIRST = 3, 5, 6

    w_in_t = w_qkv.T
    router = jnp.pad(w_router.T, ((0, 128 - experts_all), (0, 0)))
    table = rope_table(row_count)
    gain_attn = gain_attn[None]
    gain_ffn = gain_ffn[None]

    sent, anchor = kernel(
        functools.partial(select_body, shard_block, devices_dp),
        [out((shard_rows, 2 * width), BF), Far(out((1, row_count), I32))],
        Far(inverse_order[None]),
        Far(tokens),
        Far(cotangent),
        scalars=(info,),
    )

    def blocks_of(own):
        by_hi = swap(own, "hi")
        by_lo = swap(own, "lo")
        return (own, by_hi, by_lo, swap(by_hi, "lo"))

    arrived = exchange(sent.reshape(devices_dp, shard_block, 2 * width))
    slot_pick, slot_pick_t, bias, cosine, sine, meta = kernel(
        functools.partial(index_body, shard_block, copies, per_dp, part_rows, experts_all),
        [
            Far(out((own_slots, row_count), BF)),
            Far(out((row_count, own_slots), BF)),
            Far(out((row_count, row_count), BF)),
            Far(out((row_count, HD), F32)),
            Far(out((row_count, HD), F32)),
            Far(out((row_count, 128), BF)),
        ],
        Far(token_order[None]),
        Far(routes.T),
        Far(fill_order),
        Far(table),
        scalars=(info, seq_lengths),
        vmem=24,
    )
    own = tie(arrived, Far(slot_pick))
    blocks = blocks_of(own.reshape(shard_rows, 2 * width))
    far_blocks = [Far(b) for b in blocks]

    (sent_grads,) = kernel(
        send_grads_body, [out((own_slots, width + 128), BF)], Far(slot_pick), Far(meta), *blocks
    )
    got_grads = exchange(sent_grads.reshape(devices_dp, part_rows, width + 128))

    def sub_gather(values):
        values = values.reshape(own_slots, -1)
        if sub == 4:
            values = jnp.concatenate([values, swap(values, "hi")], 0)
        return values, swap(values, "lo")

    grads_own, grads_got = sub_gather(got_grads)
    (marks,) = kernel(
        functools.partial(meta_body, devices_dp, part_rows, sub, capacity, width),
        [Far(out((all_slots, 128), F32))],
        Far(grads_own),
        Far(grads_got),
        scalars=(info,),
        vmem=40 if sub == 4 else 16,
    )

    keep, send, qkv, mixed, normed_attn = kernel(
        functools.partial(attend_body, heads),
        [
            out((half_rows, width), F32),
            out((half_rows, width), BF),
            Far(out((row_count, 3 * inner), BF)),
            Far(out((row_count, inner), BF)),
            Far(out((row_count, width), BF)),
        ],
        Far(gain_attn),
        Far(w_in_t),
        Far(w_out),
        Far(cosine),
        Far(sine),
        Far(bias),
        *blocks,
        deps=(Far(sent_grads),),
        vmem=24,
    )

    def half_sum(keep, send):
        (half,) = kernel(fold_body, [out((half_rows, width), BF)], keep, swap(send, "lo"))
        return half, swap(half, "hi")

    after_attn, normed_own, far_normed = kernel(
        norm_body,
        [
            Far(out((half_rows, width), F32)),
            out((half_rows, width), BF),
            Far(out((half_rows, width), BF)),
        ],
        gain_ffn,
        *half_sum(keep, send),
        blocks[0],
        blocks[1],
    )
    normed_got = swap(normed_own, "lo")

    (sent_rows,) = kernel(
        send_rows_body,
        [out((own_slots, width), BF)],
        Far(slot_pick),
        normed_own,
        normed_got,
        deps=(Far(got_grads),),
    )
    got_rows = exchange(sent_rows.reshape(devices_dp, part_rows, width))

    units = w_shared_gate.shape[1]
    shared_part, shared_back, grad_sgate, grad_sup, shared_hidden = kernel(
        shared_body,
        [
            Far(out((row_count, width), F32)),
            Far(out((row_count, width), F32)),
            Far(out((row_count, units), BF)),
            Far(out((row_count, units), BF)),
            Far(out((row_count, units), BF)),
        ],
        Far(far_normed),
        Far(normed_got),
        *far_blocks,
        Far(w_shared_gate),
        Far(w_shared_up),
        Far(w_shared_down),
        deps=(Far(sent_rows),),
        vmem=24,
    )
    tree_first = (dz // 2, 2, chunk)
    shared_keep, shared_send = kernel(
        shared_grads_body,
        [Far(out(tree_first + (3 * units,), F32)), out(tree_first + (3 * units,), BF)],
        Far(far_normed),
        Far(normed_got),
        *far_blocks,
        Far(grad_sgate),
        Far(grad_sup),
        Far(shared_hidden),
        scalars=(info,),
        vmem=24,
    )

    def z_swap(values, bit):
        return lax.ppermute(values, "dz", [(i, i ^ (1 << bit)) for i in range(dz)])

    def tree_step(kept, got, which, deps=()):
        columns = kept.shape[-1]
        kept = kept.reshape(-1, 2, chunk, columns)
        shape = (kept.shape[0], chunk, columns)
        return kernel(
            functools.partial(tree_body, which),
            [Far(out(shape, F32)), out(shape, BF)],
            Far(kept),
            got.reshape(kept.shape),
            scalars=(info,),
            deps=deps,
        )

    def tree_rest(keep, got, first, deps=()):
        for bit in range(first, log2(dz)):
            keep, send = tree_step(keep, got, Z_FIRST + bit, deps)
            got = z_swap(send, bit)
        return keep, got, send

    shared_got = z_swap(shared_send, 0)
    rows_own, rows_got = sub_gather(tie(got_rows, shared_send, Far(marks)))

    hidden_units = routed_gate_weight.shape[1]
    tile = min(256, own_slots)
    tiles = all_slots // 2 // tile
    steps = 2 * tiles

    def mine_at(i):
        return (jnp.minimum(i, tiles - 1), 0)

    def other_at(i):
        return (jnp.maximum(i - tiles, 0), 0)

    def every_at(i):
        return (i, 0)

    def fixed_at(i):
        return (0, 0)

    half_slots = all_slots // 2
    expert_ins = [
        (rows_own, pl.BlockSpec((tile, width), mine_at)),
        (rows_got, pl.BlockSpec((tile, width), other_at)),
        (grads_own, pl.BlockSpec((tile, width + 128), mine_at)),
        (grads_got, pl.BlockSpec((tile, width + 128), other_at)),
        (marks, pl.BlockSpec((tile, 128), every_at)),
        (router, pl.BlockSpec((128, width), fixed_at)),
        (routed_gate_weight, pl.BlockSpec((width, hidden_units), fixed_at)),
        (routed_up_weight, pl.BlockSpec((width, hidden_units), fixed_at)),
        (w_expert_down, pl.BlockSpec((hidden_units, width), fixed_at)),
    ]
    expert_outs = [
        (out((half_slots, width), BF), pl.BlockSpec((tile, width), mine_at)),
        (out((half_slots, width), BF), pl.BlockSpec((tile, width), other_at)),
        (out((half_slots, width), BF), pl.BlockSpec((tile, width), mine_at)),
        (out((half_slots, width), BF), pl.BlockSpec((tile, width), other_at)),
        (out((all_slots, width), BF), pl.BlockSpec((tile, width), every_at)),
        (out((all_slots, hidden_units), BF), pl.BlockSpec((tile, hidden_units), every_at)),
        (out((all_slots, hidden_units), BF), pl.BlockSpec((tile, hidden_units), every_at)),
        (out((all_slots, hidden_units), BF), pl.BlockSpec((tile, hidden_units), every_at)),
        (out((all_slots, width), BF), pl.BlockSpec((tile, width), every_at)),
        (out((half_slots, 128), F32), pl.BlockSpec((tile, 128), mine_at)),
        (out((128, width), F32), pl.BlockSpec((128, width), fixed_at)),
    ]

    def expert_kernel(*refs):
        pltpu.emit_pipeline(
            functools.partial(expert_body, tiles),
            grid=(steps,),
            in_specs=[spec for _, spec in expert_ins],
            out_specs=[spec for _, spec in expert_outs],
        )(*refs)

    hbm_spec = pl.BlockSpec(memory_space=pltpu.HBM)
    (
        back_keep,
        back_send,
        part_keep,
        part_send,
        rows_all,
        expert_hidden,
        grad_egate,
        grad_eup,
        pair_grads,
        gates,
        router_part,
    ) = pl.pallas_call(
        expert_kernel,
        in_specs=[hbm_spec] * len(expert_ins),
        out_specs=tuple([hbm_spec] * len(expert_outs)),
        out_shape=tuple(pltpu.HBM(shape.shape, shape.dtype) for shape, _ in expert_outs),
        compiler_params=pltpu.CompilerParams(vmem_limit_bytes=44 * MIB),
        cost_estimate=COST,
        name="expert_body",
    )(*[in_hbm(value) for value, _ in expert_ins])

    def sub_scatter(keep, send):
        total = keep.astype(F32) + swap(send, "lo").astype(F32)
        return total[:own_slots] + swap(total[own_slots:].astype(BF), "hi").astype(F32)

    if sub == 4:
        back_sum = sub_scatter(back_keep, back_send).astype(BF)
    else:
        (back_sum,) = kernel(
            add_body, [out((own_slots, width), BF)], Far(back_keep), swap(back_send, "lo")
        )
    got_back = exchange(back_sum.reshape(devices_dp, part_rows, width))
    grad_w_expert_down = dot_t(expert_hidden, pair_grads)
    grad_w_expert_gate = dot_t(rows_all, grad_egate)
    grad_w_expert_up = dot_t(rows_all, grad_eup)
    shared_keep, shared_send = tree_step(shared_keep, shared_got, Y, (Far(back_sum),))
    shared_got = swap(shared_send, "dy")
    if sub == 4:
        part_sum = (gates[:own_slots, :1] * sub_scatter(part_keep, part_send)).astype(BF)
    else:
        (part_sum,) = kernel(
            part_body,
            [out((own_slots, width), BF)],
            Far(part_keep),
            swap(part_send, "lo"),
            Far(gates),
            deps=(Far(back_sum),),
        )
    got_back = tie(
        got_back,
        Far(grad_w_expert_down),
        Far(grad_w_expert_gate),
        Far(grad_w_expert_up),
        shared_send,
        Far(part_sum),
    ).reshape(own_slots, width)

    keep, send = kernel(
        combine_body,
        [out((half_rows, width), F32), out((half_rows, width), BF)],
        Far(slot_pick_t),
        Far(got_back),
        Far(shared_back),
    )
    part_sum = tie(part_sum, send)
    got_parts = exchange(part_sum.reshape(devices_dp, part_rows, width)).reshape(own_slots, width)
    shared_keep, shared_got, shared_got_send = tree_rest(shared_keep, shared_got, 1, (send,))
    grad_sgate, grad_sup, grad_sdown = kernel(
        shared_end_body,
        [Far(out((chunk, units), F32))] * 3,
        Far(shared_keep),
        shared_got,
    )
    after_grad, after_grad_own, far_grad, gain_ffn_part = kernel(
        norm_back_body,
        [
            Far(out((half_rows, width), F32)),
            out((half_rows, width), BF),
            Far(out((half_rows, width), BF)),
            Far(out((8, width), F32)),
        ],
        gain_ffn,
        *half_sum(keep, send),
        Far(after_attn),
        far_blocks[0],
        far_blocks[1],
    )
    after_grad_got = swap(after_grad_own, "lo")

    keep, send, projected_grad, gain_attn_part = kernel(
        functools.partial(attend_back_body, heads),
        [
            out((half_rows, width), F32),
            out((half_rows, width), BF),
            Far(out((row_count, 3 * inner), BF)),
            Far(out((8, width), F32)),
        ],
        Far(w_out),
        Far(w_in_t),
        Far(cosine),
        Far(sine),
        Far(bias),
        Far(qkv),
        after_grad_own,
        after_grad_got,
        *far_blocks,
        vmem=24,
        deps=(shared_got_send,),
    )
    keep, send = kernel(
        to_bottom_body,
        [out((half_rows, 2 * width), F32), out((half_rows, 2 * width), BF)],
        Far(slot_pick_t),
        Far(got_parts),
        Far(shared_part),
        keep,
        send,
    )
    got = swap(send, "lo")
    last_keep, last_send = kernel(
        functools.partial(last_grads_body, experts_all),
        [
            Far(out((dz, chunk, 4 * inner + 128), F32)),
            out((dz, chunk, 4 * inner + 128), BF),
        ],
        Far(normed_attn),
        Far(projected_grad),
        Far(far_grad),
        Far(after_grad_got),
        Far(mixed),
        Far(gain_ffn_part),
        Far(gain_attn_part),
        Far(router_part),
        scalars=(info,),
        vmem=24,
        deps=(send,),
    )
    last_got = swap(last_send, "dy")
    last_keep, last_send = tree_step(last_keep, last_got, Z_FIRST)
    last_got = z_swap(last_send, 0)
    own, send = kernel(
        fold_own_body,
        [out((shard_rows, 2 * width), F32), out((shard_rows, 2 * width), BF)],
        keep,
        got,
    )
    (sent_last,) = kernel(
        last_body,
        [out((shard_rows, 2 * width), BF)],
        gain_attn,
        own,
        swap(send, "hi"),
        far_blocks[0],
        Far(after_grad),
        Far(after_attn),
        deps=(Far(grad_sdown),),
    )
    got_last = exchange(sent_last.reshape(devices_dp, shard_block, 2 * width))
    got_last = tie(got_last, last_send)
    final, grad_tokens = kernel(
        return_body,
        [Far(out((row_count, width), BF)), Far(out((row_count, width), BF))],
        Far(anchor),
        *blocks_of(got_last.reshape(shard_rows, 2 * width)),
    )

    last_keep, last_got, _ = tree_rest(last_keep, last_got, 1)
    small_rows = experts_all + 8
    grad_qkv, grad_out, small = kernel(
        functools.partial(last_end_body, small_rows),
        [
            Far(out((chunk, 3 * inner), F32)),
            Far(out((inner, chunk), F32)),
            out((small_rows, chunk), F32),
        ],
        Far(last_keep),
        last_got,
    )
    small = small + swap(small, "hi")
    small = small + swap(small, "lo")
    return (
        final,
        grad_tokens,
        small[experts_all + 1],
        grad_qkv,
        grad_out,
        small[experts_all],
        small[:experts_all].T,
        grad_sgate,
        grad_sup,
        grad_sdown.T,
        grad_w_expert_gate,
        grad_w_expert_up,
        grad_w_expert_down,
    )


def solution(mesh):
    devices_dp, devices_tp = mesh.shape["dp"], mesh.shape["tensor"]
    fine = Mesh(
        mesh.devices.reshape(devices_dp // 2, 2, devices_tp // 2, 2), ("dz", "dy", "hi", "lo")
    )
    every = DP + TP
    return jax.shard_map(
        on_device,
        mesh=fine,
        in_specs=(
            P(DP, None),
            P(DP, None),
            P(),
            P(None, TP),
            P(TP, None),
            P(),
            P(),
            P(None, TP),
            P(None, TP),
            P(TP, None),
            P(None, every),
            P(None, every),
            P(every, None),
            P(DP, None),
            P(DP),
            P(DP),
            P(DP, None),
            P(DP, None),
        ),
        out_specs=(
            P(DP, None),
            P(DP, None),
            P(DP),
            P(DP, TP),
            P(TP, DP),
            P(DP),
            P(DP, None),
            P(DP, TP),
            P(DP, TP),
            P(TP, DP),
            P(None, every),
            P(None, every),
            P(every, None),
        ),
        check_vma=False,
    )
```

```python
import functools

import jax
import jax.numpy as jnp
import numpy as np
from jax import lax
from jax.experimental import pallas as pl
from jax.experimental.pallas import tpu as pltpu
from jax.sharding import Mesh, PartitionSpec as P

HD = 64
MY_BLOCK, PICK, MY_PART, MY_EXPERT, MY_DP, Y_BIT, Z_BITS = range(7)
EPSILON = 1e-06
BF = jnp.bfloat16
F32 = jnp.float32
I32 = jnp.int32
DP = ("dz", "dy")
TP = ("hi", "lo")
MIB = 1 << 20
COST = pl.CostEstimate(flops=1000, bytes_accessed=1000, transcendentals=0)


def dot(left, right):
    return jnp.dot(left, right, preferred_element_type=F32)


def dot_t(left, right):
    return lax.dot_general(left, right, (((0,), (0,)), ((), ())), preferred_element_type=F32)


def dot_bt(left, right):
    return lax.dot_general(left, right, (((1,), (1,)), ((), ())), preferred_element_type=F32)


def swap(values, axis):
    return lax.ppermute(values, axis, [(0, 1), (1, 0)])


def exchange_stacked(values):
    order = jnp.arange(values.shape[0], dtype=I32) ^ lax.axis_index(DP)
    got = lax.all_to_all(
        jnp.take(values, order, axis=0), DP, split_axis=0, concat_axis=0, tiled=True
    )
    return jnp.take(got, order, axis=0)


def exchange(pieces):
    devices = lax.axis_size(DP)
    if len(pieces) == 1:
        (values,) = pieces
        stacked = values.reshape(devices, -1, values.shape[-1])
        return [exchange_stacked(stacked).reshape(values.shape)]
    order = [7, 6, 5, 4, 3, 2, 1]
    got = list(pieces)
    for k in order:
        got[k] = lax.ppermute(pieces[k], DP, [(i, i ^ k) for i in range(devices)])
    return got


def out(shape, dtype):
    return jax.ShapeDtypeStruct(shape, dtype)


class Far:
    def __init__(self, value):
        self.value = value


class Held(Far):
    pass


class Free(Far):
    pass


class Arriving:
    def __init__(self, buffer, copy):
        self.buffer, self.copy, self.waiting = buffer, copy, True
        self.shape, self.dtype = buffer.shape, buffer.dtype

    def ready(self):
        if self.waiting:
            self.copy.wait()
            self.waiting = False

    def __getitem__(self, index):
        self.ready()
        return self.buffer[index]


class Leaving:
    def __init__(self, buffer, copy):
        self.buffer, self.copy, self.started = buffer, copy, False
        self.shape, self.dtype = buffer.shape, buffer.dtype

    def flush(self):
        if not self.started:
            self.copy.start()
            self.started = True

    def __getitem__(self, index):
        return self.buffer[index]

    def __setitem__(self, index, value):
        self.buffer[index] = value


def in_hbm(values):
    return pltpu.with_memory_space_constraint(values, pltpu.HBM)


def in_vmem(values):
    return pltpu.with_memory_space_constraint(values, pltpu.VMEM)


def at_hbm(shape):
    return pltpu.HBM(shape.shape, shape.dtype)


def at_vmem(shape):
    return pltpu.VMEM(shape.shape, shape.dtype)


def kernel(body, outs, *args, scalars=(), deps=(), vmem=16, semaphores=0):
    vmem_spec = pl.BlockSpec(memory_space=pltpu.VMEM)
    hbm_spec = pl.BlockSpec(memory_space=pltpu.HBM)
    any_spec = pl.BlockSpec(memory_space=pl.ANY)
    held = [isinstance(a, Held) for a in args]
    far_in = [isinstance(a, Far) and not h for a, h in zip(args, held)]
    free_out = [isinstance(o, Free) for o in outs]
    far_out = [isinstance(o, Far) and not f for o, f in zip(outs, free_out)]
    args = [in_hbm(a.value) if isinstance(a, Far) else in_vmem(a) for a in args]
    outs = [
        o.value if f else at_hbm(o.value) if h else at_vmem(o)
        for o, f, h in zip(outs, free_out, far_out)
    ]
    deps = [in_hbm(d.value) if isinstance(d, Far) else d for d in deps]
    moved = [x for x, f in zip(args + outs, far_in + far_out) if f]
    scratch = [pltpu.VMEM(x.shape, x.dtype) for x in moved]
    if moved:
        scratch.append(pltpu.SemaphoreType.DMA((len(moved),)))
    if semaphores:
        scratch.append(pltpu.SemaphoreType.DMA((semaphores,)))
    n_scalars, n_args, n_deps, n_outs = len(scalars), len(args), len(deps), len(outs)

    def wrapped(*refs):
        ins = list(refs[: n_scalars + n_args])
        results = list(refs[n_scalars + n_args + n_deps :][:n_outs])
        buffers = refs[n_scalars + n_args + n_deps + n_outs :]
        extra = buffers[-1:] if semaphores else ()
        buffers = buffers[:-1] if semaphores else buffers
        at = 0
        for i, far in enumerate(far_in):
            if far:
                ref = ins[n_scalars + i]
                copy = pltpu.make_async_copy(ref, buffers[at], buffers[-1].at[at])
                copy.start()
                ins[n_scalars + i] = Arriving(buffers[at], copy)
                at += 1
        for i, far in enumerate(far_out):
            if far:
                copy = pltpu.make_async_copy(buffers[at], results[i], buffers[-1].at[at])
                results[i] = Leaving(buffers[at], copy)
                at += 1
        body(*ins, *results, *extra)
        for ref in ins:
            if isinstance(ref, Arriving):
                ref.ready()
        for ref in results:
            if isinstance(ref, Leaving):
                ref.flush()
        for ref in results:
            if isinstance(ref, Leaving):
                ref.copy.wait()

    return pl.pallas_call(
        wrapped,
        out_shape=tuple(outs),
        in_specs=[pl.BlockSpec(memory_space=pltpu.SMEM)] * n_scalars
        + [hbm_spec if f or h else vmem_spec for f, h in zip(far_in, held)]
        + [any_spec] * n_deps,
        out_specs=tuple(hbm_spec if far else vmem_spec for far in far_out),
        scratch_shapes=scratch,
        compiler_params=pltpu.CompilerParams(vmem_limit_bytes=vmem * MIB),
        cost_estimate=COST,
        name=body.func.__name__ if isinstance(body, functools.partial) else body.__name__,
    )(*scalars, *args, *deps)


def tie(values, *deps):
    any_spec = pl.BlockSpec(memory_space=pl.ANY)
    vmem_spec = pl.BlockSpec(memory_space=pltpu.VMEM)
    return pl.pallas_call(
        lambda *refs: None,
        out_shape=out(values.shape, values.dtype),
        in_specs=[vmem_spec] + [any_spec] * len(deps),
        out_specs=vmem_spec,
        input_output_aliases={0: 0},
        cost_estimate=COST,
        name="tie",
    )(in_vmem(values), *[in_hbm(d.value) if isinstance(d, Far) else d for d in deps])


def rope_table(places):
    exponent = np.arange(HD // 2, dtype=np.float32) * np.float32(-2.0 / HD)
    angles = np.arange(places, dtype=np.float32)[:, None] * np.power(np.float32(10000.0), exponent)
    cosine = np.cos(angles.astype(np.float64)).astype(np.float32)
    sine = np.sin(angles.astype(np.float64)).astype(np.float32)
    rest = np.concatenate([cosine, cosine, -sine, sine], 1)
    terms = []
    for _ in range(3):
        terms.append(rest.astype(BF))
        rest = rest - terms[-1].astype(np.float32)
    return jnp.asarray(np.concatenate(terms, 1))


def iota(shape, dim):
    return lax.broadcasted_iota(I32, shape, dim)


def log2(number):
    return number.bit_length() - 1


def silu_parts(gate_in):
    sigmoid_val = 1.0 / (1.0 + jnp.exp(-gate_in))
    return (gate_in * sigmoid_val, sigmoid_val * (1.0 + gate_in * (1.0 - sigmoid_val)))


def inverse_root(values):
    return lax.rsqrt(jnp.mean(values * values, -1, keepdims=True) + EPSILON)


def rms_backward(values, root, gain, grad_normed):
    scaled = grad_normed * gain
    return root * scaled - values * (root * root * root) * jnp.mean(
        scaled * values, -1, keepdims=True
    )


def lane_rank(buckets, bucket_count):
    count = buckets.shape[1]
    rows = max(8, bucket_count)
    member = (iota((rows, count), 0) == buckets).astype(F32)
    earlier = (iota((count, count), 0) < iota((count, count), 1)).astype(F32).astype(BF)
    return jnp.sum(dot(member.astype(BF), earlier) * member, 0, keepdims=True).astype(I32)


def relative_row(block, rank, my_block, shard_block, shard_rows):
    shift = log2(shard_block)
    return (
        ((rank >> shift) ^ my_block) * shard_rows
        + block * shard_block
        + (rank & (shard_block - 1))
    )


def rope_back(grads, cosine, sine):
    return grads * cosine - half_turned(grads) * sine


def store_pieces(refs, value):
    rows = refs[0].shape[0]
    for i, ref in enumerate(refs):
        ref[...] = value[i * rows : (i + 1) * rows]


def joined(refs):
    return jnp.concatenate([ref[...] for ref in refs], 0) if len(refs) > 1 else refs[0][...]


def join_body(*refs):
    *parts, whole = refs
    rows = parts[0].shape[0]
    for i, ref in enumerate(parts):
        whole[i * rows : (i + 1) * rows, :] = ref[...]


def middle_body(block, near, far, *outs):
    for i, ref in enumerate(outs):
        ref[:block, :] = near[i * block : (i + 1) * block, :]
        ref[block:, :] = far[i * block : (i + 1) * block, :]


def store_halves(near, far, block, value, columns):
    for i in range(near.shape[0] // block):
        at = 2 * i * block
        near[i * block : (i + 1) * block, columns] = value[at : at + block]
        far[i * block : (i + 1) * block, columns] = value[at + block : at + 2 * block]


def fetch_body(*refs):
    *refs, semaphores = refs
    count = len(refs) // 2 - 1
    copies = [
        pltpu.make_async_copy(refs[i], refs[count + 1 + i], semaphores.at[i])
        for i in range(count)
    ]
    for copy in copies:
        copy.start()
    narrow, router = refs[count], refs[-1]
    experts, width = narrow.shape
    router[...] = jnp.concatenate(
        [narrow[...], jnp.zeros((router.shape[0] - experts, width), BF)], 0
    )
    for copy in copies:
        copy.wait()


def select_body(shard_block, blocks, info, inverse, tokens, cotangent, near, far, anchor):
    row_count, width = tokens.shape
    shard_rows = shard_block * blocks
    target = (inverse[...] >> log2(row_count)) ^ info[MY_DP]
    row = relative_row(target, lane_rank(target, blocks), info[MY_BLOCK], shard_block, shard_rows)
    anchor[...] = row
    pick = (iota((shard_rows, row_count), 0) == row).astype(F32).astype(BF)
    store_halves(near, far, shard_block, dot(pick, tokens[...]).astype(BF), slice(0, width))
    store_halves(near, far, shard_block, dot(pick, cotangent[...]).astype(BF), slice(width, None))


def index_body(
    shard_block,
    copies,
    per_dp,
    part_rows,
    experts_all,
    info,
    lengths,
    order,
    routes,
    fill,
    table,
    slot_pick,
    slot_pick_t,
    bias,
    cosine,
    sine,
    meta,
):
    row_count = order.shape[1]
    devices_dp = slot_pick.shape[0] // part_rows
    shard_rows = shard_block * devices_dp
    source = (order[...] >> log2(row_count)) ^ info[MY_DP]
    local = relative_row(
        source, lane_rank(source, devices_dp), info[MY_BLOCK], shard_block, shard_rows
    )
    place_pick = (iota((row_count, row_count), 0) == local).astype(F32).astype(BF)
    lanes = iota((1, row_count), 1)
    segment = jnp.zeros((1, row_count), I32)
    start = jnp.zeros((1, row_count), I32)
    end = jnp.int32(0)
    for entry in range(lengths.shape[1]):
        end = end + lengths[0, entry]
        passed = lanes >= end
        segment = segment + passed.astype(I32)
        start = jnp.maximum(start, jnp.where(passed, end, 0))
    place = lanes - start
    expert_sum = routes[0:1, :] + routes[1:2, :] + 1
    facts = jnp.concatenate(
        [segment, place >> 1, place & 1, expert_sum, jnp.zeros((4, row_count), I32)], 0
    )
    facts = facts.astype(F32).astype(BF)
    across = dot_bt(facts, place_pick)
    down = dot_bt(place_pick, facts)
    place_row = 2.0 * across[1:2] + across[2:3]
    place_col = 2.0 * down[:, 1:2] + down[:, 2:3]
    allowed = (down[:, 0:1] == across[0:1]) & (place_row <= place_col)
    bias[...] = jnp.where(allowed, 0.0, -1e30).astype(BF)
    at_place = (
        iota((row_count, row_count), 1).astype(F32) == place_col
    ).astype(F32).astype(BF)
    turned = dot(at_place, table[...])
    pieces = [turned[:, i * 128 : (i + 1) * 128] for i in range(3)]
    turned = pieces[0] + pieces[1] + pieces[2]
    cosine[...] = turned[:, :HD]
    sine[...] = turned[:, HD:]
    meta[...] = jnp.broadcast_to(down[:, 3:4], meta.shape).astype(BF)
    pairs = 2 * row_count
    fill_at = (fill[...] & 1) * row_count + (fill[...] >> 1)
    fill_pick = (iota((pairs, pairs), 0) == fill_at).astype(F32).astype(BF)
    expert_rows = max(16, experts_all)
    pair_expert = jnp.concatenate([routes[0:1, :], routes[1:2, :]], 1)
    named = (iota((expert_rows, pairs), 0) == pair_expert).astype(F32).astype(BF)
    member = dot(named, fill_pick)
    earlier = (iota((pairs, pairs), 0) < iota((pairs, pairs), 1)).astype(F32).astype(BF)
    ranks = (member * (dot(member.astype(BF), earlier) + 1.0)).astype(BF)
    ranks = dot_bt(ranks, fill_pick)
    ranks = (ranks[:, :row_count] + ranks[:, row_count:]).astype(BF)
    ranks = dot_bt(ranks, place_pick).astype(I32)
    slots = iota((part_rows, row_count), 0) + (info[MY_PART] * part_rows + 1)
    experts = iota((expert_rows, row_count), 0)
    for target in range(devices_dp):
        expert = ((target ^ info[MY_DP]) >> log2(copies)) * per_dp + info[PICK]
        chosen = jnp.sum(jnp.where(experts == expert, ranks, 0), 0, keepdims=True)
        picked = (slots == chosen).astype(F32)
        slot_pick[target * part_rows : (target + 1) * part_rows, :] = picked.astype(BF)
    slot_pick_t[...] = slot_pick[...].astype(F32).T.astype(BF)


def send_grads_body(slot_pick, meta, b0, b1, b2, b3, *sent):
    width = b0.shape[1] // 2
    grads = jnp.concatenate([b[:, width:] for b in (b0, b1, b2, b3)], 0)
    grads = jnp.concatenate([grads, meta[...]], 1)
    store_pieces(sent, dot(slot_pick[...], grads).astype(BF))


def head_parts(projected, heads):
    return [
        [projected[:, (3 * h + i) * HD : (3 * h + i + 1) * HD] for i in range(3)]
        for h in range(heads)
    ]


def half_turned(values):
    half = values.shape[1] // 2
    return jnp.concatenate([values[:, half:], values[:, :half]], 1)


def attend_body(
    heads, gain, w_in_t, w_out, cosine, sine, bias, b0, b1, b2, b3, keep, send, qkv, mixed, normed
):
    width = b0.shape[1] // 2
    half = keep.shape[0]
    tokens = jnp.concatenate([b[:, :width] for b in (b0, b1, b2, b3)], 0).astype(F32)
    normed[...] = (tokens * inverse_root(tokens) * gain[...]).astype(BF)
    projected = dot_bt(normed[...], w_in_t[...])
    cosine, sine = cosine[...], sine[...]
    parts = []
    for query, keys, values in head_parts(projected, heads):
        parts.append((query * cosine + half_turned(query) * sine).astype(BF))
        parts.append((keys * cosine + half_turned(keys) * sine).astype(BF))
        parts.append(values.astype(BF))
    qkv[...] = jnp.concatenate(parts, 1)
    scale = HD**-0.5
    mixed_heads = []
    for query, keys, values in head_parts(qkv, heads):
        scores = dot_bt(query, keys) * scale + bias[...].astype(F32)
        powers = jnp.exp(scores - jnp.max(scores, -1, keepdims=True))
        weights = powers * (1.0 / jnp.sum(powers, -1, keepdims=True))
        mixed_heads.append(dot(weights.astype(BF), values))
    mixed[...] = jnp.concatenate(mixed_heads, 1).astype(BF)
    part = dot(mixed[...], w_out[...])
    keep[...] = part[:half]
    send[...] = part[half:].astype(BF)


def fold_body(keep, got, half):
    half[...] = (keep[...] + got[...].astype(F32)).astype(BF)


def fold_own_body(keep, got, own, send):
    rows = own.shape[0]
    own[...] = keep[:rows, :] + got[:rows, :].astype(F32)
    send[...] = (keep[rows:, :] + got[rows:, :].astype(F32)).astype(BF)


def both(half, got):
    rows = half.shape[0] // 2
    mine, other = half[...].astype(F32), got[...].astype(F32)
    return mine + jnp.concatenate([other[rows:], other[:rows]], 0)


def norm_body(gain, half, got, b0, b1, after_attn, normed):
    width = half.shape[1]
    balanced = jnp.concatenate([b0[:, :width], b1[:, :width]], 0).astype(F32)
    values = balanced + both(half, got)
    after_attn[...] = values
    normed[...] = (values * inverse_root(values) * gain[...]).astype(BF)


def send_rows_body(slot_pick, own, got, *sent):
    rows = jnp.concatenate([own[...], got[...]], 0)
    store_pieces(sent, dot(slot_pick[...], rows).astype(BF))


def shared_body(
    own, got, b0, b1, b2, b3, w_gate, w_up, w_down, part, back, grad_gate, grad_up, hidden
):
    width = own.shape[1]
    rows = jnp.concatenate([own[...], got[...]], 0)
    grads = jnp.concatenate([b[:, width:] for b in (b0, b1, b2, b3)], 0)
    gate = dot(rows, w_gate[...])
    up = dot(rows, w_up[...])
    act, slope = silu_parts(gate)
    hidden[...] = (act * up).astype(BF)
    part[...] = dot(hidden[...], w_down[...])
    hidden_grad = dot_bt(grads, w_down[...])
    grad_gate[...] = (hidden_grad * up * slope).astype(BF)
    grad_up[...] = (hidden_grad * act).astype(BF)
    back[...] = dot_bt(grad_gate[...], w_gate[...]) + dot_bt(grad_up[...], w_up[...])


def store_tree(bit, sums, keep, send, columns=slice(None)):
    pairs, chunk, _ = keep.shape
    mine = bit == 0
    for i in range(pairs):
        at = 2 * i * chunk
        first, second = sums[at : at + chunk], sums[at + chunk : at + 2 * chunk]
        keep[i, :, columns] = jnp.where(mine, first, second)
        send[i, :, columns] = jnp.where(mine, second, first).astype(BF)


def shared_grads_body(
    info, own, got, b0, b1, b2, b3, grad_gate, grad_up, hidden, keep, send
):
    width = own.shape[1]
    rows = jnp.concatenate([own[...], got[...]], 0)
    grads = jnp.concatenate([b[:, width:] for b in (b0, b1, b2, b3)], 0)
    units = hidden.shape[1]
    pairs = ((rows, grad_gate[...]), (rows, grad_up[...]), (grads, hidden[...]))
    for which, (left, right) in enumerate(pairs):
        columns = slice(which * units, (which + 1) * units)
        store_tree(info[Y_BIT], dot_t(left, right), keep, send, columns)


def last_grads_body(
    experts, info, normed, projected_grad, own, got, mixed, gain_ffn, gain_attn, router, keep, send
):
    width = normed.shape[1]
    small = jnp.concatenate(
        [
            router[:experts, :],
            gain_ffn[:1, :],
            gain_attn[:1, :],
            jnp.zeros((128 - experts - 2, width), F32),
        ],
        0,
    )
    grads = jnp.concatenate([own[...], got[...]], 0)
    sums = jnp.concatenate(
        [dot_t(normed[...], projected_grad[...]), dot_t(grads, mixed[...]), small.T], 1
    )
    store_tree(info[Y_BIT], sums, keep, send)


def tree_body(which, info, kept, got, keep, send):
    bit = info[which]
    total = kept[...] + got[...].astype(F32)
    pairs = total.shape[0]
    for index in range(pairs):
        mine = bit == 0
        first, second = total[index, 0], total[index, 1]
        keep[index] = jnp.where(mine, first, second)
        send[index] = jnp.where(mine, second, first).astype(BF)


def last_end_body(small_rows, kept, got, grad_qkv, grad_out, small):
    total = kept[0] + got[0].astype(F32)
    columns, inner = grad_qkv.shape[1], grad_out.shape[0]
    grad_qkv[...] = total[:, :columns]
    grad_out[...] = total[:, columns : columns + inner].T
    small[...] = total[:, columns + inner :].T[:small_rows]


def shared_end_body(kept, got, grad_gate, grad_up, grad_down):
    total = kept[0] + got[0].astype(F32)
    units = grad_gate.shape[1]
    grad_gate[...] = total[:, :units]
    grad_up[...] = total[:, units : 2 * units]
    grad_down[...] = total[:, 2 * units :]


def add_body(keep, got, *total):
    store_pieces(total, (keep[...].astype(F32) + got[...].astype(F32)).astype(BF))


def weight_grad_body(left, right, total, sums, semaphores):
    tile = 256
    copies = []
    for i in range(left.shape[1] // tile):
        at = slice(i * tile, (i + 1) * tile)
        sums[at, :] = dot_t(left[:, at], right[...])
        copies.append(
            pltpu.make_async_copy(sums.at[at, :], total.at[at, :], semaphores.at[i])
        )
        copies[-1].start()
    for copy in copies:
        copy.wait()


def to_bottom_body(slot_pick_t, addend, attn_keep, attn_send, *refs):
    *back, keep, send = refs
    half, width = attn_keep.shape
    total = addend[...] + dot(slot_pick_t[...], joined(back))
    keep[:, :width] = total[:half]
    send[:, :width] = total[half:].astype(BF)
    keep[:, width:] = attn_keep[...]
    send[:, width:] = attn_send[...]


def meta_body(devices_dp, part_rows, sub, capacity, width, info, own, got, marks):
    my_part, my_expert = info[MY_PART], info[MY_EXPERT]
    lanes = iota((part_rows, 128), 1)
    blocks = [(ref, at, part) for part, (ref, at) in enumerate(
        [(own, i) for i in range(sub // 2)] + [(got, i) for i in range(sub // 2)]
    )]
    counts = []
    for block in range(devices_dp):
        count = jnp.zeros((1, 128), F32)
        for ref, at, _ in blocks:
            start = (at * devices_dp + block) * part_rows
            value = ref[start : start + part_rows, width:].astype(F32)
            count = count + jnp.sum((value > 0.0).astype(F32), 0, keepdims=True)
        counts.append(count)
    for block in range(devices_dp):
        earlier = jnp.zeros((1, 128), F32)
        for before in range(devices_dp):
            ahead = (before ^ info[MY_DP]) < (block ^ info[MY_DP])
            earlier = earlier + jnp.where(ahead, counts[before], 0.0)
        for ref, at, part in blocks:
            start = (at * devices_dp + block) * part_rows
            value = ref[start : start + part_rows, width:].astype(F32)
            valid = value > 0.0
            slot = iota((part_rows, 128), 0) + (my_part ^ part) * part_rows
            kept = valid & (slot.astype(F32) + earlier < capacity)
            other = value.astype(I32) - 1 - my_expert
            mark = (lanes == my_expert).astype(F32) - (lanes == other).astype(F32)
            row = (part * devices_dp + block) * part_rows
            marks[row : row + part_rows, :] = jnp.where(
                lanes == 127, kept.astype(F32), jnp.where(valid, mark, 0.0)
            )


def expert_step(rows, grads, mark, w_router, w_gate, w_up, w_down, stores):
    hidden_out, grad_gate_out, grad_up_out, pair_out = stores
    width = rows.shape[1]
    grads = grads[:, :width].astype(F32)
    kept = mark[:, 127:128] > 0.5
    mark = jnp.where(iota(mark.shape, 1) == 127, 0.0, mark)
    gap = jnp.sum(dot_bt(rows, w_router[...]) * mark, 1, keepdims=True)
    gate = 1.0 / (1.0 + jnp.exp(-gap))
    gate_other = 1.0 / (1.0 + jnp.exp(gap))
    gate_in = dot(rows, w_gate[...])
    up = dot(rows, w_up[...])
    act, slope = silu_parts(gate_in)
    hidden = (act * up).astype(BF)
    hidden_out(hidden)
    part = jnp.where(kept, dot(hidden, w_down[...]), 0.0).astype(BF)
    pair = jnp.where(kept, gate * grads, 0.0).astype(BF)
    pair_out(pair)
    gate_grad = jnp.sum(part.astype(F32) * grads, 1, keepdims=True)
    logit_grad = (gate * gate_other * gate_grad * mark).astype(BF)
    hidden_grad = dot_bt(pair, w_down[...])
    grad_gate = (hidden_grad * up * slope).astype(BF)
    grad_up = (hidden_grad * act).astype(BF)
    grad_gate_out(grad_gate)
    grad_up_out(grad_up)
    back = (dot_bt(grad_gate, w_gate[...]) + dot_bt(grad_up, w_up[...])).astype(BF).astype(F32)
    back = (back + dot(logit_grad, w_router[...])).astype(BF)
    return back, part, gate, dot_t(logit_grad, rows)


def store_at(ref, where=...):
    def store(value):
        ref[where] = value

    return store


def expert_body(
    tiles,
    rows_own,
    rows_got,
    grads_own,
    grads_got,
    marks,
    w_router,
    w_gate,
    w_up,
    w_down,
    back_keep,
    back_send,
    part_keep,
    part_send,
    rows_all,
    hidden,
    grad_gate,
    grad_up,
    pair,
    gates,
    router,
):
    step = pl.program_id(0)
    mine = step < tiles
    rows = jnp.where(mine, rows_own[...], rows_got[...])
    grads = jnp.where(mine, grads_own[...], grads_got[...])
    rows_all[...] = rows
    back, part, gate, router_term = expert_step(
        rows,
        grads,
        marks[...],
        w_router,
        w_gate,
        w_up,
        w_down,
        [store_at(ref) for ref in (hidden, grad_gate, grad_up, pair)],
    )

    @pl.when(step == 0)
    def _():
        router[...] = jnp.zeros_like(router)

    router[...] += router_term

    @pl.when(mine)
    def _():
        back_keep[...] = back
        part_keep[...] = part
        gates[...] = jnp.broadcast_to(gate, gates.shape)

    @pl.when(jnp.logical_not(mine))
    def _():
        back_send[...] = back
        part_send[...] = part


def expert_whole_body(
    tile,
    rows_own,
    rows_got,
    grads_own,
    grads_got,
    marks,
    w_router,
    w_gate,
    w_up,
    w_down,
    back_keep,
    back_send,
    part_keep,
    part_send,
    rows_all,
    hidden,
    grad_gate,
    grad_up,
    pair,
    gates,
    router,
):
    half = rows_own.shape[0]
    router[...] = jnp.zeros_like(router)

    def run(base, rows_ref, grads_ref, back_ref, part_ref):
        def step(index, _):
            at = pl.ds(pl.multiple_of(index * tile, tile), tile)
            place = pl.ds(pl.multiple_of(base + index * tile, tile), tile)
            rows = rows_ref[at, :]
            rows_all[place, :] = rows
            back, part, gate, router_term = expert_step(
                rows,
                grads_ref[at, :],
                marks[place, :],
                w_router,
                w_gate,
                w_up,
                w_down,
                [store_at(ref, (place, slice(None))) for ref in (hidden, grad_gate, grad_up, pair)],
            )
            router[...] += router_term
            back_ref[at, :] = back
            part_ref[at, :] = part
            if base == 0:
                gates[at, :] = jnp.broadcast_to(gate, (tile, 128))
            return 0

        lax.fori_loop(0, half // tile, step, 0)

    run(0, rows_own, grads_own, back_keep, part_keep)
    run(half, rows_got, grads_got, back_send, part_send)


def part_body(keep, got, gates, *total):
    gate = jnp.concatenate([gates[...]] * (keep.shape[1] // 128), 1)
    store_pieces(total, (gate * (keep[...].astype(F32) + got[...].astype(F32))).astype(BF))


def combine_body(slot_pick_t, addend, *refs):
    *back, keep, send = refs
    half = keep.shape[0]
    total = addend[...] + dot(slot_pick_t[...], joined(back))
    keep[...] = total[:half]
    send[...] = total[half:].astype(BF)


def norm_back_body(
    gain, half, got, after_attn, b0, b1, after_grad, low, gain_grad
):
    width = half.shape[1]
    normed_grad = both(half, got)
    values = after_attn[...]
    root = inverse_root(values)
    grads = jnp.concatenate([b0[:, width:], b1[:, width:]], 0).astype(F32)
    total = grads + rms_backward(values, root, gain[...], normed_grad)
    after_grad[...] = total
    low[...] = total.astype(BF)
    gain_grad[...] = jnp.broadcast_to(
        0.5 * jnp.sum(normed_grad * values * root, 0, keepdims=True), gain_grad.shape
    )


def attend_back_body(
    heads,
    w_out,
    w_in_t,
    cosine,
    sine,
    bias,
    qkv,
    own,
    got,
    b0,
    b1,
    b2,
    b3,
    keep,
    send,
    projected_grad,
    gain_grad,
):
    width = own.shape[1]
    half = keep.shape[0]
    grads = jnp.concatenate([own[...], got[...]], 0)
    mixed_grad = dot_bt(grads, w_out[...]).astype(BF)
    scale = HD**-0.5
    cosine, sine = cosine[...], sine[...]
    parts = []
    for head, (query, keys, values) in enumerate(head_parts(qkv, heads)):
        at = head * HD
        scores = dot_bt(query, keys) * scale + bias[...].astype(F32)
        powers = jnp.exp(scores - jnp.max(scores, -1, keepdims=True))
        weights = powers * (1.0 / jnp.sum(powers, -1, keepdims=True))
        mine = mixed_grad[:, at : at + HD]
        weight_grad = dot_bt(mine, values)
        delta = jnp.sum(weights * weight_grad, -1, keepdims=True)
        score_grad = (weights * (weight_grad - delta)).astype(BF)
        parts.append(rope_back(dot(score_grad, keys) * scale, cosine, sine))
        parts.append(rope_back(dot_t(score_grad, query) * scale, cosine, sine))
        parts.append(dot_t(weights.astype(BF), mine))
    projected_grad[...] = jnp.concatenate(parts, 1).astype(BF)
    part = dot(projected_grad[...], w_in_t[...])
    tokens = jnp.concatenate([b[:, :width] for b in (b0, b1, b2, b3)], 0).astype(F32)
    gain_grad[...] = jnp.broadcast_to(
        jnp.sum(part * tokens * inverse_root(tokens), 0, keepdims=True), gain_grad.shape
    )
    keep[...] = part[:half]
    send[...] = part[half:].astype(BF)


def last_body(block, gain, own, got, b0, after_grad, after_attn, near, far):
    rows = own.shape[0]
    width = own.shape[1] // 2
    tokens = b0[:, :width].astype(F32)
    sums = own[...] + got[...].astype(F32)
    total = after_grad[:rows, :] + rms_backward(
        tokens, inverse_root(tokens), gain[...], sums[:, width:]
    )
    result = (after_attn[:rows, :] + sums[:, :width]).astype(BF)
    store_halves(near, far, block, result, slice(0, width))
    store_halves(near, far, block, total.astype(BF), slice(width, None))


def return_body(anchor, b0, b1, b2, b3, final, grads):
    row_count, width = final.shape
    pick = (iota((row_count, row_count), 0) == anchor[...]).astype(F32).T.astype(BF)
    rows = jnp.concatenate([b[...] for b in (b0, b1, b2, b3)], 0)
    total = dot(pick, rows).astype(BF)
    final[...] = total[:, :width]
    grads[...] = total[:, width:]


def on_device(
    tokens,
    cotangent,
    gain_attn,
    w_qkv,
    w_out,
    gain_ffn,
    w_router,
    w_shared_gate,
    w_shared_up,
    w_shared_down,
    routed_gate_weight,
    routed_up_weight,
    w_expert_down,
    seq_lengths,
    token_order,
    inverse_order,
    routes,
    fill_order,
):
    devices_dp = lax.axis_size(DP)
    devices_tp = lax.axis_size(TP)
    dz = lax.axis_size("dz")
    row_count, width = tokens.shape
    block_rows = row_count // devices_dp
    shard_block = block_rows // devices_tp
    shard_rows = row_count // devices_tp
    half_rows = row_count // 2
    experts_all = w_router.shape[1]
    slot_rows = 4 * row_count // experts_all
    capacity = 5 * row_count * devices_dp // (2 * experts_all)
    inner = w_out.shape[0]
    heads = inner // HD
    per_dp = max(1, experts_all // devices_dp)
    copies = max(1, devices_dp // experts_all)
    sub = devices_tp // per_dp
    my_hi, my_lo = lax.axis_index("hi"), lax.axis_index("lo")
    my_z, my_y = lax.axis_index("dz"), lax.axis_index("dy")
    my_dp = my_z * 2 + my_y
    my_block = my_lo * 2 + my_hi
    pick = my_hi if per_dp == 2 else 0 * my_hi
    my_part = my_lo if per_dp == 2 else my_block
    part_rows = slot_rows // sub
    own_slots = devices_dp * part_rows
    all_slots = own_slots * sub
    my_expert = my_dp // copies * per_dp + pick
    chunk = width // devices_dp
    z_bits = [(my_z >> i) & 1 for i in range(log2(dz))]
    info = jnp.stack([my_block, pick, my_part, my_expert, my_dp, my_y] + z_bits).astype(I32)
    pieces = devices_dp if devices_dp <= 8 else 1

    small = all_slots <= 1024
    fetched = [w_qkv.T, w_out, w_shared_gate, w_shared_up, w_shared_down]
    if small:
        fetched += [routed_gate_weight, routed_up_weight, w_expert_down]
    *fetched, router = kernel(
        fetch_body,
        [out(w.shape, w.dtype) for w in fetched] + [out((128, width), BF)],
        *[Held(w) for w in fetched],
        Far(w_router.T),
        semaphores=len(fetched),
    )
    w_in_t, w_out, w_shared_gate, w_shared_up, w_shared_down = fetched[:5]
    if small:
        routed_gate_weight, routed_up_weight, w_expert_down = fetched[5:]
    table = rope_table(row_count)
    gain_attn = gain_attn[None]
    gain_ffn = gain_ffn[None]

    half_shard = out((shard_rows // 2, 2 * width), BF)
    near, far, anchor = kernel(
        functools.partial(select_body, shard_block, devices_dp),
        [half_shard, half_shard, out((1, row_count), I32)],
        Far(inverse_order[None]),
        Far(tokens),
        Far(cotangent),
        scalars=(info,),
    )

    def blocks_of(own):
        by_hi = swap(own, "hi")
        by_lo = swap(own, "lo")
        return (own, by_hi, by_lo, swap(by_hi, "lo"))

    def exchange_shard(near, far, deps=()):
        if devices_dp != 8:
            both_halves = jnp.stack([near, far]).reshape(2, dz, shard_block, 2 * width)
            stacked = both_halves.transpose(1, 0, 2, 3).reshape(devices_dp, shard_block, -1)
            return exchange_stacked(stacked).reshape(shard_rows, 2 * width)
        got = swap(far, "dy")
        middle = kernel(
            functools.partial(middle_body, shard_block),
            [out((2 * shard_block, 2 * width), BF)] * dz,
            near,
            got,
            deps=deps,
        )
        arrived = [middle[0]] + [
            lax.ppermute(middle[k], "dz", [(i, i ^ k) for i in range(dz)]) for k in (1, 2, 3)
        ]
        return arrived

    def join(parts, deps=()):
        if not isinstance(parts, (list, tuple)):
            parts = [parts]
        rows = sum(part.shape[0] for part in parts)
        return kernel(join_body, [out((rows, parts[0].shape[1]), BF)], *parts, deps=deps)[0]

    arrived = exchange_shard(near, far)
    slot_pick, slot_pick_t, bias, cosine, sine, meta = kernel(
        functools.partial(index_body, shard_block, copies, per_dp, part_rows, experts_all),
        [
            out((own_slots, row_count), BF),
            out((row_count, own_slots), BF),
            out((row_count, row_count), BF),
            out((row_count, HD), F32),
            out((row_count, HD), F32),
            out((row_count, 128), BF),
        ],
        Far(token_order[None]),
        Far(routes.T),
        Far(fill_order),
        Far(table),
        scalars=(info, seq_lengths),
        vmem=24,
    )
    blocks = blocks_of(join(arrived, (slot_pick, router)))

    keep, send, qkv, mixed, normed_attn = kernel(
        functools.partial(attend_body, heads),
        [
            out((half_rows, width), F32),
            out((half_rows, width), BF),
            out((row_count, 3 * inner), BF),
            out((row_count, inner), BF),
            out((row_count, width), BF),
        ],
        gain_attn,
        w_in_t,
        w_out,
        cosine,
        sine,
        bias,
        *blocks,
        vmem=24,
    )

    def half_sum(keep, send):
        (half,) = kernel(fold_body, [out((half_rows, width), BF)], keep, swap(send, "lo"))
        return half, swap(half, "hi")

    half, half_got = half_sum(keep, send)
    slot_piece = own_slots // pieces
    sent_grads = kernel(
        send_grads_body,
        [out((slot_piece, width + 128), BF)] * pieces,
        slot_pick,
        meta,
        *blocks,
        deps=(half,),
    )

    def sub_gather(parts, deps=()):
        values = join(parts, deps)
        if sub == 4:
            values = jnp.concatenate([values, swap(values, "hi")], 0)
        return values, swap(values, "lo")

    grads_own, grads_got = sub_gather(exchange(sent_grads))
    (marks,) = kernel(
        functools.partial(meta_body, devices_dp, part_rows, sub, capacity, width),
        [out((all_slots, 128), F32)],
        grads_own,
        grads_got,
        scalars=(info,),
        vmem=40 if sub == 4 else 16,
    )

    after_attn, normed_own = kernel(
        norm_body,
        [out((half_rows, width), F32), out((half_rows, width), BF)],
        gain_ffn,
        half,
        half_got,
        blocks[0],
        blocks[1],
    )
    normed_got = swap(normed_own, "lo")

    sent_rows = kernel(
        send_rows_body,
        [out((slot_piece, width), BF)] * pieces,
        slot_pick,
        normed_own,
        normed_got,
    )
    got_rows = exchange(sent_rows)

    units = w_shared_gate.shape[1]
    shared_part, shared_back, grad_sgate, grad_sup, shared_hidden = kernel(
        shared_body,
        [
            out((row_count, width), F32),
            out((row_count, width), F32),
            out((row_count, units), BF),
            out((row_count, units), BF),
            out((row_count, units), BF),
        ],
        normed_own,
        normed_got,
        *blocks,
        w_shared_gate,
        w_shared_up,
        w_shared_down,
        deps=(sent_rows[0],),
        vmem=24,
    )
    tree_first = (dz, chunk)
    shared_keep, shared_send = kernel(
        shared_grads_body,
        [out(tree_first + (3 * units,), F32), out(tree_first + (3 * units,), BF)],
        normed_own,
        normed_got,
        *blocks,
        grad_sgate,
        grad_sup,
        shared_hidden,
        scalars=(info,),
        vmem=24,
    )

    def z_swap(values, bit):
        return lax.ppermute(values, "dz", [(i, i ^ (1 << bit)) for i in range(dz)])

    def tree_step(kept, got, which, deps=()):
        columns = kept.shape[-1]
        kept = kept.reshape(-1, 2, chunk, columns)
        shape = (kept.shape[0], chunk, columns)
        return kernel(
            functools.partial(tree_body, which),
            [out(shape, F32), out(shape, BF)],
            kept,
            got.reshape(kept.shape),
            scalars=(info,),
            deps=deps,
        )

    def tree_rest(keep, got, first, deps=()):
        for bit in range(first, log2(dz)):
            keep, send = tree_step(keep, got, Z_BITS + bit, deps)
            got = z_swap(send, bit)
        return keep, got, send

    shared_got = swap(shared_send, "dy")
    rows_own, rows_got = sub_gather(got_rows, (shared_send, marks))

    hidden_units = routed_gate_weight.shape[1]
    tile = min(256, own_slots)
    tiles = all_slots // 2 // tile
    steps = 2 * tiles

    def mine_at(i):
        return (jnp.minimum(i, tiles - 1), 0)

    def other_at(i):
        return (jnp.maximum(i - tiles, 0), 0)

    def every_at(i):
        return (i, 0)

    def fixed_at(i):
        return (0, 0)

    half_slots = all_slots // 2
    expert_ins = [
        (rows_own, pl.BlockSpec((tile, width), mine_at)),
        (rows_got, pl.BlockSpec((tile, width), other_at)),
        (grads_own, pl.BlockSpec((tile, width + 128), mine_at)),
        (grads_got, pl.BlockSpec((tile, width + 128), other_at)),
        (marks, pl.BlockSpec((tile, 128), every_at)),
        (router, pl.BlockSpec((128, width), fixed_at)),
        (routed_gate_weight, pl.BlockSpec((width, hidden_units), fixed_at)),
        (routed_up_weight, pl.BlockSpec((width, hidden_units), fixed_at)),
        (w_expert_down, pl.BlockSpec((hidden_units, width), fixed_at)),
    ]
    expert_outs = [
        (out((half_slots, width), BF), pl.BlockSpec((tile, width), mine_at)),
        (out((half_slots, width), BF), pl.BlockSpec((tile, width), other_at)),
        (out((half_slots, width), BF), pl.BlockSpec((tile, width), mine_at)),
        (out((half_slots, width), BF), pl.BlockSpec((tile, width), other_at)),
        (out((all_slots, width), BF), pl.BlockSpec((tile, width), every_at)),
        (out((all_slots, hidden_units), BF), pl.BlockSpec((tile, hidden_units), every_at)),
        (out((all_slots, hidden_units), BF), pl.BlockSpec((tile, hidden_units), every_at)),
        (out((all_slots, hidden_units), BF), pl.BlockSpec((tile, hidden_units), every_at)),
        (out((all_slots, width), BF), pl.BlockSpec((tile, width), every_at)),
        (out((half_slots, 128), F32), pl.BlockSpec((tile, 128), mine_at)),
        (out((128, width), F32), pl.BlockSpec((128, width), fixed_at)),
    ]

    def expert_kernel(*refs):
        pltpu.emit_pipeline(
            functools.partial(expert_body, tiles),
            grid=(steps,),
            in_specs=[spec for _, spec in expert_ins],
            out_specs=[spec for _, spec in expert_outs],
        )(*refs)

    expert_args = [value for value, _ in expert_ins]
    expert_shapes = [shape for shape, _ in expert_outs]
    if small:
        results = kernel(
            functools.partial(expert_whole_body, tile), expert_shapes, *expert_args, vmem=24
        )
    else:
        hbm_spec = pl.BlockSpec(memory_space=pltpu.HBM)
        results = pl.pallas_call(
            expert_kernel,
            in_specs=[hbm_spec] * len(expert_ins),
            out_specs=tuple([hbm_spec] * len(expert_outs)),
            out_shape=tuple(at_hbm(shape) for shape in expert_shapes),
            compiler_params=pltpu.CompilerParams(vmem_limit_bytes=44 * MIB),
            cost_estimate=COST,
            name="expert_body",
        )(*[in_hbm(value) for value in expert_args])
    (
        back_keep,
        back_send,
        part_keep,
        part_send,
        rows_all,
        expert_hidden,
        grad_egate,
        grad_eup,
        pair_grads,
        gates,
        router_part,
    ) = results

    def sub_scatter(keep, send):
        total = keep.astype(F32) + swap(send, "lo").astype(F32)
        return total[:own_slots] + swap(total[own_slots:].astype(BF), "hi").astype(F32)

    if sub == 4:
        back_sum = [sub_scatter(back_keep, back_send).astype(BF)]
        part_sum = [(gates[:own_slots, :1] * sub_scatter(part_keep, part_send)).astype(BF)]
        part_got = None
    else:
        back_sum = kernel(
            add_body, [out((slot_piece, width), BF)] * pieces, back_keep, swap(back_send, "lo")
        )
        part_got = swap(part_send, "lo")
    got_back = exchange(back_sum)

    def weight_grad(left, right, deps=()):
        if not small:
            return dot_t(left, right)
        shape = (left.shape[1], right.shape[1])
        vmem_spec = pl.BlockSpec(memory_space=pltpu.VMEM)
        return pl.pallas_call(
            lambda *refs: weight_grad_body(refs[0], refs[1], *refs[-3:]),
            out_shape=pltpu.HBM(shape, F32),
            in_specs=[vmem_spec] * 2 + [pl.BlockSpec(memory_space=pl.ANY)] * len(deps),
            out_specs=pl.BlockSpec(memory_space=pltpu.HBM),
            scratch_shapes=[
                pltpu.VMEM(shape, F32),
                pltpu.SemaphoreType.DMA((shape[0] // 256,)),
            ],
            compiler_params=pltpu.CompilerParams(vmem_limit_bytes=12 * MIB),
            cost_estimate=COST,
            name="weight_grad",
        )(in_vmem(left), in_vmem(right), *deps)

    grad_w_expert_gate = weight_grad(rows_all, grad_egate, (back_sum[0],))
    grad_w_expert_up = weight_grad(rows_all, grad_eup, (back_sum[0],))

    keep, send = kernel(
        combine_body,
        [out((half_rows, width), F32), out((half_rows, width), BF)],
        slot_pick_t,
        shared_back,
        *got_back,
        deps=(Far(grad_w_expert_gate), Far(grad_w_expert_up)),
    )
    half, half_got = half_sum(keep, send)
    if part_got is not None:
        part_sum = kernel(
            part_body,
            [out((slot_piece, width), BF)] * pieces,
            part_keep,
            part_got,
            gates,
            deps=(half,),
        )
    got_parts = exchange(part_sum)
    after_grad, after_grad_own, gain_ffn_part = kernel(
        norm_back_body,
        [out((half_rows, width), F32), out((half_rows, width), BF), out((8, width), F32)],
        gain_ffn,
        half,
        half_got,
        after_attn,
        blocks[0],
        blocks[1],
    )
    after_grad_got = swap(after_grad_own, "lo")
    shared_keep, shared_send = tree_step(shared_keep, shared_got, Z_BITS, (after_grad_own,))
    shared_got = z_swap(shared_send, 0)

    keep, send, projected_grad, gain_attn_part = kernel(
        functools.partial(attend_back_body, heads),
        [
            out((half_rows, width), F32),
            out((half_rows, width), BF),
            out((row_count, 3 * inner), BF),
            out((8, width), F32),
        ],
        w_out,
        w_in_t,
        cosine,
        sine,
        bias,
        qkv,
        after_grad_own,
        after_grad_got,
        *blocks,
        vmem=24,
        deps=(shared_send,),
    )
    keep, send = kernel(
        to_bottom_body,
        [out((half_rows, 2 * width), F32), out((half_rows, 2 * width), BF)],
        slot_pick_t,
        shared_part,
        keep,
        send,
        *got_parts,
    )
    got = swap(send, "lo")
    last_keep, last_send = kernel(
        functools.partial(last_grads_body, experts_all),
        [
            out(tree_first + (4 * inner + 128,), F32),
            out(tree_first + (4 * inner + 128,), BF),
        ],
        normed_attn,
        projected_grad,
        after_grad_own,
        after_grad_got,
        mixed,
        gain_ffn_part,
        gain_attn_part,
        router_part,
        scalars=(info,),
        vmem=24,
        deps=(send,),
    )
    last_got = swap(last_send, "dy")
    own, send = kernel(
        fold_own_body,
        [out((shard_rows, 2 * width), F32), out((shard_rows, 2 * width), BF)],
        keep,
        got,
    )
    grad_w_expert_down = weight_grad(expert_hidden, pair_grads, (own,))
    shared_keep, shared_got, shared_send = tree_rest(shared_keep, shared_got, 1, (own,))
    near, far = kernel(
        functools.partial(last_body, shard_block),
        [half_shard, half_shard],
        gain_attn,
        own,
        swap(send, "hi"),
        blocks[0],
        after_grad,
        after_attn,
        deps=(Far(grad_w_expert_down), shared_send),
    )
    last_keep, last_send = tree_step(last_keep, last_got, Z_BITS, (near,))
    last_got = z_swap(last_send, 0)
    got_last = join(exchange_shard(near, far), (last_send,))
    final, grad_tokens = kernel(
        return_body,
        [Far(out((row_count, width), BF)), Far(out((row_count, width), BF))],
        anchor,
        *blocks_of(got_last),
    )

    grad_sgate, grad_sup, grad_sdown = kernel(
        shared_end_body,
        [Far(out((chunk, units), F32))] * 3,
        shared_keep,
        shared_got,
        deps=(near,),
    )
    last_keep, last_got, _ = tree_rest(last_keep, last_got, 1)
    small_rows = experts_all + 8
    grad_qkv, grad_out, sums = kernel(
        functools.partial(last_end_body, small_rows),
        [
            Far(out((chunk, 3 * inner), F32)),
            Far(out((inner, chunk), F32)),
            out((small_rows, chunk), F32),
        ],
        last_keep,
        last_got,
    )
    sums = sums + swap(sums, "hi")
    sums = sums + swap(sums, "lo")
    return (
        final,
        grad_tokens,
        sums[experts_all + 1],
        grad_qkv,
        grad_out,
        sums[experts_all],
        sums[:experts_all].T,
        grad_sgate,
        grad_sup,
        grad_sdown.T,
        grad_w_expert_gate,
        grad_w_expert_up,
        grad_w_expert_down,
    )


def solution(mesh):
    devices_dp, devices_tp = mesh.shape["dp"], mesh.shape["tensor"]
    fine = Mesh(
        mesh.devices.reshape(devices_dp // 2, 2, devices_tp // 2, 2), ("dz", "dy", "hi", "lo")
    )
    every = DP + TP
    return jax.shard_map(
        on_device,
        mesh=fine,
        in_specs=(
            P(DP, None),
            P(DP, None),
            P(),
            P(None, TP),
            P(TP, None),
            P(),
            P(),
            P(None, TP),
            P(None, TP),
            P(TP, None),
            P(None, every),
            P(None, every),
            P(every, None),
            P(DP, None),
            P(DP),
            P(DP),
            P(DP, None),
            P(DP, None),
        ),
        out_specs=(
            P(DP, None),
            P(DP, None),
            P(DP),
            P(DP, TP),
            P(TP, DP),
            P(DP),
            P(DP, None),
            P(DP, TP),
            P(DP, TP),
            P(TP, DP),
            P(None, every),
            P(None, every),
            P(every, None),
        ),
        check_vma=False,
    )
```

```python
import functools

import jax
import jax.numpy as jnp
import numpy as np
from jax import lax
from jax.experimental import pallas as pl
from jax.experimental.pallas import tpu as pltpu
from jax.sharding import Mesh, PartitionSpec as P

HD = 64
MY_BLOCK, PICK, MY_PART, MY_EXPERT, MY_DP, Y_BIT, Z_BITS = range(7)
EPSILON = 1e-06
BF = jnp.bfloat16
F32 = jnp.float32
I32 = jnp.int32
DP = ("dz", "dy")
TP = ("hi", "lo")
MIB = 1 << 20
SENT_PIECES = 4
COST = pl.CostEstimate(flops=1000, bytes_accessed=1000, transcendentals=0)


def dot(left, right):
    return jnp.dot(left, right, preferred_element_type=F32)


def dot_t(left, right):
    return lax.dot_general(left, right, (((0,), (0,)), ((), ())), preferred_element_type=F32)


def dot_bt(left, right):
    return lax.dot_general(left, right, (((1,), (1,)), ((), ())), preferred_element_type=F32)


def swap(values, axis):
    return lax.ppermute(values, axis, [(0, 1), (1, 0)])


def exchange_stacked(values):
    order = jnp.arange(values.shape[0], dtype=I32) ^ lax.axis_index(DP)
    got = lax.all_to_all(
        jnp.take(values, order, axis=0), DP, split_axis=0, concat_axis=0, tiled=True
    )
    return jnp.take(got, order, axis=0)


def exchange_part(pieces, first):
    devices = lax.axis_size(DP)
    if first == 0 and len(pieces) == 1:
        (values,) = pieces
        stacked = values.reshape(devices, -1, values.shape[-1])
        return [exchange_stacked(stacked).reshape(values.shape)]
    return [
        lax.ppermute(piece, DP, [(i, i ^ k) for i in range(devices)]) if k else piece
        for k, piece in enumerate(pieces, first)
    ]


def out(shape, dtype):
    return jax.ShapeDtypeStruct(shape, dtype)


class Far:
    def __init__(self, value):
        self.value = value


class Held(Far):
    pass


class Free(Far):
    pass


class Arriving:
    def __init__(self, buffer, copy):
        self.buffer, self.copy, self.waiting = buffer, copy, True
        self.shape, self.dtype = buffer.shape, buffer.dtype

    def ready(self):
        if self.waiting:
            self.copy.wait()
            self.waiting = False

    def __getitem__(self, index):
        self.ready()
        return self.buffer[index]


class Leaving:
    def __init__(self, buffer, copy):
        self.buffer, self.copy, self.started = buffer, copy, False
        self.shape, self.dtype = buffer.shape, buffer.dtype

    def flush(self):
        if not self.started:
            self.copy.start()
            self.started = True

    def __getitem__(self, index):
        return self.buffer[index]

    def __setitem__(self, index, value):
        self.buffer[index] = value


def in_hbm(values):
    return pltpu.with_memory_space_constraint(values, pltpu.HBM)


def in_vmem(values):
    if values.size * values.dtype.itemsize > 4 * MIB:
        return values
    return pltpu.with_memory_space_constraint(values, pltpu.VMEM)


def at_hbm(shape):
    return pltpu.HBM(shape.shape, shape.dtype)


def at_vmem(shape):
    if shape.size * shape.dtype.itemsize > 4 * MIB:
        return shape
    return pltpu.VMEM(shape.shape, shape.dtype)


def kernel(body, outs, *args, scalars=(), deps=(), vmem=16, semaphores=0):
    vmem_spec = pl.BlockSpec(memory_space=pltpu.VMEM)
    hbm_spec = pl.BlockSpec(memory_space=pltpu.HBM)
    any_spec = pl.BlockSpec(memory_space=pl.ANY)
    held = [isinstance(a, Held) for a in args]
    far_in = [isinstance(a, Far) and not h for a, h in zip(args, held)]
    free_out = [isinstance(o, Free) for o in outs]
    far_out = [isinstance(o, Far) and not f for o, f in zip(outs, free_out)]
    args = [in_hbm(a.value) if isinstance(a, Far) else in_vmem(a) for a in args]
    outs = [
        o.value if f else at_hbm(o.value) if h else at_vmem(o)
        for o, f, h in zip(outs, free_out, far_out)
    ]
    deps = [in_hbm(d.value) if isinstance(d, Far) else d for d in deps]
    moved = [x for x, f in zip(args + outs, far_in + far_out) if f]
    scratch = [pltpu.VMEM(x.shape, x.dtype) for x in moved]
    if moved:
        scratch.append(pltpu.SemaphoreType.DMA((len(moved),)))
    if semaphores:
        scratch.append(pltpu.SemaphoreType.DMA((semaphores,)))
    n_scalars, n_args, n_deps, n_outs = len(scalars), len(args), len(deps), len(outs)

    def wrapped(*refs):
        ins = list(refs[: n_scalars + n_args])
        results = list(refs[n_scalars + n_args + n_deps :][:n_outs])
        buffers = refs[n_scalars + n_args + n_deps + n_outs :]
        extra = buffers[-1:] if semaphores else ()
        buffers = buffers[:-1] if semaphores else buffers
        at = 0
        for i, far in enumerate(far_in):
            if far:
                ref = ins[n_scalars + i]
                copy = pltpu.make_async_copy(ref, buffers[at], buffers[-1].at[at])
                copy.start()
                ins[n_scalars + i] = Arriving(buffers[at], copy)
                at += 1
        for i, far in enumerate(far_out):
            if far:
                copy = pltpu.make_async_copy(buffers[at], results[i], buffers[-1].at[at])
                results[i] = Leaving(buffers[at], copy)
                at += 1
        body(*ins, *results, *extra)
        for ref in ins:
            if isinstance(ref, Arriving):
                ref.ready()
        for ref in results:
            if isinstance(ref, Leaving):
                ref.flush()
        for ref in results:
            if isinstance(ref, Leaving):
                ref.copy.wait()

    return pl.pallas_call(
        wrapped,
        out_shape=tuple(outs),
        in_specs=[pl.BlockSpec(memory_space=pltpu.SMEM)] * n_scalars
        + [hbm_spec if f or h else vmem_spec for f, h in zip(far_in, held)]
        + [any_spec] * n_deps,
        out_specs=tuple(hbm_spec if far else vmem_spec for far in far_out),
        scratch_shapes=scratch,
        compiler_params=pltpu.CompilerParams(vmem_limit_bytes=vmem * MIB),
        cost_estimate=COST,
        name=body.func.__name__ if isinstance(body, functools.partial) else body.__name__,
    )(*scalars, *args, *deps)


def tie(values, *deps):
    any_spec = pl.BlockSpec(memory_space=pl.ANY)
    vmem_spec = pl.BlockSpec(memory_space=pltpu.VMEM)
    return pl.pallas_call(
        lambda *refs: None,
        out_shape=out(values.shape, values.dtype),
        in_specs=[vmem_spec] + [any_spec] * len(deps),
        out_specs=vmem_spec,
        input_output_aliases={0: 0},
        cost_estimate=COST,
        name="tie",
    )(in_vmem(values), *[in_hbm(d.value) if isinstance(d, Far) else d for d in deps])


def rope_table(places):
    exponent = np.arange(HD // 2, dtype=np.float32) * np.float32(-2.0 / HD)
    angles = np.arange(places, dtype=np.float32)[:, None] * np.power(np.float32(10000.0), exponent)
    cosine = np.cos(angles.astype(np.float64)).astype(np.float32)
    sine = np.sin(angles.astype(np.float64)).astype(np.float32)
    rest = np.concatenate([cosine, cosine, -sine, sine], 1)
    terms = []
    for _ in range(3):
        terms.append(rest.astype(BF))
        rest = rest - terms[-1].astype(np.float32)
    return jnp.asarray(np.concatenate(terms, 1))


def iota(shape, dim):
    return lax.broadcasted_iota(I32, shape, dim)


def log2(number):
    return number.bit_length() - 1


def silu_parts(gate_in):
    sigmoid_val = 1.0 / (1.0 + jnp.exp(-gate_in))
    return (gate_in * sigmoid_val, sigmoid_val * (1.0 + gate_in * (1.0 - sigmoid_val)))


def inverse_root(values):
    return lax.rsqrt(jnp.mean(values * values, -1, keepdims=True) + EPSILON)


def rms_backward(values, root, gain, grad_normed):
    scaled = grad_normed * gain
    return root * scaled - values * (root * root * root) * jnp.mean(
        scaled * values, -1, keepdims=True
    )


def lane_rank(buckets, bucket_count):
    count = buckets.shape[1]
    rows = max(8, bucket_count)
    member = (iota((rows, count), 0) == buckets).astype(F32)
    earlier = (iota((count, count), 0) < iota((count, count), 1)).astype(F32).astype(BF)
    return jnp.sum(dot(member.astype(BF), earlier) * member, 0, keepdims=True).astype(I32)


def relative_row(block, rank, my_block, shard_block, shard_rows):
    shift = log2(shard_block)
    return (
        ((rank >> shift) ^ my_block) * shard_rows
        + block * shard_block
        + (rank & (shard_block - 1))
    )


def rope_back(grads, cosine, sine):
    return grads * cosine - half_turned(grads) * sine


def store_pieces(refs, value):
    rows = refs[0].shape[0]
    for i, ref in enumerate(refs):
        ref[...] = value[i * rows : (i + 1) * rows]


def joined(refs):
    return jnp.concatenate([ref[...] for ref in refs], 0) if len(refs) > 1 else refs[0][...]


def join_body(*refs):
    *parts, whole = refs
    rows = parts[0].shape[0]
    for i, ref in enumerate(parts):
        whole[i * rows : (i + 1) * rows, :] = ref[...]


def middle_body(block, near, far, *outs):
    for i, ref in enumerate(outs):
        ref[:block, :] = near[i * block : (i + 1) * block, :]
        ref[block:, :] = far[i * block : (i + 1) * block, :]


def store_halves(near, far, block, value, columns):
    for i in range(near.shape[0] // block):
        at = 2 * i * block
        near[i * block : (i + 1) * block, columns] = value[at : at + block]
        far[i * block : (i + 1) * block, columns] = value[at + block : at + 2 * block]


def fetch_body(*refs):
    *refs, semaphores = refs
    count = len(refs) // 2
    copies = [
        pltpu.make_async_copy(refs[i], refs[count + i], semaphores.at[i]) for i in range(count)
    ]
    for copy in copies:
        copy.start()
    for copy in copies:
        copy.wait()


def select_body(shard_block, blocks, info, inverse, tokens, cotangent, near, far, anchor):
    row_count, width = tokens.shape
    shard_rows = shard_block * blocks
    target = (inverse[...] >> log2(row_count)) ^ info[MY_DP]
    row = relative_row(target, lane_rank(target, blocks), info[MY_BLOCK], shard_block, shard_rows)
    anchor[...] = row
    pick = (iota((shard_rows, row_count), 0) == row).astype(F32).astype(BF)
    store_halves(near, far, shard_block, dot(pick, tokens[...]).astype(BF), slice(0, width))
    store_halves(near, far, shard_block, dot(pick, cotangent[...]).astype(BF), slice(width, None))


def index_body(
    shard_block,
    copies,
    per_dp,
    part_rows,
    experts_all,
    info,
    lengths,
    order,
    routes,
    fill,
    table,
    slot_pick,
    slot_pick_t,
    bias,
    cosine,
    sine,
    meta,
):
    row_count = order.shape[1]
    devices_dp = slot_pick.shape[0] // part_rows
    shard_rows = shard_block * devices_dp
    source = (order[...] >> log2(row_count)) ^ info[MY_DP]
    local = relative_row(
        source, lane_rank(source, devices_dp), info[MY_BLOCK], shard_block, shard_rows
    )
    place_pick = (iota((row_count, row_count), 0) == local).astype(F32).astype(BF)
    lanes = iota((1, row_count), 1)
    segment = jnp.zeros((1, row_count), I32)
    start = jnp.zeros((1, row_count), I32)
    end = jnp.int32(0)
    for entry in range(lengths.shape[1]):
        end = end + lengths[0, entry]
        passed = lanes >= end
        segment = segment + passed.astype(I32)
        start = jnp.maximum(start, jnp.where(passed, end, 0))
    place = lanes - start
    expert_sum = routes[0:1, :] + routes[1:2, :] + 1
    facts = jnp.concatenate(
        [segment, place >> 1, place & 1, expert_sum, jnp.zeros((4, row_count), I32)], 0
    )
    facts = facts.astype(F32).astype(BF)
    across = dot_bt(facts, place_pick)
    down = dot_bt(place_pick, facts)
    place_row = 2.0 * across[1:2] + across[2:3]
    place_col = 2.0 * down[:, 1:2] + down[:, 2:3]
    allowed = (down[:, 0:1] == across[0:1]) & (place_row <= place_col)
    bias[...] = jnp.where(allowed, 0.0, -1e30).astype(BF)
    at_place = (
        iota((row_count, row_count), 1).astype(F32) == place_col
    ).astype(F32).astype(BF)
    turned = dot(at_place, table[...])
    pieces = [turned[:, i * 128 : (i + 1) * 128] for i in range(3)]
    turned = pieces[0] + pieces[1] + pieces[2]
    cosine[...] = turned[:, :HD]
    sine[...] = turned[:, HD:]
    meta[...] = jnp.broadcast_to(down[:, 3:4], meta.shape).astype(BF)
    pairs = 2 * row_count
    fill_at = (fill[...] & 1) * row_count + (fill[...] >> 1)
    fill_pick = (iota((pairs, pairs), 0) == fill_at).astype(F32).astype(BF)
    expert_rows = max(16, experts_all)
    pair_expert = jnp.concatenate([routes[0:1, :], routes[1:2, :]], 1)
    named = (iota((expert_rows, pairs), 0) == pair_expert).astype(F32).astype(BF)
    member = dot(named, fill_pick)
    earlier = (iota((pairs, pairs), 0) < iota((pairs, pairs), 1)).astype(F32).astype(BF)
    ranks = (member * (dot(member.astype(BF), earlier) + 1.0)).astype(BF)
    ranks = dot_bt(ranks, fill_pick)
    ranks = (ranks[:, :row_count] + ranks[:, row_count:]).astype(BF)
    ranks = dot_bt(ranks, place_pick).astype(I32)
    slots = iota((part_rows, row_count), 0) + (info[MY_PART] * part_rows + 1)
    experts = iota((expert_rows, row_count), 0)
    for target in range(devices_dp):
        expert = ((target ^ info[MY_DP]) >> log2(copies)) * per_dp + info[PICK]
        chosen = jnp.sum(jnp.where(experts == expert, ranks, 0), 0, keepdims=True)
        picked = (slots == chosen).astype(F32)
        slot_pick[target * part_rows : (target + 1) * part_rows, :] = picked.astype(BF)
    slot_pick_t[...] = slot_pick[...].astype(F32).T.astype(BF)


def head_parts(projected, heads):
    return [
        [projected[:, (3 * h + i) * HD : (3 * h + i + 1) * HD] for i in range(3)]
        for h in range(heads)
    ]


def half_turned(values):
    half = values.shape[1] // 2
    return jnp.concatenate([values[:, half:], values[:, :half]], 1)


def attend_body(
    heads, gain, w_in_t, w_out, cosine, sine, bias, b0, b1, b2, b3, keep, send, qkv, mixed, normed
):
    width = b0.shape[1] // 2
    half = keep.shape[0]
    tokens = jnp.concatenate([b[:, :width] for b in (b0, b1, b2, b3)], 0).astype(F32)
    normed[...] = (tokens * inverse_root(tokens) * gain[...]).astype(BF)
    projected = dot_bt(normed[...], w_in_t[...])
    cosine, sine = cosine[...], sine[...]
    parts = []
    for query, keys, values in head_parts(projected, heads):
        parts.append((query * cosine + half_turned(query) * sine).astype(BF))
        parts.append((keys * cosine + half_turned(keys) * sine).astype(BF))
        parts.append(values.astype(BF))
    qkv[...] = jnp.concatenate(parts, 1)
    scale = HD**-0.5
    mixed_heads = []
    for query, keys, values in head_parts(qkv, heads):
        scores = dot_bt(query, keys) * scale + bias[...].astype(F32)
        powers = jnp.exp(scores - jnp.max(scores, -1, keepdims=True))
        weights = powers * (1.0 / jnp.sum(powers, -1, keepdims=True))
        mixed_heads.append(dot(weights.astype(BF), values))
    mixed[...] = jnp.concatenate(mixed_heads, 1).astype(BF)
    part = dot(mixed[...], w_out[...])
    keep[...] = part[:half]
    send[...] = part[half:].astype(BF)


def fold_body(keep, got, half):
    half[...] = (keep[...] + got[...].astype(F32)).astype(BF)


def fold_own_body(keep, got, own, send):
    rows = own.shape[0]
    own[...] = keep[:rows, :] + got[:rows, :].astype(F32)
    send[...] = (keep[rows:, :] + got[rows:, :].astype(F32)).astype(BF)


def both(half, got):
    rows = half.shape[0] // 2
    mine, other = half[...].astype(F32), got[...].astype(F32)
    return mine + jnp.concatenate([other[rows:], other[:rows]], 0)


def norm_body(gain, half, got, b0, b1, after_attn, normed):
    width = half.shape[1]
    balanced = jnp.concatenate([b0[:, :width], b1[:, :width]], 0).astype(F32)
    values = balanced + both(half, got)
    after_attn[...] = values
    normed[...] = (values * inverse_root(values) * gain[...]).astype(BF)


def send_body(slot_pick, own, got, meta, b0, b1, b2, b3, *sent):
    width = own.shape[1]
    rows = jnp.concatenate([own[...], got[...]], 0)
    grads = jnp.concatenate([b[:, width:] for b in (b0, b1, b2, b3)], 0)
    rows = jnp.concatenate([rows, grads, meta[...]], 1)
    store_pieces(sent, dot(slot_pick[...], rows).astype(BF))


def shared_body(
    own, got, b0, b1, b2, b3, w_gate, w_up, w_down, part, back, grad_gate, grad_up, hidden
):
    width = own.shape[1]
    rows = jnp.concatenate([own[...], got[...]], 0)
    grads = jnp.concatenate([b[:, width:] for b in (b0, b1, b2, b3)], 0)
    gate = dot(rows, w_gate[...])
    up = dot(rows, w_up[...])
    act, slope = silu_parts(gate)
    hidden[...] = (act * up).astype(BF)
    part[...] = dot(hidden[...], w_down[...])
    hidden_grad = dot_bt(grads, w_down[...])
    grad_gate[...] = (hidden_grad * up * slope).astype(BF)
    grad_up[...] = (hidden_grad * act).astype(BF)
    back[...] = dot_bt(grad_gate[...], w_gate[...]) + dot_bt(grad_up[...], w_up[...])


def store_tree(info, sums, keeps, sends):
    chunk, columns = keeps[0].shape[1:]
    sides = ((sums[:, :columns], Y_BIT, 1), (sums[:, columns:], Z_BITS, 2))
    for (values, which, stride), keep, send in zip(sides, keeps, sends):
        mine = info[which] == 0
        for i in range(keep.shape[0]):
            at = (2 * i if stride == 1 else i // 2 * 4 + i % 2) * chunk
            first, second = values[at : at + chunk], values[at + stride * chunk :][:chunk]
            keep[i] = jnp.where(mine, first, second)
            send[i] = jnp.where(mine, second, first).astype(BF)


def shared_grads_body(
    info, own, got, b0, b1, b2, b3, grad_gate, grad_up, hidden, *refs
):
    width = own.shape[1]
    rows = jnp.concatenate([own[...], got[...]], 0)
    grads = jnp.concatenate([b[:, width:] for b in (b0, b1, b2, b3)], 0)
    sums = jnp.concatenate(
        [dot_t(rows, grad_gate[...]), dot_t(rows, grad_up[...]), dot_t(grads, hidden[...])], 1
    )
    store_tree(info, sums, refs[:2], refs[2:])


def halved(info, which, total, keep, send):
    mine = info[which] == 0
    for index in range(keep.shape[0]):
        first, second = total[2 * index], total[2 * index + 1]
        keep[index] = jnp.where(mine, first, second)
        send[index] = jnp.where(mine, second, first).astype(BF)


def tree_second_body(info, kept_a, got_a, kept_b, got_b, keep_a, keep_b, send_a, send_b):
    halved(info, Z_BITS, kept_a[...] + got_a[...].astype(F32), keep_a, send_a)
    halved(info, Y_BIT, kept_b[...] + got_b[...].astype(F32), keep_b, send_b)


def tree_third_body(info, kept_a, got_a, kept_b, got_b, keep, send):
    total = jnp.concatenate(
        [kept_a[...] + got_a[...].astype(F32), kept_b[...] + got_b[...].astype(F32)], 2
    )
    halved(info, Z_BITS + 1, total, keep, send)


def last_grads_body(
    experts, info, normed, projected_grad, own, got, mixed, gain_ffn, gain_attn, router, *refs
):
    width = normed.shape[1]
    small = jnp.concatenate(
        [
            router[:experts, :],
            gain_ffn[:1, :],
            gain_attn[:1, :],
            jnp.zeros((128 - experts - 2, width), F32),
        ],
        0,
    )
    grads = jnp.concatenate([own[...], got[...]], 0)
    sums = jnp.concatenate(
        [dot_t(normed[...], projected_grad[...]), dot_t(grads, mixed[...]), small.T], 1
    )
    store_tree(info, sums, refs[:2], refs[2:])


def tree_body(which, info, kept, got, keep, send):
    halved(info, which, kept[...] + got[...].astype(F32), keep, send)


def last_end_body(small_rows, kept, got, grad_qkv, grad_out, small):
    total = kept[0] + got[0].astype(F32)
    columns, inner = grad_qkv.shape[1], grad_out.shape[0]
    grad_qkv[...] = total[:, :columns]
    grad_out[...] = total[:, columns : columns + inner].T
    small[...] = total[:, columns + inner :].T[:small_rows]


def small_end_body(own, by_lo, by_hi, by_both, gain_ffn, gain_attn, router):
    experts = router.shape[0]
    total = (own[...] + by_lo[...]) + (by_hi[...] + by_both[...])
    router[...] = total[:experts]
    gain_ffn[...] = total[experts : experts + 1]
    gain_attn[...] = total[experts + 1 : experts + 2]


def shared_end_body(kept, got, grad_gate, grad_up, grad_down):
    total = kept[0] + got[0].astype(F32)
    units = grad_gate.shape[1]
    grad_gate[...] = total[:, :units]
    grad_up[...] = total[:, units : 2 * units]
    grad_down[...] = total[:, 2 * units :]


def add_body(keep, gates, *refs):
    width = keep.shape[1] // 2
    count = SENT_PIECES
    got, total = refs[:count], refs[count:]
    gate = jnp.concatenate([gates[...]] * (width // 128), 1)
    sums = keep[...].astype(F32) + joined(got).astype(F32)
    store_pieces(total, jnp.concatenate([sums[:, :width], gate * sums[:, width:]], 1).astype(BF))


def weight_grad_body(left, right, total, sums, semaphores):
    tile = 256
    copies = []
    for i in range(left.shape[1] // tile):
        at = slice(i * tile, (i + 1) * tile)
        sums[at, :] = dot_t(left[:, at], right[...])
        copies.append(
            pltpu.make_async_copy(sums.at[at, :], total.at[at, :], semaphores.at[i])
        )
        copies[-1].start()
    for copy in copies:
        copy.wait()


def meta_body(devices_dp, part_rows, sub, capacity, width, info, own, got, marks):
    my_part, my_expert = info[MY_PART], info[MY_EXPERT]
    lanes = iota((part_rows, 128), 1)
    blocks = [(ref, at, part) for part, (ref, at) in enumerate(
        [(own, i) for i in range(sub // 2)] + [(got, i) for i in range(sub // 2)]
    )]
    counts = []
    for block in range(devices_dp):
        count = jnp.zeros((1, 128), F32)
        for ref, at, _ in blocks:
            start = (at * devices_dp + block) * part_rows
            value = ref[start : start + part_rows, width:].astype(F32)
            count = count + jnp.sum((value > 0.0).astype(F32), 0, keepdims=True)
        counts.append(count)
    for block in range(devices_dp):
        earlier = jnp.zeros((1, 128), F32)
        for before in range(devices_dp):
            ahead = (before ^ info[MY_DP]) < (block ^ info[MY_DP])
            earlier = earlier + jnp.where(ahead, counts[before], 0.0)
        for ref, at, part in blocks:
            start = (at * devices_dp + block) * part_rows
            value = ref[start : start + part_rows, width:].astype(F32)
            valid = value > 0.0
            slot = iota((part_rows, 128), 0) + (my_part ^ part) * part_rows
            kept = valid & (slot.astype(F32) + earlier < capacity)
            other = value.astype(I32) - 1 - my_expert
            mark = (lanes == my_expert).astype(F32) - (lanes == other).astype(F32)
            row = (part * devices_dp + block) * part_rows
            marks[row : row + part_rows, :] = jnp.where(
                lanes == 127, kept.astype(F32), jnp.where(valid, mark, 0.0)
            )


def expert_step(packed, mark, w_router, w_gate, w_up, w_down, stores):
    hidden_out, grad_gate_out, grad_up_out, pair_out = stores
    width = w_gate.shape[0]
    rows, grads = packed[:, :width], packed[:, width : 2 * width].astype(F32)
    kept = mark[:, 127:128] > 0.5
    mark = mark[:, : w_router.shape[0]]
    gap = jnp.sum(dot_bt(rows, w_router[...]) * mark, 1, keepdims=True)
    gate = 1.0 / (1.0 + jnp.exp(-gap))
    gate_other = 1.0 / (1.0 + jnp.exp(gap))
    gate_in = dot(rows, w_gate[...])
    up = dot(rows, w_up[...])
    act, slope = silu_parts(gate_in)
    hidden = (act * up).astype(BF)
    hidden_out(hidden)
    part = jnp.where(kept, dot(hidden, w_down[...]), 0.0).astype(BF)
    pair = jnp.where(kept, gate * grads, 0.0).astype(BF)
    pair_out(pair)
    gate_grad = jnp.sum(part.astype(F32) * grads, 1, keepdims=True)
    logit_grad = (gate * gate_other * gate_grad * mark).astype(BF)
    hidden_grad = dot_bt(pair, w_down[...])
    grad_gate = (hidden_grad * up * slope).astype(BF)
    grad_up = (hidden_grad * act).astype(BF)
    grad_gate_out(grad_gate)
    grad_up_out(grad_up)
    back = (dot_bt(grad_gate, w_gate[...]) + dot_bt(grad_up, w_up[...])).astype(BF).astype(F32)
    back = (back + dot(logit_grad, w_router[...])).astype(BF)
    return back, part, gate, dot_t(logit_grad, rows)


def store_at(ref, where=...):
    def store(value):
        ref[where] = value

    return store


def expert_body(
    tiles,
    packed_own,
    packed_got,
    marks,
    w_router,
    w_gate,
    w_up,
    w_down,
    keep,
    send,
    rows_all,
    hidden,
    grad_gate,
    grad_up,
    pair,
    gates,
    router,
):
    step = pl.program_id(0)
    mine = step < tiles
    width = rows_all.shape[1]
    packed = jnp.where(mine, packed_own[...], packed_got[...])
    rows_all[...] = packed[:, :width]
    back, part, gate, router_term = expert_step(
        packed,
        marks[...],
        w_router,
        w_gate,
        w_up,
        w_down,
        [store_at(ref) for ref in (hidden, grad_gate, grad_up, pair)],
    )

    @pl.when(step == 0)
    def _():
        router[...] = jnp.zeros_like(router)

    router[...] += router_term

    @pl.when(mine)
    def _():
        keep[:, :width] = back
        keep[:, width:] = part
        gates[...] = jnp.broadcast_to(gate, gates.shape)

    @pl.when(jnp.logical_not(mine))
    def _():
        send[:, :width] = back
        send[:, width:] = part


def expert_whole_body(
    tile,
    packed_own,
    packed_got,
    marks,
    w_router,
    w_gate,
    w_up,
    w_down,
    keep,
    *refs,
):
    send = refs[:SENT_PIECES]
    rows_all, hidden, grad_gate, grad_up, pair, gates, router = refs[SENT_PIECES:]
    half = packed_own.shape[0]
    width = rows_all.shape[1]
    router[...] = jnp.zeros_like(router)

    def run(base, packed_ref, put):
        def step(index, _):
            at = pl.ds(pl.multiple_of(index * tile, tile), tile)
            place = pl.ds(pl.multiple_of(base + index * tile, tile), tile)
            packed = packed_ref[at, : 2 * width]
            rows_all[place, :] = packed[:, :width]
            back, part, gate, router_term = expert_step(
                packed,
                marks[place, :],
                w_router,
                w_gate,
                w_up,
                w_down,
                [store_at(ref, (place, slice(None))) for ref in (hidden, grad_gate, grad_up, pair)],
            )
            router[...] += router_term
            put(index, at, back, part)
            if base == 0:
                gates[at, :] = jnp.broadcast_to(gate, (tile, 128))
            return 0

        lax.fori_loop(0, half // tile, step, 0)

    def put_own(index, at, back, part):
        keep[at, :width] = back
        keep[at, width:] = part

    def put_got(index, at, back, part):
        rows = half // SENT_PIECES
        each = tile // rows
        for i, ref in enumerate(send):

            @pl.when(index == i // each)
            def _(i=i, ref=ref):
                inside = slice(i % each * rows, (i % each + 1) * rows)
                ref[:, :width] = back[inside]
                ref[:, width:] = part[inside]

    run(0, packed_own, put_own)
    run(half, packed_got, put_got)


def combine_body(slot_pick_t, back_addend, out_addend, *refs):
    *back, keep, send, out_keep, out_send = refs
    half, width = keep.shape
    total = dot(slot_pick_t[...], joined(back))
    back_total = back_addend[...] + total[:, :width]
    out_total = out_addend[...] + total[:, width:]
    keep[...] = back_total[:half]
    send[...] = back_total[half:].astype(BF)
    out_keep[...] = out_total[:half]
    out_send[...] = out_total[half:].astype(BF)


def norm_back_body(
    gain, half, got, after_attn, b0, b1, after_grad, low, gain_grad
):
    width = half.shape[1]
    normed_grad = both(half, got)
    values = after_attn[...]
    root = inverse_root(values)
    grads = jnp.concatenate([b0[:, width:], b1[:, width:]], 0).astype(F32)
    total = grads + rms_backward(values, root, gain[...], normed_grad)
    after_grad[...] = total
    low[...] = total.astype(BF)
    gain_grad[...] = jnp.broadcast_to(
        0.5 * jnp.sum(normed_grad * values * root, 0, keepdims=True), gain_grad.shape
    )


def attend_back_body(
    heads,
    w_out,
    w_in_t,
    cosine,
    sine,
    bias,
    qkv,
    own,
    got,
    b0,
    b1,
    b2,
    b3,
    keep,
    send,
    projected_grad,
    gain_grad,
):
    width = own.shape[1]
    half = keep.shape[0]
    grads = jnp.concatenate([own[...], got[...]], 0)
    mixed_grad = dot_bt(grads, w_out[...]).astype(BF)
    scale = HD**-0.5
    cosine, sine = cosine[...], sine[...]
    parts = []
    for head, (query, keys, values) in enumerate(head_parts(qkv, heads)):
        at = head * HD
        scores = dot_bt(query, keys) * scale + bias[...].astype(F32)
        powers = jnp.exp(scores - jnp.max(scores, -1, keepdims=True))
        weights = powers * (1.0 / jnp.sum(powers, -1, keepdims=True))
        mine = mixed_grad[:, at : at + HD]
        weight_grad = dot_bt(mine, values)
        delta = jnp.sum(weights * weight_grad, -1, keepdims=True)
        score_grad = (weights * (weight_grad - delta)).astype(BF)
        parts.append(rope_back(dot(score_grad, keys) * scale, cosine, sine))
        parts.append(rope_back(dot_t(score_grad, query) * scale, cosine, sine))
        parts.append(dot_t(weights.astype(BF), mine))
    projected_grad[...] = jnp.concatenate(parts, 1).astype(BF)
    part = dot(projected_grad[...], w_in_t[...])
    tokens = jnp.concatenate([b[:, :width] for b in (b0, b1, b2, b3)], 0).astype(F32)
    gain_grad[...] = jnp.broadcast_to(
        jnp.sum(part * tokens * inverse_root(tokens), 0, keepdims=True), gain_grad.shape
    )
    keep[...] = part[:half]
    send[...] = part[half:].astype(BF)


def last_body(
    block, gain, own, got, b0, after_grad, after_attn, out_own, out_got, near, far
):
    rows, width = own.shape
    tokens = b0[:, :width].astype(F32)
    normed_grad = own[...] + got[...].astype(F32)
    total = after_grad[:rows, :] + rms_backward(
        tokens, inverse_root(tokens), gain[...], normed_grad
    )
    result = after_attn[:rows, :] + out_own[...] + out_got[...].astype(F32)
    store_halves(near, far, block, result.astype(BF), slice(0, width))
    store_halves(near, far, block, total.astype(BF), slice(width, None))


def return_body(anchor, b0, b1, b2, b3, final, grads):
    row_count, width = final.shape
    pick = (iota((row_count, row_count), 0) == anchor[...]).astype(F32).T.astype(BF)
    rows = jnp.concatenate([b[...] for b in (b0, b1, b2, b3)], 0)
    total = dot(pick, rows).astype(BF)
    final[...] = total[:, :width]
    grads[...] = total[:, width:]


def on_device(
    tokens,
    cotangent,
    gain_attn,
    w_qkv,
    w_out,
    gain_ffn,
    w_router,
    w_shared_gate,
    w_shared_up,
    w_shared_down,
    routed_gate_weight,
    routed_up_weight,
    w_expert_down,
    seq_lengths,
    token_order,
    inverse_order,
    routes,
    fill_order,
):
    devices_dp = lax.axis_size(DP)
    devices_tp = lax.axis_size(TP)
    dz = lax.axis_size("dz")
    row_count, width = tokens.shape
    block_rows = row_count // devices_dp
    shard_block = block_rows // devices_tp
    shard_rows = row_count // devices_tp
    half_rows = row_count // 2
    experts_all = w_router.shape[1]
    slot_rows = 4 * row_count // experts_all
    capacity = 5 * row_count * devices_dp // (2 * experts_all)
    inner = w_out.shape[0]
    heads = inner // HD
    per_dp = max(1, experts_all // devices_dp)
    copies = max(1, devices_dp // experts_all)
    sub = devices_tp // per_dp
    my_hi, my_lo = lax.axis_index("hi"), lax.axis_index("lo")
    my_z, my_y = lax.axis_index("dz"), lax.axis_index("dy")
    my_dp = my_z * 2 + my_y
    my_block = my_lo * 2 + my_hi
    pick = my_hi if per_dp == 2 else 0 * my_hi
    my_part = my_lo if per_dp == 2 else my_block
    part_rows = slot_rows // sub
    own_slots = devices_dp * part_rows
    all_slots = own_slots * sub
    my_expert = my_dp // copies * per_dp + pick
    chunk = width // devices_dp
    z_bits = [(my_z >> i) & 1 for i in range(log2(dz))]
    info = jnp.stack([my_block, pick, my_part, my_expert, my_dp, my_y] + z_bits).astype(I32)
    pieces = devices_dp if devices_dp <= 8 else 1

    small = all_slots <= 1024

    def fetch(weights, deps=()):
        return kernel(
            fetch_body,
            [out(w.shape, w.dtype) for w in weights],
            *[Held(w) for w in weights],
            semaphores=len(weights),
            deps=deps,
        )

    table = rope_table(row_count)
    gain_attn = gain_attn[None]
    gain_ffn = gain_ffn[None]

    half_shard = out((shard_rows // 2, 2 * width), BF)
    near, far, anchor = kernel(
        functools.partial(select_body, shard_block, devices_dp),
        [half_shard, half_shard, out((1, row_count), I32)],
        Far(inverse_order[None]),
        Far(tokens),
        Far(cotangent),
        scalars=(info,),
    )

    def blocks_of(own, deps):
        (by_hi,) = kernel(join_body, [out(own.shape, BF)], swap(own, "hi"), deps=deps)
        by_lo = swap(own, "lo")
        return (own, by_hi, by_lo, swap(by_hi, "lo"))

    def z_steps(parts):
        return [parts[0]] + [
            lax.ppermute(parts[k], "dz", [(i, i ^ k) for i in range(dz)]) for k in range(1, dz)
        ]

    def exchange_halves(near, far, deps=()):
        width_sent = near.shape[1]
        block = near.shape[0] // dz
        if devices_dp != 8:
            both_halves = jnp.stack([near, far]).reshape(2, dz, block, width_sent)
            stacked = both_halves.transpose(1, 0, 2, 3).reshape(devices_dp, block, width_sent)
            return [exchange_stacked(stacked).reshape(devices_dp * block, width_sent)]
        middle = kernel(
            functools.partial(middle_body, block),
            [out((2 * block, width_sent), BF)] * dz,
            near,
            swap(far, "dy"),
            deps=deps,
        )
        return z_steps(middle)

    def join(parts, deps=()):
        if not isinstance(parts, (list, tuple)):
            parts = [parts]
        if not small:
            return jnp.concatenate(parts, 0)
        rows = sum(part.shape[0] for part in parts)
        return kernel(join_body, [out((rows, parts[0].shape[1]), BF)], *parts, deps=deps)[0]

    slot_pick, slot_pick_t, bias, cosine, sine, meta = kernel(
        functools.partial(index_body, shard_block, copies, per_dp, part_rows, experts_all),
        [
            out((own_slots, row_count), BF),
            out((row_count, own_slots), BF),
            out((row_count, row_count), BF),
            out((row_count, HD), F32),
            out((row_count, HD), F32),
            out((row_count, 128), BF),
        ],
        Far(token_order[None]),
        Far(routes.T),
        Far(fill_order),
        Far(table),
        scalars=(info, seq_lengths),
        vmem=24,
    )
    router = w_router.T
    w_in_t, w_out = fetch([w_qkv.T, w_out], (slot_pick,))
    blocks = blocks_of(join(exchange_halves(near, far)), (slot_pick, w_in_t))

    keep, send, qkv, mixed, normed_attn = kernel(
        functools.partial(attend_body, heads),
        [
            out((half_rows, width), F32),
            out((half_rows, width), BF),
            out((row_count, 3 * inner), BF),
            out((row_count, inner), BF),
            out((row_count, width), BF),
        ],
        gain_attn,
        w_in_t,
        w_out,
        cosine,
        sine,
        bias,
        *blocks,
        vmem=24,
    )

    def half_sum(keep, send):
        (half,) = kernel(fold_body, [out((half_rows, width), BF)], keep, swap(send, "lo"))
        return half, swap(half, "hi")

    half, half_got = half_sum(keep, send)
    after_attn, normed_own = kernel(
        norm_body,
        [out((half_rows, width), F32), out((half_rows, width), BF)],
        gain_ffn,
        half,
        half_got,
        blocks[0],
        blocks[1],
    )
    normed_got = swap(normed_own, "lo")

    slot_piece = own_slots // pieces
    packed_width = 2 * width + 128
    sent_rows = kernel(
        send_body,
        [out((slot_piece, packed_width), BF)] * pieces,
        slot_pick,
        normed_own,
        normed_got,
        meta,
        *blocks,
    )
    got_rows = exchange_part(sent_rows, 0)

    def sub_gather(parts, deps=()):
        values = join(parts, deps)
        if sub == 4:
            values = jnp.concatenate([values, swap(values, "hi")], 0)
        return values, swap(values, "lo")

    units = w_shared_gate.shape[1]
    shared_part, shared_back, grad_sgate, grad_sup, shared_hidden = kernel(
        shared_body,
        [
            out((row_count, width), F32),
            out((row_count, width), F32),
            out((row_count, units), BF),
            out((row_count, units), BF),
            out((row_count, units), BF),
        ],
        normed_own,
        normed_got,
        *blocks,
        Far(w_shared_gate),
        Far(w_shared_up),
        Far(w_shared_down),
        deps=sent_rows[:1],
        vmem=24,
    )
    def tree_outs(columns_a, columns_b):
        return [
            out((dz, chunk, columns), dtype)
            for dtype in (F32, BF)
            for columns in (columns_a, columns_b)
        ]

    shared_tree = kernel(
        shared_grads_body,
        tree_outs(3 * units // 2, 3 * units // 2),
        normed_own,
        normed_got,
        *blocks,
        grad_sgate,
        grad_sup,
        shared_hidden,
        scalars=(info,),
        vmem=24,
    )

    def z_swap(values, bit):
        return lax.ppermute(values, "dz", [(i, i ^ (1 << bit)) for i in range(dz)])

    def tree_first(parts):
        keep_a, keep_b, send_a, send_b = parts
        return keep_a, swap(send_a, "dy"), keep_b, z_swap(send_b, 0)

    def tree_second(parts, deps=()):
        kept_a, got_a, kept_b, got_b = parts
        shapes = [
            out((dz // 2, chunk, kept.shape[2]), dtype)
            for dtype in (F32, BF)
            for kept in (kept_a, kept_b)
        ]
        keep_a, keep_b, send_a, send_b = kernel(
            tree_second_body, shapes, kept_a, got_a, kept_b, got_b, scalars=(info,), deps=deps
        )
        return (keep_a, z_swap(send_a, 0), keep_b, swap(send_b, "dy")), send_b

    def tree_third(parts, deps=()):
        columns = parts[0].shape[2] + parts[2].shape[2]
        shape = (dz // 4, chunk, columns)
        keep, send = kernel(
            tree_third_body,
            [out(shape, F32), out(shape, BF)],
            *parts,
            scalars=(info,),
            deps=deps,
        )
        sent, got = send, z_swap(send, 1)
        for bit in range(2, log2(dz)):
            shape = (keep.shape[0] // 2, chunk, columns)
            keep, send = kernel(
                functools.partial(tree_body, Z_BITS + bit),
                [out(shape, F32), out(shape, BF)],
                keep,
                got,
                scalars=(info,),
            )
            got = z_swap(send, bit)
        return keep, got, sent

    shared_tree = tree_first(shared_tree)
    if small:
        routed_gate_weight, routed_up_weight, w_expert_down, router = fetch(
            [routed_gate_weight, routed_up_weight, w_expert_down, router], (shared_tree[0],)
        )
    packed_own, packed_got = sub_gather(got_rows, (router,))
    (marks,) = kernel(
        functools.partial(
            meta_body, devices_dp, part_rows, sub, capacity, 2 * width if small else 0
        ),
        [out((all_slots, 128), F32)],
        packed_own if small else packed_own[:, 2 * width :],
        packed_got if small else packed_got[:, 2 * width :],
        scalars=(info,),
    )

    hidden_units = routed_gate_weight.shape[1]
    tile = min(256, own_slots)
    tiles = all_slots // 2 // tile
    steps = 2 * tiles

    def mine_at(i):
        return (jnp.minimum(i, tiles - 1), 0)

    def other_at(i):
        return (jnp.maximum(i - tiles, 0), 0)

    def every_at(i):
        return (i, 0)

    def fixed_at(i):
        return (0, 0)

    half_slots = all_slots // 2
    expert_ins = [
        (packed_own, pl.BlockSpec((tile, packed_width), mine_at)),
        (packed_got, pl.BlockSpec((tile, packed_width), other_at)),
        (marks, pl.BlockSpec((tile, 128), every_at)),
        (router, pl.BlockSpec((experts_all, width), fixed_at)),
        (routed_gate_weight, pl.BlockSpec((width, hidden_units), fixed_at)),
        (routed_up_weight, pl.BlockSpec((width, hidden_units), fixed_at)),
        (w_expert_down, pl.BlockSpec((hidden_units, width), fixed_at)),
    ]
    expert_outs = [
        (out((half_slots, 2 * width), BF), pl.BlockSpec((tile, 2 * width), mine_at)),
        (out((half_slots, 2 * width), BF), pl.BlockSpec((tile, 2 * width), other_at)),
        (out((all_slots, width), BF), pl.BlockSpec((tile, width), every_at)),
        (out((all_slots, hidden_units), BF), pl.BlockSpec((tile, hidden_units), every_at)),
        (out((all_slots, hidden_units), BF), pl.BlockSpec((tile, hidden_units), every_at)),
        (out((all_slots, hidden_units), BF), pl.BlockSpec((tile, hidden_units), every_at)),
        (out((all_slots, width), BF), pl.BlockSpec((tile, width), every_at)),
        (out((half_slots, 128), F32), pl.BlockSpec((tile, 128), mine_at)),
        (out((experts_all, width), F32), pl.BlockSpec((experts_all, width), fixed_at)),
    ]

    def expert_kernel(*refs):
        pltpu.emit_pipeline(
            functools.partial(expert_body, tiles),
            grid=(steps,),
            in_specs=[spec for _, spec in expert_ins],
            out_specs=[spec for _, spec in expert_outs],
        )(*refs)

    expert_args = [value for value, _ in expert_ins]
    expert_shapes = [shape for shape, _ in expert_outs]
    if small:
        piece = out((half_slots // SENT_PIECES, 2 * width), BF)
        keep, *results = kernel(
            functools.partial(expert_whole_body, tile),
            expert_shapes[:1] + [piece] * SENT_PIECES + expert_shapes[2:],
            *expert_args,
            vmem=24,
        )
        results = [keep, results[:SENT_PIECES]] + results[SENT_PIECES:]
    else:
        hbm_spec = pl.BlockSpec(memory_space=pltpu.HBM)
        results = pl.pallas_call(
            expert_kernel,
            in_specs=[hbm_spec] * len(expert_ins),
            out_specs=tuple([hbm_spec] * len(expert_outs)),
            out_shape=tuple(at_hbm(shape) for shape in expert_shapes),
            compiler_params=pltpu.CompilerParams(vmem_limit_bytes=44 * MIB),
            cost_estimate=COST,
            name="expert_body",
        )(*[in_hbm(value) for value in expert_args])
    (
        keep,
        send,
        rows_all,
        expert_hidden,
        grad_egate,
        grad_eup,
        pair_grads,
        gates,
        router_part,
    ) = results

    def sub_scatter(keep, send):
        total = keep.astype(F32) + swap(send, "lo").astype(F32)
        return total[:own_slots] + swap(total[own_slots:].astype(BF), "hi").astype(F32)

    shared_tree, shared_sent = tree_second(shared_tree)
    if sub == 4:
        total = sub_scatter(keep, send)
        gated = gates[:own_slots, :1] * total[:, width:]
        sent_back = [jnp.concatenate([total[:, :width], gated], 1).astype(BF)]
    else:
        sent_back = kernel(
            add_body,
            [out((slot_piece, 2 * width), BF)] * pieces,
            keep,
            gates,
            *[swap(piece, "lo") for piece in send],
            deps=(shared_sent,),
        )

    def weight_grad(left, right, deps=()):
        if not small:
            return dot_t(left, right)
        shape = (left.shape[1], right.shape[1])
        vmem_spec = pl.BlockSpec(memory_space=pltpu.VMEM)
        return pl.pallas_call(
            lambda *refs: weight_grad_body(refs[0], refs[1], *refs[-3:]),
            out_shape=pltpu.HBM(shape, F32),
            in_specs=[vmem_spec] * 2 + [pl.BlockSpec(memory_space=pl.ANY)] * len(deps),
            out_specs=pl.BlockSpec(memory_space=pltpu.HBM),
            scratch_shapes=[
                pltpu.VMEM(shape, F32),
                pltpu.SemaphoreType.DMA((shape[0] // 256,)),
            ],
            compiler_params=pltpu.CompilerParams(vmem_limit_bytes=12 * MIB),
            cost_estimate=COST,
            name="weight_grad",
        )(in_vmem(left), in_vmem(right), *deps)

    grad_w_expert_gate = weight_grad(rows_all, grad_egate, (sent_back[0],))
    got_back = exchange_part(sent_back, 0)
    grad_w_expert_up = weight_grad(rows_all, grad_eup, (sent_back[0],))
    grad_w_expert_down = weight_grad(expert_hidden, pair_grads, (sent_back[0],))
    keep, send, out_keep, out_send = kernel(
        combine_body,
        [out((half_rows, width), F32), out((half_rows, width), BF)] * 2,
        slot_pick_t,
        shared_back,
        shared_part,
        *got_back,
        deps=(
            Far(grad_w_expert_gate),
            Far(grad_w_expert_up),
            Far(grad_w_expert_down),
        ),
    )
    half, half_got = half_sum(keep, send)

    def own_sum(keep, send, deps=()):
        own, send = kernel(
            fold_own_body,
            [out((shard_rows, width), F32), out((shard_rows, width), BF)],
            keep,
            swap(send, "lo"),
            deps=deps,
        )
        return own, send

    out_own, out_send = own_sum(out_keep, out_send, (half,))
    shared_keep, shared_got, shared_sent = tree_third(shared_tree, (half,))
    after_grad, after_grad_own, gain_ffn_part = kernel(
        norm_back_body,
        [out((half_rows, width), F32), out((half_rows, width), BF), out((8, width), F32)],
        gain_ffn,
        half,
        half_got,
        after_attn,
        blocks[0],
        blocks[1],
        deps=(out_send,),
    )
    after_grad_got = swap(after_grad_own, "lo")

    keep, send, projected_grad, gain_attn_part = kernel(
        functools.partial(attend_back_body, heads),
        [
            out((half_rows, width), F32),
            out((half_rows, width), BF),
            out((row_count, 3 * inner), BF),
            out((8, width), F32),
        ],
        w_out,
        w_in_t,
        cosine,
        sine,
        bias,
        qkv,
        after_grad_own,
        after_grad_got,
        *blocks,
        vmem=24,
        deps=(shared_sent,),
    )
    last_columns = 4 * inner + 128
    last_tree = kernel(
        functools.partial(last_grads_body, experts_all),
        tree_outs(512, last_columns - 512),
        normed_attn,
        projected_grad,
        after_grad_own,
        after_grad_got,
        mixed,
        gain_ffn_part,
        gain_attn_part,
        router_part,
        scalars=(info,),
        vmem=24,
        deps=(send,),
    )
    last_tree = tree_first(last_tree)
    own, send = own_sum(keep, send)
    grad_sgate, grad_sup, grad_sdown = kernel(
        shared_end_body,
        [Far(out((chunk, units), F32))] * 3,
        shared_keep,
        shared_got,
    )
    near, far = kernel(
        functools.partial(last_body, shard_block),
        [half_shard, half_shard],
        gain_attn,
        own,
        swap(send, "hi"),
        blocks[0],
        after_grad,
        after_attn,
        out_own,
        swap(out_send, "hi"),
    )
    last_tree, last_sent = tree_second(last_tree, (near,))
    got_last = exchange_halves(near, far, (last_sent, Far(grad_sgate)))
    last_keep, last_got, last_sent = tree_third(last_tree, got_last[:1])
    small_rows = experts_all + 8
    grad_qkv, grad_out, sums = kernel(
        functools.partial(last_end_body, small_rows),
        [
            Far(out((chunk, 3 * inner), F32)),
            Far(out((inner, chunk), F32)),
            out((small_rows, chunk), F32),
        ],
        last_keep,
        last_got,
    )
    got_last = join(got_last, (last_sent,))
    final, grad_tokens = kernel(
        return_body,
        [Far(out((row_count, width), BF)), Far(out((row_count, width), BF))],
        anchor,
        *blocks_of(got_last, (sums,)),
    )

    gain_ffn_sum, gain_attn_sum, router_sum = kernel(
        small_end_body,
        [Far(out((1, chunk), F32)), Far(out((1, chunk), F32)), Far(out((experts_all, chunk), F32))],
        sums,
        *[lax.ppermute(sums, TP, [(i, i ^ k) for i in range(4)]) for k in (1, 2, 3)],
    )
    return (
        final,
        grad_tokens,
        gain_attn_sum.reshape(chunk),
        grad_qkv,
        grad_out,
        gain_ffn_sum.reshape(chunk),
        router_sum.T,
        grad_sgate,
        grad_sup,
        grad_sdown.T,
        grad_w_expert_gate,
        grad_w_expert_up,
        grad_w_expert_down,
    )


def solution(mesh):
    devices_dp, devices_tp = mesh.shape["dp"], mesh.shape["tensor"]
    fine = Mesh(
        mesh.devices.reshape(devices_dp // 2, 2, devices_tp // 2, 2), ("dz", "dy", "hi", "lo")
    )
    every = DP + TP
    return jax.shard_map(
        on_device,
        mesh=fine,
        in_specs=(
            P(DP, None),
            P(DP, None),
            P(),
            P(None, TP),
            P(TP, None),
            P(),
            P(),
            P(None, TP),
            P(None, TP),
            P(TP, None),
            P(None, every),
            P(None, every),
            P(every, None),
            P(DP, None),
            P(DP),
            P(DP),
            P(DP, None),
            P(DP, None),
        ),
        out_specs=(
            P(DP, None),
            P(DP, None),
            P(DP),
            P(DP, TP),
            P(TP, DP),
            P(DP),
            P(DP, None),
            P(DP, TP),
            P(DP, TP),
            P(TP, DP),
            P(None, every),
            P(None, every),
            P(every, None),
        ),
        check_vma=False,
    )
```

```python
import functools

import jax
import jax.numpy as jnp
import numpy as np
from jax import lax
from jax.experimental import pallas as pl
from jax.experimental.pallas import tpu as pltpu
from jax.sharding import Mesh, PartitionSpec as P

HD = 64
MY_BLOCK, PICK, MY_PART, MY_EXPERT, MY_DP, Y_BIT, Z_BITS = range(7)
EPSILON = 1e-06
BF = jnp.bfloat16
F32 = jnp.float32
I32 = jnp.int32
DP = ("dz", "dy")
TP = ("hi", "lo")
MIB = 1 << 20
SENT_PIECES = 4
COST = pl.CostEstimate(flops=1000, bytes_accessed=1000, transcendentals=0)


def dot(left, right):
    return jnp.dot(left, right, preferred_element_type=F32)


def dot_t(left, right):
    return lax.dot_general(left, right, (((0,), (0,)), ((), ())), preferred_element_type=F32)


def dot_bt(left, right):
    return lax.dot_general(left, right, (((1,), (1,)), ((), ())), preferred_element_type=F32)


def swap(values, axis):
    return lax.ppermute(values, axis, [(0, 1), (1, 0)])


def exchange_stacked(values):
    order = jnp.arange(values.shape[0], dtype=I32) ^ lax.axis_index(DP)
    got = lax.all_to_all(
        jnp.take(values, order, axis=0), DP, split_axis=0, concat_axis=0, tiled=True
    )
    return jnp.take(got, order, axis=0)


def exchange(pieces):
    devices = lax.axis_size(DP)
    if len(pieces) == 1:
        (values,) = pieces
        stacked = values.reshape(devices, -1, values.shape[-1])
        return [exchange_stacked(stacked).reshape(values.shape)]
    return exchange_some(dict(enumerate(pieces)))


def exchange_some(pieces):
    devices = lax.axis_size(DP)
    got = dict(pieces)
    for k in (4, 5, 6, 7, 2, 3, 1):
        if k in got:
            got[k] = lax.ppermute(pieces[k], DP, [(i, i ^ k) for i in range(devices)])
    return [got[k] for k in sorted(got)]


def out(shape, dtype):
    return jax.ShapeDtypeStruct(shape, dtype)


class Far:
    def __init__(self, value):
        self.value = value


class Held(Far):
    pass


class Free(Far):
    pass


class Arriving:
    def __init__(self, buffer, copy):
        self.buffer, self.copy, self.waiting = buffer, copy, True
        self.shape, self.dtype = buffer.shape, buffer.dtype

    def ready(self):
        if self.waiting:
            self.copy.wait()
            self.waiting = False

    def __getitem__(self, index):
        self.ready()
        return self.buffer[index]


class Leaving:
    def __init__(self, buffer, copy):
        self.buffer, self.copy, self.started = buffer, copy, False
        self.shape, self.dtype = buffer.shape, buffer.dtype

    def flush(self):
        if not self.started:
            self.copy.start()
            self.started = True

    def __getitem__(self, index):
        return self.buffer[index]

    def __setitem__(self, index, value):
        self.buffer[index] = value


def in_hbm(values):
    return pltpu.with_memory_space_constraint(values, pltpu.HBM)


def in_vmem(values):
    if values.size * values.dtype.itemsize > 4 * MIB:
        return values
    return pltpu.with_memory_space_constraint(values, pltpu.VMEM)


def at_hbm(shape):
    return pltpu.HBM(shape.shape, shape.dtype)


def at_vmem(shape):
    if shape.size * shape.dtype.itemsize > 4 * MIB:
        return shape
    return pltpu.VMEM(shape.shape, shape.dtype)


def kernel(body, outs, *args, scalars=(), deps=(), vmem=16, semaphores=0):
    vmem_spec = pl.BlockSpec(memory_space=pltpu.VMEM)
    hbm_spec = pl.BlockSpec(memory_space=pltpu.HBM)
    any_spec = pl.BlockSpec(memory_space=pl.ANY)
    held = [isinstance(a, Held) for a in args]
    far_in = [isinstance(a, Far) and not h for a, h in zip(args, held)]
    free_out = [isinstance(o, Free) for o in outs]
    far_out = [isinstance(o, Far) and not f for o, f in zip(outs, free_out)]
    args = [in_hbm(a.value) if isinstance(a, Far) else in_vmem(a) for a in args]
    outs = [
        o.value if f else at_hbm(o.value) if h else at_vmem(o)
        for o, f, h in zip(outs, free_out, far_out)
    ]
    deps = [in_hbm(d.value) if isinstance(d, Far) else d for d in deps]
    moved = [x for x, f in zip(args + outs, far_in + far_out) if f]
    scratch = [pltpu.VMEM(x.shape, x.dtype) for x in moved]
    if moved:
        scratch.append(pltpu.SemaphoreType.DMA((len(moved),)))
    if semaphores:
        scratch.append(pltpu.SemaphoreType.DMA((semaphores,)))
    n_scalars, n_args, n_deps, n_outs = len(scalars), len(args), len(deps), len(outs)

    def wrapped(*refs):
        ins = list(refs[: n_scalars + n_args])
        results = list(refs[n_scalars + n_args + n_deps :][:n_outs])
        buffers = refs[n_scalars + n_args + n_deps + n_outs :]
        extra = buffers[-1:] if semaphores else ()
        buffers = buffers[:-1] if semaphores else buffers
        at = 0
        for i, far in enumerate(far_in):
            if far:
                ref = ins[n_scalars + i]
                copy = pltpu.make_async_copy(ref, buffers[at], buffers[-1].at[at])
                copy.start()
                ins[n_scalars + i] = Arriving(buffers[at], copy)
                at += 1
        for i, far in enumerate(far_out):
            if far:
                copy = pltpu.make_async_copy(buffers[at], results[i], buffers[-1].at[at])
                results[i] = Leaving(buffers[at], copy)
                at += 1
        body(*ins, *results, *extra)
        for ref in ins:
            if isinstance(ref, Arriving):
                ref.ready()
        for ref in results:
            if isinstance(ref, Leaving):
                ref.flush()
        for ref in results:
            if isinstance(ref, Leaving):
                ref.copy.wait()

    return pl.pallas_call(
        wrapped,
        out_shape=tuple(outs),
        in_specs=[pl.BlockSpec(memory_space=pltpu.SMEM)] * n_scalars
        + [hbm_spec if f or h else vmem_spec for f, h in zip(far_in, held)]
        + [any_spec] * n_deps,
        out_specs=tuple(hbm_spec if far else vmem_spec for far in far_out),
        scratch_shapes=scratch,
        compiler_params=pltpu.CompilerParams(vmem_limit_bytes=vmem * MIB),
        cost_estimate=COST,
        name=body.func.__name__ if isinstance(body, functools.partial) else body.__name__,
    )(*scalars, *args, *deps)


def tie(values, *deps):
    any_spec = pl.BlockSpec(memory_space=pl.ANY)
    vmem_spec = pl.BlockSpec(memory_space=pltpu.VMEM)
    return pl.pallas_call(
        lambda *refs: None,
        out_shape=out(values.shape, values.dtype),
        in_specs=[vmem_spec] + [any_spec] * len(deps),
        out_specs=vmem_spec,
        input_output_aliases={0: 0},
        cost_estimate=COST,
        name="tie",
    )(in_vmem(values), *[in_hbm(d.value) if isinstance(d, Far) else d for d in deps])


def rope_table(places):
    exponent = np.arange(HD // 2, dtype=np.float32) * np.float32(-2.0 / HD)
    angles = np.arange(places, dtype=np.float32)[:, None] * np.power(np.float32(10000.0), exponent)
    cosine = np.cos(angles.astype(np.float64)).astype(np.float32)
    sine = np.sin(angles.astype(np.float64)).astype(np.float32)
    rest = np.concatenate([cosine, cosine, -sine, sine], 1)
    terms = []
    for _ in range(3):
        terms.append(rest.astype(BF))
        rest = rest - terms[-1].astype(np.float32)
    return jnp.asarray(np.concatenate(terms, 1))


def iota(shape, dim):
    return lax.broadcasted_iota(I32, shape, dim)


def log2(number):
    return number.bit_length() - 1


def silu_parts(gate_in):
    sigmoid_val = 1.0 / (1.0 + jnp.exp(-gate_in))
    return (gate_in * sigmoid_val, sigmoid_val * (1.0 + gate_in * (1.0 - sigmoid_val)))


def inverse_root(values):
    return lax.rsqrt(jnp.mean(values * values, -1, keepdims=True) + EPSILON)


def rms_backward(values, root, gain, grad_normed):
    scaled = grad_normed * gain
    return root * scaled - values * (root * root * root) * jnp.mean(
        scaled * values, -1, keepdims=True
    )


def lane_rank(buckets, bucket_count):
    count = buckets.shape[1]
    rows = max(8, bucket_count)
    member = (iota((rows, count), 0) == buckets).astype(F32)
    earlier = (iota((count, count), 0) < iota((count, count), 1)).astype(F32).astype(BF)
    return jnp.sum(dot(member.astype(BF), earlier) * member, 0, keepdims=True).astype(I32)


def relative_row(block, rank, my_block, shard_block, shard_rows):
    shift = log2(shard_block)
    return (
        ((rank >> shift) ^ my_block) * shard_rows
        + block * shard_block
        + (rank & (shard_block - 1))
    )


def rope_back(grads, cosine, sine):
    return grads * cosine - half_turned(grads) * sine


def store_pieces(refs, value):
    rows = refs[0].shape[0]
    for i, ref in enumerate(refs):
        ref[...] = value[i * rows : (i + 1) * rows]


def joined(refs):
    return jnp.concatenate([ref[...] for ref in refs], 0) if len(refs) > 1 else refs[0][...]


def join_body(*refs):
    *parts, whole = refs
    rows = parts[0].shape[0]
    for i, ref in enumerate(parts):
        whole[i * rows : (i + 1) * rows, :] = ref[...]


def middle_body(block, near, far, *outs):
    for i, ref in enumerate(outs):
        ref[:block, :] = near[i * block : (i + 1) * block, :]
        ref[block:, :] = far[i * block : (i + 1) * block, :]


def store_halves(near, far, block, value, columns):
    for i in range(near.shape[0] // block):
        at = 2 * i * block
        near[i * block : (i + 1) * block, columns] = value[at : at + block]
        far[i * block : (i + 1) * block, columns] = value[at + block : at + 2 * block]


def fetch_body(*refs):
    *refs, semaphores = refs
    count = len(refs) // 2
    copies = [
        pltpu.make_async_copy(refs[i], refs[count + i], semaphores.at[i]) for i in range(count)
    ]
    for copy in copies:
        copy.start()
    for copy in copies:
        copy.wait()


def select_body(shard_block, blocks, info, inverse, tokens, cotangent, near, far, anchor):
    row_count, width = tokens.shape
    shard_rows = shard_block * blocks
    target = (inverse[...] >> log2(row_count)) ^ info[MY_DP]
    row = relative_row(target, lane_rank(target, blocks), info[MY_BLOCK], shard_block, shard_rows)
    anchor[...] = row
    pick = (iota((shard_rows, row_count), 0) == row).astype(F32).astype(BF)
    store_halves(near, far, shard_block, dot(pick, tokens[...]).astype(BF), slice(0, width))
    store_halves(near, far, shard_block, dot(pick, cotangent[...]).astype(BF), slice(width, None))


def index_body(
    shard_block,
    copies,
    per_dp,
    part_rows,
    experts_all,
    info,
    lengths,
    order,
    routes,
    fill,
    table,
    slot_pick,
    slot_pick_t,
    bias,
    cosine,
    sine,
    meta,
):
    row_count = order.shape[1]
    devices_dp = slot_pick.shape[0] // part_rows
    shard_rows = shard_block * devices_dp
    source = (order[...] >> log2(row_count)) ^ info[MY_DP]
    local = relative_row(
        source, lane_rank(source, devices_dp), info[MY_BLOCK], shard_block, shard_rows
    )
    place_pick = (iota((row_count, row_count), 0) == local).astype(F32).astype(BF)
    lanes = iota((1, row_count), 1)
    segment = jnp.zeros((1, row_count), I32)
    start = jnp.zeros((1, row_count), I32)
    end = jnp.int32(0)
    for entry in range(lengths.shape[1]):
        end = end + lengths[0, entry]
        passed = lanes >= end
        segment = segment + passed.astype(I32)
        start = jnp.maximum(start, jnp.where(passed, end, 0))
    place = lanes - start
    expert_sum = routes[0:1, :] + routes[1:2, :] + 1
    facts = jnp.concatenate(
        [segment, place >> 1, place & 1, expert_sum, jnp.zeros((4, row_count), I32)], 0
    )
    facts = facts.astype(F32).astype(BF)
    across = dot_bt(facts, place_pick)
    down = dot_bt(place_pick, facts)
    place_row = 2.0 * across[1:2] + across[2:3]
    place_col = 2.0 * down[:, 1:2] + down[:, 2:3]
    allowed = (down[:, 0:1] == across[0:1]) & (place_row <= place_col)
    bias[...] = jnp.where(allowed, 0.0, -1e30).astype(BF)
    at_place = (
        iota((row_count, row_count), 1).astype(F32) == place_col
    ).astype(F32).astype(BF)
    turned = dot(at_place, table[...])
    pieces = [turned[:, i * 128 : (i + 1) * 128] for i in range(3)]
    turned = pieces[0] + pieces[1] + pieces[2]
    cosine[...] = turned[:, :HD]
    sine[...] = turned[:, HD:]
    meta[...] = jnp.broadcast_to(down[:, 3:4], meta.shape).astype(BF)
    pairs = 2 * row_count
    fill_at = (fill[...] & 1) * row_count + (fill[...] >> 1)
    fill_pick = (iota((pairs, pairs), 0) == fill_at).astype(F32).astype(BF)
    expert_rows = max(16, experts_all)
    pair_expert = jnp.concatenate([routes[0:1, :], routes[1:2, :]], 1)
    named = (iota((expert_rows, pairs), 0) == pair_expert).astype(F32).astype(BF)
    member = dot(named, fill_pick)
    earlier = (iota((pairs, pairs), 0) < iota((pairs, pairs), 1)).astype(F32).astype(BF)
    ranks = (member * (dot(member.astype(BF), earlier) + 1.0)).astype(BF)
    ranks = dot_bt(ranks, fill_pick)
    ranks = (ranks[:, :row_count] + ranks[:, row_count:]).astype(BF)
    ranks = dot_bt(ranks, place_pick).astype(I32)
    slots = iota((part_rows, row_count), 0) + (info[MY_PART] * part_rows + 1)
    experts = iota((expert_rows, row_count), 0)
    for target in range(devices_dp):
        expert = ((target ^ info[MY_DP]) >> log2(copies)) * per_dp + info[PICK]
        chosen = jnp.sum(jnp.where(experts == expert, ranks, 0), 0, keepdims=True)
        picked = (slots == chosen).astype(F32)
        slot_pick[target * part_rows : (target + 1) * part_rows, :] = picked.astype(BF)
    slot_pick_t[...] = slot_pick[...].astype(F32).T.astype(BF)


def head_parts(projected, heads):
    return [
        [projected[:, (3 * h + i) * HD : (3 * h + i + 1) * HD] for i in range(3)]
        for h in range(heads)
    ]


def half_turned(values):
    half = values.shape[1] // 2
    return jnp.concatenate([values[:, half:], values[:, :half]], 1)


def attend_body(
    heads, gain, w_in_t, w_out, cosine, sine, bias, b0, b1, b2, b3, keep, send, qkv, mixed, normed
):
    width = b0.shape[1] // 2
    half = keep.shape[0]
    tokens = jnp.concatenate([b[:, :width] for b in (b0, b1, b2, b3)], 0).astype(F32)
    normed[...] = (tokens * inverse_root(tokens) * gain[...]).astype(BF)
    projected = dot_bt(normed[...], w_in_t[...])
    cosine, sine = cosine[...], sine[...]
    parts = []
    for query, keys, values in head_parts(projected, heads):
        parts.append((query * cosine + half_turned(query) * sine).astype(BF))
        parts.append((keys * cosine + half_turned(keys) * sine).astype(BF))
        parts.append(values.astype(BF))
    qkv[...] = jnp.concatenate(parts, 1)
    scale = HD**-0.5
    mixed_heads = []
    for query, keys, values in head_parts(qkv, heads):
        scores = dot_bt(query, keys) * scale + bias[...].astype(F32)
        powers = jnp.exp(scores - jnp.max(scores, -1, keepdims=True))
        weights = powers * (1.0 / jnp.sum(powers, -1, keepdims=True))
        mixed_heads.append(dot(weights.astype(BF), values))
    mixed[...] = jnp.concatenate(mixed_heads, 1).astype(BF)
    part = dot(mixed[...], w_out[...])
    keep[...] = part[:half]
    send[...] = part[half:].astype(BF)


def fold_body(keep, got, half):
    half[...] = (keep[...] + got[...].astype(F32)).astype(BF)


def fold_own_body(keep, got, own, send):
    rows = own.shape[0]
    own[...] = keep[:rows, :] + got[:rows, :].astype(F32)
    send[...] = (keep[rows:, :] + got[rows:, :].astype(F32)).astype(BF)


def both(half, got):
    rows = half.shape[0] // 2
    mine, other = half[...].astype(F32), got[...].astype(F32)
    return mine + jnp.concatenate([other[rows:], other[:rows]], 0)


def norm_body(gain, half, got, b0, b1, after_attn, normed):
    width = half.shape[1]
    balanced = jnp.concatenate([b0[:, :width], b1[:, :width]], 0).astype(F32)
    values = balanced + both(half, got)
    after_attn[...] = values
    normed[...] = (values * inverse_root(values) * gain[...]).astype(BF)


def send_body(slot_pick, own, got, meta, b0, b1, b2, b3, *sent):
    width = own.shape[1]
    rows = jnp.concatenate([own[...], got[...]], 0)
    rows = dot(slot_pick[...], rows).astype(BF)
    count = sent[0].shape[0]
    near = sum(ref.shape[1] > width for ref in sent) * count
    grads = jnp.concatenate([b[:, width:] for b in (b0, b1, b2, b3)], 0)
    grads = jnp.concatenate([grads, meta[...]], 1)
    grads = dot(slot_pick[:near, :], grads).astype(BF)
    for i, ref in enumerate(sent):
        at = slice(i * count, (i + 1) * count)
        ref[:, :width] = rows[at]
        if ref.shape[1] > width:
            ref[:, width:] = grads[at]


def send_grads_body(first, slot_pick, meta, b0, b1, b2, b3, *sent):
    width = b0.shape[1] // 2
    grads = jnp.concatenate([b[:, width:] for b in (b0, b1, b2, b3)], 0)
    grads = jnp.concatenate([grads, meta[...]], 1)
    store_pieces(sent, dot(slot_pick[first:, :], grads).astype(BF))


def join_packed_body(near, *refs):
    *parts, whole = refs
    count, width = parts[near].shape
    far = (len(parts) - near) // 2
    for i in range(near):
        whole[i * count : (i + 1) * count, :] = parts[i][...]
    for i in range(far):
        at = slice((near + i) * count, (near + i + 1) * count)
        whole[at, :width] = parts[near + i][...]
        whole[at, width:] = parts[near + far + i][...]


def shared_body(
    own, got, b0, b1, b2, b3, w_gate, w_up, w_down, part, back, grad_gate, grad_up, hidden
):
    width = own.shape[1]
    rows = jnp.concatenate([own[...], got[...]], 0)
    grads = jnp.concatenate([b[:, width:] for b in (b0, b1, b2, b3)], 0)
    gate = dot(rows, w_gate[...])
    up = dot(rows, w_up[...])
    act, slope = silu_parts(gate)
    hidden[...] = (act * up).astype(BF)
    part[...] = dot(hidden[...], w_down[...])
    hidden_grad = dot_bt(grads, w_down[...])
    grad_gate[...] = (hidden_grad * up * slope).astype(BF)
    grad_up[...] = (hidden_grad * act).astype(BF)
    back[...] = dot_bt(grad_gate[...], w_gate[...]) + dot_bt(grad_up[...], w_up[...])


def store_tree(info, sums, keeps, sends):
    chunk, columns = keeps[0].shape[1:]
    sides = ((sums[:, :columns], Y_BIT, 1), (sums[:, columns:], Z_BITS, 2))
    for (values, which, stride), keep, send in zip(sides, keeps, sends):
        mine = info[which] == 0
        for i in range(keep.shape[0]):
            at = (2 * i if stride == 1 else i // 2 * 4 + i % 2) * chunk
            first, second = values[at : at + chunk], values[at + stride * chunk :][:chunk]
            keep[i] = jnp.where(mine, first, second)
            send[i] = jnp.where(mine, second, first).astype(BF)


def shared_grads_body(
    info, own, got, b0, b1, b2, b3, grad_gate, grad_up, hidden, *refs
):
    width = own.shape[1]
    rows = jnp.concatenate([own[...], got[...]], 0)
    grads = jnp.concatenate([b[:, width:] for b in (b0, b1, b2, b3)], 0)
    sums = jnp.concatenate(
        [dot_t(rows, grad_gate[...]), dot_t(rows, grad_up[...]), dot_t(grads, hidden[...])], 1
    )
    store_tree(info, sums, refs[:2], refs[2:])


def halved(info, which, total, keep, send):
    mine = info[which] == 0
    for index in range(keep.shape[0]):
        first, second = total[2 * index], total[2 * index + 1]
        keep[index] = jnp.where(mine, first, second)
        send[index] = jnp.where(mine, second, first).astype(BF)


def tree_second_body(info, kept_a, got_a, kept_b, got_b, keep_a, keep_b, send_a, send_b):
    halved(info, Z_BITS, kept_a[...] + got_a[...].astype(F32), keep_a, send_a)
    halved(info, Y_BIT, kept_b[...] + got_b[...].astype(F32), keep_b, send_b)


def tree_third_body(info, kept_a, got_a, kept_b, got_b, keep, send):
    total = jnp.concatenate(
        [kept_a[...] + got_a[...].astype(F32), kept_b[...] + got_b[...].astype(F32)], 2
    )
    halved(info, Z_BITS + 1, total, keep, send)


def tree_third_rider_body(first, info, kept_a, got_a, kept_b, got_b, keep, send):
    width = kept_a.shape[2]
    total = []
    for i in range(2):
        at = slice(i * width, (i + 1) * width)
        sides = (
            kept_a[i] + got_a[first:, at].astype(F32),
            kept_b[i] + got_b[first:, at].astype(F32),
        )
        total.append(jnp.concatenate(sides, 1))
    halved(info, Z_BITS + 1, total, keep, send)


def last_grads_body(
    experts, info, normed, projected_grad, own, got, mixed, gain_ffn, gain_attn, router, *refs
):
    width = normed.shape[1]
    small = jnp.concatenate(
        [
            router[:experts, :],
            gain_ffn[:1, :],
            gain_attn[:1, :],
            jnp.zeros((128 - experts - 2, width), F32),
        ],
        0,
    )
    grads = jnp.concatenate([own[...], got[...]], 0)
    sums = jnp.concatenate(
        [dot_t(normed[...], projected_grad[...]), dot_t(grads, mixed[...]), small.T], 1
    )
    store_tree(info, sums, refs[:2], refs[2:])


def tree_body(which, info, kept, got, keep, send):
    halved(info, which, kept[...] + got[...].astype(F32), keep, send)


def last_end_body(small_rows, kept, got, grad_qkv, grad_out, small):
    total = kept[0] + got[0].astype(F32)
    columns, inner = grad_qkv.shape[1], grad_out.shape[0]
    grad_qkv[...] = total[:, :columns]
    grad_out[...] = total[:, columns : columns + inner].T
    small[...] = total[:, columns + inner :].T[:small_rows]


def small_end_body(own, by_lo, by_hi, by_both, gain_ffn, gain_attn, router):
    experts = router.shape[0]
    total = (own[...] + by_lo[...]) + (by_hi[...] + by_both[...])
    router[...] = total[:experts]
    gain_ffn[...] = total[experts : experts + 1]
    gain_attn[...] = total[experts + 1 : experts + 2]


def shared_end_body(kept, got, grad_gate, grad_up, grad_down):
    total = kept[0] + got[0].astype(F32)
    units = grad_gate.shape[1]
    grad_gate[...] = total[:, :units]
    grad_up[...] = total[:, units : 2 * units]
    grad_down[...] = total[:, 2 * units :]


def add_far_body(keep, *refs):
    got, total = refs[: SENT_PIECES // 2], refs[SENT_PIECES // 2 :]
    half = keep.shape[0] // 2
    store_pieces(total, (keep[half:, :].astype(F32) + joined(got).astype(F32)).astype(BF))


def gated_parts(keep, got, gates):
    gate = jnp.concatenate([gates] * (keep.shape[1] // 128), 1)
    return (gate * (keep.astype(F32) + got.astype(F32))).astype(BF)


def add_near_body(keep, part_keep, gates, tree_a, tree_b, *refs):
    got, part_got, total = (
        refs[: SENT_PIECES // 2],
        refs[SENT_PIECES // 2 : SENT_PIECES],
        refs[SENT_PIECES:],
    )
    half, width = keep.shape[0] // 2, keep.shape[1]
    rows = (keep[:half, :].astype(F32) + joined(got).astype(F32)).astype(BF)
    parts = gated_parts(part_keep[:half, :], joined(part_got), gates[:half, :])
    count = total[0].shape[0]
    for i, ref in enumerate(total):
        at = slice(i * count, (i + 1) * count)
        ref[:count, :width] = rows[at]
        ref[:count, width:] = parts[at]
    for tree, ref in ((tree_b, total[1]), (tree_a, total[2])):
        for i in range(2):
            ref[count:, i * width : (i + 1) * width] = tree[i]


def part_far_body(keep, gates, *refs):
    got, total = refs[: SENT_PIECES // 2], refs[SENT_PIECES // 2 :]
    half = keep.shape[0] // 2
    store_pieces(total, gated_parts(keep[half:, :], joined(got), gates[half:, :]))


def weight_grad_body(left, right, total, sums, semaphores):
    tile = 256
    copies = []
    for i in range(left.shape[1] // tile):
        at = slice(i * tile, (i + 1) * tile)
        sums[at, :] = dot_t(left[:, at], right[...])
        copies.append(
            pltpu.make_async_copy(sums.at[at, :], total.at[at, :], semaphores.at[i])
        )
        copies[-1].start()
    for copy in copies:
        copy.wait()


def meta_body(devices_dp, part_rows, sub, capacity, width, info, own, got, marks):
    my_part, my_expert = info[MY_PART], info[MY_EXPERT]
    lanes = iota((part_rows, 128), 1)
    blocks = [(ref, at, part) for part, (ref, at) in enumerate(
        [(own, i) for i in range(sub // 2)] + [(got, i) for i in range(sub // 2)]
    )]
    counts = []
    for block in range(devices_dp):
        count = jnp.zeros((1, 128), F32)
        for ref, at, _ in blocks:
            start = (at * devices_dp + block) * part_rows
            value = ref[start : start + part_rows, width:].astype(F32)
            count = count + jnp.sum((value > 0.0).astype(F32), 0, keepdims=True)
        counts.append(count)
    for block in range(devices_dp):
        earlier = jnp.zeros((1, 128), F32)
        for before in range(devices_dp):
            ahead = (before ^ info[MY_DP]) < (block ^ info[MY_DP])
            earlier = earlier + jnp.where(ahead, counts[before], 0.0)
        for ref, at, part in blocks:
            start = (at * devices_dp + block) * part_rows
            value = ref[start : start + part_rows, width:].astype(F32)
            valid = value > 0.0
            slot = iota((part_rows, 128), 0) + (my_part ^ part) * part_rows
            kept = valid & (slot.astype(F32) + earlier < capacity)
            other = value.astype(I32) - 1 - my_expert
            mark = (lanes == my_expert).astype(F32) - (lanes == other).astype(F32)
            row = (part * devices_dp + block) * part_rows
            marks[row : row + part_rows, :] = jnp.where(
                lanes == 127, kept.astype(F32), jnp.where(valid, mark, 0.0)
            )


def expert_step(packed, mark, w_router, w_gate, w_up, w_down, stores):
    hidden_out, grad_gate_out, grad_up_out, pair_out = stores
    width = w_gate.shape[0]
    rows, grads = packed[:, :width], packed[:, width : 2 * width].astype(F32)
    kept = mark[:, 127:128] > 0.5
    mark = mark[:, : w_router.shape[0]]
    gap = jnp.sum(dot_bt(rows, w_router[...]) * mark, 1, keepdims=True)
    gate = 1.0 / (1.0 + jnp.exp(-gap))
    gate_other = 1.0 / (1.0 + jnp.exp(gap))
    gate_in = dot(rows, w_gate[...])
    up = dot(rows, w_up[...])
    act, slope = silu_parts(gate_in)
    hidden = (act * up).astype(BF)
    hidden_out(hidden)
    part = jnp.where(kept, dot(hidden, w_down[...]), 0.0).astype(BF)
    pair = jnp.where(kept, gate * grads, 0.0).astype(BF)
    pair_out(pair)
    gate_grad = jnp.sum(part.astype(F32) * grads, 1, keepdims=True)
    logit_grad = (gate * gate_other * gate_grad * mark).astype(BF)
    hidden_grad = dot_bt(pair, w_down[...])
    grad_gate = (hidden_grad * up * slope).astype(BF)
    grad_up = (hidden_grad * act).astype(BF)
    grad_gate_out(grad_gate)
    grad_up_out(grad_up)
    back = (dot_bt(grad_gate, w_gate[...]) + dot_bt(grad_up, w_up[...])).astype(BF).astype(F32)
    back = (back + dot(logit_grad, w_router[...])).astype(BF)
    return back, part, gate, dot_t(logit_grad, rows)


def store_at(ref, where=...):
    def store(value):
        ref[where] = value

    return store


def expert_body(
    tiles,
    packed_own,
    packed_got,
    marks,
    w_router,
    w_gate,
    w_up,
    w_down,
    keep,
    send,
    rows_all,
    hidden,
    grad_gate,
    grad_up,
    pair,
    gates,
    router,
):
    step = pl.program_id(0)
    mine = step < tiles
    width = rows_all.shape[1]
    packed = jnp.where(mine, packed_own[...], packed_got[...])
    rows_all[...] = packed[:, :width]
    back, part, gate, router_term = expert_step(
        packed,
        marks[...],
        w_router,
        w_gate,
        w_up,
        w_down,
        [store_at(ref) for ref in (hidden, grad_gate, grad_up, pair)],
    )

    @pl.when(step == 0)
    def _():
        router[...] = jnp.zeros_like(router)

    router[...] += router_term

    @pl.when(mine)
    def _():
        keep[:, :width] = back
        keep[:, width:] = part
        gates[...] = jnp.broadcast_to(gate, gates.shape)

    @pl.when(jnp.logical_not(mine))
    def _():
        send[:, :width] = back
        send[:, width:] = part


def expert_whole_body(
    tile,
    packed_own,
    packed_got,
    marks,
    w_router,
    w_gate,
    w_up,
    w_down,
    back_keep,
    part_keep,
    *refs,
):
    back_send, part_send = refs[:SENT_PIECES], refs[SENT_PIECES : 2 * SENT_PIECES]
    rows_all, hidden, grad_gate, grad_up, pair, gates, router = refs[2 * SENT_PIECES :]
    half = packed_own.shape[0]
    width = rows_all.shape[1]
    router[...] = jnp.zeros_like(router)

    def run(base, packed_ref, put):
        def step(index, _):
            at = pl.ds(pl.multiple_of(index * tile, tile), tile)
            place = pl.ds(pl.multiple_of(base + index * tile, tile), tile)
            packed = packed_ref[at, : 2 * width]
            rows_all[place, :] = packed[:, :width]
            back, part, gate, router_term = expert_step(
                packed,
                marks[place, :],
                w_router,
                w_gate,
                w_up,
                w_down,
                [store_at(ref, (place, slice(None))) for ref in (hidden, grad_gate, grad_up, pair)],
            )
            router[...] += router_term
            put(index, at, back, part)
            if base == 0:
                gates[at, :] = jnp.broadcast_to(gate, (tile, 128))
            return 0

        lax.fori_loop(0, half // tile, step, 0)

    def put_own(index, at, back, part):
        back_keep[at, :] = back
        part_keep[at, :] = part

    def put_got(index, at, back, part):
        rows = half // SENT_PIECES
        each = tile // rows
        for i in range(SENT_PIECES):

            @pl.when(index == i // each)
            def _(i=i):
                inside = slice(i % each * rows, (i % each + 1) * rows)
                back_send[i][...] = back[inside]
                part_send[i][...] = part[inside]

    run(0, packed_own, put_own)
    run(half, packed_got, put_got)


def combine_body(slot_pick_t, addend, *refs):
    *back, keep, send = refs
    half, width = keep.shape
    count = back[-1].shape[0]
    rows = jnp.concatenate([ref[:count, :width] for ref in back], 0)
    total = addend[...] + dot(slot_pick_t[...], rows)
    keep[...] = total[:half]
    send[...] = total[half:].astype(BF)


def result_first_body(count, slot_pick_t, addend, *refs):
    *near, a, b, total = refs
    width = total.shape[1]
    rows = jnp.concatenate([ref[:count, width:] for ref in near] + [a[...], b[...]], 0)
    total[...] = addend[...] + dot(slot_pick_t[:, : rows.shape[0]], rows)


def result_second_body(slot_pick_t, addend, attn_keep, attn_send, a, b, keep, send):
    half, width = attn_keep.shape
    rows = jnp.concatenate([a[...], b[...]], 0)
    total = addend[...] + dot(slot_pick_t[:, -rows.shape[0] :], rows)
    keep[:, :width] = total[:half]
    send[:, :width] = total[half:].astype(BF)
    keep[:, width:] = attn_keep[...]
    send[:, width:] = attn_send[...]


def norm_back_body(
    gain, half, got, after_attn, b0, b1, after_grad, low, gain_grad
):
    width = half.shape[1]
    normed_grad = both(half, got)
    values = after_attn[...]
    root = inverse_root(values)
    grads = jnp.concatenate([b0[:, width:], b1[:, width:]], 0).astype(F32)
    total = grads + rms_backward(values, root, gain[...], normed_grad)
    after_grad[...] = total
    low[...] = total.astype(BF)
    gain_grad[...] = jnp.broadcast_to(
        0.5 * jnp.sum(normed_grad * values * root, 0, keepdims=True), gain_grad.shape
    )


def attend_back_body(
    heads,
    w_out,
    w_in_t,
    cosine,
    sine,
    bias,
    qkv,
    own,
    got,
    b0,
    b1,
    b2,
    b3,
    keep,
    send,
    projected_grad,
    gain_grad,
):
    width = own.shape[1]
    half = keep.shape[0]
    grads = jnp.concatenate([own[...], got[...]], 0)
    mixed_grad = dot_bt(grads, w_out[...]).astype(BF)
    scale = HD**-0.5
    cosine, sine = cosine[...], sine[...]
    parts = []
    for head, (query, keys, values) in enumerate(head_parts(qkv, heads)):
        at = head * HD
        scores = dot_bt(query, keys) * scale + bias[...].astype(F32)
        powers = jnp.exp(scores - jnp.max(scores, -1, keepdims=True))
        weights = powers * (1.0 / jnp.sum(powers, -1, keepdims=True))
        mine = mixed_grad[:, at : at + HD]
        weight_grad = dot_bt(mine, values)
        delta = jnp.sum(weights * weight_grad, -1, keepdims=True)
        score_grad = (weights * (weight_grad - delta)).astype(BF)
        parts.append(rope_back(dot(score_grad, keys) * scale, cosine, sine))
        parts.append(rope_back(dot_t(score_grad, query) * scale, cosine, sine))
        parts.append(dot_t(weights.astype(BF), mine))
    projected_grad[...] = jnp.concatenate(parts, 1).astype(BF)
    part = dot(projected_grad[...], w_in_t[...])
    tokens = jnp.concatenate([b[:, :width] for b in (b0, b1, b2, b3)], 0).astype(F32)
    gain_grad[...] = jnp.broadcast_to(
        jnp.sum(part * tokens * inverse_root(tokens), 0, keepdims=True), gain_grad.shape
    )
    keep[...] = part[:half]
    send[...] = part[half:].astype(BF)


def last_body(
    block, gain, own, got, b0, after_grad, after_attn, near, far
):
    rows, width = own.shape[0], own.shape[1] // 2
    tokens = b0[:, :width].astype(F32)
    sums = own[...] + got[...].astype(F32)
    normed_grad = sums[:, width:]
    total = after_grad[:rows, :] + rms_backward(
        tokens, inverse_root(tokens), gain[...], normed_grad
    )
    result = after_attn[:rows, :] + sums[:, :width]
    store_halves(near, far, block, result.astype(BF), slice(0, width))
    store_halves(near, far, block, total.astype(BF), slice(width, None))


def return_body(anchor, b0, b1, b2, b3, final, grads):
    row_count, width = final.shape
    pick = (iota((row_count, row_count), 0) == anchor[...]).astype(F32).T.astype(BF)
    rows = jnp.concatenate([b[...] for b in (b0, b1, b2, b3)], 0)
    total = dot(pick, rows).astype(BF)
    final[...] = total[:, :width]
    grads[...] = total[:, width:]


def on_device(
    tokens,
    cotangent,
    gain_attn,
    w_qkv,
    w_out,
    gain_ffn,
    w_router,
    w_shared_gate,
    w_shared_up,
    w_shared_down,
    routed_gate_weight,
    routed_up_weight,
    w_expert_down,
    seq_lengths,
    token_order,
    inverse_order,
    routes,
    fill_order,
):
    devices_dp = lax.axis_size(DP)
    devices_tp = lax.axis_size(TP)
    dz = lax.axis_size("dz")
    row_count, width = tokens.shape
    block_rows = row_count // devices_dp
    shard_block = block_rows // devices_tp
    shard_rows = row_count // devices_tp
    half_rows = row_count // 2
    experts_all = w_router.shape[1]
    slot_rows = 4 * row_count // experts_all
    capacity = 5 * row_count * devices_dp // (2 * experts_all)
    inner = w_out.shape[0]
    heads = inner // HD
    per_dp = max(1, experts_all // devices_dp)
    copies = max(1, devices_dp // experts_all)
    sub = devices_tp // per_dp
    my_hi, my_lo = lax.axis_index("hi"), lax.axis_index("lo")
    my_z, my_y = lax.axis_index("dz"), lax.axis_index("dy")
    my_dp = my_z * 2 + my_y
    my_block = my_lo * 2 + my_hi
    pick = my_hi if per_dp == 2 else 0 * my_hi
    my_part = my_lo if per_dp == 2 else my_block
    part_rows = slot_rows // sub
    own_slots = devices_dp * part_rows
    all_slots = own_slots * sub
    my_expert = my_dp // copies * per_dp + pick
    chunk = width // devices_dp
    z_bits = [(my_z >> i) & 1 for i in range(log2(dz))]
    info = jnp.stack([my_block, pick, my_part, my_expert, my_dp, my_y] + z_bits).astype(I32)
    pieces = devices_dp if devices_dp <= 8 else 1

    small = all_slots <= 1024

    def fetch(weights, deps=()):
        return kernel(
            fetch_body,
            [out(w.shape, w.dtype) for w in weights],
            *[Held(w) for w in weights],
            semaphores=len(weights),
            deps=deps,
        )

    table = rope_table(row_count)
    gain_attn = gain_attn[None]
    gain_ffn = gain_ffn[None]

    half_shard = out((shard_rows // 2, 2 * width), BF)
    near, far, anchor = kernel(
        functools.partial(select_body, shard_block, devices_dp),
        [half_shard, half_shard, out((1, row_count), I32)],
        Far(inverse_order[None]),
        Far(tokens),
        Far(cotangent),
        scalars=(info,),
    )

    def blocks_of(own, deps):
        (by_hi,) = kernel(join_body, [out(own.shape, BF)], swap(own, "hi"), deps=deps)
        by_lo = swap(own, "lo")
        return (own, by_hi, by_lo, swap(by_hi, "lo"))

    def z_steps(parts):
        got = list(parts)
        for k in (2, 3, 1):
            got[k] = lax.ppermute(parts[k], "dz", [(i, i ^ k) for i in range(dz)])
        return got

    def exchange_halves(near, far, deps=()):
        width_sent = near.shape[1]
        block = near.shape[0] // dz
        if devices_dp != 8:
            both_halves = jnp.stack([near, far]).reshape(2, dz, block, width_sent)
            stacked = both_halves.transpose(1, 0, 2, 3).reshape(devices_dp, block, width_sent)
            return [exchange_stacked(stacked).reshape(devices_dp * block, width_sent)]
        middle = kernel(
            functools.partial(middle_body, block),
            [out((2 * block, width_sent), BF)] * dz,
            near,
            swap(far, "dy"),
            deps=deps,
        )
        return z_steps(middle)

    def join(parts, deps=()):
        if not isinstance(parts, (list, tuple)):
            parts = [parts]
        if not small:
            return jnp.concatenate(parts, 0)
        rows = sum(part.shape[0] for part in parts)
        return kernel(join_body, [out((rows, parts[0].shape[1]), BF)], *parts, deps=deps)[0]

    slot_pick, slot_pick_t, bias, cosine, sine, meta = kernel(
        functools.partial(index_body, shard_block, copies, per_dp, part_rows, experts_all),
        [
            out((own_slots, row_count), BF),
            out((row_count, own_slots), BF),
            out((row_count, row_count), BF),
            out((row_count, HD), F32),
            out((row_count, HD), F32),
            out((row_count, 128), BF),
        ],
        Far(token_order[None]),
        Far(routes.T),
        Far(fill_order),
        Far(table),
        scalars=(info, seq_lengths),
        vmem=24,
    )
    router = w_router.T
    w_in_t, w_out = fetch([w_qkv.T, w_out], (slot_pick,))
    blocks = blocks_of(join(exchange_halves(near, far)), (slot_pick, w_in_t))

    slot_piece = own_slots // pieces
    near_pieces = pieces // 2 if small else pieces
    packed_width = 2 * width + 128
    got_grads = []
    if small:
        sent_grads = kernel(
            functools.partial(send_grads_body, near_pieces * slot_piece),
            [out((slot_piece, width + 128), BF)] * (pieces - near_pieces),
            slot_pick,
            meta,
            *blocks,
        )
        got_grads = exchange_some(dict(enumerate(sent_grads, near_pieces)))

    keep, send, qkv, mixed, normed_attn = kernel(
        functools.partial(attend_body, heads),
        [
            out((half_rows, width), F32),
            out((half_rows, width), BF),
            out((row_count, 3 * inner), BF),
            out((row_count, inner), BF),
            out((row_count, width), BF),
        ],
        gain_attn,
        w_in_t,
        w_out,
        cosine,
        sine,
        bias,
        *blocks,
        vmem=24,
    )

    def half_sum(keep, send):
        (half,) = kernel(fold_body, [out((half_rows, width), BF)], keep, swap(send, "lo"))
        return half, swap(half, "hi")

    half, half_got = half_sum(keep, send)
    fetched = [w_shared_gate, w_shared_up, w_shared_down, router]
    if small:
        fetched += [routed_gate_weight, routed_up_weight, w_expert_down]
    fetched = fetch(fetched, (half,))
    w_shared_gate, w_shared_up, w_shared_down, router = fetched[:4]
    if small:
        routed_gate_weight, routed_up_weight, w_expert_down = fetched[4:]
    after_attn, normed_own = kernel(
        norm_body,
        [out((half_rows, width), F32), out((half_rows, width), BF)],
        gain_ffn,
        half,
        half_got,
        blocks[0],
        blocks[1],
        deps=got_grads[:2] + [router],
    )
    normed_got = swap(normed_own, "lo")

    far_piece = out((slot_piece, width), BF)
    sent_rows = kernel(
        send_body,
        [out((slot_piece, packed_width), BF)] * near_pieces + [far_piece] * (pieces - near_pieces),
        slot_pick,
        normed_own,
        normed_got,
        meta,
        *blocks,
    )
    got_rows = exchange(sent_rows)

    def sub_gather(parts, deps=()):
        values = join(parts, deps)
        if sub == 4:
            values = jnp.concatenate([values, swap(values, "hi")], 0)
        return values, swap(values, "lo")

    units = w_shared_gate.shape[1]
    shared_part, shared_back, grad_sgate, grad_sup, shared_hidden = kernel(
        shared_body,
        [
            out((row_count, width), F32),
            out((row_count, width), F32),
            out((row_count, units), BF),
            out((row_count, units), BF),
            out((row_count, units), BF),
        ],
        normed_own,
        normed_got,
        *blocks,
        w_shared_gate,
        w_shared_up,
        w_shared_down,
        deps=sent_rows[:1],
        vmem=24,
    )
    def tree_outs(columns_a, columns_b):
        return [
            out((dz, chunk, columns), dtype)
            for dtype in (F32, BF)
            for columns in (columns_a, columns_b)
        ]

    shared_tree = kernel(
        shared_grads_body,
        tree_outs(3 * units // 2, 3 * units // 2),
        normed_own,
        normed_got,
        *blocks,
        grad_sgate,
        grad_sup,
        shared_hidden,
        scalars=(info,),
        vmem=24,
    )

    def z_swap(values, bit):
        return lax.ppermute(values, "dz", [(i, i ^ (1 << bit)) for i in range(dz)])

    def tree_first(parts):
        keep_a, keep_b, send_a, send_b = parts
        return keep_a, swap(send_a, "dy"), keep_b, z_swap(send_b, 0)

    def tree_second(parts, deps=(), riding=False):
        kept_a, got_a, kept_b, got_b = parts
        shapes = [
            out((dz // 2, chunk, kept.shape[2]), dtype)
            for dtype in (F32, BF)
            for kept in (kept_a, kept_b)
        ]
        keep_a, keep_b, send_a, send_b = kernel(
            tree_second_body, shapes, kept_a, got_a, kept_b, got_b, scalars=(info,), deps=deps
        )
        if riding:
            return (keep_a, send_a, keep_b, send_b), send_b
        return (keep_a, z_swap(send_a, 0), keep_b, swap(send_b, "dy")), send_b

    def tree_third(parts, deps=(), first=None):
        columns = parts[0].shape[2] + parts[2].shape[2]
        shape = (dz // 4, chunk, columns)
        keep, send = kernel(
            tree_third_body if first is None else functools.partial(tree_third_rider_body, first),
            [out(shape, F32), out(shape, BF)],
            *parts,
            scalars=(info,),
            deps=deps,
        )
        sent, got = send, z_swap(send, 1)
        for bit in range(2, log2(dz)):
            shape = (keep.shape[0] // 2, chunk, columns)
            keep, send = kernel(
                functools.partial(tree_body, Z_BITS + bit),
                [out(shape, F32), out(shape, BF)],
                keep,
                got,
                scalars=(info,),
            )
            got = z_swap(send, bit)
        return keep, got, sent

    shared_tree = tree_first(shared_tree)
    if small:
        (packed_own,) = kernel(
            functools.partial(join_packed_body, near_pieces),
            [out((own_slots, packed_width), BF)],
            *got_rows,
            *got_grads,
            deps=(shared_tree[0],),
        )
        packed_got = swap(packed_own, "lo")
    else:
        packed_own, packed_got = sub_gather(got_rows)
    (marks,) = kernel(
        functools.partial(
            meta_body, devices_dp, part_rows, sub, capacity, 2 * width if small else 0
        ),
        [out((all_slots, 128), F32)],
        packed_own if small else packed_own[:, 2 * width :],
        packed_got if small else packed_got[:, 2 * width :],
        scalars=(info,),
    )

    hidden_units = routed_gate_weight.shape[1]
    tile = min(256, own_slots)
    tiles = all_slots // 2 // tile
    steps = 2 * tiles

    def mine_at(i):
        return (jnp.minimum(i, tiles - 1), 0)

    def other_at(i):
        return (jnp.maximum(i - tiles, 0), 0)

    def every_at(i):
        return (i, 0)

    def fixed_at(i):
        return (0, 0)

    half_slots = all_slots // 2
    expert_ins = [
        (packed_own, pl.BlockSpec((tile, packed_width), mine_at)),
        (packed_got, pl.BlockSpec((tile, packed_width), other_at)),
        (marks, pl.BlockSpec((tile, 128), every_at)),
        (router, pl.BlockSpec((experts_all, width), fixed_at)),
        (routed_gate_weight, pl.BlockSpec((width, hidden_units), fixed_at)),
        (routed_up_weight, pl.BlockSpec((width, hidden_units), fixed_at)),
        (w_expert_down, pl.BlockSpec((hidden_units, width), fixed_at)),
    ]
    expert_outs = [
        (out((half_slots, 2 * width), BF), pl.BlockSpec((tile, 2 * width), mine_at)),
        (out((half_slots, 2 * width), BF), pl.BlockSpec((tile, 2 * width), other_at)),
        (out((all_slots, width), BF), pl.BlockSpec((tile, width), every_at)),
        (out((all_slots, hidden_units), BF), pl.BlockSpec((tile, hidden_units), every_at)),
        (out((all_slots, hidden_units), BF), pl.BlockSpec((tile, hidden_units), every_at)),
        (out((all_slots, hidden_units), BF), pl.BlockSpec((tile, hidden_units), every_at)),
        (out((all_slots, width), BF), pl.BlockSpec((tile, width), every_at)),
        (out((half_slots, 128), F32), pl.BlockSpec((tile, 128), mine_at)),
        (out((experts_all, width), F32), pl.BlockSpec((experts_all, width), fixed_at)),
    ]

    def expert_kernel(*refs):
        pltpu.emit_pipeline(
            functools.partial(expert_body, tiles),
            grid=(steps,),
            in_specs=[spec for _, spec in expert_ins],
            out_specs=[spec for _, spec in expert_outs],
        )(*refs)

    expert_args = [value for value, _ in expert_ins]
    expert_shapes = [shape for shape, _ in expert_outs]
    if small:
        piece = out((half_slots // SENT_PIECES, width), BF)
        results = kernel(
            functools.partial(expert_whole_body, tile),
            [out((half_slots, width), BF)] * 2 + [piece] * 2 * SENT_PIECES + expert_shapes[2:],
            *expert_args,
            vmem=24,
        )
        keep, part_keep, *results = results
        send, part_send = results[:SENT_PIECES], results[SENT_PIECES : 2 * SENT_PIECES]
        results = [keep, send] + list(results[2 * SENT_PIECES :])
    else:
        hbm_spec = pl.BlockSpec(memory_space=pltpu.HBM)
        results = pl.pallas_call(
            expert_kernel,
            in_specs=[hbm_spec] * len(expert_ins),
            out_specs=tuple([hbm_spec] * len(expert_outs)),
            out_shape=tuple(at_hbm(shape) for shape in expert_shapes),
            compiler_params=pltpu.CompilerParams(vmem_limit_bytes=44 * MIB),
            cost_estimate=COST,
            name="expert_body",
        )(*[in_hbm(value) for value in expert_args])
    (
        keep,
        send,
        rows_all,
        expert_hidden,
        grad_egate,
        grad_eup,
        pair_grads,
        gates,
        router_part,
    ) = results

    def sub_scatter(keep, send):
        total = keep.astype(F32) + swap(send, "lo").astype(F32)
        return total[:own_slots] + swap(total[own_slots:].astype(BF), "hi").astype(F32)

    if small:
        got = [swap(piece, "lo") for piece in send]
        part_got = [swap(piece, "lo") for piece in part_send]
        back_far = kernel(
            add_far_body,
            [far_piece] * (pieces - near_pieces),
            keep,
            *got[SENT_PIECES // 2 :],
            deps=(shared_tree[1], shared_tree[3]),
        )
        keep_a, send_a, keep_b, send_b = tree_second(shared_tree, riding=True)[0]
        plain = out((slot_piece, 2 * width), BF)
        loaded = out((slot_piece + chunk, 2 * width), BF)
        back_near = kernel(
            add_near_body,
            [plain, loaded, loaded, plain],
            keep,
            part_keep,
            gates,
            send_a,
            send_b,
            *got[: SENT_PIECES // 2],
            *part_got[: SENT_PIECES // 2],
        )
        sent_back = list(back_near) + list(back_far)
        sent_parts = kernel(
            part_far_body,
            [far_piece] * (pieces - near_pieces),
            part_keep,
            gates,
            *part_got[SENT_PIECES // 2 :],
            deps=sent_back[:1],
        )
    else:
        total = sub_scatter(keep, send)
        sent_back = [total[:, :width].astype(BF)]
        sent_parts = [(gates[:own_slots, :1] * total[:, width:]).astype(BF)]
        shared_tree, _ = tree_second(shared_tree)

    def weight_grad(left, right, deps=()):
        if not small:
            return dot_t(left, right)
        shape = (left.shape[1], right.shape[1])
        vmem_spec = pl.BlockSpec(memory_space=pltpu.VMEM)
        return pl.pallas_call(
            lambda *refs: weight_grad_body(refs[0], refs[1], *refs[-3:]),
            out_shape=pltpu.HBM(shape, F32),
            in_specs=[vmem_spec] * 2 + [pl.BlockSpec(memory_space=pl.ANY)] * len(deps),
            out_specs=pl.BlockSpec(memory_space=pltpu.HBM),
            scratch_shapes=[
                pltpu.VMEM(shape, F32),
                pltpu.SemaphoreType.DMA((shape[0] // 256,)),
            ],
            compiler_params=pltpu.CompilerParams(vmem_limit_bytes=12 * MIB),
            cost_estimate=COST,
            name="weight_grad",
        )(in_vmem(left), in_vmem(right), *deps)

    grad_w_expert_gate = weight_grad(rows_all, grad_egate, (sent_back[0],))
    got_back = exchange(sent_back)
    if small:
        got_parts = exchange_some(dict(enumerate(sent_parts, near_pieces)))
        shared_keep, shared_got, shared_sent = tree_third(
            (keep_a, got_back[2], keep_b, got_back[1]), first=slot_piece
        )
    else:
        got_parts = exchange(sent_parts)
        shared_keep, shared_got, shared_sent = tree_third(shared_tree)
    keep, send = kernel(
        combine_body,
        [out((half_rows, width), F32), out((half_rows, width), BF)],
        slot_pick_t,
        shared_back,
        *got_back,
        deps=(
            Far(grad_w_expert_gate),
            shared_sent,
        ),
    )
    half, half_got = half_sum(keep, send)

    def own_sum(keep, send, deps=()):
        own, send = kernel(
            fold_own_body,
            [out((shard_rows, width), F32), out((shard_rows, width), BF)],
            keep,
            swap(send, "lo"),
            deps=deps,
        )
        return own, send

    if small:
        (result_part,) = kernel(
            functools.partial(result_first_body, slot_piece),
            [out((row_count, width), F32)],
            slot_pick_t,
            shared_part,
            *got_back[:near_pieces],
            *got_parts[:2],
        )
    after_grad, after_grad_own, gain_ffn_part = kernel(
        norm_back_body,
        [out((half_rows, width), F32), out((half_rows, width), BF), out((8, width), F32)],
        gain_ffn,
        half,
        half_got,
        after_attn,
        blocks[0],
        blocks[1],
        deps=(result_part,) if small else (),
    )
    after_grad_got = swap(after_grad_own, "lo")

    keep, send, projected_grad, gain_attn_part = kernel(
        functools.partial(attend_back_body, heads),
        [
            out((half_rows, width), F32),
            out((half_rows, width), BF),
            out((row_count, 3 * inner), BF),
            out((8, width), F32),
        ],
        w_out,
        w_in_t,
        cosine,
        sine,
        bias,
        qkv,
        after_grad_own,
        after_grad_got,
        *blocks,
        vmem=24,
    )
    if small:
        keep, send = kernel(
            result_second_body,
            [out((half_rows, 2 * width), F32), out((half_rows, 2 * width), BF)],
            slot_pick_t,
            result_part,
            keep,
            send,
            *got_parts[2:],
        )
    else:
        result_part = shared_part + dot(slot_pick_t, got_parts[0])
        keep = jnp.concatenate([result_part[:half_rows], keep], 1)
        send = jnp.concatenate([result_part[half_rows:].astype(BF), send], 1)
    bottom_got = swap(send, "lo")
    last_columns = 4 * inner + 128
    last_tree = kernel(
        functools.partial(last_grads_body, experts_all),
        tree_outs(512, last_columns - 512),
        normed_attn,
        projected_grad,
        after_grad_own,
        after_grad_got,
        mixed,
        gain_ffn_part,
        gain_attn_part,
        router_part,
        scalars=(info,),
        vmem=24,
        deps=(send,),
    )
    last_tree = tree_first(last_tree)
    own, send = kernel(
        fold_own_body,
        [out((shard_rows, 2 * width), F32), out((shard_rows, 2 * width), BF)],
        keep,
        bottom_got,
    )
    grad_sgate, grad_sup, grad_sdown = kernel(
        shared_end_body,
        [Far(out((chunk, units), F32))] * 3,
        shared_keep,
        shared_got,
    )
    near, far = kernel(
        functools.partial(last_body, shard_block),
        [half_shard, half_shard],
        gain_attn,
        own,
        swap(send, "hi"),
        blocks[0],
        after_grad,
        after_attn,
    )
    last_tree, last_sent = tree_second(last_tree, (near,))
    grad_w_expert_down = weight_grad(expert_hidden, pair_grads, (last_sent,))
    got_last = exchange_halves(near, far, (last_sent,))
    last_keep, last_got, last_sent = tree_third(last_tree, got_last[:1])
    small_rows = experts_all + 8
    grad_qkv, grad_out, sums = kernel(
        functools.partial(last_end_body, small_rows),
        [
            Far(out((chunk, 3 * inner), F32)),
            Far(out((inner, chunk), F32)),
            out((small_rows, chunk), F32),
        ],
        last_keep,
        last_got,
    )
    got_last = join(got_last, (last_sent, Far(grad_sgate), Far(grad_w_expert_down)))
    grad_w_expert_up = weight_grad(rows_all, grad_eup, (got_last,))
    final, grad_tokens = kernel(
        return_body,
        [Far(out((row_count, width), BF)), Far(out((row_count, width), BF))],
        anchor,
        *blocks_of(got_last, (sums, Far(grad_w_expert_up))),
    )

    gain_ffn_sum, gain_attn_sum, router_sum = kernel(
        small_end_body,
        [Far(out((1, chunk), F32)), Far(out((1, chunk), F32)), Far(out((experts_all, chunk), F32))],
        sums,
        *[lax.ppermute(sums, TP, [(i, i ^ k) for i in range(4)]) for k in (1, 2, 3)],
        deps=(Far(final),),
    )
    return (
        final,
        grad_tokens,
        gain_attn_sum.reshape(chunk),
        grad_qkv,
        grad_out,
        gain_ffn_sum.reshape(chunk),
        router_sum.T,
        grad_sgate,
        grad_sup,
        grad_sdown.T,
        grad_w_expert_gate,
        grad_w_expert_up,
        grad_w_expert_down,
    )


def solution(mesh):
    devices_dp, devices_tp = mesh.shape["dp"], mesh.shape["tensor"]
    fine = Mesh(
        mesh.devices.reshape(devices_dp // 2, 2, devices_tp // 2, 2), ("dz", "dy", "hi", "lo")
    )
    every = DP + TP
    return jax.shard_map(
        on_device,
        mesh=fine,
        in_specs=(
            P(DP, None),
            P(DP, None),
            P(),
            P(None, TP),
            P(TP, None),
            P(),
            P(),
            P(None, TP),
            P(None, TP),
            P(TP, None),
            P(None, every),
            P(None, every),
            P(every, None),
            P(DP, None),
            P(DP),
            P(DP),
            P(DP, None),
            P(DP, None),
        ),
        out_specs=(
            P(DP, None),
            P(DP, None),
            P(DP),
            P(DP, TP),
            P(TP, DP),
            P(DP),
            P(DP, None),
            P(DP, TP),
            P(DP, TP),
            P(TP, DP),
            P(None, every),
            P(None, every),
            P(every, None),
        ),
        check_vma=False,
    )
```

```python
import functools

import jax
import jax.numpy as jnp
import numpy as np
from jax import lax
from jax.experimental import pallas as pl
from jax.experimental.pallas import tpu as pltpu
from jax.sharding import Mesh, PartitionSpec as P

HD = 64
MY_BLOCK, PICK, MY_PART, MY_EXPERT, MY_DP, Y_BIT, Z_BITS = range(7)
EPSILON = 1e-06
BF = jnp.bfloat16
F32 = jnp.float32
I32 = jnp.int32
DP = ("dz", "dy")
TP = ("hi", "lo")
MIB = 1 << 20
SENT_PIECES = 4
COST = pl.CostEstimate(flops=1000, bytes_accessed=1000, transcendentals=0)


def dot(left, right):
    return jnp.dot(left, right, preferred_element_type=F32)


def dot_t(left, right):
    return lax.dot_general(left, right, (((0,), (0,)), ((), ())), preferred_element_type=F32)


def dot_bt(left, right):
    return lax.dot_general(left, right, (((1,), (1,)), ((), ())), preferred_element_type=F32)


def swap(values, axis):
    return lax.ppermute(values, axis, [(0, 1), (1, 0)])


def exchange_stacked(values):
    order = jnp.arange(values.shape[0], dtype=I32) ^ lax.axis_index(DP)
    got = lax.all_to_all(
        jnp.take(values, order, axis=0), DP, split_axis=0, concat_axis=0, tiled=True
    )
    return jnp.take(got, order, axis=0)


def exchange(pieces):
    devices = lax.axis_size(DP)
    if len(pieces) == 1:
        (values,) = pieces
        stacked = values.reshape(devices, -1, values.shape[-1])
        return [exchange_stacked(stacked).reshape(values.shape)]
    return exchange_some(dict(enumerate(pieces)))


def exchange_some(pieces):
    devices = lax.axis_size(DP)
    got = dict(pieces)
    for k in (4, 5, 6, 7, 2, 3, 1):
        if k in got:
            got[k] = lax.ppermute(pieces[k], DP, [(i, i ^ k) for i in range(devices)])
    return [got[k] for k in sorted(got)]


def out(shape, dtype):
    return jax.ShapeDtypeStruct(shape, dtype)


class Far:
    def __init__(self, value):
        self.value = value


class Held(Far):
    pass


class Free(Far):
    pass


class Arriving:
    def __init__(self, buffer, copy):
        self.buffer, self.copy, self.waiting = buffer, copy, True
        self.shape, self.dtype = buffer.shape, buffer.dtype

    def ready(self):
        if self.waiting:
            self.copy.wait()
            self.waiting = False

    def __getitem__(self, index):
        self.ready()
        return self.buffer[index]


class Leaving:
    def __init__(self, buffer, copy):
        self.buffer, self.copy, self.started = buffer, copy, False
        self.shape, self.dtype = buffer.shape, buffer.dtype

    def flush(self):
        if not self.started:
            self.copy.start()
            self.started = True

    def __getitem__(self, index):
        return self.buffer[index]

    def __setitem__(self, index, value):
        self.buffer[index] = value


def in_hbm(values):
    return pltpu.with_memory_space_constraint(values, pltpu.HBM)


def in_vmem(values):
    if values.size * values.dtype.itemsize > 4 * MIB:
        return values
    return pltpu.with_memory_space_constraint(values, pltpu.VMEM)


def at_hbm(shape):
    return pltpu.HBM(shape.shape, shape.dtype)


def at_vmem(shape):
    if shape.size * shape.dtype.itemsize > 4 * MIB:
        return shape
    return pltpu.VMEM(shape.shape, shape.dtype)


def kernel(body, outs, *args, scalars=(), deps=(), vmem=16, semaphores=0):
    vmem_spec = pl.BlockSpec(memory_space=pltpu.VMEM)
    hbm_spec = pl.BlockSpec(memory_space=pltpu.HBM)
    any_spec = pl.BlockSpec(memory_space=pl.ANY)
    held = [isinstance(a, Held) for a in args]
    far_in = [isinstance(a, Far) and not h for a, h in zip(args, held)]
    free_out = [isinstance(o, Free) for o in outs]
    far_out = [isinstance(o, Far) and not f for o, f in zip(outs, free_out)]
    args = [in_hbm(a.value) if isinstance(a, Far) else in_vmem(a) for a in args]
    outs = [
        o.value if f else at_hbm(o.value) if h else at_vmem(o)
        for o, f, h in zip(outs, free_out, far_out)
    ]
    deps = [in_hbm(d.value) if isinstance(d, Far) else d for d in deps]
    moved = [x for x, f in zip(args + outs, far_in + far_out) if f]
    scratch = [pltpu.VMEM(x.shape, x.dtype) for x in moved]
    if moved:
        scratch.append(pltpu.SemaphoreType.DMA((len(moved),)))
    if semaphores:
        scratch.append(pltpu.SemaphoreType.DMA((semaphores,)))
    n_scalars, n_args, n_deps, n_outs = len(scalars), len(args), len(deps), len(outs)

    def wrapped(*refs):
        ins = list(refs[: n_scalars + n_args])
        results = list(refs[n_scalars + n_args + n_deps :][:n_outs])
        buffers = refs[n_scalars + n_args + n_deps + n_outs :]
        extra = buffers[-1:] if semaphores else ()
        buffers = buffers[:-1] if semaphores else buffers
        at = 0
        for i, far in enumerate(far_in):
            if far:
                ref = ins[n_scalars + i]
                copy = pltpu.make_async_copy(ref, buffers[at], buffers[-1].at[at])
                copy.start()
                ins[n_scalars + i] = Arriving(buffers[at], copy)
                at += 1
        for i, far in enumerate(far_out):
            if far:
                copy = pltpu.make_async_copy(buffers[at], results[i], buffers[-1].at[at])
                results[i] = Leaving(buffers[at], copy)
                at += 1
        body(*ins, *results, *extra)
        for ref in ins:
            if isinstance(ref, Arriving):
                ref.ready()
        for ref in results:
            if isinstance(ref, Leaving):
                ref.flush()
        for ref in results:
            if isinstance(ref, Leaving):
                ref.copy.wait()

    return pl.pallas_call(
        wrapped,
        out_shape=tuple(outs),
        in_specs=[pl.BlockSpec(memory_space=pltpu.SMEM)] * n_scalars
        + [hbm_spec if f or h else vmem_spec for f, h in zip(far_in, held)]
        + [any_spec] * n_deps,
        out_specs=tuple(hbm_spec if far else vmem_spec for far in far_out),
        scratch_shapes=scratch,
        compiler_params=pltpu.CompilerParams(vmem_limit_bytes=vmem * MIB),
        cost_estimate=COST,
        name=body.func.__name__ if isinstance(body, functools.partial) else body.__name__,
    )(*scalars, *args, *deps)


def tie(values, *deps):
    any_spec = pl.BlockSpec(memory_space=pl.ANY)
    vmem_spec = pl.BlockSpec(memory_space=pltpu.VMEM)
    return pl.pallas_call(
        lambda *refs: None,
        out_shape=out(values.shape, values.dtype),
        in_specs=[vmem_spec] + [any_spec] * len(deps),
        out_specs=vmem_spec,
        input_output_aliases={0: 0},
        cost_estimate=COST,
        name="tie",
    )(in_vmem(values), *[in_hbm(d.value) if isinstance(d, Far) else d for d in deps])


def rope_table(places):
    exponent = np.arange(HD // 2, dtype=np.float32) * np.float32(-2.0 / HD)
    angles = np.arange(places, dtype=np.float32)[:, None] * np.power(np.float32(10000.0), exponent)
    cosine = np.cos(angles.astype(np.float64)).astype(np.float32)
    sine = np.sin(angles.astype(np.float64)).astype(np.float32)
    rest = np.concatenate([cosine, cosine, -sine, sine], 1)
    terms = []
    for _ in range(3):
        terms.append(rest.astype(BF))
        rest = rest - terms[-1].astype(np.float32)
    return jnp.asarray(np.concatenate(terms, 1))


def iota(shape, dim):
    return lax.broadcasted_iota(I32, shape, dim)


def log2(number):
    return number.bit_length() - 1


def silu_parts(gate_in):
    sigmoid_val = 1.0 / (1.0 + jnp.exp(-gate_in))
    return (gate_in * sigmoid_val, sigmoid_val * (1.0 + gate_in * (1.0 - sigmoid_val)))


def inverse_root(values):
    return lax.rsqrt(jnp.mean(values * values, -1, keepdims=True) + EPSILON)


def rms_backward(values, root, gain, grad_normed):
    scaled = grad_normed * gain
    return root * scaled - values * (root * root * root) * jnp.mean(
        scaled * values, -1, keepdims=True
    )


def lane_rank(buckets, bucket_count):
    count = buckets.shape[1]
    rows = max(8, bucket_count)
    member = (iota((rows, count), 0) == buckets).astype(F32)
    earlier = (iota((count, count), 0) < iota((count, count), 1)).astype(F32).astype(BF)
    return jnp.sum(dot(member.astype(BF), earlier) * member, 0, keepdims=True).astype(I32)


def relative_row(block, rank, my_block, shard_block, shard_rows):
    shift = log2(shard_block)
    return (
        ((rank >> shift) ^ my_block) * shard_rows
        + block * shard_block
        + (rank & (shard_block - 1))
    )


def rope_back(grads, cosine, sine):
    return grads * cosine - half_turned(grads) * sine


def store_pieces(refs, value):
    rows = refs[0].shape[0]
    for i, ref in enumerate(refs):
        ref[...] = value[i * rows : (i + 1) * rows]


def joined(refs):
    return jnp.concatenate([ref[...] for ref in refs], 0) if len(refs) > 1 else refs[0][...]


def join_body(*refs):
    *parts, whole = refs
    rows = parts[0].shape[0]
    for i, ref in enumerate(parts):
        whole[i * rows : (i + 1) * rows, :] = ref[...]


def middle_body(block, near, far, *outs):
    for i, ref in enumerate(outs):
        ref[:block, :] = near[i * block : (i + 1) * block, :]
        ref[block:, :] = far[i * block : (i + 1) * block, :]


def store_halves(near, far, block, value, columns):
    for i in range(near.shape[0] // block):
        at = 2 * i * block
        near[i * block : (i + 1) * block, columns] = value[at : at + block]
        far[i * block : (i + 1) * block, columns] = value[at + block : at + 2 * block]


def fetch_body(*refs):
    *refs, semaphores = refs
    count = len(refs) // 2
    copies = [
        pltpu.make_async_copy(refs[i], refs[count + i], semaphores.at[i]) for i in range(count)
    ]
    for copy in copies:
        copy.start()
    for copy in copies:
        copy.wait()


def select_body(shard_block, blocks, info, inverse, tokens, cotangent, *refs):
    *sent, anchor = refs
    row_count, width = tokens.shape
    shard_rows = shard_block * blocks
    target = (inverse[...] >> log2(row_count)) ^ info[MY_DP]
    row = relative_row(target, lane_rank(target, blocks), info[MY_BLOCK], shard_block, shard_rows)
    anchor[...] = row
    pick = (iota((shard_rows, row_count), 0) == row).astype(F32).astype(BF)
    rows = jnp.concatenate([dot(pick, tokens[...]), dot(pick, cotangent[...])], 1)
    store_pieces(sent, rows.astype(BF))


def index_body(
    shard_block,
    copies,
    per_dp,
    part_rows,
    experts_all,
    info,
    lengths,
    order,
    routes,
    fill,
    table,
    slot_pick,
    slot_pick_t,
    bias,
    cosine,
    sine,
    meta,
):
    row_count = order.shape[1]
    devices_dp = slot_pick.shape[0] // part_rows
    shard_rows = shard_block * devices_dp
    source = (order[...] >> log2(row_count)) ^ info[MY_DP]
    local = relative_row(
        source, lane_rank(source, devices_dp), info[MY_BLOCK], shard_block, shard_rows
    )
    place_pick = (iota((row_count, row_count), 0) == local).astype(F32).astype(BF)
    lanes = iota((1, row_count), 1)
    segment = jnp.zeros((1, row_count), I32)
    start = jnp.zeros((1, row_count), I32)
    end = jnp.int32(0)
    for entry in range(lengths.shape[1]):
        end = end + lengths[0, entry]
        passed = lanes >= end
        segment = segment + passed.astype(I32)
        start = jnp.maximum(start, jnp.where(passed, end, 0))
    place = lanes - start
    expert_sum = routes[0:1, :] + routes[1:2, :] + 1
    facts = jnp.concatenate(
        [segment, place >> 1, place & 1, expert_sum, jnp.zeros((4, row_count), I32)], 0
    )
    facts = facts.astype(F32).astype(BF)
    across = dot_bt(facts, place_pick)
    down = dot_bt(place_pick, facts)
    place_row = 2.0 * across[1:2] + across[2:3]
    place_col = 2.0 * down[:, 1:2] + down[:, 2:3]
    allowed = (down[:, 0:1] == across[0:1]) & (place_row <= place_col)
    bias[...] = jnp.where(allowed, 0.0, -1e30).astype(BF)
    at_place = (
        iota((row_count, row_count), 1).astype(F32) == place_col
    ).astype(F32).astype(BF)
    turned = dot(at_place, table[...])
    pieces = [turned[:, i * 128 : (i + 1) * 128] for i in range(3)]
    turned = pieces[0] + pieces[1] + pieces[2]
    cosine[...] = turned[:, :HD]
    sine[...] = turned[:, HD:]
    meta[...] = jnp.broadcast_to(down[:, 3:4], meta.shape).astype(BF)
    pairs = 2 * row_count
    fill_at = (fill[...] & 1) * row_count + (fill[...] >> 1)
    fill_pick = (iota((pairs, pairs), 0) == fill_at).astype(F32).astype(BF)
    expert_rows = max(16, experts_all)
    pair_expert = jnp.concatenate([routes[0:1, :], routes[1:2, :]], 1)
    named = (iota((expert_rows, pairs), 0) == pair_expert).astype(F32).astype(BF)
    member = dot(named, fill_pick)
    earlier = (iota((pairs, pairs), 0) < iota((pairs, pairs), 1)).astype(F32).astype(BF)
    ranks = (member * (dot(member.astype(BF), earlier) + 1.0)).astype(BF)
    ranks = dot_bt(ranks, fill_pick)
    ranks = (ranks[:, :row_count] + ranks[:, row_count:]).astype(BF)
    ranks = dot_bt(ranks, place_pick).astype(I32)
    slots = iota((part_rows, row_count), 0) + (info[MY_PART] * part_rows + 1)
    experts = iota((expert_rows, row_count), 0)
    for target in range(devices_dp):
        expert = ((target ^ info[MY_DP]) >> log2(copies)) * per_dp + info[PICK]
        chosen = jnp.sum(jnp.where(experts == expert, ranks, 0), 0, keepdims=True)
        picked = (slots == chosen).astype(F32)
        slot_pick[target * part_rows : (target + 1) * part_rows, :] = picked.astype(BF)
    slot_pick_t[...] = slot_pick[...].astype(F32).T.astype(BF)


def head_parts(projected, heads):
    return [
        [projected[:, (3 * h + i) * HD : (3 * h + i + 1) * HD] for i in range(3)]
        for h in range(heads)
    ]


def half_turned(values):
    half = values.shape[1] // 2
    return jnp.concatenate([values[:, half:], values[:, :half]], 1)


def attend_body(
    heads,
    gain,
    w_in_t,
    w_out,
    cosine,
    sine,
    bias,
    b0,
    b1,
    b2,
    b3,
    keep,
    send,
    qkv,
    mixed,
    normed,
    weights_all,
):
    width = b0.shape[1] // 2
    half = keep.shape[0]
    tokens = jnp.concatenate([b[:, :width] for b in (b0, b1, b2, b3)], 0).astype(F32)
    normed[...] = (tokens * inverse_root(tokens) * gain[...]).astype(BF)
    projected = dot_bt(normed[...], w_in_t[...])
    cosine, sine = cosine[...], sine[...]
    parts = []
    for query, keys, values in head_parts(projected, heads):
        parts.append((query * cosine + half_turned(query) * sine).astype(BF))
        parts.append((keys * cosine + half_turned(keys) * sine).astype(BF))
        parts.append(values.astype(BF))
    qkv[...] = jnp.concatenate(parts, 1)
    scale = HD**-0.5
    mixed_heads = []
    for head, (query, keys, values) in enumerate(head_parts(qkv, heads)):
        scores = dot_bt(query, keys) * scale + bias[...].astype(F32)
        powers = jnp.exp(scores - jnp.max(scores, -1, keepdims=True))
        weights = powers * (1.0 / jnp.sum(powers, -1, keepdims=True))
        weights_all[head] = weights
        mixed_heads.append(dot(weights.astype(BF), values))
    mixed[...] = jnp.concatenate(mixed_heads, 1).astype(BF)
    part = dot(mixed[...], w_out[...])
    keep[...] = part[:half]
    send[...] = part[half:].astype(BF)


def fold_body(keep, got, half):
    half[...] = (keep[...] + got[...].astype(F32)).astype(BF)


def fold_own_body(keep, got, own, send):
    rows = own.shape[0]
    own[...] = keep[:rows, :] + got[:rows, :].astype(F32)
    send[...] = (keep[rows:, :] + got[rows:, :].astype(F32)).astype(BF)


def both(half, got):
    rows = half.shape[0] // 2
    mine, other = half[...].astype(F32), got[...].astype(F32)
    return mine + jnp.concatenate([other[rows:], other[:rows]], 0)


def norm_body(gain, half, got, b0, b1, after_attn, normed):
    width = half.shape[1]
    balanced = jnp.concatenate([b0[:, :width], b1[:, :width]], 0).astype(F32)
    values = balanced + both(half, got)
    after_attn[...] = values
    normed[...] = (values * inverse_root(values) * gain[...]).astype(BF)


def send_body(slot_pick, own, got, meta, b0, b1, b2, b3, *sent):
    width = own.shape[1]
    rows = jnp.concatenate([own[...], got[...]], 0)
    rows = dot(slot_pick[...], rows).astype(BF)
    count = sent[0].shape[0]
    near = sum(ref.shape[1] > width for ref in sent) * count
    grads = jnp.concatenate([b[:, width:] for b in (b0, b1, b2, b3)], 0)
    grads = jnp.concatenate([grads, meta[...]], 1)
    grads = dot(slot_pick[:near, :], grads).astype(BF)
    for i, ref in enumerate(sent):
        at = slice(i * count, (i + 1) * count)
        ref[:, :width] = rows[at]
        if ref.shape[1] > width:
            ref[:, width:] = grads[at]


def send_grads_body(first, slot_pick, meta, b0, b1, b2, b3, *sent):
    width = b0.shape[1] // 2
    grads = jnp.concatenate([b[:, width:] for b in (b0, b1, b2, b3)], 0)
    grads = jnp.concatenate([grads, meta[...]], 1)
    store_pieces(sent, dot(slot_pick[first:, :], grads).astype(BF))


def join_packed_body(near, *refs):
    *parts, whole = refs
    count, width = parts[near].shape
    far = (len(parts) - near) // 2
    for i in range(near):
        whole[i * count : (i + 1) * count, :] = parts[i][...]
    for i in range(far):
        at = slice((near + i) * count, (near + i + 1) * count)
        whole[at, :width] = parts[near + i][...]
        whole[at, width:] = parts[near + far + i][...]


def shared_body(
    own, got, b0, b1, b2, b3, w_gate, w_up, w_down, part, back, grad_gate, grad_up, hidden
):
    width = own.shape[1]
    rows = jnp.concatenate([own[...], got[...]], 0)
    grads = jnp.concatenate([b[:, width:] for b in (b0, b1, b2, b3)], 0)
    gate = dot(rows, w_gate[...])
    up = dot(rows, w_up[...])
    act, slope = silu_parts(gate)
    hidden[...] = (act * up).astype(BF)
    part[...] = dot(hidden[...], w_down[...])
    hidden_grad = dot_bt(grads, w_down[...])
    grad_gate[...] = (hidden_grad * up * slope).astype(BF)
    grad_up[...] = (hidden_grad * act).astype(BF)
    back[...] = dot_bt(grad_gate[...], w_gate[...]) + dot_bt(grad_up[...], w_up[...])


def store_tree(info, sums, keeps, sends):
    chunk, columns = keeps[0].shape[1:]
    sides = ((sums[:, :columns], Y_BIT, 1), (sums[:, columns:], Z_BITS, 2))
    for (values, which, stride), keep, send in zip(sides, keeps, sends):
        mine = info[which] == 0
        for i in range(keep.shape[0]):
            at = (2 * i if stride == 1 else i // 2 * 4 + i % 2) * chunk
            first, second = values[at : at + chunk], values[at + stride * chunk :][:chunk]
            keep[i] = jnp.where(mine, first, second)
            send[i] = jnp.where(mine, second, first).astype(BF)


def shared_grads_body(
    info, own, got, b0, b1, b2, b3, grad_gate, grad_up, hidden, *refs
):
    width = own.shape[1]
    rows = jnp.concatenate([own[...], got[...]], 0)
    grads = jnp.concatenate([b[:, width:] for b in (b0, b1, b2, b3)], 0)
    sums = jnp.concatenate(
        [dot_t(rows, grad_gate[...]), dot_t(rows, grad_up[...]), dot_t(grads, hidden[...])], 1
    )
    store_tree(info, sums, refs[:2], refs[2:])


def halved(info, which, total, keep, send):
    mine = info[which] == 0
    for index in range(keep.shape[0]):
        first, second = total[2 * index], total[2 * index + 1]
        keep[index] = jnp.where(mine, first, second)
        send[index] = jnp.where(mine, second, first).astype(BF)


def tree_second_body(info, kept_a, got_a, kept_b, got_b, keep_a, keep_b, send_a, send_b):
    halved(info, Z_BITS, kept_a[...] + got_a[...].astype(F32), keep_a, send_a)
    halved(info, Y_BIT, kept_b[...] + got_b[...].astype(F32), keep_b, send_b)


def tree_third_body(info, kept_a, got_a, kept_b, got_b, keep, send):
    total = jnp.concatenate(
        [kept_a[...] + got_a[...].astype(F32), kept_b[...] + got_b[...].astype(F32)], 2
    )
    halved(info, Z_BITS + 1, total, keep, send)


def last_grads_body(
    experts, info, normed, projected_grad, own, got, mixed, gain_ffn, gain_attn, router, *refs
):
    width = normed.shape[1]
    small = jnp.concatenate(
        [
            router[:experts, :],
            gain_ffn[:1, :],
            gain_attn[:1, :],
            jnp.zeros((128 - experts - 2, width), F32),
        ],
        0,
    )
    grads = jnp.concatenate([own[...], got[...]], 0)
    sums = jnp.concatenate(
        [dot_t(normed[...], projected_grad[...]), dot_t(grads, mixed[...]), small.T], 1
    )
    store_tree(info, sums, refs[:2], refs[2:])


def tree_body(which, info, kept, got, keep, send):
    halved(info, which, kept[...] + got[...].astype(F32), keep, send)


def last_end_body(small_rows, kept, got, grad_qkv, grad_out, small):
    total = kept[0] + got[0].astype(F32)
    columns, inner = grad_qkv.shape[1], grad_out.shape[0]
    grad_qkv[...] = total[:, :columns]
    grad_out[...] = total[:, columns : columns + inner].T
    small[...] = total[:, columns + inner :].T[:small_rows]


def small_end_body(own, by_lo, by_hi, by_both, gain_ffn, gain_attn, router):
    experts = router.shape[0]
    total = (own[...] + by_lo[...]) + (by_hi[...] + by_both[...])
    router[...] = total[:experts]
    gain_ffn[...] = total[experts : experts + 1]
    gain_attn[...] = total[experts + 1 : experts + 2]


def shared_end_body(kept, got, grad_gate, grad_up, grad_down):
    total = kept[0] + got[0].astype(F32)
    units = grad_gate.shape[1]
    grad_gate[...] = total[:, :units]
    grad_up[...] = total[:, units : 2 * units]
    grad_down[...] = total[:, 2 * units :]


def add_far_body(keep, *refs):
    got, total = refs[: SENT_PIECES // 2], refs[SENT_PIECES // 2 :]
    half = keep.shape[0] // 2
    store_pieces(total, (keep[half:, :].astype(F32) + joined(got).astype(F32)).astype(BF))


def gated_parts(keep, got, gates):
    gate = jnp.concatenate([gates] * (keep.shape[1] // 128), 1)
    return (gate * (keep.astype(F32) + got.astype(F32))).astype(BF)


def add_near_body(keep, part_keep, gates, *refs):
    got, part_got, total = (
        refs[: SENT_PIECES // 2],
        refs[SENT_PIECES // 2 : SENT_PIECES],
        refs[SENT_PIECES:],
    )
    half, width = keep.shape[0] // 2, keep.shape[1]
    rows = (keep[:half, :].astype(F32) + joined(got).astype(F32)).astype(BF)
    parts = gated_parts(part_keep[:half, :], joined(part_got), gates[:half, :])
    count = total[0].shape[0]
    for i, ref in enumerate(total):
        at = slice(i * count, (i + 1) * count)
        ref[:count, :width] = rows[at]
        ref[:count, width:] = parts[at]


def part_far_body(keep, gates, *refs):
    got, total = refs[: SENT_PIECES // 2], refs[SENT_PIECES // 2 :]
    half = keep.shape[0] // 2
    store_pieces(total, gated_parts(keep[half:, :], joined(got), gates[half:, :]))


def weight_grad_body(left, right, total, sums, semaphores):
    tile = 256
    copies = []
    for i in range(left.shape[1] // tile):
        at = slice(i * tile, (i + 1) * tile)
        sums[at, :] = dot_t(left[:, at], right[...])
        copies.append(
            pltpu.make_async_copy(sums.at[at, :], total.at[at, :], semaphores.at[i])
        )
        copies[-1].start()
    for copy in copies:
        copy.wait()


def meta_body(devices_dp, part_rows, sub, capacity, width, info, own, got, marks):
    my_part, my_expert = info[MY_PART], info[MY_EXPERT]
    lanes = iota((part_rows, 128), 1)
    blocks = [(ref, at, part) for part, (ref, at) in enumerate(
        [(own, i) for i in range(sub // 2)] + [(got, i) for i in range(sub // 2)]
    )]
    counts = []
    for block in range(devices_dp):
        count = jnp.zeros((1, 128), F32)
        for ref, at, _ in blocks:
            start = (at * devices_dp + block) * part_rows
            value = ref[start : start + part_rows, width:].astype(F32)
            count = count + jnp.sum((value > 0.0).astype(F32), 0, keepdims=True)
        counts.append(count)
    for block in range(devices_dp):
        earlier = jnp.zeros((1, 128), F32)
        for before in range(devices_dp):
            ahead = (before ^ info[MY_DP]) < (block ^ info[MY_DP])
            earlier = earlier + jnp.where(ahead, counts[before], 0.0)
        for ref, at, part in blocks:
            start = (at * devices_dp + block) * part_rows
            value = ref[start : start + part_rows, width:].astype(F32)
            valid = value > 0.0
            slot = iota((part_rows, 128), 0) + (my_part ^ part) * part_rows
            kept = valid & (slot.astype(F32) + earlier < capacity)
            other = value.astype(I32) - 1 - my_expert
            mark = (lanes == my_expert).astype(F32) - (lanes == other).astype(F32)
            row = (part * devices_dp + block) * part_rows
            marks[row : row + part_rows, :] = jnp.where(
                lanes == 127, kept.astype(F32), jnp.where(valid, mark, 0.0)
            )


def expert_step(packed, mark, w_router, w_gate, w_up, w_down, stores):
    hidden_out, grad_gate_out, grad_up_out, pair_out = stores
    width = w_gate.shape[0]
    rows, grads = packed[:, :width], packed[:, width : 2 * width].astype(F32)
    kept = mark[:, 127:128] > 0.5
    mark = mark[:, : w_router.shape[0]]
    gap = jnp.sum(dot_bt(rows, w_router[...]) * mark, 1, keepdims=True)
    gate = 1.0 / (1.0 + jnp.exp(-gap))
    gate_other = 1.0 / (1.0 + jnp.exp(gap))
    gate_in = dot(rows, w_gate[...])
    up = dot(rows, w_up[...])
    act, slope = silu_parts(gate_in)
    hidden = (act * up).astype(BF)
    hidden_out(hidden)
    part = jnp.where(kept, dot(hidden, w_down[...]), 0.0).astype(BF)
    pair = jnp.where(kept, gate * grads, 0.0).astype(BF)
    pair_out(pair)
    gate_grad = jnp.sum(part.astype(F32) * grads, 1, keepdims=True)
    logit_grad = (gate * gate_other * gate_grad * mark).astype(BF)
    hidden_grad = dot_bt(pair, w_down[...])
    grad_gate = (hidden_grad * up * slope).astype(BF)
    grad_up = (hidden_grad * act).astype(BF)
    grad_gate_out(grad_gate)
    grad_up_out(grad_up)
    back = (dot_bt(grad_gate, w_gate[...]) + dot_bt(grad_up, w_up[...])).astype(BF).astype(F32)
    back = (back + dot(logit_grad, w_router[...])).astype(BF)
    return back, part, gate, dot_t(logit_grad, rows)


def store_at(ref, where=...):
    def store(value):
        ref[where] = value

    return store


def expert_body(
    tiles,
    packed_own,
    packed_got,
    marks,
    w_router,
    w_gate,
    w_up,
    w_down,
    keep,
    send,
    rows_all,
    hidden,
    grad_gate,
    grad_up,
    pair,
    gates,
    router,
):
    step = pl.program_id(0)
    mine = step < tiles
    width = rows_all.shape[1]
    packed = jnp.where(mine, packed_own[...], packed_got[...])
    rows_all[...] = packed[:, :width]
    back, part, gate, router_term = expert_step(
        packed,
        marks[...],
        w_router,
        w_gate,
        w_up,
        w_down,
        [store_at(ref) for ref in (hidden, grad_gate, grad_up, pair)],
    )

    @pl.when(step == 0)
    def _():
        router[...] = jnp.zeros_like(router)

    router[...] += router_term

    @pl.when(mine)
    def _():
        keep[:, :width] = back
        keep[:, width:] = part
        gates[...] = jnp.broadcast_to(gate, gates.shape)

    @pl.when(jnp.logical_not(mine))
    def _():
        send[:, :width] = back
        send[:, width:] = part


def expert_whole_body(
    tile,
    packed_own,
    packed_got,
    marks,
    w_router,
    w_gate,
    w_up,
    w_down,
    back_keep,
    part_keep,
    *refs,
):
    back_send, part_send = refs[:SENT_PIECES], refs[SENT_PIECES : 2 * SENT_PIECES]
    rows_all, hidden, grad_gate, grad_up, pair, gates, router = refs[2 * SENT_PIECES :]
    half = packed_own.shape[0]
    width = rows_all.shape[1]
    router[...] = jnp.zeros_like(router)

    def run(base, packed_ref, put):
        def step(index, _):
            at = pl.ds(pl.multiple_of(index * tile, tile), tile)
            place = pl.ds(pl.multiple_of(base + index * tile, tile), tile)
            packed = packed_ref[at, : 2 * width]
            rows_all[place, :] = packed[:, :width]
            back, part, gate, router_term = expert_step(
                packed,
                marks[place, :],
                w_router,
                w_gate,
                w_up,
                w_down,
                [store_at(ref, (place, slice(None))) for ref in (hidden, grad_gate, grad_up, pair)],
            )
            router[...] += router_term
            put(index, at, back, part)
            if base == 0:
                gates[at, :] = jnp.broadcast_to(gate, (tile, 128))
            return 0

        lax.fori_loop(0, half // tile, step, 0)

    def put_own(index, at, back, part):
        back_keep[at, :] = back
        part_keep[at, :] = part

    def put_got(index, at, back, part):
        rows = half // SENT_PIECES
        each = tile // rows
        for i in range(SENT_PIECES):

            @pl.when(index == i // each)
            def _(i=i):
                inside = slice(i % each * rows, (i % each + 1) * rows)
                back_send[i][...] = back[inside]
                part_send[i][...] = part[inside]

    run(0, packed_own, put_own)
    run(half, packed_got, put_got)


def combine_body(slot_pick_t, addend, *refs):
    *back, keep, send = refs
    half, width = keep.shape
    count = back[-1].shape[0]
    rows = jnp.concatenate([ref[:count, :width] for ref in back], 0)
    total = addend[...] + dot(slot_pick_t[...], rows)
    keep[...] = total[:half]
    send[...] = total[half:].astype(BF)


def result_body(count, slot_pick_t, addend, attn_keep, attn_send, *refs):
    *near, a, b, c, d, keep, send = refs
    half, width = attn_keep.shape
    rows = [ref[:count, width:] for ref in near] + [ref[...] for ref in (a, b, c, d)]
    total = addend[...] + dot(slot_pick_t[...], jnp.concatenate(rows, 0))
    keep[:, :width] = total[:half]
    send[:, :width] = total[half:].astype(BF)
    keep[:, width:] = attn_keep[...]
    send[:, width:] = attn_send[...]


def norm_back_body(
    gain, half, got, after_attn, b0, b1, after_grad, low, gain_grad
):
    width = half.shape[1]
    normed_grad = both(half, got)
    values = after_attn[...]
    root = inverse_root(values)
    grads = jnp.concatenate([b0[:, width:], b1[:, width:]], 0).astype(F32)
    total = grads + rms_backward(values, root, gain[...], normed_grad)
    after_grad[...] = total
    low[...] = total.astype(BF)
    gain_grad[...] = jnp.broadcast_to(
        0.5 * jnp.sum(normed_grad * values * root, 0, keepdims=True), gain_grad.shape
    )


def attend_back_body(
    heads,
    w_out,
    w_in_t,
    cosine,
    sine,
    weights_all,
    qkv,
    own,
    got,
    b0,
    b1,
    b2,
    b3,
    keep,
    send,
    projected_grad,
    gain_grad,
):
    width = own.shape[1]
    half = keep.shape[0]
    grads = jnp.concatenate([own[...], got[...]], 0)
    mixed_grad = dot_bt(grads, w_out[...]).astype(BF)
    scale = HD**-0.5
    cosine, sine = cosine[...], sine[...]
    parts = []
    for head, (query, keys, values) in enumerate(head_parts(qkv, heads)):
        at = head * HD
        weights = weights_all[head]
        mine = mixed_grad[:, at : at + HD]
        weight_grad = dot_bt(mine, values)
        delta = jnp.sum(weights * weight_grad, -1, keepdims=True)
        score_grad = (weights * (weight_grad - delta)).astype(BF)
        parts.append(rope_back(dot(score_grad, keys) * scale, cosine, sine))
        parts.append(rope_back(dot_t(score_grad, query) * scale, cosine, sine))
        parts.append(dot_t(weights.astype(BF), mine))
    projected_grad[...] = jnp.concatenate(parts, 1).astype(BF)
    part = dot(projected_grad[...], w_in_t[...])
    tokens = jnp.concatenate([b[:, :width] for b in (b0, b1, b2, b3)], 0).astype(F32)
    gain_grad[...] = jnp.broadcast_to(
        jnp.sum(part * tokens * inverse_root(tokens), 0, keepdims=True), gain_grad.shape
    )
    keep[...] = part[:half]
    send[...] = part[half:].astype(BF)


def last_body(
    block, gain, own, got, b0, after_grad, after_attn, near, far
):
    rows, width = own.shape[0], own.shape[1] // 2
    tokens = b0[:, :width].astype(F32)
    sums = own[...] + got[...].astype(F32)
    normed_grad = sums[:, width:]
    total = after_grad[:rows, :] + rms_backward(
        tokens, inverse_root(tokens), gain[...], normed_grad
    )
    result = after_attn[:rows, :] + sums[:, :width]
    store_halves(near, far, block, result.astype(BF), slice(0, width))
    store_halves(near, far, block, total.astype(BF), slice(width, None))


def return_body(anchor, b0, b1, b2, b3, final, grads):
    row_count, width = final.shape
    pick = (iota((row_count, row_count), 0) == anchor[...]).astype(F32).T.astype(BF)
    rows = jnp.concatenate([b[...] for b in (b0, b1, b2, b3)], 0)
    total = dot(pick, rows).astype(BF)
    final[...] = total[:, :width]
    grads[...] = total[:, width:]


def on_device(
    tokens,
    cotangent,
    gain_attn,
    w_qkv,
    w_out,
    gain_ffn,
    w_router,
    w_shared_gate,
    w_shared_up,
    w_shared_down,
    routed_gate_weight,
    routed_up_weight,
    w_expert_down,
    seq_lengths,
    token_order,
    inverse_order,
    routes,
    fill_order,
):
    devices_dp = lax.axis_size(DP)
    devices_tp = lax.axis_size(TP)
    dz = lax.axis_size("dz")
    row_count, width = tokens.shape
    block_rows = row_count // devices_dp
    shard_block = block_rows // devices_tp
    shard_rows = row_count // devices_tp
    half_rows = row_count // 2
    experts_all = w_router.shape[1]
    slot_rows = 4 * row_count // experts_all
    capacity = 5 * row_count * devices_dp // (2 * experts_all)
    inner = w_out.shape[0]
    heads = inner // HD
    per_dp = max(1, experts_all // devices_dp)
    copies = max(1, devices_dp // experts_all)
    sub = devices_tp // per_dp
    my_hi, my_lo = lax.axis_index("hi"), lax.axis_index("lo")
    my_z, my_y = lax.axis_index("dz"), lax.axis_index("dy")
    my_dp = my_z * 2 + my_y
    my_block = my_lo * 2 + my_hi
    pick = my_hi if per_dp == 2 else 0 * my_hi
    my_part = my_lo if per_dp == 2 else my_block
    part_rows = slot_rows // sub
    own_slots = devices_dp * part_rows
    all_slots = own_slots * sub
    my_expert = my_dp // copies * per_dp + pick
    chunk = width // devices_dp
    z_bits = [(my_z >> i) & 1 for i in range(log2(dz))]
    info = jnp.stack([my_block, pick, my_part, my_expert, my_dp, my_y] + z_bits).astype(I32)
    pieces = devices_dp if devices_dp <= 8 else 1

    small = all_slots <= 1024

    def fetch(weights, deps=()):
        return kernel(
            fetch_body,
            [out(w.shape, w.dtype) for w in weights],
            *[Held(w) for w in weights],
            semaphores=len(weights),
            deps=deps,
        )

    table = rope_table(row_count)
    gain_attn = gain_attn[None]
    gain_ffn = gain_ffn[None]

    half_shard = out((shard_rows // 2, 2 * width), BF)
    shard_pieces = [out((shard_rows // pieces, 2 * width), BF)] * pieces
    *sent, anchor = kernel(
        functools.partial(select_body, shard_block, devices_dp),
        shard_pieces + [out((1, row_count), I32)],
        Far(inverse_order[None]),
        Far(tokens),
        Far(cotangent),
        scalars=(info,),
    )

    def blocks_of(own, deps):
        (by_hi,) = kernel(join_body, [out(own.shape, BF)], swap(own, "hi"), deps=deps)
        by_lo = swap(own, "lo")
        return (own, by_hi, by_lo, swap(by_hi, "lo"))

    def z_steps(parts):
        got = list(parts)
        for k in (2, 3, 1):
            got[k] = lax.ppermute(parts[k], "dz", [(i, i ^ k) for i in range(dz)])
        return got

    def exchange_halves(near, far, deps=()):
        width_sent = near.shape[1]
        block = near.shape[0] // dz
        if devices_dp != 8:
            both_halves = jnp.stack([near, far]).reshape(2, dz, block, width_sent)
            stacked = both_halves.transpose(1, 0, 2, 3).reshape(devices_dp, block, width_sent)
            return [exchange_stacked(stacked).reshape(devices_dp * block, width_sent)]
        middle = kernel(
            functools.partial(middle_body, block),
            [out((2 * block, width_sent), BF)] * dz,
            near,
            swap(far, "dy"),
            deps=deps,
        )
        return z_steps(middle)

    def join(parts, deps=()):
        if not isinstance(parts, (list, tuple)):
            parts = [parts]
        if not small:
            return jnp.concatenate(parts, 0)
        rows = sum(part.shape[0] for part in parts)
        return kernel(join_body, [out((rows, parts[0].shape[1]), BF)], *parts, deps=deps)[0]

    slot_pick, slot_pick_t, bias, cosine, sine, meta = kernel(
        functools.partial(index_body, shard_block, copies, per_dp, part_rows, experts_all),
        [
            out((own_slots, row_count), BF),
            out((row_count, own_slots), BF),
            out((row_count, row_count), BF),
            out((row_count, HD), F32),
            out((row_count, HD), F32),
            out((row_count, 128), BF),
        ],
        Far(token_order[None]),
        Far(routes.T),
        Far(fill_order),
        Far(table),
        scalars=(info, seq_lengths),
        vmem=24,
    )
    router = w_router.T
    w_in_t, w_out = fetch([w_qkv.T, w_out], (slot_pick,))
    blocks = blocks_of(join(exchange(sent)), (slot_pick, w_in_t))

    slot_piece = own_slots // pieces
    near_pieces = pieces // 2 if small else pieces
    packed_width = 2 * width + 128
    got_grads = []
    if small:
        sent_grads = kernel(
            functools.partial(send_grads_body, near_pieces * slot_piece),
            [out((slot_piece, width + 128), BF)] * (pieces - near_pieces),
            slot_pick,
            meta,
            *blocks,
        )
        got_grads = exchange_some(dict(enumerate(sent_grads, near_pieces)))

    keep, send, qkv, mixed, normed_attn, weights = kernel(
        functools.partial(attend_body, heads),
        [
            out((half_rows, width), F32),
            out((half_rows, width), BF),
            out((row_count, 3 * inner), BF),
            out((row_count, inner), BF),
            out((row_count, width), BF),
            out((heads, row_count, row_count), F32),
        ],
        gain_attn,
        w_in_t,
        w_out,
        cosine,
        sine,
        bias,
        *blocks,
        vmem=24,
    )

    def half_sum(keep, send):
        (half,) = kernel(fold_body, [out((half_rows, width), BF)], keep, swap(send, "lo"))
        return half, swap(half, "hi")

    half, half_got = half_sum(keep, send)
    fetched = [w_shared_gate, w_shared_up, w_shared_down, router]
    if small:
        fetched += [routed_gate_weight, routed_up_weight, w_expert_down]
    fetched = fetch(fetched, (half,))
    w_shared_gate, w_shared_up, w_shared_down, router = fetched[:4]
    if small:
        routed_gate_weight, routed_up_weight, w_expert_down = fetched[4:]
    after_attn, normed_own = kernel(
        norm_body,
        [out((half_rows, width), F32), out((half_rows, width), BF)],
        gain_ffn,
        half,
        half_got,
        blocks[0],
        blocks[1],
        deps=got_grads[:2] + [router],
    )
    normed_got = swap(normed_own, "lo")

    far_piece = out((slot_piece, width), BF)
    sent_rows = kernel(
        send_body,
        [out((slot_piece, packed_width), BF)] * near_pieces + [far_piece] * (pieces - near_pieces),
        slot_pick,
        normed_own,
        normed_got,
        meta,
        *blocks,
    )
    got_rows = exchange(sent_rows)

    def sub_gather(parts, deps=()):
        values = join(parts, deps)
        if sub == 4:
            values = jnp.concatenate([values, swap(values, "hi")], 0)
        return values, swap(values, "lo")

    units = w_shared_gate.shape[1]
    shared_part, shared_back, grad_sgate, grad_sup, shared_hidden = kernel(
        shared_body,
        [
            out((row_count, width), F32),
            out((row_count, width), F32),
            out((row_count, units), BF),
            out((row_count, units), BF),
            out((row_count, units), BF),
        ],
        normed_own,
        normed_got,
        *blocks,
        w_shared_gate,
        w_shared_up,
        w_shared_down,
        deps=sent_rows[:1],
        vmem=24,
    )
    def tree_outs(columns_a, columns_b):
        return [
            out((dz, chunk, columns), dtype)
            for dtype in (F32, BF)
            for columns in (columns_a, columns_b)
        ]

    shared_tree = kernel(
        shared_grads_body,
        tree_outs(3 * units // 2, 3 * units // 2),
        normed_own,
        normed_got,
        *blocks,
        grad_sgate,
        grad_sup,
        shared_hidden,
        scalars=(info,),
        vmem=24,
    )

    def z_swap(values, bit):
        return lax.ppermute(values, "dz", [(i, i ^ (1 << bit)) for i in range(dz)])

    def tree_first(parts):
        keep_a, keep_b, send_a, send_b = parts
        return keep_a, swap(send_a, "dy"), keep_b, z_swap(send_b, 0)

    def tree_second(parts, deps=()):
        kept_a, got_a, kept_b, got_b = parts
        shapes = [
            out((dz // 2, chunk, kept.shape[2]), dtype)
            for dtype in (F32, BF)
            for kept in (kept_a, kept_b)
        ]
        keep_a, keep_b, send_a, send_b = kernel(
            tree_second_body, shapes, kept_a, got_a, kept_b, got_b, scalars=(info,), deps=deps
        )
        return (keep_a, z_swap(send_a, 0), keep_b, swap(send_b, "dy")), send_b

    def tree_third(parts, deps=()):
        columns = parts[0].shape[2] + parts[2].shape[2]
        shape = (dz // 4, chunk, columns)
        keep, send = kernel(
            tree_third_body,
            [out(shape, F32), out(shape, BF)],
            *parts,
            scalars=(info,),
            deps=deps,
        )
        sent, got = send, z_swap(send, 1)
        for bit in range(2, log2(dz)):
            shape = (keep.shape[0] // 2, chunk, columns)
            keep, send = kernel(
                functools.partial(tree_body, Z_BITS + bit),
                [out(shape, F32), out(shape, BF)],
                keep,
                got,
                scalars=(info,),
            )
            got = z_swap(send, bit)
        return keep, got, sent

    shared_tree = tree_first(shared_tree)
    if small:
        (packed_own,) = kernel(
            functools.partial(join_packed_body, near_pieces),
            [out((own_slots, packed_width), BF)],
            *got_rows,
            *got_grads,
            deps=(shared_tree[0],),
        )
        packed_got = swap(packed_own, "lo")
    else:
        packed_own, packed_got = sub_gather(got_rows)
    (marks,) = kernel(
        functools.partial(
            meta_body, devices_dp, part_rows, sub, capacity, 2 * width if small else 0
        ),
        [out((all_slots, 128), F32)],
        packed_own if small else packed_own[:, 2 * width :],
        packed_got if small else packed_got[:, 2 * width :],
        scalars=(info,),
    )

    hidden_units = routed_gate_weight.shape[1]
    tile = min(256, own_slots)
    tiles = all_slots // 2 // tile
    steps = 2 * tiles

    def mine_at(i):
        return (jnp.minimum(i, tiles - 1), 0)

    def other_at(i):
        return (jnp.maximum(i - tiles, 0), 0)

    def every_at(i):
        return (i, 0)

    def fixed_at(i):
        return (0, 0)

    half_slots = all_slots // 2
    expert_ins = [
        (packed_own, pl.BlockSpec((tile, packed_width), mine_at)),
        (packed_got, pl.BlockSpec((tile, packed_width), other_at)),
        (marks, pl.BlockSpec((tile, 128), every_at)),
        (router, pl.BlockSpec((experts_all, width), fixed_at)),
        (routed_gate_weight, pl.BlockSpec((width, hidden_units), fixed_at)),
        (routed_up_weight, pl.BlockSpec((width, hidden_units), fixed_at)),
        (w_expert_down, pl.BlockSpec((hidden_units, width), fixed_at)),
    ]
    expert_outs = [
        (out((half_slots, 2 * width), BF), pl.BlockSpec((tile, 2 * width), mine_at)),
        (out((half_slots, 2 * width), BF), pl.BlockSpec((tile, 2 * width), other_at)),
        (out((all_slots, width), BF), pl.BlockSpec((tile, width), every_at)),
        (out((all_slots, hidden_units), BF), pl.BlockSpec((tile, hidden_units), every_at)),
        (out((all_slots, hidden_units), BF), pl.BlockSpec((tile, hidden_units), every_at)),
        (out((all_slots, hidden_units), BF), pl.BlockSpec((tile, hidden_units), every_at)),
        (out((all_slots, width), BF), pl.BlockSpec((tile, width), every_at)),
        (out((half_slots, 128), F32), pl.BlockSpec((tile, 128), mine_at)),
        (out((experts_all, width), F32), pl.BlockSpec((experts_all, width), fixed_at)),
    ]

    def expert_kernel(*refs):
        pltpu.emit_pipeline(
            functools.partial(expert_body, tiles),
            grid=(steps,),
            in_specs=[spec for _, spec in expert_ins],
            out_specs=[spec for _, spec in expert_outs],
        )(*refs)

    expert_args = [value for value, _ in expert_ins]
    expert_shapes = [shape for shape, _ in expert_outs]
    if small:
        piece = out((half_slots // SENT_PIECES, width), BF)
        results = kernel(
            functools.partial(expert_whole_body, tile),
            [out((half_slots, width), BF)] * 2 + [piece] * 2 * SENT_PIECES + expert_shapes[2:],
            *expert_args,
            vmem=24,
        )
        keep, part_keep, *results = results
        send, part_send = results[:SENT_PIECES], results[SENT_PIECES : 2 * SENT_PIECES]
        results = [keep, send] + list(results[2 * SENT_PIECES :])
    else:
        hbm_spec = pl.BlockSpec(memory_space=pltpu.HBM)
        results = pl.pallas_call(
            expert_kernel,
            in_specs=[hbm_spec] * len(expert_ins),
            out_specs=tuple([hbm_spec] * len(expert_outs)),
            out_shape=tuple(at_hbm(shape) for shape in expert_shapes),
            compiler_params=pltpu.CompilerParams(vmem_limit_bytes=44 * MIB),
            cost_estimate=COST,
            name="expert_body",
        )(*[in_hbm(value) for value in expert_args])
    (
        keep,
        send,
        rows_all,
        expert_hidden,
        grad_egate,
        grad_eup,
        pair_grads,
        gates,
        router_part,
    ) = results

    def sub_scatter(keep, send):
        total = keep.astype(F32) + swap(send, "lo").astype(F32)
        return total[:own_slots] + swap(total[own_slots:].astype(BF), "hi").astype(F32)

    if small:
        got = [swap(piece, "lo") for piece in send]
        part_got = [swap(piece, "lo") for piece in part_send]
        back_far = kernel(
            add_far_body,
            [far_piece] * (pieces - near_pieces),
            keep,
            *got[SENT_PIECES // 2 :],
            deps=(shared_tree[1], shared_tree[3]),
        )
        back_near = kernel(
            add_near_body,
            [out((slot_piece, 2 * width), BF)] * near_pieces,
            keep,
            part_keep,
            gates,
            *got[: SENT_PIECES // 2],
            *part_got[: SENT_PIECES // 2],
        )
        sent_back = list(back_near) + list(back_far)
        sent_parts = kernel(
            part_far_body,
            [far_piece] * (pieces - near_pieces),
            part_keep,
            gates,
            *part_got[SENT_PIECES // 2 :],
            deps=sent_back[:1],
        )
    else:
        total = sub_scatter(keep, send)
        sent_back = [total[:, :width].astype(BF)]
        sent_parts = [(gates[:own_slots, :1] * total[:, width:]).astype(BF)]
        shared_tree, _ = tree_second(shared_tree)

    def weight_grad(left, right, deps=()):
        if not small:
            return dot_t(left, right)
        shape = (left.shape[1], right.shape[1])
        vmem_spec = pl.BlockSpec(memory_space=pltpu.VMEM)
        return pl.pallas_call(
            lambda *refs: weight_grad_body(refs[0], refs[1], *refs[-3:]),
            out_shape=pltpu.HBM(shape, F32),
            in_specs=[vmem_spec] * 2 + [pl.BlockSpec(memory_space=pl.ANY)] * len(deps),
            out_specs=pl.BlockSpec(memory_space=pltpu.HBM),
            scratch_shapes=[
                pltpu.VMEM(shape, F32),
                pltpu.SemaphoreType.DMA((shape[0] // 256,)),
            ],
            compiler_params=pltpu.CompilerParams(vmem_limit_bytes=12 * MIB),
            cost_estimate=COST,
            name="weight_grad",
        )(in_vmem(left), in_vmem(right), *deps)

    grad_w_expert_gate = weight_grad(rows_all, grad_egate, (sent_back[0],))
    got_back = exchange(sent_back)
    if small:
        got_parts = exchange_some(dict(enumerate(sent_parts, near_pieces)))
        shared_tree, _ = tree_second(shared_tree, sent_back[:1])
    else:
        got_parts = exchange(sent_parts)
    shared_keep, shared_got, shared_sent = tree_third(shared_tree)

    keep, send = kernel(
        combine_body,
        [out((half_rows, width), F32), out((half_rows, width), BF)],
        slot_pick_t,
        shared_back,
        *got_back,
        deps=(
            Far(grad_w_expert_gate),
        ),
    )
    half, half_got = half_sum(keep, send)

    def own_sum(keep, send, deps=()):
        own, send = kernel(
            fold_own_body,
            [out((shard_rows, width), F32), out((shard_rows, width), BF)],
            keep,
            swap(send, "lo"),
            deps=deps,
        )
        return own, send

    after_grad, after_grad_own, gain_ffn_part = kernel(
        norm_back_body,
        [out((half_rows, width), F32), out((half_rows, width), BF), out((8, width), F32)],
        gain_ffn,
        half,
        half_got,
        after_attn,
        blocks[0],
        blocks[1],
        deps=got_parts[:2] + [shared_tree[1], shared_tree[3]] if small else (),
    )
    after_grad_got = swap(after_grad_own, "lo")

    keep, send, projected_grad, gain_attn_part = kernel(
        functools.partial(attend_back_body, heads),
        [
            out((half_rows, width), F32),
            out((half_rows, width), BF),
            out((row_count, 3 * inner), BF),
            out((8, width), F32),
        ],
        w_out,
        w_in_t,
        cosine,
        sine,
        weights,
        qkv,
        after_grad_own,
        after_grad_got,
        *blocks,
        vmem=24,
    )
    if small:
        keep, send = kernel(
            functools.partial(result_body, slot_piece),
            [out((half_rows, 2 * width), F32), out((half_rows, 2 * width), BF)],
            slot_pick_t,
            shared_part,
            keep,
            send,
            *got_back[:near_pieces],
            *got_parts,
        )
    else:
        result_part = shared_part + dot(slot_pick_t, got_parts[0])
        keep = jnp.concatenate([result_part[:half_rows], keep], 1)
        send = jnp.concatenate([result_part[half_rows:].astype(BF), send], 1)
    bottom_got = swap(send, "lo")
    last_columns = 4 * inner + 128
    last_tree = kernel(
        functools.partial(last_grads_body, experts_all),
        tree_outs(512, last_columns - 512),
        normed_attn,
        projected_grad,
        after_grad_own,
        after_grad_got,
        mixed,
        gain_ffn_part,
        gain_attn_part,
        router_part,
        scalars=(info,),
        vmem=24,
        deps=(send,),
    )
    last_tree = tree_first(last_tree)
    own, send = kernel(
        fold_own_body,
        [out((shard_rows, 2 * width), F32), out((shard_rows, 2 * width), BF)],
        keep,
        bottom_got,
    )
    grad_sgate, grad_sup, grad_sdown = kernel(
        shared_end_body,
        [Far(out((chunk, units), F32))] * 3,
        shared_keep,
        shared_got,
    )
    near, far = kernel(
        functools.partial(last_body, shard_block),
        [half_shard, half_shard],
        gain_attn,
        own,
        swap(send, "hi"),
        blocks[0],
        after_grad,
        after_attn,
    )
    last_tree, last_sent = tree_second(last_tree, (near,))
    grad_w_expert_down = weight_grad(expert_hidden, pair_grads, (last_sent,))
    got_last = exchange_halves(near, far, (last_sent,))
    last_keep, last_got, last_sent = tree_third(last_tree, got_last[:1])
    small_rows = experts_all + 8
    grad_qkv, grad_out, sums = kernel(
        functools.partial(last_end_body, small_rows),
        [
            Far(out((chunk, 3 * inner), F32)),
            Far(out((inner, chunk), F32)),
            out((small_rows, chunk), F32),
        ],
        last_keep,
        last_got,
    )
    got_last = join(got_last, (last_sent, Far(grad_sgate), Far(grad_w_expert_down)))
    grad_w_expert_up = weight_grad(rows_all, grad_eup, (got_last,))
    final, grad_tokens = kernel(
        return_body,
        [Far(out((row_count, width), BF)), Far(out((row_count, width), BF))],
        anchor,
        *blocks_of(got_last, (sums, Far(grad_w_expert_up))),
    )

    gain_ffn_sum, gain_attn_sum, router_sum = kernel(
        small_end_body,
        [Far(out((1, chunk), F32)), Far(out((1, chunk), F32)), Far(out((experts_all, chunk), F32))],
        sums,
        *[lax.ppermute(sums, TP, [(i, i ^ k) for i in range(4)]) for k in (1, 2, 3)],
        deps=(Far(final),),
    )
    return (
        final,
        grad_tokens,
        gain_attn_sum.reshape(chunk),
        grad_qkv,
        grad_out,
        gain_ffn_sum.reshape(chunk),
        router_sum.T,
        grad_sgate,
        grad_sup,
        grad_sdown.T,
        grad_w_expert_gate,
        grad_w_expert_up,
        grad_w_expert_down,
    )


def solution(mesh):
    devices_dp, devices_tp = mesh.shape["dp"], mesh.shape["tensor"]
    fine = Mesh(
        mesh.devices.reshape(devices_dp // 2, 2, devices_tp // 2, 2), ("dz", "dy", "hi", "lo")
    )
    every = DP + TP
    return jax.shard_map(
        on_device,
        mesh=fine,
        in_specs=(
            P(DP, None),
            P(DP, None),
            P(),
            P(None, TP),
            P(TP, None),
            P(),
            P(),
            P(None, TP),
            P(None, TP),
            P(TP, None),
            P(None, every),
            P(None, every),
            P(every, None),
            P(DP, None),
            P(DP),
            P(DP),
            P(DP, None),
            P(DP, None),
        ),
        out_specs=(
            P(DP, None),
            P(DP, None),
            P(DP),
            P(DP, TP),
            P(TP, DP),
            P(DP),
            P(DP, None),
            P(DP, TP),
            P(DP, TP),
            P(TP, DP),
            P(None, every),
            P(None, every),
            P(every, None),
        ),
        check_vma=False,
    )
```

```python
import functools

import jax
import jax.numpy as jnp
import numpy as np
from jax import lax
from jax.experimental import pallas as pl
from jax.experimental.pallas import tpu as pltpu
from jax.sharding import Mesh, PartitionSpec as P

HD = 64
MY_BLOCK, PICK, MY_PART, MY_EXPERT, MY_DP, Y_BIT, Z_BITS = range(7)
EPSILON = 1e-06
BF = jnp.bfloat16
F32 = jnp.float32
I32 = jnp.int32
DP = ("dz", "dy")
TP = ("hi", "lo")
MIB = 1 << 20
SENT_PIECES = 4
COST = pl.CostEstimate(flops=1000, bytes_accessed=1000, transcendentals=0)


def dot(left, right):
    return jnp.dot(left, right, preferred_element_type=F32)


def dot_t(left, right):
    return lax.dot_general(left, right, (((0,), (0,)), ((), ())), preferred_element_type=F32)


def dot_bt(left, right):
    return lax.dot_general(left, right, (((1,), (1,)), ((), ())), preferred_element_type=F32)


def swap(values, axis):
    return lax.ppermute(values, axis, [(0, 1), (1, 0)])


def exchange_stacked(values):
    order = jnp.arange(values.shape[0], dtype=I32) ^ lax.axis_index(DP)
    got = lax.all_to_all(
        jnp.take(values, order, axis=0), DP, split_axis=0, concat_axis=0, tiled=True
    )
    return jnp.take(got, order, axis=0)


def exchange(pieces):
    devices = lax.axis_size(DP)
    if len(pieces) == 1:
        (values,) = pieces
        stacked = values.reshape(devices, -1, values.shape[-1])
        return [exchange_stacked(stacked).reshape(values.shape)]
    return exchange_some(dict(enumerate(pieces)))


def exchange_some(pieces):
    devices = lax.axis_size(DP)
    got = dict(pieces)
    for k in (4, 5, 6, 7, 2, 3, 1):
        if k in got:
            got[k] = lax.ppermute(pieces[k], DP, [(i, i ^ k) for i in range(devices)])
    return [got[k] for k in sorted(got)]


def out(shape, dtype):
    return jax.ShapeDtypeStruct(shape, dtype)


class Far:
    def __init__(self, value):
        self.value = value


class Held(Far):
    pass


class Free(Far):
    pass


class Arriving:
    def __init__(self, buffer, copy):
        self.buffer, self.copy, self.waiting = buffer, copy, True
        self.shape, self.dtype = buffer.shape, buffer.dtype

    def ready(self):
        if self.waiting:
            self.copy.wait()
            self.waiting = False

    def __getitem__(self, index):
        self.ready()
        return self.buffer[index]


class Leaving:
    def __init__(self, buffer, copy):
        self.buffer, self.copy, self.started = buffer, copy, False
        self.shape, self.dtype = buffer.shape, buffer.dtype

    def flush(self):
        if not self.started:
            self.copy.start()
            self.started = True

    def __getitem__(self, index):
        return self.buffer[index]

    def __setitem__(self, index, value):
        self.buffer[index] = value


def in_hbm(values):
    return pltpu.with_memory_space_constraint(values, pltpu.HBM)


def in_vmem(values):
    if values.size * values.dtype.itemsize > 4 * MIB:
        return values
    return pltpu.with_memory_space_constraint(values, pltpu.VMEM)


def at_hbm(shape):
    return pltpu.HBM(shape.shape, shape.dtype)


def at_vmem(shape):
    if shape.size * shape.dtype.itemsize > 4 * MIB:
        return shape
    return pltpu.VMEM(shape.shape, shape.dtype)


def kernel(body, outs, *args, scalars=(), deps=(), vmem=16, semaphores=0):
    vmem_spec = pl.BlockSpec(memory_space=pltpu.VMEM)
    hbm_spec = pl.BlockSpec(memory_space=pltpu.HBM)
    any_spec = pl.BlockSpec(memory_space=pl.ANY)
    held = [isinstance(a, Held) for a in args]
    far_in = [isinstance(a, Far) and not h for a, h in zip(args, held)]
    free_out = [isinstance(o, Free) for o in outs]
    far_out = [isinstance(o, Far) and not f for o, f in zip(outs, free_out)]
    args = [in_hbm(a.value) if isinstance(a, Far) else in_vmem(a) for a in args]
    outs = [
        o.value if f else at_hbm(o.value) if h else at_vmem(o)
        for o, f, h in zip(outs, free_out, far_out)
    ]
    deps = [in_hbm(d.value) if isinstance(d, Far) else d for d in deps]
    moved = [x for x, f in zip(args + outs, far_in + far_out) if f]
    scratch = [pltpu.VMEM(x.shape, x.dtype) for x in moved]
    if moved:
        scratch.append(pltpu.SemaphoreType.DMA((len(moved),)))
    if semaphores:
        scratch.append(pltpu.SemaphoreType.DMA((semaphores,)))
    n_scalars, n_args, n_deps, n_outs = len(scalars), len(args), len(deps), len(outs)

    def wrapped(*refs):
        ins = list(refs[: n_scalars + n_args])
        results = list(refs[n_scalars + n_args + n_deps :][:n_outs])
        buffers = refs[n_scalars + n_args + n_deps + n_outs :]
        extra = buffers[-1:] if semaphores else ()
        buffers = buffers[:-1] if semaphores else buffers
        at = 0
        for i, far in enumerate(far_in):
            if far:
                ref = ins[n_scalars + i]
                copy = pltpu.make_async_copy(ref, buffers[at], buffers[-1].at[at])
                copy.start()
                ins[n_scalars + i] = Arriving(buffers[at], copy)
                at += 1
        for i, far in enumerate(far_out):
            if far:
                copy = pltpu.make_async_copy(buffers[at], results[i], buffers[-1].at[at])
                results[i] = Leaving(buffers[at], copy)
                at += 1
        body(*ins, *results, *extra)
        for ref in ins:
            if isinstance(ref, Arriving):
                ref.ready()
        for ref in results:
            if isinstance(ref, Leaving):
                ref.flush()
        for ref in results:
            if isinstance(ref, Leaving):
                ref.copy.wait()

    return pl.pallas_call(
        wrapped,
        out_shape=tuple(outs),
        in_specs=[pl.BlockSpec(memory_space=pltpu.SMEM)] * n_scalars
        + [hbm_spec if f or h else vmem_spec for f, h in zip(far_in, held)]
        + [any_spec] * n_deps,
        out_specs=tuple(hbm_spec if far else vmem_spec for far in far_out),
        scratch_shapes=scratch,
        compiler_params=pltpu.CompilerParams(vmem_limit_bytes=vmem * MIB),
        cost_estimate=COST,
        name=body.func.__name__ if isinstance(body, functools.partial) else body.__name__,
    )(*scalars, *args, *deps)


def tie(values, *deps):
    any_spec = pl.BlockSpec(memory_space=pl.ANY)
    vmem_spec = pl.BlockSpec(memory_space=pltpu.VMEM)
    return pl.pallas_call(
        lambda *refs: None,
        out_shape=out(values.shape, values.dtype),
        in_specs=[vmem_spec] + [any_spec] * len(deps),
        out_specs=vmem_spec,
        input_output_aliases={0: 0},
        cost_estimate=COST,
        name="tie",
    )(in_vmem(values), *[in_hbm(d.value) if isinstance(d, Far) else d for d in deps])


def rope_table(places):
    exponent = np.arange(HD // 2, dtype=np.float32) * np.float32(-2.0 / HD)
    angles = np.arange(places, dtype=np.float32)[:, None] * np.power(np.float32(10000.0), exponent)
    cosine = np.cos(angles.astype(np.float64)).astype(np.float32)
    sine = np.sin(angles.astype(np.float64)).astype(np.float32)
    rest = np.concatenate([cosine, cosine, -sine, sine], 1)
    terms = []
    for _ in range(3):
        terms.append(rest.astype(BF))
        rest = rest - terms[-1].astype(np.float32)
    return jnp.asarray(np.concatenate(terms, 1))


def iota(shape, dim):
    return lax.broadcasted_iota(I32, shape, dim)


def log2(number):
    return number.bit_length() - 1


def silu_parts(gate_in):
    sigmoid_val = 1.0 / (1.0 + jnp.exp(-gate_in))
    return (gate_in * sigmoid_val, sigmoid_val * (1.0 + gate_in * (1.0 - sigmoid_val)))


def inverse_root(values):
    return lax.rsqrt(jnp.mean(values * values, -1, keepdims=True) + EPSILON)


def rms_backward(values, root, gain, grad_normed):
    scaled = grad_normed * gain
    return root * scaled - values * (root * root * root) * jnp.mean(
        scaled * values, -1, keepdims=True
    )


def lane_rank(buckets, bucket_count):
    count = buckets.shape[1]
    rows = max(8, bucket_count)
    member = (iota((rows, count), 0) == buckets).astype(F32)
    earlier = (iota((count, count), 0) < iota((count, count), 1)).astype(F32).astype(BF)
    return jnp.sum(dot(member.astype(BF), earlier) * member, 0, keepdims=True).astype(I32)


def relative_row(block, rank, my_block, shard_block, shard_rows):
    shift = log2(shard_block)
    return (
        ((rank >> shift) ^ my_block) * shard_rows
        + block * shard_block
        + (rank & (shard_block - 1))
    )


def rope_back(grads, cosine, sine):
    return grads * cosine - half_turned(grads) * sine


def store_pieces(refs, value):
    rows = refs[0].shape[0]
    for i, ref in enumerate(refs):
        ref[...] = value[i * rows : (i + 1) * rows]


def joined(refs):
    return jnp.concatenate([ref[...] for ref in refs], 0) if len(refs) > 1 else refs[0][...]


def join_body(*refs):
    *parts, whole = refs
    rows = parts[0].shape[0]
    for i, ref in enumerate(parts):
        whole[i * rows : (i + 1) * rows, :] = ref[...]


def middle_body(block, near, far, *outs):
    for i, ref in enumerate(outs):
        ref[:block, :] = near[i * block : (i + 1) * block, :]
        ref[block:, :] = far[i * block : (i + 1) * block, :]


def store_halves(near, far, block, value, columns):
    for i in range(near.shape[0] // block):
        at = 2 * i * block
        near[i * block : (i + 1) * block, columns] = value[at : at + block]
        far[i * block : (i + 1) * block, columns] = value[at + block : at + 2 * block]


def fetch_body(*refs):
    *refs, semaphores = refs
    count = len(refs) // 2
    copies = [
        pltpu.make_async_copy(refs[i], refs[count + i], semaphores.at[i]) for i in range(count)
    ]
    for copy in copies:
        copy.start()
    for copy in copies:
        copy.wait()


def select_body(shard_block, blocks, info, inverse, tokens, cotangent, *refs):
    *sent, anchor = refs
    row_count, width = tokens.shape
    shard_rows = shard_block * blocks
    target = (inverse[...] >> log2(row_count)) ^ info[MY_DP]
    row = relative_row(target, lane_rank(target, blocks), info[MY_BLOCK], shard_block, shard_rows)
    anchor[...] = row
    pick = (iota((shard_rows, row_count), 0) == row).astype(F32).astype(BF)
    rows = jnp.concatenate([dot(pick, tokens[...]), dot(pick, cotangent[...])], 1)
    store_pieces(sent, rows.astype(BF))


def index_body(
    shard_block,
    copies,
    per_dp,
    part_rows,
    experts_all,
    info,
    lengths,
    order,
    routes,
    fill,
    table,
    slot_pick,
    slot_pick_t,
    bias,
    cosine,
    sine,
    meta,
):
    row_count = order.shape[1]
    devices_dp = slot_pick.shape[0] // part_rows
    shard_rows = shard_block * devices_dp
    source = (order[...] >> log2(row_count)) ^ info[MY_DP]
    local = relative_row(
        source, lane_rank(source, devices_dp), info[MY_BLOCK], shard_block, shard_rows
    )
    place_pick = (iota((row_count, row_count), 0) == local).astype(F32).astype(BF)
    lanes = iota((1, row_count), 1)
    segment = jnp.zeros((1, row_count), I32)
    start = jnp.zeros((1, row_count), I32)
    end = jnp.int32(0)
    for entry in range(lengths.shape[1]):
        end = end + lengths[0, entry]
        passed = lanes >= end
        segment = segment + passed.astype(I32)
        start = jnp.maximum(start, jnp.where(passed, end, 0))
    place = lanes - start
    expert_sum = routes[0:1, :] + routes[1:2, :] + 1
    facts = jnp.concatenate(
        [segment, place >> 1, place & 1, expert_sum, jnp.zeros((4, row_count), I32)], 0
    )
    facts = facts.astype(F32).astype(BF)
    across = dot_bt(facts, place_pick)
    down = dot_bt(place_pick, facts)
    place_row = 2.0 * across[1:2] + across[2:3]
    place_col = 2.0 * down[:, 1:2] + down[:, 2:3]
    allowed = (down[:, 0:1] == across[0:1]) & (place_row <= place_col)
    bias[...] = jnp.where(allowed, 0.0, -1e30).astype(BF)
    at_place = (
        iota((row_count, row_count), 1).astype(F32) == place_col
    ).astype(F32).astype(BF)
    turned = dot(at_place, table[...])
    pieces = [turned[:, i * 128 : (i + 1) * 128] for i in range(3)]
    turned = pieces[0] + pieces[1] + pieces[2]
    cosine[...] = turned[:, :HD]
    sine[...] = turned[:, HD:]
    meta[...] = jnp.broadcast_to(down[:, 3:4], meta.shape).astype(BF)
    pairs = 2 * row_count
    fill_at = (fill[...] & 1) * row_count + (fill[...] >> 1)
    fill_pick = (iota((pairs, pairs), 0) == fill_at).astype(F32).astype(BF)
    expert_rows = max(16, experts_all)
    pair_expert = jnp.concatenate([routes[0:1, :], routes[1:2, :]], 1)
    named = (iota((expert_rows, pairs), 0) == pair_expert).astype(F32).astype(BF)
    member = dot(named, fill_pick)
    earlier = (iota((pairs, pairs), 0) < iota((pairs, pairs), 1)).astype(F32).astype(BF)
    ranks = (member * (dot(member.astype(BF), earlier) + 1.0)).astype(BF)
    ranks = dot_bt(ranks, fill_pick)
    ranks = (ranks[:, :row_count] + ranks[:, row_count:]).astype(BF)
    ranks = dot_bt(ranks, place_pick).astype(I32)
    slots = iota((part_rows, row_count), 0) + (info[MY_PART] * part_rows + 1)
    experts = iota((expert_rows, row_count), 0)
    for target in range(devices_dp):
        expert = ((target ^ info[MY_DP]) >> log2(copies)) * per_dp + info[PICK]
        chosen = jnp.sum(jnp.where(experts == expert, ranks, 0), 0, keepdims=True)
        picked = (slots == chosen).astype(F32)
        slot_pick[target * part_rows : (target + 1) * part_rows, :] = picked.astype(BF)
    slot_pick_t[...] = slot_pick[...].astype(F32).T.astype(BF)


def head_parts(projected, heads):
    return [
        [projected[:, (3 * h + i) * HD : (3 * h + i + 1) * HD] for i in range(3)]
        for h in range(heads)
    ]


def half_turned(values):
    half = values.shape[1] // 2
    return jnp.concatenate([values[:, half:], values[:, :half]], 1)


def attend_body(
    heads,
    gain,
    w_in_t,
    w_out,
    cosine,
    sine,
    bias,
    b0,
    b1,
    b2,
    b3,
    keep,
    *refs,
):
    *send, qkv, mixed, normed, weights_all = refs
    width = b0.shape[1] // 2
    half = keep.shape[0]
    tokens = jnp.concatenate([b[:, :width] for b in (b0, b1, b2, b3)], 0).astype(F32)
    normed[...] = (tokens * inverse_root(tokens) * gain[...]).astype(BF)
    projected = dot_bt(normed[...], w_in_t[...])
    cosine, sine = cosine[...], sine[...]
    parts = []
    for query, keys, values in head_parts(projected, heads):
        parts.append((query * cosine + half_turned(query) * sine).astype(BF))
        parts.append((keys * cosine + half_turned(keys) * sine).astype(BF))
        parts.append(values.astype(BF))
    qkv[...] = jnp.concatenate(parts, 1)
    scale = HD**-0.5
    mixed_heads = []
    for head, (query, keys, values) in enumerate(head_parts(qkv, heads)):
        scores = dot_bt(query, keys) * scale + bias[...].astype(F32)
        powers = jnp.exp(scores - jnp.max(scores, -1, keepdims=True))
        weights = powers * (1.0 / jnp.sum(powers, -1, keepdims=True))
        weights_all[head] = weights
        mixed_heads.append(dot(weights.astype(BF), values))
    mixed[...] = jnp.concatenate(mixed_heads, 1).astype(BF)
    part = dot(mixed[...], w_out[...])
    keep[...] = part[:half]
    store_pieces(send, part[half:].astype(BF))


def fold_body(keep, *refs):
    *got, half = refs
    half[...] = (keep[...] + joined(got).astype(F32)).astype(BF)


def fold_own_body(keep, got, own, send):
    rows = own.shape[0]
    own[...] = keep[:rows, :] + got[:rows, :].astype(F32)
    send[...] = (keep[rows:, :] + got[rows:, :].astype(F32)).astype(BF)


def both(half, got):
    rows = half.shape[0] // 2
    mine, other = half[...].astype(F32), got[...].astype(F32)
    return mine + jnp.concatenate([other[rows:], other[:rows]], 0)


def norm_body(gain, half, got, b0, b1, after_attn, normed):
    width = half.shape[1]
    balanced = jnp.concatenate([b0[:, :width], b1[:, :width]], 0).astype(F32)
    values = balanced + both(half, got)
    after_attn[...] = values
    normed[...] = (values * inverse_root(values) * gain[...]).astype(BF)


def send_body(slot_pick, own, got, meta, b0, b1, b2, b3, *sent):
    width = own.shape[1]
    rows = jnp.concatenate([own[...], got[...]], 0)
    rows = dot(slot_pick[...], rows).astype(BF)
    count = sent[0].shape[0]
    near = sum(ref.shape[1] > width for ref in sent) * count
    grads = jnp.concatenate([b[:, width:] for b in (b0, b1, b2, b3)], 0)
    grads = jnp.concatenate([grads, meta[...]], 1)
    grads = dot(slot_pick[:near, :], grads).astype(BF)
    for i, ref in enumerate(sent):
        at = slice(i * count, (i + 1) * count)
        ref[:, :width] = rows[at]
        if ref.shape[1] > width:
            ref[:, width:] = grads[at]


def send_grads_body(first, slot_pick, meta, b0, b1, b2, b3, *sent):
    width = b0.shape[1] // 2
    grads = jnp.concatenate([b[:, width:] for b in (b0, b1, b2, b3)], 0)
    grads = jnp.concatenate([grads, meta[...]], 1)
    store_pieces(sent, dot(slot_pick[first:, :], grads).astype(BF))


def join_packed_body(near, *refs):
    *parts, whole = refs
    count, width = parts[near].shape
    far = (len(parts) - near) // 2
    for i in range(near):
        whole[i * count : (i + 1) * count, :] = parts[i][...]
    for i in range(far):
        at = slice((near + i) * count, (near + i + 1) * count)
        whole[at, :width] = parts[near + i][...]
        whole[at, width:] = parts[near + far + i][...]


def shared_body(
    own, got, b0, b1, b2, b3, w_gate, w_up, w_down, part, back, grad_gate, grad_up, hidden
):
    width = own.shape[1]
    rows = jnp.concatenate([own[...], got[...]], 0)
    grads = jnp.concatenate([b[:, width:] for b in (b0, b1, b2, b3)], 0)
    gate = dot(rows, w_gate[...])
    up = dot(rows, w_up[...])
    act, slope = silu_parts(gate)
    hidden[...] = (act * up).astype(BF)
    part[...] = dot(hidden[...], w_down[...])
    hidden_grad = dot_bt(grads, w_down[...])
    grad_gate[...] = (hidden_grad * up * slope).astype(BF)
    grad_up[...] = (hidden_grad * act).astype(BF)
    back[...] = dot_bt(grad_gate[...], w_gate[...]) + dot_bt(grad_up[...], w_up[...])


def store_tree(info, sums, keeps, sends):
    chunk, columns = keeps[0].shape[1:]
    sides = ((sums[:, :columns], Y_BIT, 1), (sums[:, columns:], Z_BITS, 2))
    for (values, which, stride), keep, send in zip(sides, keeps, sends):
        mine = info[which] == 0
        for i in range(keep.shape[0]):
            at = (2 * i if stride == 1 else i // 2 * 4 + i % 2) * chunk
            first, second = values[at : at + chunk], values[at + stride * chunk :][:chunk]
            keep[i] = jnp.where(mine, first, second)
            send[i] = jnp.where(mine, second, first).astype(BF)


def shared_grads_body(
    info, own, got, b0, b1, b2, b3, grad_gate, grad_up, hidden, *refs
):
    width = own.shape[1]
    rows = jnp.concatenate([own[...], got[...]], 0)
    grads = jnp.concatenate([b[:, width:] for b in (b0, b1, b2, b3)], 0)
    sums = jnp.concatenate(
        [dot_t(rows, grad_gate[...]), dot_t(rows, grad_up[...]), dot_t(grads, hidden[...])], 1
    )
    store_tree(info, sums, refs[:2], refs[2:])


def halved(info, which, total, keep, send):
    mine = info[which] == 0
    for index in range(keep.shape[0]):
        first, second = total[2 * index], total[2 * index + 1]
        keep[index] = jnp.where(mine, first, second)
        send[index] = jnp.where(mine, second, first).astype(BF)


def tree_second_body(info, kept_a, got_a, kept_b, got_b, keep_a, keep_b, send_a, send_b):
    halved(info, Z_BITS, kept_a[...] + got_a[...].astype(F32), keep_a, send_a)
    halved(info, Y_BIT, kept_b[...] + got_b[...].astype(F32), keep_b, send_b)


def tree_third_body(info, kept_a, got_a, kept_b, got_b, keep, send):
    total = jnp.concatenate(
        [kept_a[...] + got_a[...].astype(F32), kept_b[...] + got_b[...].astype(F32)], 2
    )
    halved(info, Z_BITS + 1, total, keep, send)


def last_grads_body(
    experts, info, normed, projected_grad, own, got, mixed, gain_ffn, gain_attn, router, *refs
):
    width = normed.shape[1]
    small = jnp.concatenate(
        [
            router[:experts, :],
            gain_ffn[:1, :],
            gain_attn[:1, :],
            jnp.zeros((128 - experts - 2, width), F32),
        ],
        0,
    )
    grads = jnp.concatenate([own[...], got[...]], 0)
    sums = jnp.concatenate(
        [dot_t(normed[...], projected_grad[...]), dot_t(grads, mixed[...]), small.T], 1
    )
    store_tree(info, sums, refs[:2], refs[2:])


def tree_body(which, info, kept, got, keep, send):
    halved(info, which, kept[...] + got[...].astype(F32), keep, send)


def last_end_body(small_rows, kept, got, grad_qkv, grad_out, small):
    total = kept[0] + got[0].astype(F32)
    columns, inner = grad_qkv.shape[1], grad_out.shape[0]
    grad_qkv[...] = total[:, :columns]
    grad_out[...] = total[:, columns : columns + inner].T
    small[...] = total[:, columns + inner :].T[:small_rows]


def small_end_body(own, by_lo, by_hi, by_both, gain_ffn, gain_attn, router):
    experts = router.shape[0]
    total = (own[...] + by_lo[...]) + (by_hi[...] + by_both[...])
    router[...] = total[:experts]
    gain_ffn[...] = total[experts : experts + 1]
    gain_attn[...] = total[experts + 1 : experts + 2]


def shared_end_body(kept, got, grad_gate, grad_up, grad_down):
    total = kept[0] + got[0].astype(F32)
    units = grad_gate.shape[1]
    grad_gate[...] = total[:, :units]
    grad_up[...] = total[:, units : 2 * units]
    grad_down[...] = total[:, 2 * units :]


def add_far_body(keep, *refs):
    got, total = refs[: SENT_PIECES // 2], refs[SENT_PIECES // 2 :]
    half = keep.shape[0] // 2
    store_pieces(total, (keep[half:, :].astype(F32) + joined(got).astype(F32)).astype(BF))


def gated_parts(keep, got, gates):
    gate = jnp.concatenate([gates] * (keep.shape[1] // 128), 1)
    return (gate * (keep.astype(F32) + got.astype(F32))).astype(BF)


def add_near_body(keep, part_keep, gates, *refs):
    got, part_got, total = (
        refs[: SENT_PIECES // 2],
        refs[SENT_PIECES // 2 : SENT_PIECES],
        refs[SENT_PIECES:],
    )
    half, width = keep.shape[0] // 2, keep.shape[1]
    rows = (keep[:half, :].astype(F32) + joined(got).astype(F32)).astype(BF)
    parts = gated_parts(part_keep[:half, :], joined(part_got), gates[:half, :])
    count = total[0].shape[0]
    for i, ref in enumerate(total):
        at = slice(i * count, (i + 1) * count)
        ref[:count, :width] = rows[at]
        ref[:count, width:] = parts[at]


def part_far_body(keep, gates, *refs):
    got, total = refs[: SENT_PIECES // 2], refs[SENT_PIECES // 2 :]
    half = keep.shape[0] // 2
    store_pieces(total, gated_parts(keep[half:, :], joined(got), gates[half:, :]))


def weight_grad_body(left, right, total, sums, semaphores):
    tile = 256
    copies = []
    for i in range(left.shape[1] // tile):
        at = slice(i * tile, (i + 1) * tile)
        sums[at, :] = dot_t(left[:, at], right[...])
        copies.append(
            pltpu.make_async_copy(sums.at[at, :], total.at[at, :], semaphores.at[i])
        )
        copies[-1].start()
    for copy in copies:
        copy.wait()


def meta_body(devices_dp, part_rows, sub, capacity, width, info, own, got, marks):
    my_part, my_expert = info[MY_PART], info[MY_EXPERT]
    lanes = iota((part_rows, 128), 1)
    blocks = [(ref, at, part) for part, (ref, at) in enumerate(
        [(own, i) for i in range(sub // 2)] + [(got, i) for i in range(sub // 2)]
    )]
    counts = []
    for block in range(devices_dp):
        count = jnp.zeros((1, 128), F32)
        for ref, at, _ in blocks:
            start = (at * devices_dp + block) * part_rows
            value = ref[start : start + part_rows, width:].astype(F32)
            count = count + jnp.sum((value > 0.0).astype(F32), 0, keepdims=True)
        counts.append(count)
    for block in range(devices_dp):
        earlier = jnp.zeros((1, 128), F32)
        for before in range(devices_dp):
            ahead = (before ^ info[MY_DP]) < (block ^ info[MY_DP])
            earlier = earlier + jnp.where(ahead, counts[before], 0.0)
        for ref, at, part in blocks:
            start = (at * devices_dp + block) * part_rows
            value = ref[start : start + part_rows, width:].astype(F32)
            valid = value > 0.0
            slot = iota((part_rows, 128), 0) + (my_part ^ part) * part_rows
            kept = valid & (slot.astype(F32) + earlier < capacity)
            other = value.astype(I32) - 1 - my_expert
            mark = (lanes == my_expert).astype(F32) - (lanes == other).astype(F32)
            row = (part * devices_dp + block) * part_rows
            marks[row : row + part_rows, :] = jnp.where(
                lanes == 127, kept.astype(F32), jnp.where(valid, mark, 0.0)
            )


def expert_step(packed, mark, w_router, w_gate, w_up, w_down, stores):
    hidden_out, grad_gate_out, grad_up_out, pair_out = stores
    width = w_gate.shape[0]
    rows, grads = packed[:, :width], packed[:, width : 2 * width].astype(F32)
    kept = mark[:, 127:128] > 0.5
    mark = mark[:, : w_router.shape[0]]
    gap = jnp.sum(dot_bt(rows, w_router[...]) * mark, 1, keepdims=True)
    gate = 1.0 / (1.0 + jnp.exp(-gap))
    gate_other = 1.0 / (1.0 + jnp.exp(gap))
    gate_in = dot(rows, w_gate[...])
    up = dot(rows, w_up[...])
    act, slope = silu_parts(gate_in)
    hidden = (act * up).astype(BF)
    hidden_out(hidden)
    part = jnp.where(kept, dot(hidden, w_down[...]), 0.0).astype(BF)
    pair = jnp.where(kept, gate * grads, 0.0).astype(BF)
    pair_out(pair)
    gate_grad = jnp.sum(part.astype(F32) * grads, 1, keepdims=True)
    logit_grad = (gate * gate_other * gate_grad * mark).astype(BF)
    hidden_grad = dot_bt(pair, w_down[...])
    grad_gate = (hidden_grad * up * slope).astype(BF)
    grad_up = (hidden_grad * act).astype(BF)
    grad_gate_out(grad_gate)
    grad_up_out(grad_up)
    back = (dot_bt(grad_gate, w_gate[...]) + dot_bt(grad_up, w_up[...])).astype(BF).astype(F32)
    back = (back + dot(logit_grad, w_router[...])).astype(BF)
    return back, part, gate, dot_t(logit_grad, rows)


def store_at(ref, where=...):
    def store(value):
        ref[where] = value

    return store


def expert_body(
    tiles,
    packed_own,
    packed_got,
    marks,
    w_router,
    w_gate,
    w_up,
    w_down,
    keep,
    send,
    rows_all,
    hidden,
    grad_gate,
    grad_up,
    pair,
    gates,
    router,
):
    step = pl.program_id(0)
    mine = step < tiles
    width = rows_all.shape[1]
    packed = jnp.where(mine, packed_own[...], packed_got[...])
    rows_all[...] = packed[:, :width]
    back, part, gate, router_term = expert_step(
        packed,
        marks[...],
        w_router,
        w_gate,
        w_up,
        w_down,
        [store_at(ref) for ref in (hidden, grad_gate, grad_up, pair)],
    )

    @pl.when(step == 0)
    def _():
        router[...] = jnp.zeros_like(router)

    router[...] += router_term

    @pl.when(mine)
    def _():
        keep[:, :width] = back
        keep[:, width:] = part
        gates[...] = jnp.broadcast_to(gate, gates.shape)

    @pl.when(jnp.logical_not(mine))
    def _():
        send[:, :width] = back
        send[:, width:] = part


def expert_whole_body(
    tile,
    packed_own,
    packed_got,
    marks,
    w_router,
    w_gate,
    w_up,
    w_down,
    back_keep,
    part_keep,
    *refs,
):
    back_send, part_send = refs[:SENT_PIECES], refs[SENT_PIECES : 2 * SENT_PIECES]
    rows_all, hidden, grad_gate, grad_up, pair, gates, router = refs[2 * SENT_PIECES :]
    half = packed_own.shape[0]
    width = rows_all.shape[1]
    router[...] = jnp.zeros_like(router)

    def run(base, packed_ref, put):
        def step(index, _):
            at = pl.ds(pl.multiple_of(index * tile, tile), tile)
            place = pl.ds(pl.multiple_of(base + index * tile, tile), tile)
            packed = packed_ref[at, : 2 * width]
            rows_all[place, :] = packed[:, :width]
            back, part, gate, router_term = expert_step(
                packed,
                marks[place, :],
                w_router,
                w_gate,
                w_up,
                w_down,
                [store_at(ref, (place, slice(None))) for ref in (hidden, grad_gate, grad_up, pair)],
            )
            router[...] += router_term
            put(index, at, back, part)
            if base == 0:
                gates[at, :] = jnp.broadcast_to(gate, (tile, 128))
            return 0

        lax.fori_loop(0, half // tile, step, 0)

    def put_own(index, at, back, part):
        back_keep[at, :] = back
        part_keep[at, :] = part

    def put_got(index, at, back, part):
        rows = half // SENT_PIECES
        each = tile // rows
        for i in range(SENT_PIECES):

            @pl.when(index == i // each)
            def _(i=i):
                inside = slice(i % each * rows, (i % each + 1) * rows)
                back_send[i][...] = back[inside]
                part_send[i][...] = part[inside]

    run(0, packed_own, put_own)
    run(half, packed_got, put_got)


def combine_body(slot_pick_t, addend, *refs):
    back, keep, send = refs[:-5], refs[-5], refs[-4:]
    half, width = keep.shape
    count = back[-1].shape[0]
    rows = jnp.concatenate([ref[:count, :width] for ref in back], 0)
    total = addend[...] + dot(slot_pick_t[...], rows)
    keep[...] = total[:half]
    store_pieces(send, total[half:].astype(BF))


def result_body(count, slot_pick_t, addend, attn_keep, attn_send, *refs):
    *near, a, b, c, d, keep, send = refs
    half, width = attn_keep.shape
    rows = [ref[:count, width:] for ref in near] + [ref[...] for ref in (a, b, c, d)]
    total = addend[...] + dot(slot_pick_t[...], jnp.concatenate(rows, 0))
    keep[:, :width] = total[:half]
    send[:, :width] = total[half:].astype(BF)
    keep[:, width:] = attn_keep[...]
    send[:, width:] = attn_send[...]


def norm_back_body(
    gain, half, got, after_attn, b0, b1, after_grad, low, gain_grad
):
    width = half.shape[1]
    normed_grad = both(half, got)
    values = after_attn[...]
    root = inverse_root(values)
    grads = jnp.concatenate([b0[:, width:], b1[:, width:]], 0).astype(F32)
    total = grads + rms_backward(values, root, gain[...], normed_grad)
    after_grad[...] = total
    low[...] = total.astype(BF)
    gain_grad[...] = jnp.broadcast_to(
        0.5 * jnp.sum(normed_grad * values * root, 0, keepdims=True), gain_grad.shape
    )


def attend_back_body(
    heads,
    w_out,
    w_in_t,
    cosine,
    sine,
    weights_all,
    qkv,
    own,
    got,
    b0,
    b1,
    b2,
    b3,
    keep,
    send,
    projected_grad,
    gain_grad,
):
    width = own.shape[1]
    half = keep.shape[0]
    grads = jnp.concatenate([own[...], got[...]], 0)
    mixed_grad = dot_bt(grads, w_out[...]).astype(BF)
    scale = HD**-0.5
    cosine, sine = cosine[...], sine[...]
    parts = []
    for head, (query, keys, values) in enumerate(head_parts(qkv, heads)):
        at = head * HD
        weights = weights_all[head]
        mine = mixed_grad[:, at : at + HD]
        weight_grad = dot_bt(mine, values)
        delta = jnp.sum(weights * weight_grad, -1, keepdims=True)
        score_grad = (weights * (weight_grad - delta)).astype(BF)
        parts.append(rope_back(dot(score_grad, keys) * scale, cosine, sine))
        parts.append(rope_back(dot_t(score_grad, query) * scale, cosine, sine))
        parts.append(dot_t(weights.astype(BF), mine))
    projected_grad[...] = jnp.concatenate(parts, 1).astype(BF)
    part = dot(projected_grad[...], w_in_t[...])
    tokens = jnp.concatenate([b[:, :width] for b in (b0, b1, b2, b3)], 0).astype(F32)
    gain_grad[...] = jnp.broadcast_to(
        jnp.sum(part * tokens * inverse_root(tokens), 0, keepdims=True), gain_grad.shape
    )
    keep[...] = part[:half]
    send[...] = part[half:].astype(BF)


def last_body(
    block, gain, own, got, b0, after_grad, after_attn, near, far
):
    rows, width = own.shape[0], own.shape[1] // 2
    tokens = b0[:, :width].astype(F32)
    sums = own[...] + got[...].astype(F32)
    normed_grad = sums[:, width:]
    total = after_grad[:rows, :] + rms_backward(
        tokens, inverse_root(tokens), gain[...], normed_grad
    )
    result = after_attn[:rows, :] + sums[:, :width]
    store_halves(near, far, block, result.astype(BF), slice(0, width))
    store_halves(near, far, block, total.astype(BF), slice(width, None))


def return_body(anchor, b0, b1, b2, b3, final, grads):
    row_count, width = final.shape
    pick = (iota((row_count, row_count), 0) == anchor[...]).astype(F32).T.astype(BF)
    rows = jnp.concatenate([b[...] for b in (b0, b1, b2, b3)], 0)
    total = dot(pick, rows).astype(BF)
    final[...] = total[:, :width]
    grads[...] = total[:, width:]


def on_device(
    tokens,
    cotangent,
    gain_attn,
    w_qkv,
    w_out,
    gain_ffn,
    w_router,
    w_shared_gate,
    w_shared_up,
    w_shared_down,
    routed_gate_weight,
    routed_up_weight,
    w_expert_down,
    seq_lengths,
    token_order,
    inverse_order,
    routes,
    fill_order,
):
    devices_dp = lax.axis_size(DP)
    devices_tp = lax.axis_size(TP)
    dz = lax.axis_size("dz")
    row_count, width = tokens.shape
    block_rows = row_count // devices_dp
    shard_block = block_rows // devices_tp
    shard_rows = row_count // devices_tp
    half_rows = row_count // 2
    experts_all = w_router.shape[1]
    slot_rows = 4 * row_count // experts_all
    capacity = 5 * row_count * devices_dp // (2 * experts_all)
    inner = w_out.shape[0]
    heads = inner // HD
    per_dp = max(1, experts_all // devices_dp)
    copies = max(1, devices_dp // experts_all)
    sub = devices_tp // per_dp
    my_hi, my_lo = lax.axis_index("hi"), lax.axis_index("lo")
    my_z, my_y = lax.axis_index("dz"), lax.axis_index("dy")
    my_dp = my_z * 2 + my_y
    my_block = my_lo * 2 + my_hi
    pick = my_hi if per_dp == 2 else 0 * my_hi
    my_part = my_lo if per_dp == 2 else my_block
    part_rows = slot_rows // sub
    own_slots = devices_dp * part_rows
    all_slots = own_slots * sub
    my_expert = my_dp // copies * per_dp + pick
    chunk = width // devices_dp
    z_bits = [(my_z >> i) & 1 for i in range(log2(dz))]
    info = jnp.stack([my_block, pick, my_part, my_expert, my_dp, my_y] + z_bits).astype(I32)
    pieces = devices_dp if devices_dp <= 8 else 1

    small = all_slots <= 1024

    def fetch(weights, deps=()):
        return kernel(
            fetch_body,
            [out(w.shape, w.dtype) for w in weights],
            *[Held(w) for w in weights],
            semaphores=len(weights),
            deps=deps,
        )

    table = rope_table(row_count)
    gain_attn = gain_attn[None]
    gain_ffn = gain_ffn[None]

    half_shard = out((shard_rows // 2, 2 * width), BF)
    shard_pieces = [out((shard_rows // pieces, 2 * width), BF)] * pieces
    *sent, anchor = kernel(
        functools.partial(select_body, shard_block, devices_dp),
        shard_pieces + [out((1, row_count), I32)],
        Far(inverse_order[None]),
        Far(tokens),
        Far(cotangent),
        scalars=(info,),
    )

    def blocks_of(own, deps):
        (by_hi,) = kernel(join_body, [out(own.shape, BF)], swap(own, "hi"), deps=deps)
        by_lo = swap(own, "lo")
        return (own, by_hi, by_lo, swap(by_hi, "lo"))

    def z_steps(parts):
        got = list(parts)
        for k in (2, 3, 1):
            got[k] = lax.ppermute(parts[k], "dz", [(i, i ^ k) for i in range(dz)])
        return got

    def exchange_halves(near, far, deps=()):
        width_sent = near.shape[1]
        block = near.shape[0] // dz
        if devices_dp != 8:
            both_halves = jnp.stack([near, far]).reshape(2, dz, block, width_sent)
            stacked = both_halves.transpose(1, 0, 2, 3).reshape(devices_dp, block, width_sent)
            return [exchange_stacked(stacked).reshape(devices_dp * block, width_sent)]
        middle = kernel(
            functools.partial(middle_body, block),
            [out((2 * block, width_sent), BF)] * dz,
            near,
            swap(far, "dy"),
            deps=deps,
        )
        return z_steps(middle)

    def join(parts, deps=()):
        if not isinstance(parts, (list, tuple)):
            parts = [parts]
        if not small:
            return jnp.concatenate(parts, 0)
        rows = sum(part.shape[0] for part in parts)
        return kernel(join_body, [out((rows, parts[0].shape[1]), BF)], *parts, deps=deps)[0]

    slot_pick, slot_pick_t, bias, cosine, sine, meta = kernel(
        functools.partial(index_body, shard_block, copies, per_dp, part_rows, experts_all),
        [
            out((own_slots, row_count), BF),
            out((row_count, own_slots), BF),
            out((row_count, row_count), BF),
            out((row_count, HD), F32),
            out((row_count, HD), F32),
            out((row_count, 128), BF),
        ],
        Far(token_order[None]),
        Far(routes.T),
        Far(fill_order),
        Far(table),
        scalars=(info, seq_lengths),
        vmem=24,
    )
    router = w_router.T
    w_in_t, w_out = fetch([w_qkv.T, w_out], (slot_pick,))
    blocks = blocks_of(join(exchange(sent)), (slot_pick, w_in_t))

    slot_piece = own_slots // pieces
    near_pieces = pieces // 2 if small else pieces
    packed_width = 2 * width + 128
    got_grads = []
    if small:
        sent_grads = kernel(
            functools.partial(send_grads_body, near_pieces * slot_piece),
            [out((slot_piece, width + 128), BF)] * (pieces - near_pieces),
            slot_pick,
            meta,
            *blocks,
        )
        got_grads = exchange_some(dict(enumerate(sent_grads, near_pieces)))

    keep, *send, qkv, mixed, normed_attn, weights = kernel(
        functools.partial(attend_body, heads),
        [
            out((half_rows, width), F32),
            *[out((half_rows // 4, width), BF)] * 4,
            out((row_count, 3 * inner), BF),
            out((row_count, inner), BF),
            out((row_count, width), BF),
            out((heads, row_count, row_count), F32),
        ],
        gain_attn,
        w_in_t,
        w_out,
        cosine,
        sine,
        bias,
        *blocks,
        vmem=24,
    )

    def half_sum(keep, send, deps=()):
        (half,) = kernel(
            fold_body,
            [out((half_rows, width), BF)],
            keep,
            *[swap(piece, "lo") for piece in send],
            deps=deps,
        )
        return half, swap(half, "hi")

    half, half_got = half_sum(keep, send, got_grads[:1])
    fetched = [w_shared_gate, w_shared_up, w_shared_down, router]
    if small:
        fetched += [routed_gate_weight, routed_up_weight, w_expert_down]
    fetched = fetch(fetched, (half,))
    w_shared_gate, w_shared_up, w_shared_down, router = fetched[:4]
    if small:
        routed_gate_weight, routed_up_weight, w_expert_down = fetched[4:]
    after_attn, normed_own = kernel(
        norm_body,
        [out((half_rows, width), F32), out((half_rows, width), BF)],
        gain_ffn,
        half,
        half_got,
        blocks[0],
        blocks[1],
        deps=got_grads[1:3] + [router],
    )
    normed_got = swap(normed_own, "lo")

    far_piece = out((slot_piece, width), BF)
    sent_rows = kernel(
        send_body,
        [out((slot_piece, packed_width), BF)] * near_pieces + [far_piece] * (pieces - near_pieces),
        slot_pick,
        normed_own,
        normed_got,
        meta,
        *blocks,
    )
    got_rows = exchange(sent_rows)

    def sub_gather(parts, deps=()):
        values = join(parts, deps)
        if sub == 4:
            values = jnp.concatenate([values, swap(values, "hi")], 0)
        return values, swap(values, "lo")

    units = w_shared_gate.shape[1]
    shared_part, shared_back, grad_sgate, grad_sup, shared_hidden = kernel(
        shared_body,
        [
            out((row_count, width), F32),
            out((row_count, width), F32),
            out((row_count, units), BF),
            out((row_count, units), BF),
            out((row_count, units), BF),
        ],
        normed_own,
        normed_got,
        *blocks,
        w_shared_gate,
        w_shared_up,
        w_shared_down,
        deps=sent_rows[:1],
        vmem=24,
    )
    def tree_outs(columns_a, columns_b):
        return [
            out((dz, chunk, columns), dtype)
            for dtype in (F32, BF)
            for columns in (columns_a, columns_b)
        ]

    shared_tree = kernel(
        shared_grads_body,
        tree_outs(3 * units // 2, 3 * units // 2),
        normed_own,
        normed_got,
        *blocks,
        grad_sgate,
        grad_sup,
        shared_hidden,
        scalars=(info,),
        vmem=24,
    )

    def z_swap(values, bit):
        return lax.ppermute(values, "dz", [(i, i ^ (1 << bit)) for i in range(dz)])

    def tree_first(parts):
        keep_a, keep_b, send_a, send_b = parts
        return keep_a, swap(send_a, "dy"), keep_b, z_swap(send_b, 0)

    def tree_second(parts, deps=()):
        kept_a, got_a, kept_b, got_b = parts
        shapes = [
            out((dz // 2, chunk, kept.shape[2]), dtype)
            for dtype in (F32, BF)
            for kept in (kept_a, kept_b)
        ]
        keep_a, keep_b, send_a, send_b = kernel(
            tree_second_body, shapes, kept_a, got_a, kept_b, got_b, scalars=(info,), deps=deps
        )
        return (keep_a, z_swap(send_a, 0), keep_b, swap(send_b, "dy")), send_b

    def tree_third(parts, deps=()):
        columns = parts[0].shape[2] + parts[2].shape[2]
        shape = (dz // 4, chunk, columns)
        keep, send = kernel(
            tree_third_body,
            [out(shape, F32), out(shape, BF)],
            *parts,
            scalars=(info,),
            deps=deps,
        )
        sent, got = send, z_swap(send, 1)
        for bit in range(2, log2(dz)):
            shape = (keep.shape[0] // 2, chunk, columns)
            keep, send = kernel(
                functools.partial(tree_body, Z_BITS + bit),
                [out(shape, F32), out(shape, BF)],
                keep,
                got,
                scalars=(info,),
            )
            got = z_swap(send, bit)
        return keep, got, sent

    shared_tree = tree_first(shared_tree)
    if small:
        (packed_own,) = kernel(
            functools.partial(join_packed_body, near_pieces),
            [out((own_slots, packed_width), BF)],
            *got_rows,
            *got_grads,
            deps=(shared_tree[0],),
        )
        packed_got = swap(packed_own, "lo")
    else:
        packed_own, packed_got = sub_gather(got_rows)
    (marks,) = kernel(
        functools.partial(
            meta_body, devices_dp, part_rows, sub, capacity, 2 * width if small else 0
        ),
        [out((all_slots, 128), F32)],
        packed_own if small else packed_own[:, 2 * width :],
        packed_got if small else packed_got[:, 2 * width :],
        scalars=(info,),
    )

    hidden_units = routed_gate_weight.shape[1]
    tile = min(256, own_slots)
    tiles = all_slots // 2 // tile
    steps = 2 * tiles

    def mine_at(i):
        return (jnp.minimum(i, tiles - 1), 0)

    def other_at(i):
        return (jnp.maximum(i - tiles, 0), 0)

    def every_at(i):
        return (i, 0)

    def fixed_at(i):
        return (0, 0)

    half_slots = all_slots // 2
    expert_ins = [
        (packed_own, pl.BlockSpec((tile, packed_width), mine_at)),
        (packed_got, pl.BlockSpec((tile, packed_width), other_at)),
        (marks, pl.BlockSpec((tile, 128), every_at)),
        (router, pl.BlockSpec((experts_all, width), fixed_at)),
        (routed_gate_weight, pl.BlockSpec((width, hidden_units), fixed_at)),
        (routed_up_weight, pl.BlockSpec((width, hidden_units), fixed_at)),
        (w_expert_down, pl.BlockSpec((hidden_units, width), fixed_at)),
    ]
    expert_outs = [
        (out((half_slots, 2 * width), BF), pl.BlockSpec((tile, 2 * width), mine_at)),
        (out((half_slots, 2 * width), BF), pl.BlockSpec((tile, 2 * width), other_at)),
        (out((all_slots, width), BF), pl.BlockSpec((tile, width), every_at)),
        (out((all_slots, hidden_units), BF), pl.BlockSpec((tile, hidden_units), every_at)),
        (out((all_slots, hidden_units), BF), pl.BlockSpec((tile, hidden_units), every_at)),
        (out((all_slots, hidden_units), BF), pl.BlockSpec((tile, hidden_units), every_at)),
        (out((all_slots, width), BF), pl.BlockSpec((tile, width), every_at)),
        (out((half_slots, 128), F32), pl.BlockSpec((tile, 128), mine_at)),
        (out((experts_all, width), F32), pl.BlockSpec((experts_all, width), fixed_at)),
    ]

    def expert_kernel(*refs):
        pltpu.emit_pipeline(
            functools.partial(expert_body, tiles),
            grid=(steps,),
            in_specs=[spec for _, spec in expert_ins],
            out_specs=[spec for _, spec in expert_outs],
        )(*refs)

    expert_args = [value for value, _ in expert_ins]
    expert_shapes = [shape for shape, _ in expert_outs]
    if small:
        piece = out((half_slots // SENT_PIECES, width), BF)
        results = kernel(
            functools.partial(expert_whole_body, tile),
            [out((half_slots, width), BF)] * 2 + [piece] * 2 * SENT_PIECES + expert_shapes[2:],
            *expert_args,
            vmem=24,
        )
        keep, part_keep, *results = results
        send, part_send = results[:SENT_PIECES], results[SENT_PIECES : 2 * SENT_PIECES]
        results = [keep, send] + list(results[2 * SENT_PIECES :])
    else:
        hbm_spec = pl.BlockSpec(memory_space=pltpu.HBM)
        results = pl.pallas_call(
            expert_kernel,
            in_specs=[hbm_spec] * len(expert_ins),
            out_specs=tuple([hbm_spec] * len(expert_outs)),
            out_shape=tuple(at_hbm(shape) for shape in expert_shapes),
            compiler_params=pltpu.CompilerParams(vmem_limit_bytes=44 * MIB),
            cost_estimate=COST,
            name="expert_body",
        )(*[in_hbm(value) for value in expert_args])
    (
        keep,
        send,
        rows_all,
        expert_hidden,
        grad_egate,
        grad_eup,
        pair_grads,
        gates,
        router_part,
    ) = results

    def sub_scatter(keep, send):
        total = keep.astype(F32) + swap(send, "lo").astype(F32)
        return total[:own_slots] + swap(total[own_slots:].astype(BF), "hi").astype(F32)

    if small:
        got = [swap(piece, "lo") for piece in send]
        part_got = [swap(piece, "lo") for piece in part_send]
        back_far = kernel(
            add_far_body,
            [far_piece] * (pieces - near_pieces),
            keep,
            *got[SENT_PIECES // 2 :],
            deps=(shared_tree[1], shared_tree[3]),
        )
        back_near = kernel(
            add_near_body,
            [out((slot_piece, 2 * width), BF)] * near_pieces,
            keep,
            part_keep,
            gates,
            *got[: SENT_PIECES // 2],
            *part_got[: SENT_PIECES // 2],
        )
        sent_back = list(back_near) + list(back_far)
        sent_parts = kernel(
            part_far_body,
            [far_piece] * (pieces - near_pieces),
            part_keep,
            gates,
            *part_got[SENT_PIECES // 2 :],
            deps=sent_back[:1],
        )
    else:
        total = sub_scatter(keep, send)
        sent_back = [total[:, :width].astype(BF)]
        sent_parts = [(gates[:own_slots, :1] * total[:, width:]).astype(BF)]
        shared_tree, _ = tree_second(shared_tree)

    def weight_grad(left, right, deps=()):
        if not small:
            return dot_t(left, right)
        shape = (left.shape[1], right.shape[1])
        vmem_spec = pl.BlockSpec(memory_space=pltpu.VMEM)
        return pl.pallas_call(
            lambda *refs: weight_grad_body(refs[0], refs[1], *refs[-3:]),
            out_shape=pltpu.HBM(shape, F32),
            in_specs=[vmem_spec] * 2 + [pl.BlockSpec(memory_space=pl.ANY)] * len(deps),
            out_specs=pl.BlockSpec(memory_space=pltpu.HBM),
            scratch_shapes=[
                pltpu.VMEM(shape, F32),
                pltpu.SemaphoreType.DMA((shape[0] // 256,)),
            ],
            compiler_params=pltpu.CompilerParams(vmem_limit_bytes=12 * MIB),
            cost_estimate=COST,
            name="weight_grad",
        )(in_vmem(left), in_vmem(right), *deps)

    grad_w_expert_gate = weight_grad(rows_all, grad_egate, (sent_back[0],))
    got_back = exchange(sent_back)
    if small:
        got_parts = exchange_some(dict(enumerate(sent_parts, near_pieces)))
        shared_tree, _ = tree_second(shared_tree, sent_back[:1])
    else:
        got_parts = exchange(sent_parts)
    shared_keep, shared_got, shared_sent = tree_third(shared_tree)

    keep, *send = kernel(
        combine_body,
        [out((half_rows, width), F32)] + [out((half_rows // 4, width), BF)] * 4,
        slot_pick_t,
        shared_back,
        *got_back,
        deps=(
            Far(grad_w_expert_gate),
        ),
    )
    half, half_got = half_sum(keep, send, got_parts[:1] if small else ())

    def own_sum(keep, send, deps=()):
        own, send = kernel(
            fold_own_body,
            [out((shard_rows, width), F32), out((shard_rows, width), BF)],
            keep,
            swap(send, "lo"),
            deps=deps,
        )
        return own, send

    after_grad, after_grad_own, gain_ffn_part = kernel(
        norm_back_body,
        [out((half_rows, width), F32), out((half_rows, width), BF), out((8, width), F32)],
        gain_ffn,
        half,
        half_got,
        after_attn,
        blocks[0],
        blocks[1],
        deps=got_parts[1:3] + [shared_tree[1], shared_tree[3]] if small else (),
    )
    after_grad_got = swap(after_grad_own, "lo")

    keep, send, projected_grad, gain_attn_part = kernel(
        functools.partial(attend_back_body, heads),
        [
            out((half_rows, width), F32),
            out((half_rows, width), BF),
            out((row_count, 3 * inner), BF),
            out((8, width), F32),
        ],
        w_out,
        w_in_t,
        cosine,
        sine,
        weights,
        qkv,
        after_grad_own,
        after_grad_got,
        *blocks,
        vmem=24,
    )
    if small:
        keep, send = kernel(
            functools.partial(result_body, slot_piece),
            [out((half_rows, 2 * width), F32), out((half_rows, 2 * width), BF)],
            slot_pick_t,
            shared_part,
            keep,
            send,
            *got_back[:near_pieces],
            *got_parts,
        )
    else:
        result_part = shared_part + dot(slot_pick_t, got_parts[0])
        keep = jnp.concatenate([result_part[:half_rows], keep], 1)
        send = jnp.concatenate([result_part[half_rows:].astype(BF), send], 1)
    bottom_got = swap(send, "lo")
    last_columns = 4 * inner + 128
    last_tree = kernel(
        functools.partial(last_grads_body, experts_all),
        tree_outs(512, last_columns - 512),
        normed_attn,
        projected_grad,
        after_grad_own,
        after_grad_got,
        mixed,
        gain_ffn_part,
        gain_attn_part,
        router_part,
        scalars=(info,),
        vmem=24,
        deps=(send,),
    )
    last_tree = tree_first(last_tree)
    own, send = kernel(
        fold_own_body,
        [out((shard_rows, 2 * width), F32), out((shard_rows, 2 * width), BF)],
        keep,
        bottom_got,
    )
    grad_sgate, grad_sup, grad_sdown = kernel(
        shared_end_body,
        [Far(out((chunk, units), F32))] * 3,
        shared_keep,
        shared_got,
    )
    near, far = kernel(
        functools.partial(last_body, shard_block),
        [half_shard, half_shard],
        gain_attn,
        own,
        swap(send, "hi"),
        blocks[0],
        after_grad,
        after_attn,
    )
    last_tree, last_sent = tree_second(last_tree, (near,))
    grad_w_expert_down = weight_grad(expert_hidden, pair_grads, (last_sent,))
    got_last = exchange_halves(near, far, (last_sent,))
    last_keep, last_got, last_sent = tree_third(last_tree, got_last[:1])
    small_rows = experts_all + 8
    grad_qkv, grad_out, sums = kernel(
        functools.partial(last_end_body, small_rows),
        [
            Far(out((chunk, 3 * inner), F32)),
            Far(out((inner, chunk), F32)),
            out((small_rows, chunk), F32),
        ],
        last_keep,
        last_got,
    )
    got_last = join(got_last, (last_sent, Far(grad_sgate), Far(grad_w_expert_down)))
    grad_w_expert_up = weight_grad(rows_all, grad_eup, (got_last,))
    final, grad_tokens = kernel(
        return_body,
        [Far(out((row_count, width), BF)), Far(out((row_count, width), BF))],
        anchor,
        *blocks_of(got_last, (sums, Far(grad_w_expert_up))),
    )

    gain_ffn_sum, gain_attn_sum, router_sum = kernel(
        small_end_body,
        [Far(out((1, chunk), F32)), Far(out((1, chunk), F32)), Far(out((experts_all, chunk), F32))],
        sums,
        *[lax.ppermute(sums, TP, [(i, i ^ k) for i in range(4)]) for k in (1, 2, 3)],
        deps=(Far(final),),
    )
    return (
        final,
        grad_tokens,
        gain_attn_sum.reshape(chunk),
        grad_qkv,
        grad_out,
        gain_ffn_sum.reshape(chunk),
        router_sum.T,
        grad_sgate,
        grad_sup,
        grad_sdown.T,
        grad_w_expert_gate,
        grad_w_expert_up,
        grad_w_expert_down,
    )


def solution(mesh):
    devices_dp, devices_tp = mesh.shape["dp"], mesh.shape["tensor"]
    fine = Mesh(
        mesh.devices.reshape(devices_dp // 2, 2, devices_tp // 2, 2), ("dz", "dy", "hi", "lo")
    )
    every = DP + TP
    return jax.shard_map(
        on_device,
        mesh=fine,
        in_specs=(
            P(DP, None),
            P(DP, None),
            P(),
            P(None, TP),
            P(TP, None),
            P(),
            P(),
            P(None, TP),
            P(None, TP),
            P(TP, None),
            P(None, every),
            P(None, every),
            P(every, None),
            P(DP, None),
            P(DP),
            P(DP),
            P(DP, None),
            P(DP, None),
        ),
        out_specs=(
            P(DP, None),
            P(DP, None),
            P(DP),
            P(DP, TP),
            P(TP, DP),
            P(DP),
            P(DP, None),
            P(DP, TP),
            P(DP, TP),
            P(TP, DP),
            P(None, every),
            P(None, every),
            P(every, None),
        ),
        check_vma=False,
    )
```

```python
import functools

import jax
import jax.numpy as jnp
import numpy as np
from jax import lax
from jax.experimental import pallas as pl
from jax.experimental.pallas import tpu as pltpu
from jax.sharding import Mesh, PartitionSpec as P

HD = 64
MY_BLOCK, PICK, MY_PART, MY_EXPERT, MY_DP, Y_BIT, Z_BITS = range(7)
EPSILON = 1e-06
BF = jnp.bfloat16
F32 = jnp.float32
I32 = jnp.int32
DP = ("dz", "dy")
TP = ("hi", "lo")
MIB = 1 << 20
SENT_PIECES = 4
COST = pl.CostEstimate(flops=1000, bytes_accessed=1000, transcendentals=0)


def dot(left, right):
    return jnp.dot(left, right, preferred_element_type=F32)


def dot_t(left, right):
    return lax.dot_general(left, right, (((0,), (0,)), ((), ())), preferred_element_type=F32)


def dot_bt(left, right):
    return lax.dot_general(left, right, (((1,), (1,)), ((), ())), preferred_element_type=F32)


def swap(values, axis):
    return lax.ppermute(values, axis, [(0, 1), (1, 0)])


def exchange_stacked(values):
    order = jnp.arange(values.shape[0], dtype=I32) ^ lax.axis_index(DP)
    got = lax.all_to_all(
        jnp.take(values, order, axis=0), DP, split_axis=0, concat_axis=0, tiled=True
    )
    return jnp.take(got, order, axis=0)


def exchange(pieces):
    devices = lax.axis_size(DP)
    if len(pieces) == 1:
        (values,) = pieces
        stacked = values.reshape(devices, -1, values.shape[-1])
        return [exchange_stacked(stacked).reshape(values.shape)]
    return exchange_some(dict(enumerate(pieces)))


def exchange_some(pieces):
    devices = lax.axis_size(DP)
    got = dict(pieces)
    for k in (4, 5, 6, 7, 2, 3, 1):
        if k in got:
            got[k] = lax.ppermute(pieces[k], DP, [(i, i ^ k) for i in range(devices)])
    return [got[k] for k in sorted(got)]


def out(shape, dtype):
    return jax.ShapeDtypeStruct(shape, dtype)


class Far:
    def __init__(self, value):
        self.value = value


class Held(Far):
    pass


class Free(Far):
    pass


class Arriving:
    def __init__(self, buffer, copy):
        self.buffer, self.copy, self.waiting = buffer, copy, True
        self.shape, self.dtype = buffer.shape, buffer.dtype

    def ready(self):
        if self.waiting:
            self.copy.wait()
            self.waiting = False

    def __getitem__(self, index):
        self.ready()
        return self.buffer[index]


class Leaving:
    def __init__(self, buffer, copy):
        self.buffer, self.copy, self.started = buffer, copy, False
        self.shape, self.dtype = buffer.shape, buffer.dtype

    def flush(self):
        if not self.started:
            self.copy.start()
            self.started = True

    def __getitem__(self, index):
        return self.buffer[index]

    def __setitem__(self, index, value):
        self.buffer[index] = value


def in_hbm(values):
    return pltpu.with_memory_space_constraint(values, pltpu.HBM)


def in_vmem(values):
    if values.size * values.dtype.itemsize > 4 * MIB:
        return values
    return pltpu.with_memory_space_constraint(values, pltpu.VMEM)


def at_hbm(shape):
    return pltpu.HBM(shape.shape, shape.dtype)


def at_vmem(shape):
    if shape.size * shape.dtype.itemsize > 4 * MIB:
        return shape
    return pltpu.VMEM(shape.shape, shape.dtype)


def kernel(body, outs, *args, scalars=(), deps=(), vmem=16, semaphores=0):
    vmem_spec = pl.BlockSpec(memory_space=pltpu.VMEM)
    hbm_spec = pl.BlockSpec(memory_space=pltpu.HBM)
    any_spec = pl.BlockSpec(memory_space=pl.ANY)
    held = [isinstance(a, Held) for a in args]
    far_in = [isinstance(a, Far) and not h for a, h in zip(args, held)]
    free_out = [isinstance(o, Free) for o in outs]
    far_out = [isinstance(o, Far) and not f for o, f in zip(outs, free_out)]
    args = [in_hbm(a.value) if isinstance(a, Far) else in_vmem(a) for a in args]
    outs = [
        o.value if f else at_hbm(o.value) if h else at_vmem(o)
        for o, f, h in zip(outs, free_out, far_out)
    ]
    deps = [in_hbm(d.value) if isinstance(d, Far) else d for d in deps]
    moved = [x for x, f in zip(args + outs, far_in + far_out) if f]
    scratch = [pltpu.VMEM(x.shape, x.dtype) for x in moved]
    if moved:
        scratch.append(pltpu.SemaphoreType.DMA((len(moved),)))
    if semaphores:
        scratch.append(pltpu.SemaphoreType.DMA((semaphores,)))
    n_scalars, n_args, n_deps, n_outs = len(scalars), len(args), len(deps), len(outs)

    def wrapped(*refs):
        ins = list(refs[: n_scalars + n_args])
        results = list(refs[n_scalars + n_args + n_deps :][:n_outs])
        buffers = refs[n_scalars + n_args + n_deps + n_outs :]
        extra = buffers[-1:] if semaphores else ()
        buffers = buffers[:-1] if semaphores else buffers
        at = 0
        for i, far in enumerate(far_in):
            if far:
                ref = ins[n_scalars + i]
                copy = pltpu.make_async_copy(ref, buffers[at], buffers[-1].at[at])
                copy.start()
                ins[n_scalars + i] = Arriving(buffers[at], copy)
                at += 1
        for i, far in enumerate(far_out):
            if far:
                copy = pltpu.make_async_copy(buffers[at], results[i], buffers[-1].at[at])
                results[i] = Leaving(buffers[at], copy)
                at += 1
        body(*ins, *results, *extra)
        for ref in ins:
            if isinstance(ref, Arriving):
                ref.ready()
        for ref in results:
            if isinstance(ref, Leaving):
                ref.flush()
        for ref in results:
            if isinstance(ref, Leaving):
                ref.copy.wait()

    return pl.pallas_call(
        wrapped,
        out_shape=tuple(outs),
        in_specs=[pl.BlockSpec(memory_space=pltpu.SMEM)] * n_scalars
        + [hbm_spec if f or h else vmem_spec for f, h in zip(far_in, held)]
        + [any_spec] * n_deps,
        out_specs=tuple(hbm_spec if far else vmem_spec for far in far_out),
        scratch_shapes=scratch,
        compiler_params=pltpu.CompilerParams(vmem_limit_bytes=vmem * MIB),
        cost_estimate=COST,
        name=body.func.__name__ if isinstance(body, functools.partial) else body.__name__,
    )(*scalars, *args, *deps)


def tie(values, *deps):
    any_spec = pl.BlockSpec(memory_space=pl.ANY)
    vmem_spec = pl.BlockSpec(memory_space=pltpu.VMEM)
    return pl.pallas_call(
        lambda *refs: None,
        out_shape=out(values.shape, values.dtype),
        in_specs=[vmem_spec] + [any_spec] * len(deps),
        out_specs=vmem_spec,
        input_output_aliases={0: 0},
        cost_estimate=COST,
        name="tie",
    )(in_vmem(values), *[in_hbm(d.value) if isinstance(d, Far) else d for d in deps])


def rope_table(places):
    exponent = np.arange(HD // 2, dtype=np.float32) * np.float32(-2.0 / HD)
    angles = np.arange(places, dtype=np.float32)[:, None] * np.power(np.float32(10000.0), exponent)
    cosine = np.cos(angles.astype(np.float64)).astype(np.float32)
    sine = np.sin(angles.astype(np.float64)).astype(np.float32)
    rest = np.concatenate([cosine, cosine, -sine, sine], 1)
    terms = []
    for _ in range(3):
        terms.append(rest.astype(BF))
        rest = rest - terms[-1].astype(np.float32)
    return jnp.asarray(np.concatenate(terms, 1))


def iota(shape, dim):
    return lax.broadcasted_iota(I32, shape, dim)


def log2(number):
    return number.bit_length() - 1


def silu_parts(gate_in):
    sigmoid_val = 1.0 / (1.0 + jnp.exp(-gate_in))
    return (gate_in * sigmoid_val, sigmoid_val * (1.0 + gate_in * (1.0 - sigmoid_val)))


def inverse_root(values):
    return lax.rsqrt(jnp.mean(values * values, -1, keepdims=True) + EPSILON)


def rms_backward(values, root, gain, grad_normed):
    scaled = grad_normed * gain
    return root * scaled - values * (root * root * root) * jnp.mean(
        scaled * values, -1, keepdims=True
    )


def lane_rank(buckets, bucket_count):
    count = buckets.shape[1]
    rows = max(8, bucket_count)
    member = (iota((rows, count), 0) == buckets).astype(F32)
    earlier = (iota((count, count), 0) < iota((count, count), 1)).astype(F32).astype(BF)
    return jnp.sum(dot(member.astype(BF), earlier) * member, 0, keepdims=True).astype(I32)


def relative_row(block, rank, my_block, shard_block, shard_rows):
    shift = log2(shard_block)
    return (
        ((rank >> shift) ^ my_block) * shard_rows
        + block * shard_block
        + (rank & (shard_block - 1))
    )


def rope_back(grads, cosine, sine):
    return grads * cosine - half_turned(grads) * sine


def store_pieces(refs, value):
    rows = refs[0].shape[0]
    for i, ref in enumerate(refs):
        ref[...] = value[i * rows : (i + 1) * rows]


def joined(refs):
    return jnp.concatenate([ref[...] for ref in refs], 0) if len(refs) > 1 else refs[0][...]


def join_body(*refs):
    *parts, whole = refs
    rows = parts[0].shape[0]
    for i, ref in enumerate(parts):
        whole[i * rows : (i + 1) * rows, :] = ref[...]


def middle_body(block, near, far, *outs):
    for i, ref in enumerate(outs):
        ref[:block, :] = near[i * block : (i + 1) * block, :]
        ref[block:, :] = far[i * block : (i + 1) * block, :]


def store_halves(near, far, block, value, columns):
    for i in range(near.shape[0] // block):
        at = 2 * i * block
        near[i * block : (i + 1) * block, columns] = value[at : at + block]
        far[i * block : (i + 1) * block, columns] = value[at + block : at + 2 * block]


def fetch_body(*refs):
    *refs, semaphores = refs
    count = len(refs) // 2
    copies = [
        pltpu.make_async_copy(refs[i], refs[count + i], semaphores.at[i]) for i in range(count)
    ]
    for copy in copies:
        copy.start()
    for copy in copies:
        copy.wait()


def select_body(shard_block, blocks, info, inverse, tokens, cotangent, *refs):
    *sent, anchor = refs
    row_count, width = tokens.shape
    shard_rows = shard_block * blocks
    target = (inverse[...] >> log2(row_count)) ^ info[MY_DP]
    row = relative_row(target, lane_rank(target, blocks), info[MY_BLOCK], shard_block, shard_rows)
    anchor[...] = row
    pick = (iota((shard_rows, row_count), 0) == row).astype(F32).astype(BF)
    rows = jnp.concatenate([dot(pick, tokens[...]), dot(pick, cotangent[...])], 1)
    store_pieces(sent, rows.astype(BF))


def index_body(
    shard_block,
    copies,
    per_dp,
    part_rows,
    experts_all,
    info,
    lengths,
    order,
    routes,
    fill,
    table,
    slot_pick,
    slot_pick_t,
    bias,
    cosine,
    sine,
    meta,
):
    row_count = order.shape[1]
    devices_dp = slot_pick.shape[0] // part_rows
    shard_rows = shard_block * devices_dp
    source = (order[...] >> log2(row_count)) ^ info[MY_DP]
    local = relative_row(
        source, lane_rank(source, devices_dp), info[MY_BLOCK], shard_block, shard_rows
    )
    place_pick = (iota((row_count, row_count), 0) == local).astype(F32).astype(BF)
    lanes = iota((1, row_count), 1)
    segment = jnp.zeros((1, row_count), I32)
    start = jnp.zeros((1, row_count), I32)
    end = jnp.int32(0)
    for entry in range(lengths.shape[1]):
        end = end + lengths[0, entry]
        passed = lanes >= end
        segment = segment + passed.astype(I32)
        start = jnp.maximum(start, jnp.where(passed, end, 0))
    place = lanes - start
    expert_sum = routes[0:1, :] + routes[1:2, :] + 1
    facts = jnp.concatenate(
        [segment, place >> 1, place & 1, expert_sum, jnp.zeros((4, row_count), I32)], 0
    )
    facts = facts.astype(F32).astype(BF)
    across = dot_bt(facts, place_pick)
    down = dot_bt(place_pick, facts)
    place_row = 2.0 * across[1:2] + across[2:3]
    place_col = 2.0 * down[:, 1:2] + down[:, 2:3]
    allowed = (down[:, 0:1] == across[0:1]) & (place_row <= place_col)
    bias[...] = jnp.where(allowed, 0.0, -1e30).astype(BF)
    at_place = (
        iota((row_count, row_count), 1).astype(F32) == place_col
    ).astype(F32).astype(BF)
    turned = dot(at_place, table[...])
    pieces = [turned[:, i * 128 : (i + 1) * 128] for i in range(3)]
    turned = pieces[0] + pieces[1] + pieces[2]
    cosine[...] = turned[:, :HD]
    sine[...] = turned[:, HD:]
    meta[...] = jnp.broadcast_to(down[:, 3:4], meta.shape).astype(BF)
    pairs = 2 * row_count
    fill_at = (fill[...] & 1) * row_count + (fill[...] >> 1)
    fill_pick = (iota((pairs, pairs), 0) == fill_at).astype(F32).astype(BF)
    expert_rows = max(16, experts_all)
    pair_expert = jnp.concatenate([routes[0:1, :], routes[1:2, :]], 1)
    named = (iota((expert_rows, pairs), 0) == pair_expert).astype(F32).astype(BF)
    member = dot(named, fill_pick)
    earlier = (iota((pairs, pairs), 0) < iota((pairs, pairs), 1)).astype(F32).astype(BF)
    ranks = (member * (dot(member.astype(BF), earlier) + 1.0)).astype(BF)
    ranks = dot_bt(ranks, fill_pick)
    ranks = (ranks[:, :row_count] + ranks[:, row_count:]).astype(BF)
    ranks = dot_bt(ranks, place_pick).astype(I32)
    slots = iota((part_rows, row_count), 0) + (info[MY_PART] * part_rows + 1)
    experts = iota((expert_rows, row_count), 0)
    for target in range(devices_dp):
        expert = ((target ^ info[MY_DP]) >> log2(copies)) * per_dp + info[PICK]
        chosen = jnp.sum(jnp.where(experts == expert, ranks, 0), 0, keepdims=True)
        picked = (slots == chosen).astype(F32)
        slot_pick[target * part_rows : (target + 1) * part_rows, :] = picked.astype(BF)
    slot_pick_t[...] = slot_pick[...].astype(F32).T.astype(BF)


def head_parts(projected, heads):
    return [
        [projected[:, (3 * h + i) * HD : (3 * h + i + 1) * HD] for i in range(3)]
        for h in range(heads)
    ]


def half_turned(values):
    half = values.shape[1] // 2
    return jnp.concatenate([values[:, half:], values[:, :half]], 1)


def attend_body(
    heads,
    gain,
    w_in_t,
    w_out,
    cosine,
    sine,
    bias,
    b0,
    b1,
    b2,
    b3,
    keep,
    *refs,
):
    *send, qkv, mixed, normed, weights_all = refs
    width = b0.shape[1] // 2
    half = keep.shape[0]
    tokens = jnp.concatenate([b[:, :width] for b in (b0, b1, b2, b3)], 0).astype(F32)
    normed[...] = (tokens * inverse_root(tokens) * gain[...]).astype(BF)
    projected = dot_bt(normed[...], w_in_t[...])
    cosine, sine = cosine[...], sine[...]
    parts = []
    for query, keys, values in head_parts(projected, heads):
        parts.append((query * cosine + half_turned(query) * sine).astype(BF))
        parts.append((keys * cosine + half_turned(keys) * sine).astype(BF))
        parts.append(values.astype(BF))
    qkv[...] = jnp.concatenate(parts, 1)
    scale = HD**-0.5
    mixed_heads = []
    for head, (query, keys, values) in enumerate(head_parts(qkv, heads)):
        scores = dot_bt(query, keys) * scale + bias[...].astype(F32)
        powers = jnp.exp(scores - jnp.max(scores, -1, keepdims=True))
        weights = powers * (1.0 / jnp.sum(powers, -1, keepdims=True))
        weights_all[head] = weights
        mixed_heads.append(dot(weights.astype(BF), values))
    mixed[...] = jnp.concatenate(mixed_heads, 1).astype(BF)
    part = dot(mixed[...], w_out[...])
    keep[...] = part[:half]
    store_pieces(send, part[half:].astype(BF))


def fold_body(keep, *refs):
    *got, half = refs
    half[...] = (keep[...] + joined(got).astype(F32)).astype(BF)


def fold_own_body(keep, got, own, send):
    rows = own.shape[0]
    own[...] = keep[:rows, :] + got[:rows, :].astype(F32)
    send[...] = (keep[rows:, :] + got[rows:, :].astype(F32)).astype(BF)


def both(half, got):
    rows = half.shape[0] // 2
    mine, other = half[...].astype(F32), got[...].astype(F32)
    return mine + jnp.concatenate([other[rows:], other[:rows]], 0)


def norm_body(gain, half, got, b0, b1, after_attn, normed):
    width = half.shape[1]
    balanced = jnp.concatenate([b0[:, :width], b1[:, :width]], 0).astype(F32)
    values = balanced + both(half, got)
    after_attn[...] = values
    normed[...] = (values * inverse_root(values) * gain[...]).astype(BF)


def send_body(slot_pick, own, got, meta, b0, b1, b2, b3, *sent):
    width = own.shape[1]
    rows = jnp.concatenate([own[...], got[...]], 0)
    rows = dot(slot_pick[...], rows).astype(BF)
    count = sent[0].shape[0]
    near = sum(ref.shape[1] > width for ref in sent) * count
    grads = jnp.concatenate([b[:, width:] for b in (b0, b1, b2, b3)], 0)
    grads = jnp.concatenate([grads, meta[...]], 1)
    grads = dot(slot_pick[:near, :], grads).astype(BF)
    for i, ref in enumerate(sent):
        at = slice(i * count, (i + 1) * count)
        ref[:, :width] = rows[at]
        if ref.shape[1] > width:
            ref[:, width:] = grads[at]


def send_grads_body(first, slot_pick, meta, b0, b1, b2, b3, *sent):
    width = b0.shape[1] // 2
    grads = jnp.concatenate([b[:, width:] for b in (b0, b1, b2, b3)], 0)
    grads = jnp.concatenate([grads, meta[...]], 1)
    store_pieces(sent, dot(slot_pick[first:, :], grads).astype(BF))


def join_packed_body(near, *refs):
    *parts, whole = refs
    count, width = parts[near].shape
    far = (len(parts) - near) // 2
    for i in range(near):
        whole[i * count : (i + 1) * count, :] = parts[i][...]
    for i in range(far):
        at = slice((near + i) * count, (near + i + 1) * count)
        whole[at, :width] = parts[near + i][...]
        whole[at, width:] = parts[near + far + i][...]


def shared_body(
    own, got, b0, b1, b2, b3, w_gate, w_up, w_down, part, back, grad_gate, grad_up, hidden
):
    width = own.shape[1]
    rows = jnp.concatenate([own[...], got[...]], 0)
    grads = jnp.concatenate([b[:, width:] for b in (b0, b1, b2, b3)], 0)
    gate = dot(rows, w_gate[...])
    up = dot(rows, w_up[...])
    act, slope = silu_parts(gate)
    hidden[...] = (act * up).astype(BF)
    part[...] = dot(hidden[...], w_down[...])
    hidden_grad = dot_bt(grads, w_down[...])
    grad_gate[...] = (hidden_grad * up * slope).astype(BF)
    grad_up[...] = (hidden_grad * act).astype(BF)
    back[...] = dot_bt(grad_gate[...], w_gate[...]) + dot_bt(grad_up[...], w_up[...])


def store_tree(info, sums, keeps, sends):
    chunk, columns = keeps[0].shape[1:]
    sides = ((sums[:, :columns], Y_BIT, 1), (sums[:, columns:], Z_BITS, 2))
    for (values, which, stride), keep, send in zip(sides, keeps, sends):
        mine = info[which] == 0
        for i in range(keep.shape[0]):
            at = (2 * i if stride == 1 else i // 2 * 4 + i % 2) * chunk
            first, second = values[at : at + chunk], values[at + stride * chunk :][:chunk]
            keep[i] = jnp.where(mine, first, second)
            send[i] = jnp.where(mine, second, first).astype(BF)


def shared_grads_body(
    info, own, got, b0, b1, b2, b3, grad_gate, grad_up, hidden, *refs
):
    width = own.shape[1]
    rows = jnp.concatenate([own[...], got[...]], 0)
    grads = jnp.concatenate([b[:, width:] for b in (b0, b1, b2, b3)], 0)
    sums = jnp.concatenate(
        [dot_t(rows, grad_gate[...]), dot_t(rows, grad_up[...]), dot_t(grads, hidden[...])], 1
    )
    store_tree(info, sums, refs[:2], refs[2:])


def halved(info, which, total, keep, send):
    mine = info[which] == 0
    for index in range(keep.shape[0]):
        first, second = total[2 * index], total[2 * index + 1]
        keep[index] = jnp.where(mine, first, second)
        send[index] = jnp.where(mine, second, first).astype(BF)


def tree_second_body(info, kept_a, got_a, kept_b, got_b, keep_a, keep_b, send_a, send_b):
    halved(info, Z_BITS, kept_a[...] + got_a[...].astype(F32), keep_a, send_a)
    halved(info, Y_BIT, kept_b[...] + got_b[...].astype(F32), keep_b, send_b)


def tree_third_body(info, kept_a, got_a, kept_b, got_b, keep, send):
    total = jnp.concatenate(
        [kept_a[...] + got_a[...].astype(F32), kept_b[...] + got_b[...].astype(F32)], 2
    )
    halved(info, Z_BITS + 1, total, keep, send)


def last_grads_body(
    experts, info, normed, projected_grad, own, got, mixed, gain_ffn, gain_attn, router, *refs
):
    width = normed.shape[1]
    small = jnp.concatenate(
        [
            router[:experts, :],
            gain_ffn[:1, :],
            gain_attn[:1, :],
            jnp.zeros((128 - experts - 2, width), F32),
        ],
        0,
    )
    grads = jnp.concatenate([own[...], got[...]], 0)
    sums = jnp.concatenate(
        [dot_t(normed[...], projected_grad[...]), dot_t(grads, mixed[...]), small.T], 1
    )
    store_tree(info, sums, refs[:2], refs[2:])


def tree_body(which, info, kept, got, keep, send):
    halved(info, which, kept[...] + got[...].astype(F32), keep, send)


def last_end_body(small_rows, kept, got, grad_qkv, grad_out, small):
    total = kept[0] + got[0].astype(F32)
    columns, inner = grad_qkv.shape[1], grad_out.shape[0]
    grad_qkv[...] = total[:, :columns]
    grad_out[...] = total[:, columns : columns + inner].T
    small[...] = total[:, columns + inner :].T[:small_rows]


def small_end_body(own, by_lo, by_hi, by_both, gain_ffn, gain_attn, router):
    experts = router.shape[0]
    total = (own[...] + by_lo[...]) + (by_hi[...] + by_both[...])
    router[...] = total[:experts]
    gain_ffn[...] = total[experts : experts + 1]
    gain_attn[...] = total[experts + 1 : experts + 2]


def shared_end_body(kept, got, grad_gate, grad_up, grad_down):
    total = kept[0] + got[0].astype(F32)
    units = grad_gate.shape[1]
    grad_gate[...] = total[:, :units]
    grad_up[...] = total[:, units : 2 * units]
    grad_down[...] = total[:, 2 * units :]


def add_far_body(keep, *refs):
    got, total = refs[: SENT_PIECES // 2], refs[SENT_PIECES // 2 :]
    half = keep.shape[0] // 2
    store_pieces(total, (keep[half:, :].astype(F32) + joined(got).astype(F32)).astype(BF))


def gated_parts(keep, got, gates):
    gate = jnp.concatenate([gates] * (keep.shape[1] // 128), 1)
    return (gate * (keep.astype(F32) + got.astype(F32))).astype(BF)


def add_near_body(keep, part_keep, gates, *refs):
    got, part_got, total = (
        refs[: SENT_PIECES // 2],
        refs[SENT_PIECES // 2 : SENT_PIECES],
        refs[SENT_PIECES:],
    )
    half, width = keep.shape[0] // 2, keep.shape[1]
    rows = (keep[:half, :].astype(F32) + joined(got).astype(F32)).astype(BF)
    parts = gated_parts(part_keep[:half, :], joined(part_got), gates[:half, :])
    count = total[0].shape[0]
    for i, ref in enumerate(total):
        at = slice(i * count, (i + 1) * count)
        ref[:count, :width] = rows[at]
        ref[:count, width:] = parts[at]


def part_far_body(keep, gates, *refs):
    got, total = refs[: SENT_PIECES // 2], refs[SENT_PIECES // 2 :]
    half = keep.shape[0] // 2
    store_pieces(total, gated_parts(keep[half:, :], joined(got), gates[half:, :]))


def weight_grad_body(left, right, total, sums, semaphores):
    tile = 256
    copies = []
    for i in range(left.shape[1] // tile):
        at = slice(i * tile, (i + 1) * tile)
        sums[at, :] = dot_t(left[:, at], right[...])
        copies.append(
            pltpu.make_async_copy(sums.at[at, :], total.at[at, :], semaphores.at[i])
        )
        copies[-1].start()
    for copy in copies:
        copy.wait()


def meta_body(devices_dp, part_rows, sub, capacity, width, info, own, got, marks):
    my_part, my_expert = info[MY_PART], info[MY_EXPERT]
    lanes = iota((part_rows, 128), 1)
    blocks = [(ref, at, part) for part, (ref, at) in enumerate(
        [(own, i) for i in range(sub // 2)] + [(got, i) for i in range(sub // 2)]
    )]
    counts = []
    for block in range(devices_dp):
        count = jnp.zeros((1, 128), F32)
        for ref, at, _ in blocks:
            start = (at * devices_dp + block) * part_rows
            value = ref[start : start + part_rows, width:].astype(F32)
            count = count + jnp.sum((value > 0.0).astype(F32), 0, keepdims=True)
        counts.append(count)
    for block in range(devices_dp):
        earlier = jnp.zeros((1, 128), F32)
        for before in range(devices_dp):
            ahead = (before ^ info[MY_DP]) < (block ^ info[MY_DP])
            earlier = earlier + jnp.where(ahead, counts[before], 0.0)
        for ref, at, part in blocks:
            start = (at * devices_dp + block) * part_rows
            value = ref[start : start + part_rows, width:].astype(F32)
            valid = value > 0.0
            slot = iota((part_rows, 128), 0) + (my_part ^ part) * part_rows
            kept = valid & (slot.astype(F32) + earlier < capacity)
            other = value.astype(I32) - 1 - my_expert
            mark = (lanes == my_expert).astype(F32) - (lanes == other).astype(F32)
            row = (part * devices_dp + block) * part_rows
            marks[row : row + part_rows, :] = jnp.where(
                lanes == 127, kept.astype(F32), jnp.where(valid, mark, 0.0)
            )


def expert_step(packed, mark, w_router, w_gate, w_up, w_down, stores):
    hidden_out, grad_gate_out, grad_up_out, pair_out = stores
    width = w_gate.shape[0]
    rows, grads = packed[:, :width], packed[:, width : 2 * width].astype(F32)
    kept = mark[:, 127:128] > 0.5
    mark = mark[:, : w_router.shape[0]]
    gap = jnp.sum(dot_bt(rows, w_router[...]) * mark, 1, keepdims=True)
    gate = 1.0 / (1.0 + jnp.exp(-gap))
    gate_other = 1.0 / (1.0 + jnp.exp(gap))
    gate_in = dot(rows, w_gate[...])
    up = dot(rows, w_up[...])
    act, slope = silu_parts(gate_in)
    hidden = (act * up).astype(BF)
    hidden_out(hidden)
    part = jnp.where(kept, dot(hidden, w_down[...]), 0.0).astype(BF)
    pair = jnp.where(kept, gate * grads, 0.0).astype(BF)
    pair_out(pair)
    gate_grad = jnp.sum(part.astype(F32) * grads, 1, keepdims=True)
    logit_grad = (gate * gate_other * gate_grad * mark).astype(BF)
    hidden_grad = dot_bt(pair, w_down[...])
    grad_gate = (hidden_grad * up * slope).astype(BF)
    grad_up = (hidden_grad * act).astype(BF)
    grad_gate_out(grad_gate)
    grad_up_out(grad_up)
    back = (dot_bt(grad_gate, w_gate[...]) + dot_bt(grad_up, w_up[...])).astype(BF).astype(F32)
    back = (back + dot(logit_grad, w_router[...])).astype(BF)
    return back, part, gate, dot_t(logit_grad, rows)


def store_at(ref, where=...):
    def store(value):
        ref[where] = value

    return store


def expert_body(
    tiles,
    packed_own,
    packed_got,
    marks,
    w_router,
    w_gate,
    w_up,
    w_down,
    keep,
    send,
    rows_all,
    hidden,
    grad_gate,
    grad_up,
    pair,
    gates,
    router,
):
    step = pl.program_id(0)
    mine = step < tiles
    width = rows_all.shape[1]
    packed = jnp.where(mine, packed_own[...], packed_got[...])
    rows_all[...] = packed[:, :width]
    back, part, gate, router_term = expert_step(
        packed,
        marks[...],
        w_router,
        w_gate,
        w_up,
        w_down,
        [store_at(ref) for ref in (hidden, grad_gate, grad_up, pair)],
    )

    @pl.when(step == 0)
    def _():
        router[...] = jnp.zeros_like(router)

    router[...] += router_term

    @pl.when(mine)
    def _():
        keep[:, :width] = back
        keep[:, width:] = part
        gates[...] = jnp.broadcast_to(gate, gates.shape)

    @pl.when(jnp.logical_not(mine))
    def _():
        send[:, :width] = back
        send[:, width:] = part


def expert_whole_body(
    tile,
    packed_own,
    packed_got,
    marks,
    w_router,
    w_gate,
    w_up,
    w_down,
    back_keep,
    part_keep,
    *refs,
):
    back_send, part_send = refs[:SENT_PIECES], refs[SENT_PIECES : 2 * SENT_PIECES]
    rows_all, hidden, grad_gate, grad_up, pair, gates, router = refs[2 * SENT_PIECES :]
    half = packed_own.shape[0]
    width = rows_all.shape[1]
    router[...] = jnp.zeros_like(router)

    def run(base, packed_ref, put):
        def step(index, _):
            at = pl.ds(pl.multiple_of(index * tile, tile), tile)
            place = pl.ds(pl.multiple_of(base + index * tile, tile), tile)
            packed = packed_ref[at, : 2 * width]
            rows_all[place, :] = packed[:, :width]
            back, part, gate, router_term = expert_step(
                packed,
                marks[place, :],
                w_router,
                w_gate,
                w_up,
                w_down,
                [store_at(ref, (place, slice(None))) for ref in (hidden, grad_gate, grad_up, pair)],
            )
            router[...] += router_term
            put(index, at, back, part)
            if base == 0:
                gates[at, :] = jnp.broadcast_to(gate, (tile, 128))
            return 0

        lax.fori_loop(0, half // tile, step, 0)

    def put_own(index, at, back, part):
        back_keep[at, :] = back
        part_keep[at, :] = part

    def put_got(index, at, back, part):
        rows = half // SENT_PIECES
        each = tile // rows
        for i in range(SENT_PIECES):

            @pl.when(index == i // each)
            def _(i=i):
                inside = slice(i % each * rows, (i % each + 1) * rows)
                back_send[i][...] = back[inside]
                part_send[i][...] = part[inside]

    run(0, packed_own, put_own)
    run(half, packed_got, put_got)


def combine_body(slot_pick_t, addend, *refs):
    back, keep, send = refs[:-5], refs[-5], refs[-4:]
    half, width = keep.shape
    count = back[-1].shape[0]
    rows = jnp.concatenate([ref[:count, :width] for ref in back], 0)
    total = addend[...] + dot(slot_pick_t[...], rows)
    keep[...] = total[:half]
    store_pieces(send, total[half:].astype(BF))


def result_body(count, slot_pick_t, addend, attn_keep, attn_send, *refs):
    *near, a, b, c, d, keep, send = refs
    half, width = attn_keep.shape
    rows = [ref[:count, width:] for ref in near] + [ref[...] for ref in (a, b, c, d)]
    total = addend[...] + dot(slot_pick_t[...], jnp.concatenate(rows, 0))
    keep[:, :width] = total[:half]
    send[:, :width] = total[half:].astype(BF)
    keep[:, width:] = attn_keep[...]
    send[:, width:] = attn_send[...]


def norm_back_body(
    gain, half, got, after_attn, b0, b1, after_grad, low, gain_grad
):
    width = half.shape[1]
    normed_grad = both(half, got)
    values = after_attn[...]
    root = inverse_root(values)
    grads = jnp.concatenate([b0[:, width:], b1[:, width:]], 0).astype(F32)
    total = grads + rms_backward(values, root, gain[...], normed_grad)
    after_grad[...] = total
    low[...] = total.astype(BF)
    gain_grad[...] = jnp.broadcast_to(
        0.5 * jnp.sum(normed_grad * values * root, 0, keepdims=True), gain_grad.shape
    )


def attend_back_body(
    heads,
    w_out,
    w_in_t,
    cosine,
    sine,
    weights_all,
    qkv,
    own,
    got,
    b0,
    b1,
    b2,
    b3,
    keep,
    send,
    projected_grad,
    gain_grad,
):
    width = own.shape[1]
    half = keep.shape[0]
    grads = jnp.concatenate([own[...], got[...]], 0)
    mixed_grad = dot_bt(grads, w_out[...]).astype(BF)
    scale = HD**-0.5
    cosine, sine = cosine[...], sine[...]
    parts = []
    for head, (query, keys, values) in enumerate(head_parts(qkv, heads)):
        at = head * HD
        weights = weights_all[head]
        mine = mixed_grad[:, at : at + HD]
        weight_grad = dot_bt(mine, values)
        delta = jnp.sum(weights * weight_grad, -1, keepdims=True)
        score_grad = (weights * (weight_grad - delta)).astype(BF)
        parts.append(rope_back(dot(score_grad, keys) * scale, cosine, sine))
        parts.append(rope_back(dot_t(score_grad, query) * scale, cosine, sine))
        parts.append(dot_t(weights.astype(BF), mine))
    projected_grad[...] = jnp.concatenate(parts, 1).astype(BF)
    part = dot(projected_grad[...], w_in_t[...])
    tokens = jnp.concatenate([b[:, :width] for b in (b0, b1, b2, b3)], 0).astype(F32)
    gain_grad[...] = jnp.broadcast_to(
        jnp.sum(part * tokens * inverse_root(tokens), 0, keepdims=True), gain_grad.shape
    )
    keep[...] = part[:half]
    send[...] = part[half:].astype(BF)


def last_body(
    block, gain, own, got, b0, after_grad, after_attn, near, far
):
    rows, width = own.shape[0], own.shape[1] // 2
    tokens = b0[:, :width].astype(F32)
    sums = own[...] + got[...].astype(F32)
    normed_grad = sums[:, width:]
    total = after_grad[:rows, :] + rms_backward(
        tokens, inverse_root(tokens), gain[...], normed_grad
    )
    result = after_attn[:rows, :] + sums[:, :width]
    store_halves(near, far, block, result.astype(BF), slice(0, width))
    store_halves(near, far, block, total.astype(BF), slice(width, None))


def return_body(anchor, b0, b1, b2, b3, final, grads):
    row_count, width = final.shape
    pick = (iota((row_count, row_count), 0) == anchor[...]).astype(F32).T.astype(BF)
    rows = jnp.concatenate([b[...] for b in (b0, b1, b2, b3)], 0)
    total = dot(pick, rows).astype(BF)
    final[...] = total[:, :width]
    grads[...] = total[:, width:]


def on_device(
    tokens,
    cotangent,
    gain_attn,
    w_qkv,
    w_out,
    gain_ffn,
    w_router,
    w_shared_gate,
    w_shared_up,
    w_shared_down,
    routed_gate_weight,
    routed_up_weight,
    w_expert_down,
    seq_lengths,
    token_order,
    inverse_order,
    routes,
    fill_order,
):
    devices_dp = lax.axis_size(DP)
    devices_tp = lax.axis_size(TP)
    dz = lax.axis_size("dz")
    row_count, width = tokens.shape
    block_rows = row_count // devices_dp
    shard_block = block_rows // devices_tp
    shard_rows = row_count // devices_tp
    half_rows = row_count // 2
    experts_all = w_router.shape[1]
    slot_rows = 4 * row_count // experts_all
    capacity = 5 * row_count * devices_dp // (2 * experts_all)
    inner = w_out.shape[0]
    heads = inner // HD
    per_dp = max(1, experts_all // devices_dp)
    copies = max(1, devices_dp // experts_all)
    sub = devices_tp // per_dp
    my_hi, my_lo = lax.axis_index("hi"), lax.axis_index("lo")
    my_z, my_y = lax.axis_index("dz"), lax.axis_index("dy")
    my_dp = my_z * 2 + my_y
    my_block = my_lo * 2 + my_hi
    pick = my_hi if per_dp == 2 else 0 * my_hi
    my_part = my_lo if per_dp == 2 else my_block
    part_rows = slot_rows // sub
    own_slots = devices_dp * part_rows
    all_slots = own_slots * sub
    my_expert = my_dp // copies * per_dp + pick
    chunk = width // devices_dp
    z_bits = [(my_z >> i) & 1 for i in range(log2(dz))]
    info = jnp.stack([my_block, pick, my_part, my_expert, my_dp, my_y] + z_bits).astype(I32)
    pieces = devices_dp if devices_dp <= 8 else 1

    small = all_slots <= 1024

    def fetch(weights, deps=()):
        return kernel(
            fetch_body,
            [out(w.shape, w.dtype) for w in weights],
            *[Held(w) for w in weights],
            semaphores=len(weights),
            deps=deps,
        )

    table = rope_table(row_count)
    gain_attn = gain_attn[None]
    gain_ffn = gain_ffn[None]

    half_shard = out((shard_rows // 2, 2 * width), BF)
    shard_pieces = [out((shard_rows // pieces, 2 * width), BF)] * pieces
    *sent, anchor = kernel(
        functools.partial(select_body, shard_block, devices_dp),
        shard_pieces + [out((1, row_count), I32)],
        Far(inverse_order[None]),
        Far(tokens),
        Far(cotangent),
        scalars=(info,),
    )

    def blocks_of(own, deps):
        (by_hi,) = kernel(join_body, [out(own.shape, BF)], swap(own, "hi"), deps=deps)
        by_lo = swap(own, "lo")
        return (own, by_hi, by_lo, swap(by_hi, "lo"))

    def z_steps(parts):
        got = list(parts)
        for k in (2, 3, 1):
            got[k] = lax.ppermute(parts[k], "dz", [(i, i ^ k) for i in range(dz)])
        return got

    def exchange_halves(near, far, deps=()):
        width_sent = near.shape[1]
        block = near.shape[0] // dz
        if devices_dp != 8:
            both_halves = jnp.stack([near, far]).reshape(2, dz, block, width_sent)
            stacked = both_halves.transpose(1, 0, 2, 3).reshape(devices_dp, block, width_sent)
            return [exchange_stacked(stacked).reshape(devices_dp * block, width_sent)]
        middle = kernel(
            functools.partial(middle_body, block),
            [out((2 * block, width_sent), BF)] * dz,
            near,
            swap(far, "dy"),
            deps=deps,
        )
        return z_steps(middle)

    def join(parts, deps=()):
        if not isinstance(parts, (list, tuple)):
            parts = [parts]
        if not small:
            return jnp.concatenate(parts, 0)
        rows = sum(part.shape[0] for part in parts)
        return kernel(join_body, [out((rows, parts[0].shape[1]), BF)], *parts, deps=deps)[0]

    slot_pick, slot_pick_t, bias, cosine, sine, meta = kernel(
        functools.partial(index_body, shard_block, copies, per_dp, part_rows, experts_all),
        [
            out((own_slots, row_count), BF),
            out((row_count, own_slots), BF),
            out((row_count, row_count), BF),
            out((row_count, HD), F32),
            out((row_count, HD), F32),
            out((row_count, 128), BF),
        ],
        Far(token_order[None]),
        Far(routes.T),
        Far(fill_order),
        Far(table),
        scalars=(info, seq_lengths),
        vmem=24,
    )
    router = w_router.T
    w_in_t, w_out = fetch([w_qkv.T, w_out], (slot_pick,))
    blocks = blocks_of(join(exchange(sent)), (slot_pick, w_in_t))

    slot_piece = own_slots // pieces
    near_pieces = pieces // 2 if small else pieces
    packed_width = 2 * width + 128
    got_grads = []
    if small:
        sent_grads = kernel(
            functools.partial(send_grads_body, near_pieces * slot_piece),
            [out((slot_piece, width + 128), BF)] * (pieces - near_pieces),
            slot_pick,
            meta,
            *blocks,
        )
        got_grads = exchange_some(dict(enumerate(sent_grads, near_pieces)))

    keep, *send, qkv, mixed, normed_attn, weights = kernel(
        functools.partial(attend_body, heads),
        [
            out((half_rows, width), F32),
            *[out((half_rows // 4, width), BF)] * 4,
            out((row_count, 3 * inner), BF),
            out((row_count, inner), BF),
            out((row_count, width), BF),
            out((heads, row_count, row_count), F32),
        ],
        gain_attn,
        w_in_t,
        w_out,
        cosine,
        sine,
        bias,
        *blocks,
        vmem=24,
    )

    def half_sum(keep, send, deps=()):
        (half,) = kernel(
            fold_body,
            [out((half_rows, width), BF)],
            keep,
            *[swap(piece, "lo") for piece in send],
            deps=deps,
        )
        return half, swap(half, "hi")

    half, half_got = half_sum(keep, send, got_grads[:1])
    fetched = [w_shared_gate, w_shared_up, w_shared_down, router]
    if small:
        fetched += [routed_gate_weight, routed_up_weight, w_expert_down]
    fetched = fetch(fetched, (half,))
    w_shared_gate, w_shared_up, w_shared_down, router = fetched[:4]
    if small:
        routed_gate_weight, routed_up_weight, w_expert_down = fetched[4:]
    after_attn, normed_own = kernel(
        norm_body,
        [out((half_rows, width), F32), out((half_rows, width), BF)],
        gain_ffn,
        half,
        half_got,
        blocks[0],
        blocks[1],
        deps=got_grads[1:3] + [router],
    )
    normed_got = swap(normed_own, "lo")

    far_piece = out((slot_piece, width), BF)
    sent_rows = kernel(
        send_body,
        [out((slot_piece, packed_width), BF)] * near_pieces + [far_piece] * (pieces - near_pieces),
        slot_pick,
        normed_own,
        normed_got,
        meta,
        *blocks,
    )
    got_rows = exchange(sent_rows)

    def sub_gather(parts, deps=()):
        values = join(parts, deps)
        if sub == 4:
            values = jnp.concatenate([values, swap(values, "hi")], 0)
        return values, swap(values, "lo")

    units = w_shared_gate.shape[1]
    shared_part, shared_back, grad_sgate, grad_sup, shared_hidden = kernel(
        shared_body,
        [
            out((row_count, width), F32),
            out((row_count, width), F32),
            out((row_count, units), BF),
            out((row_count, units), BF),
            out((row_count, units), BF),
        ],
        normed_own,
        normed_got,
        *blocks,
        w_shared_gate,
        w_shared_up,
        w_shared_down,
        deps=sent_rows[:1],
        vmem=24,
    )
    def tree_outs(columns_a, columns_b):
        return [
            out((dz, chunk, columns), dtype)
            for dtype in (F32, BF)
            for columns in (columns_a, columns_b)
        ]

    shared_tree = kernel(
        shared_grads_body,
        tree_outs(3 * units // 2, 3 * units // 2),
        normed_own,
        normed_got,
        *blocks,
        grad_sgate,
        grad_sup,
        shared_hidden,
        scalars=(info,),
        vmem=24,
    )

    def z_swap(values, bit):
        return lax.ppermute(values, "dz", [(i, i ^ (1 << bit)) for i in range(dz)])

    def tree_first(parts):
        keep_a, keep_b, send_a, send_b = parts
        return keep_a, swap(send_a, "dy"), keep_b, z_swap(send_b, 0)

    def tree_second(parts, deps=()):
        kept_a, got_a, kept_b, got_b = parts
        shapes = [
            out((dz // 2, chunk, kept.shape[2]), dtype)
            for dtype in (F32, BF)
            for kept in (kept_a, kept_b)
        ]
        keep_a, keep_b, send_a, send_b = kernel(
            tree_second_body, shapes, kept_a, got_a, kept_b, got_b, scalars=(info,), deps=deps
        )
        return (keep_a, z_swap(send_a, 0), keep_b, swap(send_b, "dy")), send_b

    def tree_third(parts, deps=()):
        columns = parts[0].shape[2] + parts[2].shape[2]
        shape = (dz // 4, chunk, columns)
        keep, send = kernel(
            tree_third_body,
            [out(shape, F32), out(shape, BF)],
            *parts,
            scalars=(info,),
            deps=deps,
        )
        sent, got = send, z_swap(send, 1)
        for bit in range(2, log2(dz)):
            shape = (keep.shape[0] // 2, chunk, columns)
            keep, send = kernel(
                functools.partial(tree_body, Z_BITS + bit),
                [out(shape, F32), out(shape, BF)],
                keep,
                got,
                scalars=(info,),
            )
            got = z_swap(send, bit)
        return keep, got, sent

    shared_tree = tree_first(shared_tree)
    if small:
        (packed_own,) = kernel(
            functools.partial(join_packed_body, near_pieces),
            [out((own_slots, packed_width), BF)],
            *got_rows,
            *got_grads,
            deps=(shared_tree[0],),
        )
        packed_got = swap(packed_own, "lo")
    else:
        packed_own, packed_got = sub_gather(got_rows)
    (marks,) = kernel(
        functools.partial(
            meta_body, devices_dp, part_rows, sub, capacity, 2 * width if small else 0
        ),
        [out((all_slots, 128), F32)],
        packed_own if small else packed_own[:, 2 * width :],
        packed_got if small else packed_got[:, 2 * width :],
        scalars=(info,),
    )

    hidden_units = routed_gate_weight.shape[1]
    tile = min(512, own_slots)
    tiles = all_slots // 2 // tile
    steps = 2 * tiles

    def mine_at(i):
        return (jnp.minimum(i, tiles - 1), 0)

    def other_at(i):
        return (jnp.maximum(i - tiles, 0), 0)

    def every_at(i):
        return (i, 0)

    def fixed_at(i):
        return (0, 0)

    half_slots = all_slots // 2
    expert_ins = [
        (packed_own, pl.BlockSpec((tile, packed_width), mine_at)),
        (packed_got, pl.BlockSpec((tile, packed_width), other_at)),
        (marks, pl.BlockSpec((tile, 128), every_at)),
        (router, pl.BlockSpec((experts_all, width), fixed_at)),
        (routed_gate_weight, pl.BlockSpec((width, hidden_units), fixed_at)),
        (routed_up_weight, pl.BlockSpec((width, hidden_units), fixed_at)),
        (w_expert_down, pl.BlockSpec((hidden_units, width), fixed_at)),
    ]
    expert_outs = [
        (out((half_slots, 2 * width), BF), pl.BlockSpec((tile, 2 * width), mine_at)),
        (out((half_slots, 2 * width), BF), pl.BlockSpec((tile, 2 * width), other_at)),
        (out((all_slots, width), BF), pl.BlockSpec((tile, width), every_at)),
        (out((all_slots, hidden_units), BF), pl.BlockSpec((tile, hidden_units), every_at)),
        (out((all_slots, hidden_units), BF), pl.BlockSpec((tile, hidden_units), every_at)),
        (out((all_slots, hidden_units), BF), pl.BlockSpec((tile, hidden_units), every_at)),
        (out((all_slots, width), BF), pl.BlockSpec((tile, width), every_at)),
        (out((half_slots, 128), F32), pl.BlockSpec((tile, 128), mine_at)),
        (out((experts_all, width), F32), pl.BlockSpec((experts_all, width), fixed_at)),
    ]

    def expert_kernel(*refs):
        pltpu.emit_pipeline(
            functools.partial(expert_body, tiles),
            grid=(steps,),
            in_specs=[spec for _, spec in expert_ins],
            out_specs=[spec for _, spec in expert_outs],
        )(*refs)

    expert_args = [value for value, _ in expert_ins]
    expert_shapes = [shape for shape, _ in expert_outs]
    if small:
        piece = out((half_slots // SENT_PIECES, width), BF)
        results = kernel(
            functools.partial(expert_whole_body, tile),
            [out((half_slots, width), BF)] * 2 + [piece] * 2 * SENT_PIECES + expert_shapes[2:],
            *expert_args,
            vmem=22,
        )
        keep, part_keep, *results = results
        send, part_send = results[:SENT_PIECES], results[SENT_PIECES : 2 * SENT_PIECES]
        results = [keep, send] + list(results[2 * SENT_PIECES :])
    else:
        hbm_spec = pl.BlockSpec(memory_space=pltpu.HBM)
        results = pl.pallas_call(
            expert_kernel,
            in_specs=[hbm_spec] * len(expert_ins),
            out_specs=tuple([hbm_spec] * len(expert_outs)),
            out_shape=tuple(at_hbm(shape) for shape in expert_shapes),
            compiler_params=pltpu.CompilerParams(vmem_limit_bytes=44 * MIB),
            cost_estimate=COST,
            name="expert_body",
        )(*[in_hbm(value) for value in expert_args])
    (
        keep,
        send,
        rows_all,
        expert_hidden,
        grad_egate,
        grad_eup,
        pair_grads,
        gates,
        router_part,
    ) = results

    def sub_scatter(keep, send):
        total = keep.astype(F32) + swap(send, "lo").astype(F32)
        return total[:own_slots] + swap(total[own_slots:].astype(BF), "hi").astype(F32)

    if small:
        got = [swap(piece, "lo") for piece in send]
        part_got = [swap(piece, "lo") for piece in part_send]
        back_far = kernel(
            add_far_body,
            [far_piece] * (pieces - near_pieces),
            keep,
            *got[SENT_PIECES // 2 :],
            deps=(shared_tree[1], shared_tree[3]),
        )
        back_near = kernel(
            add_near_body,
            [out((slot_piece, 2 * width), BF)] * near_pieces,
            keep,
            part_keep,
            gates,
            *got[: SENT_PIECES // 2],
            *part_got[: SENT_PIECES // 2],
        )
        sent_back = list(back_near) + list(back_far)
        sent_parts = kernel(
            part_far_body,
            [far_piece] * (pieces - near_pieces),
            part_keep,
            gates,
            *part_got[SENT_PIECES // 2 :],
            deps=sent_back[:1],
        )
    else:
        total = sub_scatter(keep, send)
        sent_back = [total[:, :width].astype(BF)]
        sent_parts = [(gates[:own_slots, :1] * total[:, width:]).astype(BF)]
        shared_tree, _ = tree_second(shared_tree)

    def weight_grad(left, right, deps=()):
        if not small:
            return dot_t(left, right)
        shape = (left.shape[1], right.shape[1])
        vmem_spec = pl.BlockSpec(memory_space=pltpu.VMEM)
        return pl.pallas_call(
            lambda *refs: weight_grad_body(refs[0], refs[1], *refs[-3:]),
            out_shape=pltpu.HBM(shape, F32),
            in_specs=[vmem_spec] * 2 + [pl.BlockSpec(memory_space=pl.ANY)] * len(deps),
            out_specs=pl.BlockSpec(memory_space=pltpu.HBM),
            scratch_shapes=[
                pltpu.VMEM(shape, F32),
                pltpu.SemaphoreType.DMA((shape[0] // 256,)),
            ],
            compiler_params=pltpu.CompilerParams(vmem_limit_bytes=12 * MIB),
            cost_estimate=COST,
            name="weight_grad",
        )(in_vmem(left), in_vmem(right), *deps)

    grad_w_expert_gate = weight_grad(rows_all, grad_egate, (sent_back[0],))
    got_back = exchange(sent_back)
    if small:
        got_parts = exchange_some(dict(enumerate(sent_parts, near_pieces)))
        shared_tree, _ = tree_second(shared_tree, sent_back[:1])
    else:
        got_parts = exchange(sent_parts)
    shared_keep, shared_got, shared_sent = tree_third(shared_tree)

    keep, *send = kernel(
        combine_body,
        [out((half_rows, width), F32)] + [out((half_rows // 4, width), BF)] * 4,
        slot_pick_t,
        shared_back,
        *got_back,
        deps=(
            Far(grad_w_expert_gate),
        ),
    )
    half, half_got = half_sum(keep, send, got_parts[:1] if small else ())

    def own_sum(keep, send, deps=()):
        own, send = kernel(
            fold_own_body,
            [out((shard_rows, width), F32), out((shard_rows, width), BF)],
            keep,
            swap(send, "lo"),
            deps=deps,
        )
        return own, send

    after_grad, after_grad_own, gain_ffn_part = kernel(
        norm_back_body,
        [out((half_rows, width), F32), out((half_rows, width), BF), out((8, width), F32)],
        gain_ffn,
        half,
        half_got,
        after_attn,
        blocks[0],
        blocks[1],
        deps=got_parts[1:3] + [shared_tree[1], shared_tree[3]] if small else (),
    )
    after_grad_got = swap(after_grad_own, "lo")

    keep, send, projected_grad, gain_attn_part = kernel(
        functools.partial(attend_back_body, heads),
        [
            out((half_rows, width), F32),
            out((half_rows, width), BF),
            out((row_count, 3 * inner), BF),
            out((8, width), F32),
        ],
        w_out,
        w_in_t,
        cosine,
        sine,
        weights,
        qkv,
        after_grad_own,
        after_grad_got,
        *blocks,
        vmem=24,
    )
    if small:
        keep, send = kernel(
            functools.partial(result_body, slot_piece),
            [out((half_rows, 2 * width), F32), out((half_rows, 2 * width), BF)],
            slot_pick_t,
            shared_part,
            keep,
            send,
            *got_back[:near_pieces],
            *got_parts,
        )
    else:
        result_part = shared_part + dot(slot_pick_t, got_parts[0])
        keep = jnp.concatenate([result_part[:half_rows], keep], 1)
        send = jnp.concatenate([result_part[half_rows:].astype(BF), send], 1)
    bottom_got = swap(send, "lo")
    last_columns = 4 * inner + 128
    last_tree = kernel(
        functools.partial(last_grads_body, experts_all),
        tree_outs(512, last_columns - 512),
        normed_attn,
        projected_grad,
        after_grad_own,
        after_grad_got,
        mixed,
        gain_ffn_part,
        gain_attn_part,
        router_part,
        scalars=(info,),
        vmem=24,
        deps=(send,),
    )
    last_tree = tree_first(last_tree)
    own, send = kernel(
        fold_own_body,
        [out((shard_rows, 2 * width), F32), out((shard_rows, 2 * width), BF)],
        keep,
        bottom_got,
    )
    grad_sgate, grad_sup, grad_sdown = kernel(
        shared_end_body,
        [Far(out((chunk, units), F32))] * 3,
        shared_keep,
        shared_got,
    )
    near, far = kernel(
        functools.partial(last_body, shard_block),
        [half_shard, half_shard],
        gain_attn,
        own,
        swap(send, "hi"),
        blocks[0],
        after_grad,
        after_attn,
    )
    last_tree, last_sent = tree_second(last_tree, (near,))
    grad_w_expert_down = weight_grad(expert_hidden, pair_grads, (last_sent,))
    got_last = exchange_halves(near, far, (last_sent,))
    last_keep, last_got, last_sent = tree_third(last_tree, got_last[:1])
    small_rows = experts_all + 8
    grad_qkv, grad_out, sums = kernel(
        functools.partial(last_end_body, small_rows),
        [
            Far(out((chunk, 3 * inner), F32)),
            Far(out((inner, chunk), F32)),
            out((small_rows, chunk), F32),
        ],
        last_keep,
        last_got,
    )
    got_last = join(got_last, (last_sent, Far(grad_sgate), Far(grad_w_expert_down)))
    grad_w_expert_up = weight_grad(rows_all, grad_eup, (got_last,))
    final, grad_tokens = kernel(
        return_body,
        [Far(out((row_count, width), BF)), Far(out((row_count, width), BF))],
        anchor,
        *blocks_of(got_last, (sums, Far(grad_w_expert_up))),
    )

    gain_ffn_sum, gain_attn_sum, router_sum = kernel(
        small_end_body,
        [Far(out((1, chunk), F32)), Far(out((1, chunk), F32)), Far(out((experts_all, chunk), F32))],
        sums,
        *[lax.ppermute(sums, TP, [(i, i ^ k) for i in range(4)]) for k in (1, 2, 3)],
        deps=(Far(final),),
    )
    return (
        final,
        grad_tokens,
        gain_attn_sum.reshape(chunk),
        grad_qkv,
        grad_out,
        gain_ffn_sum.reshape(chunk),
        router_sum.T,
        grad_sgate,
        grad_sup,
        grad_sdown.T,
        grad_w_expert_gate,
        grad_w_expert_up,
        grad_w_expert_down,
    )


def solution(mesh):
    devices_dp, devices_tp = mesh.shape["dp"], mesh.shape["tensor"]
    fine = Mesh(
        mesh.devices.reshape(devices_dp // 2, 2, devices_tp // 2, 2), ("dz", "dy", "hi", "lo")
    )
    every = DP + TP
    return jax.shard_map(
        on_device,
        mesh=fine,
        in_specs=(
            P(DP, None),
            P(DP, None),
            P(),
            P(None, TP),
            P(TP, None),
            P(),
            P(),
            P(None, TP),
            P(None, TP),
            P(TP, None),
            P(None, every),
            P(None, every),
            P(every, None),
            P(DP, None),
            P(DP),
            P(DP),
            P(DP, None),
            P(DP, None),
        ),
        out_specs=(
            P(DP, None),
            P(DP, None),
            P(DP),
            P(DP, TP),
            P(TP, DP),
            P(DP),
            P(DP, None),
            P(DP, TP),
            P(DP, TP),
            P(TP, DP),
            P(None, every),
            P(None, every),
            P(every, None),
        ),
        check_vma=False,
    )
```

```python
import functools

import jax
import jax.numpy as jnp
import numpy as np
from jax import lax
from jax.experimental import pallas as pl
from jax.experimental.pallas import tpu as pltpu
from jax.sharding import Mesh, PartitionSpec as P

HD = 64
MY_BLOCK, PICK, MY_PART, MY_EXPERT, MY_DP, Y_BIT, Z_BITS = range(7)
EPSILON = 1e-06
BF = jnp.bfloat16
F32 = jnp.float32
I32 = jnp.int32
DP = ("dz", "dy")
TP = ("hi", "lo")
MIB = 1 << 20
SENT_PIECES = 4
COST = pl.CostEstimate(flops=1000, bytes_accessed=1000, transcendentals=0)


def dot(left, right):
    return jnp.dot(left, right, preferred_element_type=F32)


def dot_t(left, right):
    return lax.dot_general(left, right, (((0,), (0,)), ((), ())), preferred_element_type=F32)


def dot_bt(left, right):
    return lax.dot_general(left, right, (((1,), (1,)), ((), ())), preferred_element_type=F32)


def swap(values, axis):
    return lax.ppermute(values, axis, [(0, 1), (1, 0)])


def exchange_stacked(values):
    order = jnp.arange(values.shape[0], dtype=I32) ^ lax.axis_index(DP)
    got = lax.all_to_all(
        jnp.take(values, order, axis=0), DP, split_axis=0, concat_axis=0, tiled=True
    )
    return jnp.take(got, order, axis=0)


def exchange(pieces):
    devices = lax.axis_size(DP)
    if len(pieces) == 1:
        (values,) = pieces
        stacked = values.reshape(devices, -1, values.shape[-1])
        return [exchange_stacked(stacked).reshape(values.shape)]
    return exchange_some(dict(enumerate(pieces)))


def exchange_some(pieces):
    devices = lax.axis_size(DP)
    got = dict(pieces)
    for k in (4, 5, 6, 7, 2, 3, 1):
        if k in got:
            got[k] = lax.ppermute(pieces[k], DP, [(i, i ^ k) for i in range(devices)])
    return [got[k] for k in sorted(got)]


def out(shape, dtype):
    return jax.ShapeDtypeStruct(shape, dtype)


class Far:
    def __init__(self, value):
        self.value = value


class Held(Far):
    pass


class Free(Far):
    pass


class Arriving:
    def __init__(self, buffer, copy):
        self.buffer, self.copy, self.waiting = buffer, copy, True
        self.shape, self.dtype = buffer.shape, buffer.dtype

    def ready(self):
        if self.waiting:
            self.copy.wait()
            self.waiting = False

    def __getitem__(self, index):
        self.ready()
        return self.buffer[index]


class Leaving:
    def __init__(self, buffer, copy):
        self.buffer, self.copy, self.started = buffer, copy, False
        self.shape, self.dtype = buffer.shape, buffer.dtype

    def flush(self):
        if not self.started:
            self.copy.start()
            self.started = True

    def __getitem__(self, index):
        return self.buffer[index]

    def __setitem__(self, index, value):
        self.buffer[index] = value


def in_hbm(values):
    return pltpu.with_memory_space_constraint(values, pltpu.HBM)


def in_vmem(values):
    if values.size * values.dtype.itemsize > 4 * MIB:
        return values
    return pltpu.with_memory_space_constraint(values, pltpu.VMEM)


def at_hbm(shape):
    return pltpu.HBM(shape.shape, shape.dtype)


def at_vmem(shape):
    if shape.size * shape.dtype.itemsize > 4 * MIB:
        return shape
    return pltpu.VMEM(shape.shape, shape.dtype)


def kernel(body, outs, *args, scalars=(), deps=(), vmem=16, semaphores=0):
    vmem_spec = pl.BlockSpec(memory_space=pltpu.VMEM)
    hbm_spec = pl.BlockSpec(memory_space=pltpu.HBM)
    any_spec = pl.BlockSpec(memory_space=pl.ANY)
    held = [isinstance(a, Held) for a in args]
    far_in = [isinstance(a, Far) and not h for a, h in zip(args, held)]
    free_out = [isinstance(o, Free) for o in outs]
    far_out = [isinstance(o, Far) and not f for o, f in zip(outs, free_out)]
    args = [in_hbm(a.value) if isinstance(a, Far) else in_vmem(a) for a in args]
    outs = [
        o.value if f else at_hbm(o.value) if h else at_vmem(o)
        for o, f, h in zip(outs, free_out, far_out)
    ]
    deps = [in_hbm(d.value) if isinstance(d, Far) else d for d in deps]
    moved = [x for x, f in zip(args + outs, far_in + far_out) if f]
    scratch = [pltpu.VMEM(x.shape, x.dtype) for x in moved]
    if moved:
        scratch.append(pltpu.SemaphoreType.DMA((len(moved),)))
    if semaphores:
        scratch.append(pltpu.SemaphoreType.DMA((semaphores,)))
    n_scalars, n_args, n_deps, n_outs = len(scalars), len(args), len(deps), len(outs)

    def wrapped(*refs):
        ins = list(refs[: n_scalars + n_args])
        results = list(refs[n_scalars + n_args + n_deps :][:n_outs])
        buffers = refs[n_scalars + n_args + n_deps + n_outs :]
        extra = buffers[-1:] if semaphores else ()
        buffers = buffers[:-1] if semaphores else buffers
        at = 0
        for i, far in enumerate(far_in):
            if far:
                ref = ins[n_scalars + i]
                copy = pltpu.make_async_copy(ref, buffers[at], buffers[-1].at[at])
                copy.start()
                ins[n_scalars + i] = Arriving(buffers[at], copy)
                at += 1
        for i, far in enumerate(far_out):
            if far:
                copy = pltpu.make_async_copy(buffers[at], results[i], buffers[-1].at[at])
                results[i] = Leaving(buffers[at], copy)
                at += 1
        body(*ins, *results, *extra)
        for ref in ins:
            if isinstance(ref, Arriving):
                ref.ready()
        for ref in results:
            if isinstance(ref, Leaving):
                ref.flush()
        for ref in results:
            if isinstance(ref, Leaving):
                ref.copy.wait()

    return pl.pallas_call(
        wrapped,
        out_shape=tuple(outs),
        in_specs=[pl.BlockSpec(memory_space=pltpu.SMEM)] * n_scalars
        + [hbm_spec if f or h else vmem_spec for f, h in zip(far_in, held)]
        + [any_spec] * n_deps,
        out_specs=tuple(hbm_spec if far else vmem_spec for far in far_out),
        scratch_shapes=scratch,
        compiler_params=pltpu.CompilerParams(vmem_limit_bytes=vmem * MIB),
        cost_estimate=COST,
        name=body.func.__name__ if isinstance(body, functools.partial) else body.__name__,
    )(*scalars, *args, *deps)


def tie(values, *deps):
    any_spec = pl.BlockSpec(memory_space=pl.ANY)
    vmem_spec = pl.BlockSpec(memory_space=pltpu.VMEM)
    return pl.pallas_call(
        lambda *refs: None,
        out_shape=out(values.shape, values.dtype),
        in_specs=[vmem_spec] + [any_spec] * len(deps),
        out_specs=vmem_spec,
        input_output_aliases={0: 0},
        cost_estimate=COST,
        name="tie",
    )(in_vmem(values), *[in_hbm(d.value) if isinstance(d, Far) else d for d in deps])


def rope_table(places):
    exponent = np.arange(HD // 2, dtype=np.float32) * np.float32(-2.0 / HD)
    angles = np.arange(places, dtype=np.float32)[:, None] * np.power(np.float32(10000.0), exponent)
    cosine = np.cos(angles.astype(np.float64)).astype(np.float32)
    sine = np.sin(angles.astype(np.float64)).astype(np.float32)
    rest = np.concatenate([cosine, cosine, -sine, sine], 1)
    terms = []
    for _ in range(3):
        terms.append(rest.astype(BF))
        rest = rest - terms[-1].astype(np.float32)
    return jnp.asarray(np.concatenate(terms, 1))


def iota(shape, dim):
    return lax.broadcasted_iota(I32, shape, dim)


def log2(number):
    return number.bit_length() - 1


def silu_parts(gate_in):
    sigmoid_val = 0.5 * jnp.tanh(0.5 * gate_in) + 0.5
    return (gate_in * sigmoid_val, sigmoid_val * (1.0 + gate_in * (1.0 - sigmoid_val)))


def inverse_root(values):
    return lax.rsqrt(jnp.mean(values * values, -1, keepdims=True) + EPSILON)


def rms_backward(values, root, gain, grad_normed):
    scaled = grad_normed * gain
    return root * scaled - values * (root * root * root) * jnp.mean(
        scaled * values, -1, keepdims=True
    )


def lane_rank(buckets, bucket_count):
    count = buckets.shape[1]
    rows = max(8, bucket_count)
    member = (iota((rows, count), 0) == buckets).astype(F32)
    earlier = (iota((count, count), 0) < iota((count, count), 1)).astype(F32).astype(BF)
    return jnp.sum(dot(member.astype(BF), earlier) * member, 0, keepdims=True).astype(I32)


def relative_row(block, rank, my_block, shard_block, shard_rows):
    shift = log2(shard_block)
    return (
        ((rank >> shift) ^ my_block) * shard_rows
        + block * shard_block
        + (rank & (shard_block - 1))
    )


def rope_back(grads, cosine, sine):
    return grads * cosine - half_turned(grads) * sine


def store_pieces(refs, value):
    rows = refs[0].shape[0]
    for i, ref in enumerate(refs):
        ref[...] = value[i * rows : (i + 1) * rows]


def joined(refs):
    return jnp.concatenate([ref[...] for ref in refs], 0) if len(refs) > 1 else refs[0][...]


def join_body(*refs):
    *parts, whole = refs
    rows = parts[0].shape[0]
    for i, ref in enumerate(parts):
        whole[i * rows : (i + 1) * rows, :] = ref[...]


def middle_body(block, near, far, *outs):
    for i, ref in enumerate(outs):
        ref[:block, :] = near[i * block : (i + 1) * block, :]
        ref[block:, :] = far[i * block : (i + 1) * block, :]


def store_halves(near, far, block, value, columns):
    for i in range(near.shape[0] // block):
        at = 2 * i * block
        near[i * block : (i + 1) * block, columns] = value[at : at + block]
        far[i * block : (i + 1) * block, columns] = value[at + block : at + 2 * block]


def fetch_body(*refs):
    *refs, semaphores = refs
    count = len(refs) // 2
    copies = [
        pltpu.make_async_copy(refs[i], refs[count + i], semaphores.at[i]) for i in range(count)
    ]
    for copy in copies:
        copy.start()
    for copy in copies:
        copy.wait()


def select_body(shard_block, blocks, info, inverse, tokens, cotangent, *refs):
    *sent, anchor = refs
    row_count, width = tokens.shape
    shard_rows = shard_block * blocks
    target = (inverse[...] >> log2(row_count)) ^ info[MY_DP]
    row = relative_row(target, lane_rank(target, blocks), info[MY_BLOCK], shard_block, shard_rows)
    anchor[...] = row
    pick = (iota((shard_rows, row_count), 0) == row).astype(F32).astype(BF)
    rows = jnp.concatenate([dot(pick, tokens[...]), dot(pick, cotangent[...])], 1)
    store_pieces(sent, rows.astype(BF))


def index_body(
    shard_block,
    copies,
    per_dp,
    part_rows,
    experts_all,
    info,
    lengths,
    order,
    routes,
    fill,
    table,
    slot_pick,
    slot_pick_t,
    bias,
    cosine,
    sine,
    meta,
):
    row_count = order.shape[1]
    devices_dp = slot_pick.shape[0] // part_rows
    shard_rows = shard_block * devices_dp
    source = (order[...] >> log2(row_count)) ^ info[MY_DP]
    local = relative_row(
        source, lane_rank(source, devices_dp), info[MY_BLOCK], shard_block, shard_rows
    )
    place_pick = (iota((row_count, row_count), 0) == local).astype(F32).astype(BF)
    lanes = iota((1, row_count), 1)
    segment = jnp.zeros((1, row_count), I32)
    start = jnp.zeros((1, row_count), I32)
    end = jnp.int32(0)
    for entry in range(lengths.shape[1]):
        end = end + lengths[0, entry]
        passed = lanes >= end
        segment = segment + passed.astype(I32)
        start = jnp.maximum(start, jnp.where(passed, end, 0))
    place = lanes - start
    expert_sum = routes[0:1, :] + routes[1:2, :] + 1
    facts = jnp.concatenate(
        [segment, place >> 1, place & 1, expert_sum, jnp.zeros((4, row_count), I32)], 0
    )
    facts = facts.astype(F32).astype(BF)
    across = dot_bt(facts, place_pick)
    down = dot_bt(place_pick, facts)
    place_row = 2.0 * across[1:2] + across[2:3]
    place_col = 2.0 * down[:, 1:2] + down[:, 2:3]
    allowed = (down[:, 0:1] == across[0:1]) & (place_row <= place_col)
    bias[...] = jnp.where(allowed, 0.0, -1e30).astype(BF)
    at_place = (
        iota((row_count, row_count), 1).astype(F32) == place_col
    ).astype(F32).astype(BF)
    turned = dot(at_place, table[...])
    pieces = [turned[:, i * 128 : (i + 1) * 128] for i in range(3)]
    turned = pieces[0] + pieces[1] + pieces[2]
    cosine[...] = turned[:, :HD]
    sine[...] = turned[:, HD:]
    meta[...] = jnp.broadcast_to(down[:, 3:4], meta.shape).astype(BF)
    pairs = 2 * row_count
    fill_at = (fill[...] & 1) * row_count + (fill[...] >> 1)
    fill_pick = (iota((pairs, pairs), 0) == fill_at).astype(F32).astype(BF)
    expert_rows = max(16, experts_all)
    pair_expert = jnp.concatenate([routes[0:1, :], routes[1:2, :]], 1)
    named = (iota((expert_rows, pairs), 0) == pair_expert).astype(F32).astype(BF)
    member = dot(named, fill_pick)
    earlier = (iota((pairs, pairs), 0) < iota((pairs, pairs), 1)).astype(F32).astype(BF)
    ranks = (member * (dot(member.astype(BF), earlier) + 1.0)).astype(BF)
    ranks = dot_bt(ranks, fill_pick)
    ranks = (ranks[:, :row_count] + ranks[:, row_count:]).astype(BF)
    ranks = dot_bt(ranks, place_pick).astype(I32)
    slots = iota((part_rows, row_count), 0) + (info[MY_PART] * part_rows + 1)
    experts = iota((expert_rows, row_count), 0)
    for target in range(devices_dp):
        expert = ((target ^ info[MY_DP]) >> log2(copies)) * per_dp + info[PICK]
        chosen = jnp.sum(jnp.where(experts == expert, ranks, 0), 0, keepdims=True)
        picked = (slots == chosen).astype(F32)
        slot_pick[target * part_rows : (target + 1) * part_rows, :] = picked.astype(BF)
    slot_pick_t[...] = slot_pick[...].astype(F32).T.astype(BF)


def head_parts(projected, heads):
    return [
        [projected[:, (3 * h + i) * HD : (3 * h + i + 1) * HD] for i in range(3)]
        for h in range(heads)
    ]


def half_turned(values):
    half = values.shape[1] // 2
    return jnp.concatenate([values[:, half:], values[:, :half]], 1)


def attend_body(
    heads,
    gain,
    w_in_t,
    w_out,
    cosine,
    sine,
    bias,
    b0,
    b1,
    b2,
    b3,
    keep,
    *refs,
):
    *send, qkv, mixed, normed, weights_all = refs
    width = b0.shape[1] // 2
    half = keep.shape[0]
    tokens = jnp.concatenate([b[:, :width] for b in (b0, b1, b2, b3)], 0).astype(F32)
    normed[...] = (tokens * inverse_root(tokens) * gain[...]).astype(BF)
    projected = dot_bt(normed[...], w_in_t[...])
    cosine, sine = cosine[...], sine[...]
    parts = []
    for query, keys, values in head_parts(projected, heads):
        parts.append((query * cosine + half_turned(query) * sine).astype(BF))
        parts.append((keys * cosine + half_turned(keys) * sine).astype(BF))
        parts.append(values.astype(BF))
    qkv[...] = jnp.concatenate(parts, 1)
    scale = HD**-0.5
    mixed_heads = []
    for head, (query, keys, values) in enumerate(head_parts(qkv, heads)):
        scores = dot_bt(query, keys) * scale + bias[...].astype(F32)
        powers = jnp.exp(scores - jnp.max(scores, -1, keepdims=True))
        weights = powers * (1.0 / jnp.sum(powers, -1, keepdims=True))
        weights_all[head] = weights
        mixed_heads.append(dot(weights.astype(BF), values))
    mixed[...] = jnp.concatenate(mixed_heads, 1).astype(BF)
    part = dot(mixed[...], w_out[...])
    keep[...] = part[:half]
    store_pieces(send, part[half:].astype(BF))


def fold_body(keep, *refs):
    *got, half = refs
    half[...] = (keep[...] + joined(got).astype(F32)).astype(BF)


def fold_own_body(keep, got, own, send):
    rows = own.shape[0]
    own[...] = keep[:rows, :] + got[:rows, :].astype(F32)
    send[...] = (keep[rows:, :] + got[rows:, :].astype(F32)).astype(BF)


def both(half, got):
    rows = half.shape[0] // 2
    mine, other = half[...].astype(F32), got[...].astype(F32)
    return mine + jnp.concatenate([other[rows:], other[:rows]], 0)


def norm_body(gain, half, got, b0, b1, after_attn, normed):
    width = half.shape[1]
    balanced = jnp.concatenate([b0[:, :width], b1[:, :width]], 0).astype(F32)
    values = balanced + both(half, got)
    after_attn[...] = values
    normed[...] = (values * inverse_root(values) * gain[...]).astype(BF)


def send_body(slot_pick, own, got, meta, b0, b1, b2, b3, *sent):
    width = own.shape[1]
    rows = jnp.concatenate([own[...], got[...]], 0)
    rows = dot(slot_pick[...], rows).astype(BF)
    count = sent[0].shape[0]
    near = sum(ref.shape[1] > width for ref in sent) * count
    grads = jnp.concatenate([b[:, width:] for b in (b0, b1, b2, b3)], 0)
    grads = jnp.concatenate([grads, meta[...]], 1)
    grads = dot(slot_pick[:near, :], grads).astype(BF)
    for i, ref in enumerate(sent):
        at = slice(i * count, (i + 1) * count)
        ref[:, :width] = rows[at]
        if ref.shape[1] > width:
            ref[:, width:] = grads[at]


def send_grads_body(first, slot_pick, meta, b0, b1, b2, b3, *sent):
    width = b0.shape[1] // 2
    grads = jnp.concatenate([b[:, width:] for b in (b0, b1, b2, b3)], 0)
    grads = jnp.concatenate([grads, meta[...]], 1)
    store_pieces(sent, dot(slot_pick[first:, :], grads).astype(BF))


def join_packed_body(near, *refs):
    *parts, whole = refs
    count, width = parts[near].shape
    far = (len(parts) - near) // 2
    for i in range(near):
        whole[i * count : (i + 1) * count, :] = parts[i][...]
    for i in range(far):
        at = slice((near + i) * count, (near + i + 1) * count)
        whole[at, :width] = parts[near + i][...]
        whole[at, width:] = parts[near + far + i][...]


def shared_body(
    own, got, b0, b1, b2, b3, w_gate, w_up, w_down, part, back, grad_gate, grad_up, hidden
):
    width = own.shape[1]
    rows = jnp.concatenate([own[...], got[...]], 0)
    grads = jnp.concatenate([b[:, width:] for b in (b0, b1, b2, b3)], 0)
    gate = dot(rows, w_gate[...])
    up = dot(rows, w_up[...])
    act, slope = silu_parts(gate)
    hidden[...] = (act * up).astype(BF)
    part[...] = dot(hidden[...], w_down[...])
    hidden_grad = dot_bt(grads, w_down[...])
    grad_gate[...] = (hidden_grad * up * slope).astype(BF)
    grad_up[...] = (hidden_grad * act).astype(BF)
    back[...] = dot_bt(grad_gate[...], w_gate[...]) + dot_bt(grad_up[...], w_up[...])


def store_tree(info, sums, keeps, sends):
    chunk, columns = keeps[0].shape[1:]
    sides = ((sums[:, :columns], Y_BIT, 1), (sums[:, columns:], Z_BITS, 2))
    for (values, which, stride), keep, send in zip(sides, keeps, sends):
        mine = info[which] == 0
        for i in range(keep.shape[0]):
            at = (2 * i if stride == 1 else i // 2 * 4 + i % 2) * chunk
            first, second = values[at : at + chunk], values[at + stride * chunk :][:chunk]
            keep[i] = jnp.where(mine, first, second)
            send[i] = jnp.where(mine, second, first).astype(BF)


def shared_grads_body(
    info, own, got, b0, b1, b2, b3, grad_gate, grad_up, hidden, *refs
):
    width = own.shape[1]
    rows = jnp.concatenate([own[...], got[...]], 0)
    grads = jnp.concatenate([b[:, width:] for b in (b0, b1, b2, b3)], 0)
    sums = jnp.concatenate(
        [dot_t(rows, grad_gate[...]), dot_t(rows, grad_up[...]), dot_t(grads, hidden[...])], 1
    )
    store_tree(info, sums, refs[:2], refs[2:])


def halved(info, which, total, keep, send):
    mine = info[which] == 0
    for index in range(keep.shape[0]):
        first, second = total[2 * index], total[2 * index + 1]
        keep[index] = jnp.where(mine, first, second)
        send[index] = jnp.where(mine, second, first).astype(BF)


def tree_second_body(info, kept_a, got_a, kept_b, got_b, keep_a, keep_b, send_a, send_b):
    halved(info, Z_BITS, kept_a[...] + got_a[...].astype(F32), keep_a, send_a)
    halved(info, Y_BIT, kept_b[...] + got_b[...].astype(F32), keep_b, send_b)


def tree_third_body(info, kept_a, got_a, kept_b, got_b, keep, send):
    total = jnp.concatenate(
        [kept_a[...] + got_a[...].astype(F32), kept_b[...] + got_b[...].astype(F32)], 2
    )
    halved(info, Z_BITS + 1, total, keep, send)


def last_grads_body(
    experts, info, normed, projected_grad, own, got, mixed, gain_ffn, gain_attn, router, *refs
):
    width = normed.shape[1]
    small = jnp.concatenate(
        [
            router[:experts, :],
            gain_ffn[:1, :],
            gain_attn[:1, :],
            jnp.zeros((128 - experts - 2, width), F32),
        ],
        0,
    )
    grads = jnp.concatenate([own[...], got[...]], 0)
    sums = jnp.concatenate(
        [dot_t(normed[...], projected_grad[...]), dot_t(grads, mixed[...]), small.T], 1
    )
    store_tree(info, sums, refs[:2], refs[2:])


def tree_body(which, info, kept, got, keep, send):
    halved(info, which, kept[...] + got[...].astype(F32), keep, send)


def last_end_body(small_rows, kept, got, grad_qkv, grad_out, small):
    total = kept[0] + got[0].astype(F32)
    columns, inner = grad_qkv.shape[1], grad_out.shape[0]
    grad_qkv[...] = total[:, :columns]
    grad_out[...] = total[:, columns : columns + inner].T
    small[...] = total[:, columns + inner :].T[:small_rows]


def small_end_body(own, by_lo, by_hi, by_both, gain_ffn, gain_attn, router):
    experts = router.shape[0]
    total = (own[...] + by_lo[...]) + (by_hi[...] + by_both[...])
    router[...] = total[:experts]
    gain_ffn[...] = total[experts : experts + 1]
    gain_attn[...] = total[experts + 1 : experts + 2]


def shared_end_body(kept, got, grad_gate, grad_up, grad_down):
    total = kept[0] + got[0].astype(F32)
    units = grad_gate.shape[1]
    grad_gate[...] = total[:, :units]
    grad_up[...] = total[:, units : 2 * units]
    grad_down[...] = total[:, 2 * units :]


def add_far_body(keep, *refs):
    got, total = refs[: SENT_PIECES // 2], refs[SENT_PIECES // 2 :]
    half = keep.shape[0] // 2
    store_pieces(total, (keep[half:, :].astype(F32) + joined(got).astype(F32)).astype(BF))


def gated_parts(keep, got, gates):
    gate = jnp.concatenate([gates] * (keep.shape[1] // 128), 1)
    return (gate * (keep.astype(F32) + got.astype(F32))).astype(BF)


def add_near_body(keep, part_keep, gates, *refs):
    got, part_got, total = (
        refs[: SENT_PIECES // 2],
        refs[SENT_PIECES // 2 : SENT_PIECES],
        refs[SENT_PIECES:],
    )
    half, width = keep.shape[0] // 2, keep.shape[1]
    rows = (keep[:half, :].astype(F32) + joined(got).astype(F32)).astype(BF)
    parts = gated_parts(part_keep[:half, :], joined(part_got), gates[:half, :])
    count = total[0].shape[0]
    for i, ref in enumerate(total):
        at = slice(i * count, (i + 1) * count)
        ref[:count, :width] = rows[at]
        ref[:count, width:] = parts[at]


def part_far_body(keep, gates, *refs):
    got, total = refs[: SENT_PIECES // 2], refs[SENT_PIECES // 2 :]
    half = keep.shape[0] // 2
    store_pieces(total, gated_parts(keep[half:, :], joined(got), gates[half:, :]))


def weight_grad_body(left, right, total, sums, semaphores):
    tile = 256
    copies = []
    for i in range(left.shape[1] // tile):
        at = slice(i * tile, (i + 1) * tile)
        sums[at, :] = dot_t(left[:, at], right[...])
        copies.append(
            pltpu.make_async_copy(sums.at[at, :], total.at[at, :], semaphores.at[i])
        )
        copies[-1].start()
    for copy in copies:
        copy.wait()


def meta_body(devices_dp, part_rows, sub, capacity, width, info, own, got, marks):
    my_part, my_expert = info[MY_PART], info[MY_EXPERT]
    lanes = iota((part_rows, 128), 1)
    blocks = [(ref, at, part) for part, (ref, at) in enumerate(
        [(own, i) for i in range(sub // 2)] + [(got, i) for i in range(sub // 2)]
    )]
    counts = []
    for block in range(devices_dp):
        count = jnp.zeros((1, 128), F32)
        for ref, at, _ in blocks:
            start = (at * devices_dp + block) * part_rows
            value = ref[start : start + part_rows, width:].astype(F32)
            count = count + jnp.sum((value > 0.0).astype(F32), 0, keepdims=True)
        counts.append(count)
    for block in range(devices_dp):
        earlier = jnp.zeros((1, 128), F32)
        for before in range(devices_dp):
            ahead = (before ^ info[MY_DP]) < (block ^ info[MY_DP])
            earlier = earlier + jnp.where(ahead, counts[before], 0.0)
        for ref, at, part in blocks:
            start = (at * devices_dp + block) * part_rows
            value = ref[start : start + part_rows, width:].astype(F32)
            valid = value > 0.0
            slot = iota((part_rows, 128), 0) + (my_part ^ part) * part_rows
            kept = valid & (slot.astype(F32) + earlier < capacity)
            other = value.astype(I32) - 1 - my_expert
            mark = (lanes == my_expert).astype(F32) - (lanes == other).astype(F32)
            row = (part * devices_dp + block) * part_rows
            marks[row : row + part_rows, :] = jnp.where(
                lanes == 127, kept.astype(F32), jnp.where(valid, mark, 0.0)
            )


def expert_step(packed, mark, w_router, w_gate, w_up, w_down, stores):
    hidden_out, grad_gate_out, grad_up_out, pair_out = stores
    width = w_gate.shape[0]
    rows, grads = packed[:, :width], packed[:, width : 2 * width].astype(F32)
    kept = mark[:, 127:128] > 0.5
    mark = mark[:, : w_router.shape[0]]
    gap = jnp.sum(dot_bt(rows, w_router[...]) * mark, 1, keepdims=True)
    gate = 1.0 / (1.0 + jnp.exp(-gap))
    gate_other = 1.0 / (1.0 + jnp.exp(gap))
    gate_in = dot(rows, w_gate[...])
    up = dot(rows, w_up[...])
    act, slope = silu_parts(gate_in)
    hidden = (act * up).astype(BF)
    hidden_out(hidden)
    part = jnp.where(kept, dot(hidden, w_down[...]), 0.0).astype(BF)
    pair = jnp.where(kept, gate * grads, 0.0).astype(BF)
    pair_out(pair)
    gate_grad = jnp.sum(part.astype(F32) * grads, 1, keepdims=True)
    logit_grad = (gate * gate_other * gate_grad * mark).astype(BF)
    hidden_grad = dot_bt(pair, w_down[...])
    grad_gate = (hidden_grad * up * slope).astype(BF)
    grad_up = (hidden_grad * act).astype(BF)
    grad_gate_out(grad_gate)
    grad_up_out(grad_up)
    back = (dot_bt(grad_gate, w_gate[...]) + dot_bt(grad_up, w_up[...])).astype(BF).astype(F32)
    back = (back + dot(logit_grad, w_router[...])).astype(BF)
    return back, part, gate, dot_t(logit_grad, rows)


def store_at(ref, where=...):
    def store(value):
        ref[where] = value

    return store


def expert_body(
    tiles,
    packed_own,
    packed_got,
    marks,
    w_router,
    w_gate,
    w_up,
    w_down,
    keep,
    send,
    rows_all,
    hidden,
    grad_gate,
    grad_up,
    pair,
    gates,
    router,
):
    step = pl.program_id(0)
    mine = step < tiles
    width = rows_all.shape[1]
    packed = jnp.where(mine, packed_own[...], packed_got[...])
    rows_all[...] = packed[:, :width]
    back, part, gate, router_term = expert_step(
        packed,
        marks[...],
        w_router,
        w_gate,
        w_up,
        w_down,
        [store_at(ref) for ref in (hidden, grad_gate, grad_up, pair)],
    )

    @pl.when(step == 0)
    def _():
        router[...] = jnp.zeros_like(router)

    router[...] += router_term

    @pl.when(mine)
    def _():
        keep[:, :width] = back
        keep[:, width:] = part
        gates[...] = jnp.broadcast_to(gate, gates.shape)

    @pl.when(jnp.logical_not(mine))
    def _():
        send[:, :width] = back
        send[:, width:] = part


def expert_whole_body(
    tile,
    packed_own,
    packed_got,
    marks,
    w_router,
    w_gate,
    w_up,
    w_down,
    back_keep,
    part_keep,
    *refs,
):
    back_send, part_send = refs[:SENT_PIECES], refs[SENT_PIECES : 2 * SENT_PIECES]
    rows_all, hidden, grad_gate, grad_up, pair, gates, router = refs[2 * SENT_PIECES :]
    half = packed_own.shape[0]
    width = rows_all.shape[1]
    router[...] = jnp.zeros_like(router)

    def run(base, packed_ref, put):
        def step(index, _):
            at = pl.ds(pl.multiple_of(index * tile, tile), tile)
            place = pl.ds(pl.multiple_of(base + index * tile, tile), tile)
            packed = packed_ref[at, : 2 * width]
            rows_all[place, :] = packed[:, :width]
            back, part, gate, router_term = expert_step(
                packed,
                marks[place, :],
                w_router,
                w_gate,
                w_up,
                w_down,
                [store_at(ref, (place, slice(None))) for ref in (hidden, grad_gate, grad_up, pair)],
            )
            router[...] += router_term
            put(index, at, back, part)
            if base == 0:
                gates[at, :] = jnp.broadcast_to(gate, (tile, 128))
            return 0

        lax.fori_loop(0, half // tile, step, 0)

    def put_own(index, at, back, part):
        back_keep[at, :] = back
        part_keep[at, :] = part

    def put_got(index, at, back, part):
        rows = half // SENT_PIECES
        each = tile // rows
        for i in range(SENT_PIECES):

            @pl.when(index == i // each)
            def _(i=i):
                inside = slice(i % each * rows, (i % each + 1) * rows)
                back_send[i][...] = back[inside]
                part_send[i][...] = part[inside]

    run(0, packed_own, put_own)
    run(half, packed_got, put_got)


def combine_body(slot_pick_t, addend, *refs):
    back, keep, send = refs[:-5], refs[-5], refs[-4:]
    half, width = keep.shape
    count = back[-1].shape[0]
    rows = jnp.concatenate([ref[:count, :width] for ref in back], 0)
    total = addend[...] + dot(slot_pick_t[...], rows)
    keep[...] = total[:half]
    store_pieces(send, total[half:].astype(BF))


def result_body(count, slot_pick_t, addend, attn_keep, attn_send, *refs):
    *near, a, b, c, d, keep, send = refs
    half, width = attn_keep.shape
    rows = [ref[:count, width:] for ref in near] + [ref[...] for ref in (a, b, c, d)]
    total = addend[...] + dot(slot_pick_t[...], jnp.concatenate(rows, 0))
    keep[:, :width] = total[:half]
    send[:, :width] = total[half:].astype(BF)
    keep[:, width:] = attn_keep[...]
    send[:, width:] = attn_send[...]


def norm_back_body(
    gain, half, got, after_attn, b0, b1, after_grad, low, gain_grad
):
    width = half.shape[1]
    normed_grad = both(half, got)
    values = after_attn[...]
    root = inverse_root(values)
    grads = jnp.concatenate([b0[:, width:], b1[:, width:]], 0).astype(F32)
    total = grads + rms_backward(values, root, gain[...], normed_grad)
    after_grad[...] = total
    low[...] = total.astype(BF)
    gain_grad[...] = jnp.broadcast_to(
        0.5 * jnp.sum(normed_grad * values * root, 0, keepdims=True), gain_grad.shape
    )


def attend_back_body(
    heads,
    w_out,
    w_in_t,
    cosine,
    sine,
    weights_all,
    qkv,
    own,
    got,
    b0,
    b1,
    b2,
    b3,
    keep,
    send,
    projected_grad,
    gain_grad,
):
    width = own.shape[1]
    half = keep.shape[0]
    grads = jnp.concatenate([own[...], got[...]], 0)
    mixed_grad = dot_bt(grads, w_out[...]).astype(BF)
    scale = HD**-0.5
    cosine, sine = cosine[...], sine[...]
    parts = []
    for head, (query, keys, values) in enumerate(head_parts(qkv, heads)):
        at = head * HD
        weights = weights_all[head]
        mine = mixed_grad[:, at : at + HD]
        weight_grad = dot_bt(mine, values)
        delta = jnp.sum(weights * weight_grad, -1, keepdims=True)
        score_grad = (weights * (weight_grad - delta)).astype(BF)
        parts.append(rope_back(dot(score_grad, keys) * scale, cosine, sine))
        parts.append(rope_back(dot_t(score_grad, query) * scale, cosine, sine))
        parts.append(dot_t(weights.astype(BF), mine))
    projected_grad[...] = jnp.concatenate(parts, 1).astype(BF)
    part = dot(projected_grad[...], w_in_t[...])
    tokens = jnp.concatenate([b[:, :width] for b in (b0, b1, b2, b3)], 0).astype(F32)
    gain_grad[...] = jnp.broadcast_to(
        jnp.sum(part * tokens * inverse_root(tokens), 0, keepdims=True), gain_grad.shape
    )
    keep[...] = part[:half]
    send[...] = part[half:].astype(BF)


def last_body(
    block, gain, own, got, b0, after_grad, after_attn, near, far
):
    rows, width = own.shape[0], own.shape[1] // 2
    tokens = b0[:, :width].astype(F32)
    sums = own[...] + got[...].astype(F32)
    normed_grad = sums[:, width:]
    total = after_grad[:rows, :] + rms_backward(
        tokens, inverse_root(tokens), gain[...], normed_grad
    )
    result = after_attn[:rows, :] + sums[:, :width]
    store_halves(near, far, block, result.astype(BF), slice(0, width))
    store_halves(near, far, block, total.astype(BF), slice(width, None))


def return_body(anchor, b0, b1, b2, b3, final, grads):
    row_count, width = final.shape
    pick = (iota((row_count, row_count), 0) == anchor[...]).astype(F32).T.astype(BF)
    rows = jnp.concatenate([b[...] for b in (b0, b1, b2, b3)], 0)
    total = dot(pick, rows).astype(BF)
    final[...] = total[:, :width]
    grads[...] = total[:, width:]


def on_device(
    tokens,
    cotangent,
    gain_attn,
    w_qkv,
    w_out,
    gain_ffn,
    w_router,
    w_shared_gate,
    w_shared_up,
    w_shared_down,
    routed_gate_weight,
    routed_up_weight,
    w_expert_down,
    seq_lengths,
    token_order,
    inverse_order,
    routes,
    fill_order,
):
    devices_dp = lax.axis_size(DP)
    devices_tp = lax.axis_size(TP)
    dz = lax.axis_size("dz")
    row_count, width = tokens.shape
    block_rows = row_count // devices_dp
    shard_block = block_rows // devices_tp
    shard_rows = row_count // devices_tp
    half_rows = row_count // 2
    experts_all = w_router.shape[1]
    slot_rows = 4 * row_count // experts_all
    capacity = 5 * row_count * devices_dp // (2 * experts_all)
    inner = w_out.shape[0]
    heads = inner // HD
    per_dp = max(1, experts_all // devices_dp)
    copies = max(1, devices_dp // experts_all)
    sub = devices_tp // per_dp
    my_hi, my_lo = lax.axis_index("hi"), lax.axis_index("lo")
    my_z, my_y = lax.axis_index("dz"), lax.axis_index("dy")
    my_dp = my_z * 2 + my_y
    my_block = my_lo * 2 + my_hi
    pick = my_hi if per_dp == 2 else 0 * my_hi
    my_part = my_lo if per_dp == 2 else my_block
    part_rows = slot_rows // sub
    own_slots = devices_dp * part_rows
    all_slots = own_slots * sub
    my_expert = my_dp // copies * per_dp + pick
    chunk = width // devices_dp
    z_bits = [(my_z >> i) & 1 for i in range(log2(dz))]
    info = jnp.stack([my_block, pick, my_part, my_expert, my_dp, my_y] + z_bits).astype(I32)
    pieces = devices_dp if devices_dp <= 8 else 1

    small = all_slots <= 1024

    def fetch(weights, deps=()):
        return kernel(
            fetch_body,
            [out(w.shape, w.dtype) for w in weights],
            *[Held(w) for w in weights],
            semaphores=len(weights),
            deps=deps,
        )

    table = rope_table(row_count)
    gain_attn = gain_attn[None]
    gain_ffn = gain_ffn[None]

    half_shard = out((shard_rows // 2, 2 * width), BF)
    shard_pieces = [out((shard_rows // pieces, 2 * width), BF)] * pieces
    *sent, anchor = kernel(
        functools.partial(select_body, shard_block, devices_dp),
        shard_pieces + [out((1, row_count), I32)],
        Far(inverse_order[None]),
        Far(tokens),
        Far(cotangent),
        scalars=(info,),
    )

    def blocks_of(own, deps):
        (by_hi,) = kernel(join_body, [out(own.shape, BF)], swap(own, "hi"), deps=deps)
        by_lo = swap(own, "lo")
        return (own, by_hi, by_lo, swap(by_hi, "lo"))

    def z_steps(parts):
        got = list(parts)
        for k in (2, 3, 1):
            got[k] = lax.ppermute(parts[k], "dz", [(i, i ^ k) for i in range(dz)])
        return got

    def exchange_halves(near, far, deps=()):
        width_sent = near.shape[1]
        block = near.shape[0] // dz
        if devices_dp != 8:
            both_halves = jnp.stack([near, far]).reshape(2, dz, block, width_sent)
            stacked = both_halves.transpose(1, 0, 2, 3).reshape(devices_dp, block, width_sent)
            return [exchange_stacked(stacked).reshape(devices_dp * block, width_sent)]
        middle = kernel(
            functools.partial(middle_body, block),
            [out((2 * block, width_sent), BF)] * dz,
            near,
            swap(far, "dy"),
            deps=deps,
        )
        return z_steps(middle)

    def join(parts, deps=()):
        if not isinstance(parts, (list, tuple)):
            parts = [parts]
        if not small:
            return jnp.concatenate(parts, 0)
        rows = sum(part.shape[0] for part in parts)
        return kernel(join_body, [out((rows, parts[0].shape[1]), BF)], *parts, deps=deps)[0]

    slot_pick, slot_pick_t, bias, cosine, sine, meta = kernel(
        functools.partial(index_body, shard_block, copies, per_dp, part_rows, experts_all),
        [
            out((own_slots, row_count), BF),
            out((row_count, own_slots), BF),
            out((row_count, row_count), BF),
            out((row_count, HD), F32),
            out((row_count, HD), F32),
            out((row_count, 128), BF),
        ],
        Far(token_order[None]),
        Far(routes.T),
        Far(fill_order),
        Far(table),
        scalars=(info, seq_lengths),
        vmem=24,
    )
    router = w_router.T
    w_in_t, w_out = fetch([w_qkv.T, w_out], (slot_pick,))
    blocks = blocks_of(join(exchange(sent)), (slot_pick, w_in_t))

    slot_piece = own_slots // pieces
    near_pieces = pieces // 2 if small else pieces
    packed_width = 2 * width + 128
    got_grads = []
    if small:
        sent_grads = kernel(
            functools.partial(send_grads_body, near_pieces * slot_piece),
            [out((slot_piece, width + 128), BF)] * (pieces - near_pieces),
            slot_pick,
            meta,
            *blocks,
        )
        got_grads = exchange_some(dict(enumerate(sent_grads, near_pieces)))

    keep, *send, qkv, mixed, normed_attn, weights = kernel(
        functools.partial(attend_body, heads),
        [
            out((half_rows, width), F32),
            *[out((half_rows // 4, width), BF)] * 4,
            out((row_count, 3 * inner), BF),
            out((row_count, inner), BF),
            out((row_count, width), BF),
            out((heads, row_count, row_count), F32),
        ],
        gain_attn,
        w_in_t,
        w_out,
        cosine,
        sine,
        bias,
        *blocks,
        vmem=24,
    )

    def half_sum(keep, send, deps=()):
        (half,) = kernel(
            fold_body,
            [out((half_rows, width), BF)],
            keep,
            *[swap(piece, "lo") for piece in send],
            deps=deps,
        )
        return half, swap(half, "hi")

    half, half_got = half_sum(keep, send, got_grads[:1])
    fetched = [w_shared_gate, w_shared_up, w_shared_down, router]
    if small:
        fetched += [routed_gate_weight, routed_up_weight, w_expert_down]
    fetched = fetch(fetched, (half,))
    w_shared_gate, w_shared_up, w_shared_down, router = fetched[:4]
    if small:
        routed_gate_weight, routed_up_weight, w_expert_down = fetched[4:]
    after_attn, normed_own = kernel(
        norm_body,
        [out((half_rows, width), F32), out((half_rows, width), BF)],
        gain_ffn,
        half,
        half_got,
        blocks[0],
        blocks[1],
        deps=got_grads[1:3] + [router],
    )
    normed_got = swap(normed_own, "lo")

    far_piece = out((slot_piece, width), BF)
    sent_rows = kernel(
        send_body,
        [out((slot_piece, packed_width), BF)] * near_pieces + [far_piece] * (pieces - near_pieces),
        slot_pick,
        normed_own,
        normed_got,
        meta,
        *blocks,
    )
    got_rows = exchange(sent_rows)

    def sub_gather(parts, deps=()):
        values = join(parts, deps)
        if sub == 4:
            values = jnp.concatenate([values, swap(values, "hi")], 0)
        return values, swap(values, "lo")

    units = w_shared_gate.shape[1]
    shared_part, shared_back, grad_sgate, grad_sup, shared_hidden = kernel(
        shared_body,
        [
            out((row_count, width), F32),
            out((row_count, width), F32),
            out((row_count, units), BF),
            out((row_count, units), BF),
            out((row_count, units), BF),
        ],
        normed_own,
        normed_got,
        *blocks,
        w_shared_gate,
        w_shared_up,
        w_shared_down,
        deps=sent_rows[:1],
        vmem=24,
    )
    def tree_outs(columns_a, columns_b):
        return [
            out((dz, chunk, columns), dtype)
            for dtype in (F32, BF)
            for columns in (columns_a, columns_b)
        ]

    shared_tree = kernel(
        shared_grads_body,
        tree_outs(3 * units // 2, 3 * units // 2),
        normed_own,
        normed_got,
        *blocks,
        grad_sgate,
        grad_sup,
        shared_hidden,
        scalars=(info,),
        vmem=24,
    )

    def z_swap(values, bit):
        return lax.ppermute(values, "dz", [(i, i ^ (1 << bit)) for i in range(dz)])

    def tree_first(parts):
        keep_a, keep_b, send_a, send_b = parts
        return keep_a, swap(send_a, "dy"), keep_b, z_swap(send_b, 0)

    def tree_second(parts, deps=()):
        kept_a, got_a, kept_b, got_b = parts
        shapes = [
            out((dz // 2, chunk, kept.shape[2]), dtype)
            for dtype in (F32, BF)
            for kept in (kept_a, kept_b)
        ]
        keep_a, keep_b, send_a, send_b = kernel(
            tree_second_body, shapes, kept_a, got_a, kept_b, got_b, scalars=(info,), deps=deps
        )
        return (keep_a, z_swap(send_a, 0), keep_b, swap(send_b, "dy")), send_b

    def tree_third(parts, deps=()):
        columns = parts[0].shape[2] + parts[2].shape[2]
        shape = (dz // 4, chunk, columns)
        keep, send = kernel(
            tree_third_body,
            [out(shape, F32), out(shape, BF)],
            *parts,
            scalars=(info,),
            deps=deps,
        )
        sent, got = send, z_swap(send, 1)
        for bit in range(2, log2(dz)):
            shape = (keep.shape[0] // 2, chunk, columns)
            keep, send = kernel(
                functools.partial(tree_body, Z_BITS + bit),
                [out(shape, F32), out(shape, BF)],
                keep,
                got,
                scalars=(info,),
            )
            got = z_swap(send, bit)
        return keep, got, sent

    shared_tree = tree_first(shared_tree)
    if small:
        (packed_own,) = kernel(
            functools.partial(join_packed_body, near_pieces),
            [out((own_slots, packed_width), BF)],
            *got_rows,
            *got_grads,
            deps=(shared_tree[0],),
        )
        packed_got = swap(packed_own, "lo")
    else:
        packed_own, packed_got = sub_gather(got_rows)
    (marks,) = kernel(
        functools.partial(
            meta_body, devices_dp, part_rows, sub, capacity, 2 * width if small else 0
        ),
        [out((all_slots, 128), F32)],
        packed_own if small else packed_own[:, 2 * width :],
        packed_got if small else packed_got[:, 2 * width :],
        scalars=(info,),
    )

    hidden_units = routed_gate_weight.shape[1]
    tile = min(512, own_slots)
    tiles = all_slots // 2 // tile
    steps = 2 * tiles

    def mine_at(i):
        return (jnp.minimum(i, tiles - 1), 0)

    def other_at(i):
        return (jnp.maximum(i - tiles, 0), 0)

    def every_at(i):
        return (i, 0)

    def fixed_at(i):
        return (0, 0)

    half_slots = all_slots // 2
    expert_ins = [
        (packed_own, pl.BlockSpec((tile, packed_width), mine_at)),
        (packed_got, pl.BlockSpec((tile, packed_width), other_at)),
        (marks, pl.BlockSpec((tile, 128), every_at)),
        (router, pl.BlockSpec((experts_all, width), fixed_at)),
        (routed_gate_weight, pl.BlockSpec((width, hidden_units), fixed_at)),
        (routed_up_weight, pl.BlockSpec((width, hidden_units), fixed_at)),
        (w_expert_down, pl.BlockSpec((hidden_units, width), fixed_at)),
    ]
    expert_outs = [
        (out((half_slots, 2 * width), BF), pl.BlockSpec((tile, 2 * width), mine_at)),
        (out((half_slots, 2 * width), BF), pl.BlockSpec((tile, 2 * width), other_at)),
        (out((all_slots, width), BF), pl.BlockSpec((tile, width), every_at)),
        (out((all_slots, hidden_units), BF), pl.BlockSpec((tile, hidden_units), every_at)),
        (out((all_slots, hidden_units), BF), pl.BlockSpec((tile, hidden_units), every_at)),
        (out((all_slots, hidden_units), BF), pl.BlockSpec((tile, hidden_units), every_at)),
        (out((all_slots, width), BF), pl.BlockSpec((tile, width), every_at)),
        (out((half_slots, 128), F32), pl.BlockSpec((tile, 128), mine_at)),
        (out((experts_all, width), F32), pl.BlockSpec((experts_all, width), fixed_at)),
    ]

    def expert_kernel(*refs):
        pltpu.emit_pipeline(
            functools.partial(expert_body, tiles),
            grid=(steps,),
            in_specs=[spec for _, spec in expert_ins],
            out_specs=[spec for _, spec in expert_outs],
        )(*refs)

    expert_args = [value for value, _ in expert_ins]
    expert_shapes = [shape for shape, _ in expert_outs]
    if small:
        piece = out((half_slots // SENT_PIECES, width), BF)
        results = kernel(
            functools.partial(expert_whole_body, tile),
            [out((half_slots, width), BF)] * 2 + [piece] * 2 * SENT_PIECES + expert_shapes[2:],
            *expert_args,
            vmem=22,
        )
        keep, part_keep, *results = results
        send, part_send = results[:SENT_PIECES], results[SENT_PIECES : 2 * SENT_PIECES]
        results = [keep, send] + list(results[2 * SENT_PIECES :])
    else:
        hbm_spec = pl.BlockSpec(memory_space=pltpu.HBM)
        results = pl.pallas_call(
            expert_kernel,
            in_specs=[hbm_spec] * len(expert_ins),
            out_specs=tuple([hbm_spec] * len(expert_outs)),
            out_shape=tuple(at_hbm(shape) for shape in expert_shapes),
            compiler_params=pltpu.CompilerParams(vmem_limit_bytes=44 * MIB),
            cost_estimate=COST,
            name="expert_body",
        )(*[in_hbm(value) for value in expert_args])
    (
        keep,
        send,
        rows_all,
        expert_hidden,
        grad_egate,
        grad_eup,
        pair_grads,
        gates,
        router_part,
    ) = results

    def sub_scatter(keep, send):
        total = keep.astype(F32) + swap(send, "lo").astype(F32)
        return total[:own_slots] + swap(total[own_slots:].astype(BF), "hi").astype(F32)

    if small:
        got = [swap(piece, "lo") for piece in send]
        part_got = [swap(piece, "lo") for piece in part_send]
        back_far = kernel(
            add_far_body,
            [far_piece] * (pieces - near_pieces),
            keep,
            *got[SENT_PIECES // 2 :],
            deps=(shared_tree[1], shared_tree[3]),
        )
        back_near = kernel(
            add_near_body,
            [out((slot_piece, 2 * width), BF)] * near_pieces,
            keep,
            part_keep,
            gates,
            *got[: SENT_PIECES // 2],
            *part_got[: SENT_PIECES // 2],
        )
        sent_back = list(back_near) + list(back_far)
        sent_parts = kernel(
            part_far_body,
            [far_piece] * (pieces - near_pieces),
            part_keep,
            gates,
            *part_got[SENT_PIECES // 2 :],
            deps=sent_back[:1],
        )
    else:
        total = sub_scatter(keep, send)
        sent_back = [total[:, :width].astype(BF)]
        sent_parts = [(gates[:own_slots, :1] * total[:, width:]).astype(BF)]
        shared_tree, _ = tree_second(shared_tree)

    def weight_grad(left, right, deps=()):
        if not small:
            return dot_t(left, right)
        shape = (left.shape[1], right.shape[1])
        vmem_spec = pl.BlockSpec(memory_space=pltpu.VMEM)
        return pl.pallas_call(
            lambda *refs: weight_grad_body(refs[0], refs[1], *refs[-3:]),
            out_shape=pltpu.HBM(shape, F32),
            in_specs=[vmem_spec] * 2 + [pl.BlockSpec(memory_space=pl.ANY)] * len(deps),
            out_specs=pl.BlockSpec(memory_space=pltpu.HBM),
            scratch_shapes=[
                pltpu.VMEM(shape, F32),
                pltpu.SemaphoreType.DMA((shape[0] // 256,)),
            ],
            compiler_params=pltpu.CompilerParams(vmem_limit_bytes=12 * MIB),
            cost_estimate=COST,
            name="weight_grad",
        )(in_vmem(left), in_vmem(right), *deps)

    grad_w_expert_gate = weight_grad(rows_all, grad_egate, (sent_back[0],))
    got_back = exchange(sent_back)
    if small:
        got_parts = exchange_some(dict(enumerate(sent_parts, near_pieces)))
        shared_tree, _ = tree_second(shared_tree, sent_back[:1])
    else:
        got_parts = exchange(sent_parts)
    shared_keep, shared_got, shared_sent = tree_third(shared_tree)

    keep, *send = kernel(
        combine_body,
        [out((half_rows, width), F32)] + [out((half_rows // 4, width), BF)] * 4,
        slot_pick_t,
        shared_back,
        *got_back,
        deps=(
            Far(grad_w_expert_gate),
        ),
    )
    half, half_got = half_sum(keep, send, got_parts[:1] if small else ())

    def own_sum(keep, send, deps=()):
        own, send = kernel(
            fold_own_body,
            [out((shard_rows, width), F32), out((shard_rows, width), BF)],
            keep,
            swap(send, "lo"),
            deps=deps,
        )
        return own, send

    after_grad, after_grad_own, gain_ffn_part = kernel(
        norm_back_body,
        [out((half_rows, width), F32), out((half_rows, width), BF), out((8, width), F32)],
        gain_ffn,
        half,
        half_got,
        after_attn,
        blocks[0],
        blocks[1],
        deps=got_parts[1:3] + [shared_tree[1], shared_tree[3]] if small else (),
    )
    after_grad_got = swap(after_grad_own, "lo")

    keep, send, projected_grad, gain_attn_part = kernel(
        functools.partial(attend_back_body, heads),
        [
            out((half_rows, width), F32),
            out((half_rows, width), BF),
            out((row_count, 3 * inner), BF),
            out((8, width), F32),
        ],
        w_out,
        w_in_t,
        cosine,
        sine,
        weights,
        qkv,
        after_grad_own,
        after_grad_got,
        *blocks,
        vmem=24,
    )
    if small:
        keep, send = kernel(
            functools.partial(result_body, slot_piece),
            [out((half_rows, 2 * width), F32), out((half_rows, 2 * width), BF)],
            slot_pick_t,
            shared_part,
            keep,
            send,
            *got_back[:near_pieces],
            *got_parts,
        )
    else:
        result_part = shared_part + dot(slot_pick_t, got_parts[0])
        keep = jnp.concatenate([result_part[:half_rows], keep], 1)
        send = jnp.concatenate([result_part[half_rows:].astype(BF), send], 1)
    bottom_got = swap(send, "lo")
    last_columns = 4 * inner + 128
    last_tree = kernel(
        functools.partial(last_grads_body, experts_all),
        tree_outs(512, last_columns - 512),
        normed_attn,
        projected_grad,
        after_grad_own,
        after_grad_got,
        mixed,
        gain_ffn_part,
        gain_attn_part,
        router_part,
        scalars=(info,),
        vmem=24,
        deps=(send,),
    )
    last_tree = tree_first(last_tree)
    own, send = kernel(
        fold_own_body,
        [out((shard_rows, 2 * width), F32), out((shard_rows, 2 * width), BF)],
        keep,
        bottom_got,
    )
    grad_sgate, grad_sup, grad_sdown = kernel(
        shared_end_body,
        [Far(out((chunk, units), F32))] * 3,
        shared_keep,
        shared_got,
    )
    near, far = kernel(
        functools.partial(last_body, shard_block),
        [half_shard, half_shard],
        gain_attn,
        own,
        swap(send, "hi"),
        blocks[0],
        after_grad,
        after_attn,
    )
    last_tree, last_sent = tree_second(last_tree, (near,))
    grad_w_expert_down = weight_grad(expert_hidden, pair_grads, (last_sent,))
    got_last = exchange_halves(near, far, (last_sent,))
    last_keep, last_got, last_sent = tree_third(last_tree, got_last[:1])
    small_rows = experts_all + 8
    grad_qkv, grad_out, sums = kernel(
        functools.partial(last_end_body, small_rows),
        [
            Far(out((chunk, 3 * inner), F32)),
            Far(out((inner, chunk), F32)),
            out((small_rows, chunk), F32),
        ],
        last_keep,
        last_got,
    )
    got_last = join(got_last, (last_sent, Far(grad_sgate), Far(grad_w_expert_down)))
    grad_w_expert_up = weight_grad(rows_all, grad_eup, (got_last,))
    final, grad_tokens = kernel(
        return_body,
        [Far(out((row_count, width), BF)), Far(out((row_count, width), BF))],
        anchor,
        *blocks_of(got_last, (sums, Far(grad_w_expert_up))),
    )

    gain_ffn_sum, gain_attn_sum, router_sum = kernel(
        small_end_body,
        [Far(out((1, chunk), F32)), Far(out((1, chunk), F32)), Far(out((experts_all, chunk), F32))],
        sums,
        *[lax.ppermute(sums, TP, [(i, i ^ k) for i in range(4)]) for k in (1, 2, 3)],
        deps=(Far(final),),
    )
    return (
        final,
        grad_tokens,
        gain_attn_sum.reshape(chunk),
        grad_qkv,
        grad_out,
        gain_ffn_sum.reshape(chunk),
        router_sum.T,
        grad_sgate,
        grad_sup,
        grad_sdown.T,
        grad_w_expert_gate,
        grad_w_expert_up,
        grad_w_expert_down,
    )


def solution(mesh):
    devices_dp, devices_tp = mesh.shape["dp"], mesh.shape["tensor"]
    fine = Mesh(
        mesh.devices.reshape(devices_dp // 2, 2, devices_tp // 2, 2), ("dz", "dy", "hi", "lo")
    )
    every = DP + TP
    return jax.shard_map(
        on_device,
        mesh=fine,
        in_specs=(
            P(DP, None),
            P(DP, None),
            P(),
            P(None, TP),
            P(TP, None),
            P(),
            P(),
            P(None, TP),
            P(None, TP),
            P(TP, None),
            P(None, every),
            P(None, every),
            P(every, None),
            P(DP, None),
            P(DP),
            P(DP),
            P(DP, None),
            P(DP, None),
        ),
        out_specs=(
            P(DP, None),
            P(DP, None),
            P(DP),
            P(DP, TP),
            P(TP, DP),
            P(DP),
            P(DP, None),
            P(DP, TP),
            P(DP, TP),
            P(TP, DP),
            P(None, every),
            P(None, every),
            P(every, None),
        ),
        check_vma=False,
    )
```
